32 devices in a mesh: dp: 4 (over z), blk: 4 (over x, core), head: 2 (over y).
Axes of the slice: x: 2, y: 2, z: 4, core: 2. Of those that a mesh axis runs over, the one named last changes fastest.
Arguments:
- tokens: bfloat16 [4, 1024, 1024], P('dp', ('blk', 'head')), may hold values from -6 to 6
- segment_ids: int32 [4, 1024], P('dp', 'blk'), may hold values from -1 to 15, as said below
- cotangent: bfloat16 [4, 1024, 1024], P('dp', ('blk', 'head')), may hold values from -6 to 6
- w_query: bfloat16 [1024, 1024], P(('blk', 'head')), may hold values from -0.1875 to 0.1875
- w_key: bfloat16 [1024, 1024], P(('blk', 'head')), may hold values from -0.1875 to 0.1875
- w_value: bfloat16 [1024, 1024], P(('blk', 'head')), may hold values from -0.1875 to 0.1875
- w_out: bfloat16 [1024, 1024], P(('blk', 'head')), may hold values from -6 to 6
- w_in: bfloat16 [1024, 4096], P(('blk', 'head')), may hold values from -0.1875 to 0.1875
- w_back: bfloat16 [4096, 1024], P(('blk', 'head')), may hold values from -0.09375 to 0.09375
- bias_query: bfloat16 [1024], P(('blk', 'head')), may hold values from -3 to 3
- bias_value: bfloat16 [1024], P(('blk', 'head')), may hold values from -3 to 3
- bias_out: bfloat16 [1024], P(('blk', 'head')), may hold values from -3 to 3
- bias_in: bfloat16 [4096], P(('blk', 'head')), may hold values from -3 to 3
- bias_back: bfloat16 [1024], P(('blk', 'head')), may hold values from -3 to 3
- first_gain: bfloat16 [1024], P(('blk', 'head')), may hold values from 0.5 to 1.5
- first_shift: bfloat16 [1024], P(('blk', 'head')), may hold values from -3 to 3
- second_gain: bfloat16 [1024], P(('blk', 'head')), may hold values from 0.5 to 1.5
- second_shift: bfloat16 [1024], P(('blk', 'head')), may hold values from -3 to 3
Outputs:
- layer_output: bfloat16 [4, 1024, 1024], P('dp', ('blk', 'head'))
- input_grad: float32 [4, 1024, 1024], P('dp', ('blk', 'head'))
- grad_w_query: float32 [1024, 1024], P(('blk', 'head'))
- grad_w_key: float32 [1024, 1024], P(('blk', 'head'))
- grad_w_value: float32 [1024, 1024], P(('blk', 'head'))
- grad_w_out: float32 [1024, 1024], P(('blk', 'head'))
- grad_w_in: float32 [1024, 4096], P(('blk', 'head'))
- grad_w_back: float32 [4096, 1024], P(('blk', 'head'))
- grad_bias_query: float32 [1024], P(('blk', 'head'))
- grad_bias_value: float32 [1024], P(('blk', 'head'))
- grad_bias_out: float32 [1024], P(('blk', 'head'))
- grad_bias_in: float32 [4096], P(('blk', 'head'))
- grad_bias_back: float32 [1024], P(('blk', 'head'))
- grad_first_gain: float32 [1024], P(('blk', 'head'))
- grad_first_shift: float32 [1024], P(('blk', 'head'))
- grad_second_gain: float32 [1024], P(('blk', 'head'))
- grad_second_shift: float32 [1024], P(('blk', 'head'))
The draws below stay inside these ranges and needn't reach their ends.
Inputs may be any that keep to these rules, and one draw needn't show every extreme that they name: `segment_ids`: within a sequence the ids start at 0 and rise by one from document to document before the slack; each document has 64 to 512 positions but for the last one, which the sequence's end or its slack cuts; the last 1 to 64 positions of every sequence are slack, marked -1; one sequence of the whole batch, drawn from the seed, is a single document up to its slack, and another one is packed with documents of exactly 64 positions and has a single slack position.
All inputs are finite; a program needn't handle non-finite values.
Results may differ from the reference program's by a relative error of at most 0.025.
Values may be sent and summed in bfloat16 or wider, within the bound.
A program may use at most 256 MiB of HBM per device.

```python
import math
import jax
import jax.numpy as jnp
from jax import lax

D = 1024
H = 16
HD = 64
FF = 4096
SEQ_TOK = 128
SEQS = 4
LEN = 1024
DOC_LO = 64
DOC_HI = 512


def draw_segment_ids(key, part):
    key = jax.random.fold_in(key, 7)
    key_lengths, key_slack, key_pick, key_other = jax.random.split(key, 4)
    doc_count = LEN // DOC_LO + 2
    lengths = jax.random.randint(key_lengths, (SEQS, doc_count), DOC_LO, DOC_HI + 1)
    bounds = jnp.cumsum(lengths, axis=1)
    places = jnp.arange(LEN, dtype=jnp.int32)
    numbers = jnp.sum((bounds[:, None, :] <= places[None, :, None]).astype(jnp.int32), axis=2)
    chosen = jax.random.randint(key_pick, (), 0, SEQS)
    packed_full = (chosen + 1 + jax.random.randint(key_other, (), 0, SEQS - 1)) % SEQS
    rows_all = jnp.arange(SEQS, dtype=jnp.int32)
    single_doc = rows_all == chosen
    shortest = rows_all == packed_full
    numbers = jnp.where(single_doc[:, None], 0, numbers)
    numbers = jnp.where(shortest[:, None], (places // DOC_LO)[None, :], numbers)
    slack_len = jax.random.randint(key_slack, (SEQS, 1), 1, SEQ_TOK // 2 + 1)
    slack_len = jnp.where(shortest[:, None], 1, slack_len)
    return jnp.where(places[None, :] >= LEN - slack_len, -1, numbers).astype(jnp.int32)


def strengthened(result, rng, source, target, parts, factor):
    def block_of(axis_at):
        return (jnp.arange(result.shape[axis_at]) // (result.shape[axis_at] // parts)).reshape((-1,) + (1,) * (result.ndim - 1 - axis_at))

    first = jax.random.permutation(rng, parts)[block_of(target)]
    second = (block_of(target) + parts // 2) % parts
    return jnp.where((block_of(source) == first) | (block_of(source) == second), factor * result, result)


def level_of(stream_key, shape, cuts, smallest, top_value):
    def one(dim, shards_of):
        steps = jax.random.uniform(jax.random.fold_in(jax.random.fold_in(stream_key, 6), dim), (shards_of,), jnp.float32, smallest / len(cuts), top_value / len(cuts))
        return jnp.repeat(jnp.exp(steps), shape[dim] // shards_of).reshape((-1,) + (1,) * (len(shape) - dim - 1))

    loudness = one(*cuts[0])
    for cut in cuts[1:]:
        loudness = loudness * one(*cut)
    return loudness


def noise(own_key, shape, scale, limit, shards=(), kind=jnp.bfloat16):
    level = level_of(own_key, shape, shards, -0.22, 0.18) if shards else 1.0
    entries = jax.random.normal(own_key, shape, jnp.float32) * scale * level
    return jnp.minimum(jnp.maximum(entries, -limit), limit).astype(kind)


def bell_draw_with(stream_key, dims, scale, reach, cuts, heavy, kind=jnp.bfloat16):
    result = scale * jax.random.normal(stream_key, dims, jnp.float32)
    if cuts:
        result = result * level_of(stream_key, dims, cuts, -0.22, 0.18)
    return jnp.clip(strengthened(result, jax.random.fold_in(stream_key, 3), *heavy), -reach, reach).astype(kind)


def setup_inputs(seed: int = 0) -> dict:
    key_list = jax.random.split(jax.random.key(seed), 19)
    tokens = noise(key_list[0], (SEQS, LEN, D), 1.0, 6.0, ((0, 4), (1, 8)))
    segment_ids = draw_segment_ids(jax.random.fold_in(key_list[18], 71), 0)
    cotangent = bell_draw_with(key_list[2], (SEQS, LEN, D), 1.0, 6.0, ((0, 4), (1, 8)), (1, 2, 8, 2.0))
    w_query = noise(key_list[3], (D, D), D ** -0.5, 0.1875, ((0, 8),))
    w_key = noise(key_list[4], (D, D), D ** -0.5, 0.1875, ((0, 8),))
    w_value = noise(key_list[5], (D, D), D ** -0.5, 0.1875, ((0, 8),))
    w_out = noise(key_list[6], (D, D), 1 ** -0.5, 6.0, ((0, 8),))
    w_in = noise(key_list[7], (D, FF), D ** -0.5, 0.1875, ((0, 8),))
    w_back = noise(key_list[8], (FF, D), FF ** -0.5, 0.09375, ((0, 8),))
    bias_query = noise(key_list[9], (D,), 0.5, 3.0, ((0, 8),))
    bias_value = noise(key_list[10], (D,), 0.5, 3.0, ((0, 8),))
    bias_out = noise(key_list[11], (D,), 0.5, 3.0, ((0, 8),))
    bias_in = noise(key_list[12], (FF,), 0.5, 3.0, ((0, 8),))
    bias_back = noise(key_list[13], (D,), 0.5, 3.0, ((0, 8),))
    first_gain = jnp.clip(1.0 + 0.1 * jax.random.normal(key_list[14], (D,), jnp.float32), 0.5, 1.5).astype(jnp.bfloat16)
    first_shift = noise(key_list[15], (D,), 0.5, 3.0, ((0, 8),))
    second_gain = jnp.clip(1.0 + 0.1 * jax.random.normal(key_list[16], (D,), jnp.float32), 0.5, 1.5).astype(jnp.bfloat16)
    second_shift = noise(key_list[17], (D,), 0.5, 3.0, ((0, 8),))
    return dict(tokens=tokens, segment_ids=segment_ids, cotangent=cotangent, w_query=w_query, w_key=w_key, w_value=w_value, w_out=w_out, w_in=w_in, w_back=w_back, bias_query=bias_query, bias_value=bias_value, bias_out=bias_out, bias_in=bias_in, bias_back=bias_back, first_gain=first_gain, first_shift=first_shift, second_gain=second_gain, second_shift=second_shift)


@jax.custom_vjp
def low(v):
    return lax.optimization_barrier(v.astype(jnp.bfloat16)).astype(jnp.float32)

@jax.custom_vjp
def low_back(v):
    return v

def low_keep(v):
    return (low(v), None)

def low_pass(kept, grad):
    return (grad,)

def back_keep(v):
    return (v, None)

def back_low(kept, grad):
    return (low(grad),)
low.defvjp(low_keep, low_pass)
low_back.defvjp(back_keep, back_low)

def matmul(left_side, right_side):
    return jnp.dot(left_side, right_side, precision=lax.Precision.HIGHEST, preferred_element_type=jnp.float32)

def layer_norm(value_rows, gain_row, shift_row):
    centre = lax.optimization_barrier(jnp.mean(value_rows, -1, keepdims=True))
    centred = value_rows - centre
    spread = lax.optimization_barrier(jnp.mean(centred * centred, -1, keepdims=True))
    return centred * lax.rsqrt(spread + 1e-05) * gain_row + shift_row

def attend(queries, keys_all, values_all, segments):
    length = queries.shape[0]
    block_rows = math.gcd(length, 512)
    valid_keys = segments >= 0

    def one_block(block_in):
        query_block, block_ids = block_in
        scores = low_back(jnp.einsum('qhd,khd->hqk', query_block, keys_all, precision=lax.Precision.HIGHEST))
        allowed = ((block_ids[:, None] == segments[None, :]) & valid_keys[None, :])[None]
        masked = jnp.where(allowed, scores, -1e+30)
        row_max = lax.optimization_barrier(jnp.max(masked, -1, keepdims=True))
        row_sum = lax.optimization_barrier(jnp.sum(jnp.where(allowed, jnp.exp(masked - row_max), 0.0), -1, keepdims=True))
        log_sum = row_max + jnp.log(jnp.maximum(row_sum, 1.0))
        weights_now = jnp.where(allowed, jnp.exp(masked - log_sum), 0.0)
        return jnp.einsum('hqk,khd->qhd', low(weights_now), values_all, precision=lax.Precision.HIGHEST)
    blocks_out = lax.map(jax.checkpoint(one_block), (queries.reshape(-1, block_rows, H, HD), segments.reshape(-1, block_rows)))
    return blocks_out.reshape(length, H * HD)

def layer(params, inputs_now, segments):
    w_query, w_key, w_value, w_out, w_in, w_back, bias_query, bias_value, bias_out, bias_in, bias_back, first_gain, first_shift, second_gain, second_shift = params
    length = inputs_now.shape[0]
    queries = low(low_back((matmul(inputs_now, w_query) + bias_query) * 0.125))
    keys_all = low(low_back(matmul(inputs_now, w_key)))
    values_all = low(low_back(matmul(inputs_now, w_value) + bias_value))
    context = attend(queries.reshape(length, H, HD), keys_all.reshape(length, H, HD), values_all.reshape(length, H, HD), segments)
    context = low(low_back(context))
    first_norm = layer_norm(inputs_now + low_back(matmul(context, w_out) + bias_out), first_gain, first_shift)
    inner_rows = low_back(matmul(low(first_norm), w_in) + bias_in)
    hidden_low = low(jax.nn.gelu(inner_rows, approximate=False))
    second_sum = first_norm + low_back(matmul(hidden_low, w_back) + bias_back)
    return layer_norm(second_sum, second_gain, second_shift)

def reference(tokens, segment_ids, cotangent, w_query, w_key, w_value, w_out, w_in, w_back, bias_query, bias_value, bias_out, bias_in, bias_back, first_gain, first_shift, second_gain, second_shift):
    params = tuple((weight.astype(jnp.float32) for weight in (w_query, w_key, w_value, w_out, w_in, w_back, bias_query, bias_value, bias_out, bias_in, bias_back, first_gain, first_shift, second_gain, second_shift)))

    def per_sequence(totals, inputs_all):
        inputs_now, segments, grad_output = inputs_all
        output_now, pull_back = jax.vjp(lambda weights_in, rows_in: layer(weights_in, rows_in, segments), params, inputs_now.astype(jnp.float32))
        grads_now, grad_inputs = pull_back(grad_output.astype(jnp.float32))
        totals = tuple((first_one + second_one for first_one, second_one in zip(totals, grads_now)))
        return (totals, (output_now.astype(jnp.bfloat16), grad_inputs))
    zeros_start = tuple((jnp.zeros_like(weight) for weight in params))
    totals, (outputs_all, grads_all) = lax.scan(per_sequence, zeros_start, (tokens, segment_ids, cotangent))
    grad_wq, grad_wk, grad_wv, grad_wo, grad_wi, grad_wb, grad_bq, grad_bv, grad_bo, grad_bi, grad_bb, grad_g1, grad_s1, grad_g2, grad_s2 = totals
    return (outputs_all, grads_all, grad_wq, grad_wk, grad_wv, grad_wo, grad_wi, grad_wb, grad_bq, grad_bv, grad_bo, grad_bi, grad_bb, grad_g1, grad_s1, grad_g2, grad_s2)
```

```python
from functools import partial

import jax
import jax.numpy as jnp
from jax import lax
from jax.sharding import PartitionSpec as P

HD = 64
BF = jnp.bfloat16
F32 = jnp.float32
GROUP = ("blk", "head")


def mm(a, b, dims):
    return lax.dot_general(a, b, (dims, ((), ())), preferred_element_type=F32)


NN = ((1,), (0,))
NT = ((1,), (1,))
TN = ((0,), (0,))


def norm_parts(v):
    c = v - jnp.mean(v, -1, keepdims=True)
    r = lax.rsqrt(jnp.mean(c * c, -1, keepdims=True) + 1e-05)
    return c * r, r


def norm_back(e, n, r):
    return r * (e - jnp.mean(e, -1, keepdims=True) - n * jnp.mean(e * n, -1, keepdims=True))


def sharded_plan(
    tokens, segment_ids, cotangent,
    w_query, w_key, w_value, w_out, w_in, w_back,
    bias_query, bias_value, bias_out, bias_in, bias_back,
    first_gain, first_shift, second_gain, second_shift,
):
    tokens = tokens[0]
    head_at = lax.axis_index("head")
    rows_here = tokens.shape[0]
    ids_own = lax.dynamic_slice(segment_ids[0], (head_at * rows_here,), (rows_here,))
    vecs = jnp.stack([bias_out, bias_back, first_gain, first_shift, second_gain, second_shift])
    gather = partial(lax.all_gather, axis_name=GROUP, axis=0, tiled=True)
    to_cols = partial(lax.all_to_all, axis_name=GROUP, split_axis=1, concat_axis=0, tiled=True)
    to_rows = partial(lax.all_to_all, axis_name=GROUP, split_axis=0, concat_axis=1, tiled=True)
    scatter = partial(lax.psum_scatter, axis_name=GROUP, scatter_dimension=0, tiled=True)
    ids = gather(ids_own)
    vec_full = lax.all_gather(vecs, GROUP, axis=1, tiled=True).astype(F32)
    b_out, b_back, g1, s1, g2, s2 = [vec_full[i][None] for i in range(6)]
    tok_all = gather(tokens)
    w_qkv = to_cols(jnp.concatenate([w.reshape(rows_here, -1, 128) for w in (w_query, w_key, w_value)], 2).reshape(rows_here, -1))
    width = w_qkv.shape[1] // 3
    wq, wk, wv = w_qkv[:, :width], w_qkv[:, width:2 * width], w_qkv[:, 2 * width:]
    q = ((mm(tok_all, wq, NN) + bias_query.astype(F32)) * 0.125).astype(BF)
    k = mm(tok_all, wk, NN).astype(BF)
    v = (mm(tok_all, wv, NN) + bias_value.astype(F32)).astype(BF)
    allowed = (ids[:, None] == ids[None, :]) & (ids[:, None] >= 0)
    heads = width // HD
    probs, ctx = [], []
    for h in range(heads):
        sl = slice(h * HD, (h + 1) * HD)
        s = jnp.where(allowed, mm(k[:, sl], q[:, sl], NT), -1e30)
        top = jnp.max(s, 0, keepdims=True)
        ex = jnp.where(allowed, jnp.exp(s - top), 0.0)
        total = jnp.maximum(jnp.sum(ex, 0, keepdims=True), 1.0)
        p = ex * (1.0 / total)
        probs.append(p)
        ctx.append(mm(p.astype(BF), v[:, sl], TN))
    ctx = jnp.concatenate(ctx, 1).astype(BF)
    ctx_tok = to_rows(ctx)
    out_full = gather(w_out)
    h1 = tokens.astype(F32) + mm(ctx_tok, out_full, NN) + b_out
    n1, r1 = norm_parts(h1)
    y1 = n1 * g1 + s1
    y1_all = gather(y1.astype(BF))
    in_cols = to_cols(w_in)
    z = mm(y1_all, in_cols, NN) + bias_in.astype(F32)
    gelu = partial(jax.nn.gelu, approximate=False)
    hidden, gelu_pull = jax.vjp(gelu, z)
    hidden = hidden.astype(BF)
    h2 = y1 + scatter(mm(hidden, w_back, NN).astype(BF)).astype(F32) + b_back
    n2, r2 = norm_parts(h2)
    output = (n2 * g2 + s2).astype(BF)
    cot = cotangent[0].astype(F32)
    dh2 = norm_back(cot * g2, n2, r2)
    df_all = gather(dh2.astype(BF))
    d_back = mm(hidden, df_all, TN)
    dz = gelu_pull(mm(df_all, w_back, NT))[0].astype(BF)
    d_in = to_rows(mm(y1_all, dz, TN).astype(BF))
    dy1 = dh2 + scatter(mm(dz, in_cols, NT).astype(BF)).astype(F32)
    dh1 = norm_back(dy1 * g1, n1, r1)
    da = dh1.astype(BF)
    da_all = gather(da)
    d_out = mm(ctx, da_all, TN)
    dc = to_cols(mm(da, out_full, NT).astype(BF))
    dq, dk, dv = [], [], []
    for h in range(heads):
        sl = slice(h * HD, (h + 1) * HD)
        p = probs[h]
        dp = mm(v[:, sl], dc[:, sl], NT)
        delta = jnp.sum(p * dp, 0, keepdims=True)
        ds = (p * (dp - delta)).astype(BF)
        dq.append(mm(ds, k[:, sl], TN).astype(BF) * 0.125)
        dk.append(mm(ds, q[:, sl], NN).astype(BF))
        dv.append(mm(p.astype(BF), dc[:, sl], NN).astype(BF))
    dq, dk, dv = [jnp.concatenate(x, 1) for x in (dq, dk, dv)]
    d_qkv = jnp.concatenate([dq, dk, dv], 1)
    dw_qkv = to_rows(mm(tok_all, d_qkv, TN).astype(BF)).reshape(rows_here, -1, 3, width)
    input_grad = dh1 + scatter(mm(d_qkv, w_qkv, NT).astype(BF)).astype(F32)
    me = lax.axis_index("blk") * lax.axis_size("head") + head_at

    def own_cols(x):
        return lax.dynamic_slice(x, (0, me * rows_here), (x.shape[0], rows_here))

    col = lambda x: jnp.sum(x.astype(F32), 0, keepdims=True)
    small = jnp.concatenate(
        [col(cot * n2), col(cot), col(dy1 * n1), col(dy1)], 0
    )
    small = lax.psum_scatter(small, GROUP, scatter_dimension=1, tiled=True)
    small = jnp.concatenate(
        [small, col(dq), col(dv), col(own_cols(da_all)), col(own_cols(df_all)), col(dz).reshape(-1, rows_here)], 0
    )
    small = jnp.concatenate([small, jnp.zeros((-small.shape[0] % 16, rows_here), F32)], 0)
    wide = w_back.shape[1]
    packed = jnp.concatenate(
        [
            dw_qkv.transpose(0, 2, 1, 3).reshape(-1, wide),
            d_out.astype(BF),
            d_in.reshape(-1, wide),
            d_back.astype(BF),
            small.astype(BF).reshape(-1, wide),
        ],
        0,
    )
    total = lax.psum(packed, "dp").astype(F32)
    at = 3 * rows_here
    sq = total[:at].reshape(rows_here, 3, wide)
    t_out = total[at:at + rows_here]
    at += rows_here
    t_in = total[at:at + d_in.size // wide].reshape(d_in.shape)
    at += d_in.size // wide
    t_back = total[at:at + d_back.shape[0]]
    at += d_back.shape[0]
    sv = total[at:].reshape(small.shape)
    return (
        output[None], input_grad[None], sq[:, 0], sq[:, 1], sq[:, 2], t_out, t_in, t_back,
        sv[4], sv[5], sv[6], sv[8:8 + w_back.shape[0] // rows_here].reshape(-1), sv[7], sv[2], sv[3], sv[0], sv[1],
    )


def pick_plan(mesh):
    group = mesh.shape["blk"] * mesh.shape["head"]
    return sharded_plan if group == 8 else general_plan


def flat_dot(left_side, right_side):
    return jnp.dot(
        left_side.reshape(-1, left_side.shape[-1]), right_side, preferred_element_type=jnp.float32
    )


def inner_dot(left_side, right_side):
    return jnp.einsum(
        "ra,rb->ab",
        left_side.reshape(-1, left_side.shape[-1]),
        right_side.reshape(-1, right_side.shape[-1]),
        preferred_element_type=jnp.float32,
    )


def layer_norm(value_rows, gain_row, shift_row):
    centre = jnp.mean(value_rows, -1, keepdims=True)
    centred = value_rows - centre
    spread = jnp.mean(centred * centred, -1, keepdims=True)
    return centred * lax.rsqrt(spread + 1e-05) * gain_row + shift_row


def head_view(array_in):
    return array_in.reshape(array_in.shape[0], array_in.shape[1], -1, HD)


def allowed_pairs(query_ids, key_ids):
    same_doc = (query_ids[:, :, None] == key_ids[:, None, :]) & (key_ids[:, None, :] >= 0)
    return same_doc[:, None]


def forward_step(state_now, arrived, local_data):
    running_max, running_sum, weighted = state_now
    key_block, value_block, key_ids = arrived
    query_block, query_ids = local_data
    scores = jnp.einsum(
        "gqhd,gkhd->ghqk",
        head_view(query_block),
        head_view(key_block),
        preferred_element_type=jnp.float32,
    )
    allowed = allowed_pairs(query_ids, key_ids)
    masked = jnp.where(allowed, scores, -1e30)
    new_max = jnp.maximum(running_max, jnp.max(masked, -1))
    exponents = jnp.where(allowed, jnp.exp(masked - new_max[..., None]), 0.0)
    running_sum = jnp.sum(exponents, -1)
    weighted = jnp.einsum(
        "ghqk,gkhd->ghqd",
        exponents.astype(jnp.bfloat16),
        head_view(value_block),
        preferred_element_type=jnp.float32,
    )
    return (new_max, running_sum, weighted)


def probabilities(query_block, key_block, query_ids, key_ids, log_sums):
    scores = jnp.einsum(
        "gqhd,gkhd->ghqk",
        head_view(query_block),
        head_view(key_block),
        preferred_element_type=jnp.float32,
    )
    allowed = allowed_pairs(query_ids, key_ids)
    masked = jnp.where(allowed, scores, -1e30)
    return jnp.where(allowed, jnp.exp(masked - log_sums.transpose(0, 2, 1)[..., None]), 0.0)


def score_grads(weights_now, grad_block, value_block, deltas):
    grad_weights = jnp.einsum(
        "gqhd,gkhd->ghqk",
        head_view(grad_block),
        head_view(value_block),
        preferred_element_type=jnp.float32,
    )
    return (weights_now * (grad_weights - deltas.transpose(0, 2, 1)[..., None])).astype(
        jnp.bfloat16
    )


def heads_to_rows(array_in):
    return array_in.transpose(0, 2, 1, 3).reshape(array_in.shape[0], array_in.shape[2], -1)


def general_plan(
    tokens,
    segment_ids,
    cotangent,
    w_query,
    w_key,
    w_value,
    w_out,
    w_in,
    w_back,
    bias_query,
    bias_value,
    bias_out,
    bias_in,
    bias_back,
    first_gain,
    first_shift,
    second_gain,
    second_shift,
):
    (
        query_full,
        key_full,
        value_full,
        out_full,
        in_full,
        back_full,
        query_bias,
        value_bias,
        out_bias,
        in_bias,
        back_bias,
        gain_one,
        shift_one,
        gain_two,
        shift_two,
    ) = (
        lax.all_gather(w_query, ("blk", "head"), axis=0, tiled=True),
        lax.all_gather(w_key, ("blk", "head"), axis=0, tiled=True),
        lax.all_gather(w_value, ("blk", "head"), axis=0, tiled=True),
        lax.all_gather(w_out, ("blk", "head"), axis=0, tiled=True),
        lax.all_gather(w_in, ("blk", "head"), axis=0, tiled=True),
        lax.all_gather(w_back, ("blk", "head"), axis=0, tiled=True),
        lax.all_gather(bias_query, ("blk", "head"), axis=0, tiled=True),
        lax.all_gather(bias_value, ("blk", "head"), axis=0, tiled=True),
        lax.all_gather(bias_out, ("blk", "head"), axis=0, tiled=True),
        lax.all_gather(bias_in, ("blk", "head"), axis=0, tiled=True),
        lax.all_gather(bias_back, ("blk", "head"), axis=0, tiled=True),
        lax.all_gather(first_gain, ("blk", "head"), axis=0, tiled=True),
        lax.all_gather(first_shift, ("blk", "head"), axis=0, tiled=True),
        lax.all_gather(second_gain, ("blk", "head"), axis=0, tiled=True),
        lax.all_gather(second_shift, ("blk", "head"), axis=0, tiled=True),
    )
    query_bias = query_bias.astype(jnp.float32)
    value_bias = value_bias.astype(jnp.float32)
    out_bias = out_bias.astype(jnp.float32)
    in_bias = in_bias.astype(jnp.float32)
    back_bias = back_bias.astype(jnp.float32)
    gain_one = gain_one.astype(jnp.float32)
    shift_one = shift_one.astype(jnp.float32)
    gain_two = gain_two.astype(jnp.float32)
    shift_two = shift_two.astype(jnp.float32)
    seq_count = tokens.shape[0]
    query_tok = (
        ((flat_dot(tokens, query_full) + query_bias) * 0.125)
        .astype(jnp.bfloat16)
        .reshape(tokens.shape)
    )
    key_tok = flat_dot(tokens, key_full).astype(jnp.bfloat16).reshape(tokens.shape)
    value_tok = (
        (flat_dot(tokens, value_full) + value_bias).astype(jnp.bfloat16).reshape(tokens.shape)
    )
    query_heads, key_heads, value_heads = (
        lax.all_to_all(query_tok, "head", split_axis=2, concat_axis=1, tiled=True),
        lax.all_to_all(key_tok, "head", split_axis=2, concat_axis=1, tiled=True),
        lax.all_to_all(value_tok, "head", split_axis=2, concat_axis=1, tiled=True),
    )
    rows_here = query_heads.shape[1]
    width_heads = query_heads.shape[2]
    heads_here = width_heads // HD
    start_state = (
        jnp.full((seq_count, heads_here, rows_here), -1e30, jnp.float32),
        jnp.zeros((seq_count, heads_here, rows_here), jnp.float32),
        jnp.zeros((seq_count, heads_here, rows_here, HD), jnp.float32),
    )
    running_max, running_sum, weighted = forward_step(
        start_state,
        (
            lax.all_gather(key_heads, "blk", axis=1, tiled=True),
            lax.all_gather(value_heads, "blk", axis=1, tiled=True),
            lax.all_gather(segment_ids, "blk", axis=1, tiled=True),
        ),
        (query_heads, segment_ids),
    )
    floored = jnp.maximum(running_sum, 1.0)
    ctx_heads = heads_to_rows(weighted / floored[..., None])
    log_sums = (running_max + jnp.log(floored)).transpose(0, 2, 1)
    ctx_tok = lax.all_to_all(
        ctx_heads.astype(jnp.bfloat16), "head", split_axis=1, concat_axis=2, tiled=True
    )
    first_sum = tokens.astype(jnp.float32) + (flat_dot(ctx_tok, out_full) + out_bias).reshape(
        tokens.shape
    )
    first_norm = layer_norm(first_sum, gain_one, shift_one)
    first_low = first_norm.astype(jnp.bfloat16)
    inner_rows = flat_dot(first_low, in_full) + in_bias
    hidden_low = jax.nn.gelu(inner_rows, approximate=False).astype(jnp.bfloat16)
    second_sum = first_norm + (flat_dot(hidden_low, back_full) + back_bias).reshape(tokens.shape)
    output_now, second_pull = jax.vjp(layer_norm, second_sum, gain_two, shift_two)
    grad_second, grad_gain_two, grad_shift_two = second_pull(cotangent.astype(jnp.float32))
    grad_branch = grad_second.astype(jnp.bfloat16)
    grad_back_bias = jnp.sum(grad_branch.astype(jnp.float32), (0, 1))
    grad_back = inner_dot(hidden_low, grad_branch)
    grad_hidden = flat_dot(grad_branch, back_full.T)
    unused_value, gelu_pull = jax.vjp(partial(jax.nn.gelu, approximate=False), inner_rows)
    grad_inner = gelu_pull(grad_hidden)[0].astype(jnp.bfloat16)
    grad_in_bias = jnp.sum(grad_inner.astype(jnp.float32), 0)
    grad_in = inner_dot(first_low, grad_inner)
    grad_first_norm = grad_second + flat_dot(grad_inner, in_full.T).reshape(tokens.shape)
    unused_norm, first_pull = jax.vjp(layer_norm, first_sum, gain_one, shift_one)
    grad_first, grad_gain_one, grad_shift_one = first_pull(grad_first_norm)
    grad_attn = grad_first.astype(jnp.bfloat16)
    grad_out_bias = jnp.sum(grad_attn.astype(jnp.float32), (0, 1))
    grad_out = inner_dot(ctx_tok, grad_attn)
    grad_ctx_tok = flat_dot(grad_attn, out_full.T).astype(jnp.bfloat16).reshape(tokens.shape)
    grad_ctx = lax.all_to_all(grad_ctx_tok, "head", split_axis=2, concat_axis=1, tiled=True)
    deltas = jnp.sum(head_view(grad_ctx).astype(jnp.float32) * head_view(ctx_heads), -1)
    key_block = lax.all_gather(key_heads, "blk", axis=1, tiled=True)
    value_block = lax.all_gather(value_heads, "blk", axis=1, tiled=True)
    key_ids = lax.all_gather(segment_ids, "blk", axis=1, tiled=True)
    weights_now = probabilities(query_heads, key_block, segment_ids, key_ids, log_sums)
    dscores = score_grads(weights_now, grad_ctx, value_block, deltas)
    grad_query_heads = jnp.einsum(
        "ghqk,gkhd->ghqd", dscores, head_view(key_block), preferred_element_type=jnp.float32
    )
    key_part = jnp.einsum(
        "ghqk,gqhd->gkhd", dscores, head_view(query_heads), preferred_element_type=jnp.float32
    )
    value_part = jnp.einsum(
        "ghqk,gqhd->gkhd",
        weights_now.astype(jnp.bfloat16),
        head_view(grad_ctx),
        preferred_element_type=jnp.float32,
    )
    both_parts = jnp.concatenate(
        [
            key_part.reshape(key_part.shape[0], key_part.shape[1], -1),
            value_part.reshape(value_part.shape[0], value_part.shape[1], -1),
        ],
        2,
    )
    grad_query_heads, pair_grads = (grad_query_heads, both_parts)
    pair_home = lax.psum_scatter(
        pair_grads.astype(jnp.bfloat16), "blk", scatter_dimension=1, tiled=True
    ).astype(jnp.float32)
    grad_key_heads = pair_home[:, :, :width_heads].astype(jnp.bfloat16)
    grad_value_heads = pair_home[:, :, width_heads:].astype(jnp.bfloat16)
    grad_query_rows = heads_to_rows(grad_query_heads).astype(jnp.bfloat16)
    grad_query_tok, grad_key_tok, grad_value_tok = (
        lax.all_to_all(grad_query_rows, "head", split_axis=1, concat_axis=2, tiled=True),
        lax.all_to_all(grad_key_heads, "head", split_axis=1, concat_axis=2, tiled=True),
        lax.all_to_all(grad_value_heads, "head", split_axis=1, concat_axis=2, tiled=True),
    )
    grad_query_tok = grad_query_tok * 0.125
    grad_inputs = grad_first + (
        flat_dot(grad_query_tok, query_full.T)
        + flat_dot(grad_key_tok, key_full.T)
        + flat_dot(grad_value_tok, value_full.T)
    ).reshape(tokens.shape)
    (
        shard_wq,
        shard_wk,
        shard_wv,
        shard_wo,
        shard_wi,
        shard_wb,
        shard_bq,
        shard_bv,
        shard_bo,
        shard_bi,
        shard_bb,
        shard_g1,
        shard_s1,
        shard_g2,
        shard_s2,
    ) = (
        lax.psum_scatter(
            inner_dot(tokens, grad_query_tok), ("blk", "head"), scatter_dimension=0, tiled=True
        ),
        lax.psum_scatter(
            inner_dot(tokens, grad_key_tok), ("blk", "head"), scatter_dimension=0, tiled=True
        ),
        lax.psum_scatter(
            inner_dot(tokens, grad_value_tok), ("blk", "head"), scatter_dimension=0, tiled=True
        ),
        lax.psum_scatter(grad_out, ("blk", "head"), scatter_dimension=0, tiled=True),
        lax.psum_scatter(grad_in, ("blk", "head"), scatter_dimension=0, tiled=True),
        lax.psum_scatter(grad_back, ("blk", "head"), scatter_dimension=0, tiled=True),
        lax.psum_scatter(
            jnp.sum(grad_query_tok.astype(jnp.float32), (0, 1)),
            ("blk", "head"),
            scatter_dimension=0,
            tiled=True,
        ),
        lax.psum_scatter(
            jnp.sum(grad_value_tok.astype(jnp.float32), (0, 1)),
            ("blk", "head"),
            scatter_dimension=0,
            tiled=True,
        ),
        lax.psum_scatter(grad_out_bias, ("blk", "head"), scatter_dimension=0, tiled=True),
        lax.psum_scatter(grad_in_bias, ("blk", "head"), scatter_dimension=0, tiled=True),
        lax.psum_scatter(grad_back_bias, ("blk", "head"), scatter_dimension=0, tiled=True),
        lax.psum_scatter(grad_gain_one, ("blk", "head"), scatter_dimension=0, tiled=True),
        lax.psum_scatter(grad_shift_one, ("blk", "head"), scatter_dimension=0, tiled=True),
        lax.psum_scatter(grad_gain_two, ("blk", "head"), scatter_dimension=0, tiled=True),
        lax.psum_scatter(grad_shift_two, ("blk", "head"), scatter_dimension=0, tiled=True),
    )
    (
        total_wq,
        total_wk,
        total_wv,
        total_wo,
        total_wi,
        total_wb,
        total_bq,
        total_bv,
        total_bo,
        total_bi,
        total_bb,
        total_g1,
        total_s1,
        total_g2,
        total_s2,
    ) = (
        lax.psum(shard_wq.astype(jnp.bfloat16), "dp").astype(jnp.float32),
        lax.psum(shard_wk.astype(jnp.bfloat16), "dp").astype(jnp.float32),
        lax.psum(shard_wv.astype(jnp.bfloat16), "dp").astype(jnp.float32),
        lax.psum(shard_wo.astype(jnp.bfloat16), "dp").astype(jnp.float32),
        lax.psum(shard_wi.astype(jnp.bfloat16), "dp").astype(jnp.float32),
        lax.psum(shard_wb.astype(jnp.bfloat16), "dp").astype(jnp.float32),
        lax.psum(shard_bq.astype(jnp.bfloat16), "dp").astype(jnp.float32),
        lax.psum(shard_bv.astype(jnp.bfloat16), "dp").astype(jnp.float32),
        lax.psum(shard_bo.astype(jnp.bfloat16), "dp").astype(jnp.float32),
        lax.psum(shard_bi.astype(jnp.bfloat16), "dp").astype(jnp.float32),
        lax.psum(shard_bb.astype(jnp.bfloat16), "dp").astype(jnp.float32),
        lax.psum(shard_g1.astype(jnp.bfloat16), "dp").astype(jnp.float32),
        lax.psum(shard_s1.astype(jnp.bfloat16), "dp").astype(jnp.float32),
        lax.psum(shard_g2.astype(jnp.bfloat16), "dp").astype(jnp.float32),
        lax.psum(shard_s2.astype(jnp.bfloat16), "dp").astype(jnp.float32),
    )
    return (
        output_now.astype(jnp.bfloat16),
        grad_inputs,
        total_wq,
        total_wk,
        total_wv,
        total_wo,
        total_wi,
        total_wb,
        total_bq,
        total_bv,
        total_bo,
        total_bi,
        total_bb,
        total_g1,
        total_s1,
        total_g2,
        total_s2,
    )


def solution(mesh):
    in_specs = (
        P("dp", ("blk", "head"), None),
        P("dp", "blk"),
        P("dp", ("blk", "head"), None),
        P(("blk", "head"), None),
        P(("blk", "head"), None),
        P(("blk", "head"), None),
        P(("blk", "head"), None),
        P(("blk", "head"), None),
        P(("blk", "head"), None),
        P(("blk", "head")),
        P(("blk", "head")),
        P(("blk", "head")),
        P(("blk", "head")),
        P(("blk", "head")),
        P(("blk", "head")),
        P(("blk", "head")),
        P(("blk", "head")),
        P(("blk", "head")),
    )
    out_specs = (
        P("dp", ("blk", "head"), None),
        P("dp", ("blk", "head"), None),
        P(("blk", "head"), None),
        P(("blk", "head"), None),
        P(("blk", "head"), None),
        P(("blk", "head"), None),
        P(("blk", "head"), None),
        P(("blk", "head"), None),
        P(("blk", "head")),
        P(("blk", "head")),
        P(("blk", "head")),
        P(("blk", "head")),
        P(("blk", "head")),
        P(("blk", "head")),
        P(("blk", "head")),
        P(("blk", "head")),
        P(("blk", "head")),
    )
    plan = pick_plan(mesh)
    return jax.shard_map(
        plan, mesh=mesh, in_specs=in_specs, out_specs=out_specs, check_vma=False
    )
```

```python
from functools import partial
from types import SimpleNamespace

import jax
import jax.numpy as jnp
from jax import lax
from jax.experimental import pallas as pl
from jax.experimental.pallas import tpu as pltpu
from jax.sharding import PartitionSpec as P

HD = 64
BF = jnp.bfloat16
F32 = jnp.float32
GROUP = ("blk", "head")
MESH = pl.DeviceIdType.MESH
NN = ((1,), (0,))
NT = ((1,), (1,))
TN = ((0,), (0,))


def mm(a, b, dims):
    return lax.dot_general(a, b, (dims, ((), ())), preferred_element_type=F32)


def norm_parts(v):
    c = v - jnp.mean(v, -1, keepdims=True)
    r = lax.rsqrt(jnp.mean(c * c, -1, keepdims=True) + 1e-05)
    return c * r, r


def norm_back(e, n, r):
    return r * (e - jnp.mean(e, -1, keepdims=True) - n * jnp.mean(e * n, -1, keepdims=True))


def colsum(x):
    return jnp.sum(x.astype(F32), 0, keepdims=True)


def rows(ref):
    x = ref[...]
    return x.reshape(-1, x.shape[-1])


def layer_kernel(names, *refs):
    R = SimpleNamespace(**dict(zip(names, refs, strict=True)))
    dp, blk, head = [lax.axis_index(a) for a in ("dp", "blk", "head")]
    core, chip_x = lax.rem(blk, 2), lax.div(blk, 2)
    T, D = R.tok.shape
    W = R.q.shape[-1]
    FW = R.wi.shape[1] // 8

    def dev(p, flip):
        hh = lax.rem(head + lax.rem(p, 2), 2)
        bb = lax.rem(chip_x + lax.div(p, 2), 2) * 2 + lax.rem(core + flip, 2)
        return (dp, bb, hh), bb * 2 + hh

    def c32(i):
        return jnp.asarray(i, jnp.int32)

    me = blk * 2 + head
    partner, partner_at = dev(c32(0), 1)
    z_end = lax.rem(dp, 3) == 0
    z_other = jnp.where(dp == 0, 1, jnp.where(dp == 3, 2, jnp.where(dp == 1, 0, 3)))
    z_mid = jnp.where(dp == 1, 2, 1)

    def rcopy(src, dst, ssem, rsem, to):
        return pltpu.make_async_remote_copy(src, dst, ssem, rsem, device_id=to, device_id_type=MESH)

    def lanes(i, w):
        return pl.ds(pl.multiple_of(i * w, w), w)

    bar = pltpu.get_barrier_semaphore()
    for e in range(1, 8):
        to, _ = dev(c32(e // 2), e % 2)
        pl.semaphore_signal(bar, 1, device_id=to, device_id_type=MESH)
    for j in range(1, 4):
        pl.semaphore_signal(bar, 1, device_id=(lax.rem(dp + j, 4), blk, head), device_id_type=MESH)
    pl.semaphore_wait(bar, 10)

    half = (pl.ds(0, T // 2), pl.ds(T // 2, T // 2))
    by_y, by_x, by_both = 1, 2, 3

    def ag_direct(buf, r, p, h):
        to, _ = dev(c32(p), 0)
        part = buf.at[me, half[h]]
        return rcopy(part, part, R.ag_s.at[r, p, h], R.ag_r.at[r, p, h], to)

    def ag_relay(buf, r, h):
        via, over = (by_x, by_y) if h == 0 else (by_y, by_x)
        _, at = dev(c32(via), 0)
        to, _ = dev(c32(over), 0)
        part = buf.at[at, half[h]]
        return rcopy(part, part, R.ag_s.at[r, by_both, h], R.ag_r.at[r, by_both, h], to)

    def ag_home(buf, r):
        return rcopy(buf.at[me], buf.at[me], R.ag_fs.at[r, 0, 0], R.ag_f.at[r, 0, 0], partner)

    def ag_forward(buf, r, p, h):
        _, at = dev(c32(p), 0)
        part = buf.at[at, half[h]]
        return rcopy(part, part, R.ag_fs.at[r, p, h], R.ag_f.at[r, p, h], partner)

    def ag_start(buf, r):
        ag_direct(buf, r, by_x, 0).start()
        ag_direct(buf, r, by_y, 1).start()
        ag_direct(buf, r, by_x, 1).start()
        ag_direct(buf, r, by_y, 0).start()
        ag_home(buf, r).start()

    def ag_got(buf, r, p, h):
        (ag_relay(buf, r, h) if p == by_both else ag_direct(buf, r, p, h)).wait_recv()
        ag_forward(buf, r, p, h).start()

    def ag_wait(buf, r, p):
        @pl.when(p == 0)
        def _():
            ag_home(buf, r).wait_recv()

        @pl.when(p == by_y)
        def _():
            ag_got(buf, r, by_x, 0)
            ag_relay(buf, r, 0).start()
            ag_got(buf, r, by_y, 1)
            ag_relay(buf, r, 1).start()
            ag_got(buf, r, by_y, 0)
            for h in (0, 1):
                ag_forward(buf, r, by_y, h).wait_recv()

        @pl.when(p == by_x)
        def _():
            ag_got(buf, r, by_x, 1)
            for h in (0, 1):
                ag_forward(buf, r, by_x, h).wait_recv()

        @pl.when(p == by_both)
        def _():
            ag_got(buf, r, by_both, 0)
            ag_got(buf, r, by_both, 1)
            for h in (0, 1):
                ag_forward(buf, r, by_both, h).wait_recv()

    def ag_finish(buf, r):
        ag_home(buf, r).wait_send()
        for h in (0, 1):
            ag_direct(buf, r, by_x, h).wait_send()
            ag_direct(buf, r, by_y, h).wait_send()
            ag_relay(buf, r, h).wait_send()
            for p in (by_y, by_x, by_both):
                ag_forward(buf, r, p, h).wait_send()

    def pair(buf, p):
        a, b = dev(p, 0)[1], dev(p, 1)[1]
        return a, b, jnp.concatenate([buf[a], buf[b]], 0)

    def rs_chip(r, p):
        return rcopy(R.snd_c.at[p], R.rcv_c.at[r, p], R.rs_cs.at[r, p], R.rs_cr.at[r, p], partner)

    def rs_link(r, p, h):
        over = p if p != by_both else (by_x, by_y)[h]
        to, _ = dev(c32(over), 0)
        return rcopy(
            R.snd_l.at[p, half[h]], R.rcv_l.at[r, p, half[h]], R.rs_ls.at[r, p, h], R.rs_lr.at[r, p, h], to
        )

    def rs_put(r, p, part):
        R.snd_c[p] = part[T:].astype(BF)
        rs_chip(r, p).start()
        R.keep[p] = part[:T]

    def rs_combine(r, p):
        rs_chip(r, p).wait_recv()
        both = R.keep[p] + R.rcv_c[r, p].astype(F32)
        R.keep[p] = both
        R.snd_l[p] = both.astype(BF)

        @pl.when(p == by_y)
        def _():
            rs_link(r, by_y, 1).start()

        @pl.when(p == by_x)
        def _():
            rs_link(r, by_x, 0).start()

        @pl.when(p == by_both)
        def _():
            rs_link(r, by_both, 0).start()
            rs_link(r, by_both, 1).start()

    def rs_relay(r):
        for p, h in ((by_y, 0), (by_x, 1)):
            rs_link(r, by_both, h).wait_recv()
            R.snd_l[p, half[h]] = (R.keep[p, half[h]] + R.rcv_l[r, by_both, half[h]].astype(F32)).astype(BF)
            rs_link(r, p, h).start()

    def rs_final(r):
        rs_chip(r, c32(0)).wait_recv()
        acc = R.keep[0] + R.rcv_c[r, 0].astype(F32)
        for p in (by_y, by_x):
            for h in (0, 1):
                rs_link(r, p, h).wait_recv()
            acc = acc + R.rcv_l[r, p].astype(F32)
        for p in range(4):
            rs_chip(r, c32(p)).wait_send()
            if p:
                for h in (0, 1):
                    rs_link(r, p, h).wait_send()
        return acc

    zbufs = {
        "b": [(lambda x, i=i: x.at[i]) for i in range(4)],
        "i": [(lambda x, i=i: x.at[pl.ds(2 * i, 2)]) for i in range(4)],
        "o": [lambda x: x],
        "s": [lambda x: x],
        "w": [(lambda x, i=i: x.at[i]) for i in range(8)],
    }
    chunks = [(k, cut) for k in zbufs for cut in zbufs[k]]
    Z_IN, Z_OUT, Z_SMALL, Z_QKV, Z_ALL = 4, 8, 9, 10, 18

    def zrefs(c):
        k, cut = chunks[c]
        return cut(getattr(R, "zown_" + k)), cut(getattr(R, "zsum_" + k)), cut(getattr(R, "zmid_" + k))

    def z_up(c):
        own, tot, _ = zrefs(c)
        return rcopy(own, tot, R.z_s.at[c, 0], R.z_r.at[c, 0], (z_other, blk, head))

    def z_across(c):
        own, _, mid = zrefs(c)
        return rcopy(own, mid, R.z_s.at[c, 0], R.z_r.at[c, 1], (z_mid, blk, head))

    def z_down(c):
        _, tot, _ = zrefs(c)
        return rcopy(tot, tot, R.z_s.at[c, 1], R.z_r.at[c, 0], (z_other, blk, head))

    def z_produce(c):
        @pl.when(z_end)
        def _():
            z_up(c).start()

    def z_one(c):
        @pl.when(jnp.logical_not(z_end))
        def _():
            own, tot, _ = zrefs(c)
            z_up(c).wait_recv()
            own[...] = (own[...].astype(F32) + tot[...].astype(F32)).astype(BF)
            z_across(c).start()

    def z_two(c):
        @pl.when(jnp.logical_not(z_end))
        def _():
            own, tot, mid = zrefs(c)
            z_across(c).wait_recv()
            tot[...] = (own[...].astype(F32) + mid[...].astype(F32)).astype(BF)
            z_down(c).start()

    def z_finish(c):
        @pl.when(z_end)
        def _():
            z_up(c).wait_send()
            z_down(c).wait_recv()

        @pl.when(jnp.logical_not(z_end))
        def _():
            z_across(c).wait_send()
            z_down(c).wait_send()

    tok_all, y1_all, df_all, da_all = R.tok_all, R.y1_all, R.df_all, R.da_all
    local = [
        pltpu.make_async_copy(R.tok, tok_all.at[me], R.loc.at[0]),
        pltpu.make_async_copy(R.wb, R.wb_v, R.loc.at[1]),
        pltpu.make_async_copy(R.wo, R.wo_v, R.loc.at[2]),
        pltpu.make_async_copy(R.wi.at[:, lanes(me, FW)], R.win.at[me], R.loc.at[3]),
        pltpu.make_async_copy(R.cot, R.cot_v, R.loc.at[4]),
    ]
    for j, w in enumerate((R.wq, R.wk, R.wv)):
        local.append(pltpu.make_async_copy(w.at[:, lanes(me, W)], R.wqkv.at[me, :, pl.ds(j * W, W)], R.loc.at[5 + j]))
    for cp in local:
        cp.start()
    vecs = [x[...].astype(F32).reshape(1, T) for x in (R.bo, R.bb, R.g1, R.s1, R.g2, R.s2)]
    vecs.append(R.ids[0:1, lanes(head, T)].astype(F32))
    R.vec[...] = jnp.concatenate(vecs + [jnp.zeros((1, T), F32)], 0)
    R.vec_all[me] = R.vec[...]

    def vec_copy(e):
        to, _ = dev(c32(e // 2), e % 2)
        return rcopy(R.vec, R.vec_all.at[me], R.vec_s.at[e], R.vec_r.at[e], to)

    def qkv_copy(e, j):
        to, at = dev(c32(e // 2), e % 2)
        w = (R.wq, R.wk, R.wv)[j]
        return rcopy(w.at[:, lanes(at, W)], R.wqkv.at[me, :, pl.ds(j * W, W)], R.qkv_s.at[e, j], R.qkv_r.at[e, j], to)

    def win_copy(e):
        to, at = dev(c32(e // 2), e % 2)
        return rcopy(R.wi.at[:, lanes(at, FW)], R.win.at[me], R.win_s.at[e], R.win_r.at[e], to)

    far_first = (6, 7, 2, 3, 4, 5, 1)
    with jax.named_scope("start_copies"):
        for e in far_first:
            vec_copy(e).start()
        for e in far_first:
            for j in range(3):
                qkv_copy(e, j).start()
        local[0].wait()
        ag_start(tok_all, 0)

    with jax.named_scope("vectors"):
        for e in range(1, 8):
            vec_copy(e).wait_recv()
        for s in range(8):
            v = R.vec_all[s]
            R.vfull[:, s * T:(s + 1) * T] = v
            ids = jnp.broadcast_to(v[6:7], (T, T)).T
            R.segk[s] = jnp.where(ids < 0, -2.0, ids)

    with jax.named_scope("wait_qkv_weights"):
        for e in range(1, 8):
            for j in range(3):
                qkv_copy(e, j).wait_recv()
        for j in range(5, 8):
            local[j].wait()

    def qkv_step(p, carry):
        ag_wait(tok_all, 0, p)
        a, b, x = pair(tok_all, p)
        y = mm(x, rows(R.wqkv), NN)
        qq = ((y[:, :W] + R.bq[...].astype(F32).reshape(1, W)) * 0.125).astype(BF)
        kk = y[:, W:2 * W].astype(BF)
        vv = (y[:, 2 * W:] + R.bv[...].astype(F32).reshape(1, W)).astype(BF)
        for at, sl in ((a, slice(0, T)), (b, slice(T, 2 * T))):
            R.q[at], R.k[at], R.v[at] = qq[sl], kk[sl], vv[sl]
        return carry

    with jax.named_scope("project_qkv"):
        lax.fori_loop(0, 4, qkv_step, 0)
    for e in far_first:
        win_copy(e).start()
    for i in (1, 2, 3, 4):
        local[i].wait()

    def head_mask(h, like):
        lane = lax.broadcasted_iota(jnp.int32, like.shape, 1)
        return jnp.where(lax.div(lane, HD) == h, like, jnp.zeros_like(like))

    heads = W // HD

    def ids_of(a, b):
        return jnp.concatenate([R.vec_all[a, 6:7], R.vec_all[b, 6:7]], 1)

    def attend_step(i, carry):
        p = 3 - i
        a, b, qp = pair(R.q, p)
        segq = ids_of(a, b)
        segk = rows(R.segk)
        allowed = jnp.concatenate([segk, segk], 1) == segq
        kk = rows(R.k)
        outs = []
        for h in range(heads):
            s = jnp.where(allowed, mm(kk, head_mask(h, qp), NT), -1e30)
            ex = jnp.exp(s - jnp.max(s, 0, keepdims=True))
            total = jnp.maximum(jnp.sum(ex, 0, keepdims=True), 1.0)
            pt = (ex * jnp.where(segq >= 0, 1.0 / total, 0.0)).astype(BF)
            R.pt[h, p] = pt
            outs.append(mm(R.vt[h * HD:(h + 1) * HD, :], pt, NN))
        ct = jnp.concatenate(outs, 0).astype(BF)
        R.ctxt[:, lanes(a, T)] = ct[:, :T]
        R.ctxt[:, lanes(b, T)] = ct[:, T:]
        rs_put(0, p, mm(ct, R.wo_v[...], TN))

        @pl.when(p < 3)
        def _():
            rs_combine(0, p + 1)

        return carry

    with jax.named_scope("attend"):
        R.vt[...] = rows(R.v).T
        lax.fori_loop(0, 4, attend_step, 0)

    with jax.named_scope("first_norm"):
        rs_relay(0)
        rs = rs_final(0)
        h1 = tok_all[me].astype(F32) + rs + R.vfull[0:1]
        n1, r1 = norm_parts(h1)
        y1 = n1 * R.vfull[2:3] + R.vfull[3:4]
        R.n1[...], R.y1[...] = n1, y1
        R.r1[...] = jnp.broadcast_to(r1, R.r1.shape)
        y1_all[me] = y1.astype(BF)
        ag_start(y1_all, 1)
    R.kt[...] = rows(R.k).T

    with jax.named_scope("wait_hidden_weights"):
        for e in range(1, 8):
            win_copy(e).wait_recv()

    def hidden_step(p, carry):
        ag_wait(y1_all, 1, p)
        a, b, x = pair(y1_all, p)
        z = hidden_in(x)
        cdf = 0.5 * (1.0 + lax.erf(z * 0.7071067811865476))
        low = (z * cdf).astype(BF)
        slope = cdf + z * (jnp.exp(-0.5 * z * z) * 0.3989422804014327)
        R.hid[a], R.hid[b] = low[:T], low[T:]
        R.slope[a], R.slope[b] = slope[:T], slope[T:]
        rs_put(1, p, mm(low, R.wb_v[...], NN))

        @pl.when(p > 1)
        def _():
            rs_combine(1, p - 1)

        return carry

    def hidden_in(x):
        return mm(x, rows(R.win), NN) + R.bi[...].astype(F32).reshape(1, FW)

    with jax.named_scope("hidden"):
        lax.fori_loop(0, 4, hidden_step, 0)
        rs_combine(1, c32(3))

    with jax.named_scope("second_norm"):
        rs_relay(1)
        rs = rs_final(1)
        h2 = R.y1[...] + rs + R.vfull[1:2]
        n2, r2 = norm_parts(h2)
        gain = R.vfull[4:5]
        R.out[...] = (n2 * gain + R.vfull[5:6]).astype(BF)
        cot = R.cot_v[...].astype(F32)
        dh2 = norm_back(cot * gain, n2, r2)
        R.dh2[...] = dh2
        df_all[me] = dh2.astype(BF)
        ag_start(df_all, 2)
        R.sv[0:1, :] = colsum(cot * n2)
        R.sv[1:2, :] = colsum(cot)

    def hidden_back_step(p, carry):
        ag_wait(df_all, 2, p)
        a, b, x = pair(df_all, p)
        slope = jnp.concatenate([R.slope[a], R.slope[b]], 0)
        dz = (mm(x, R.wb_v[...], NT) * slope).astype(BF)
        R.dz[a], R.dz[b] = dz[:T], dz[T:]
        rs_put(2, p, mm(dz, rows(R.win), NT))

        @pl.when(p > 1)
        def _():
            rs_combine(2, p - 1)

        return carry

    with jax.named_scope("hidden_back"):
        lax.fori_loop(0, 4, hidden_back_step, 0)
        rs_combine(2, c32(3))

    with jax.named_scope("grad_back"):
        for i in range(4):
            g = mm(R.hid[:, :, i * T:(i + 1) * T].reshape(8 * T, T), rows(df_all), TN)
            R.zown_b[i] = g.astype(BF)
            z_produce(i)
        rs_relay(2)

    def din_copy(p, flip):
        to, at = dev(p, flip)
        return rcopy(R.din_snd.at[at], R.zown_i.at[me], R.din_s.at[p, flip], R.din_r.at[p, flip], to)

    def din_step(p, carry):
        a, b = dev(p, 0)[1], dev(p, 1)[1]
        x = jnp.concatenate([y1_all[:, :, lanes(a, T)], y1_all[:, :, lanes(b, T)]], 2).reshape(8 * T, 2 * T)
        g = mm(x, rows(R.dz), TN).astype(BF)
        R.din_snd[b] = g[T:]
        din_copy(p, 1).start()

        @pl.when(p == 0)
        def _():
            R.zown_i[me] = g[:T]

        @pl.when(p > 0)
        def _():
            R.din_snd[a] = g[:T]
            din_copy(p, 0).start()

        return carry

    with jax.named_scope("grad_in"):
        lax.fori_loop(0, 4, din_step, 0)
    z_one(0)

    with jax.named_scope("first_norm_back"):
        rs = rs_final(2)
        dy1 = R.dh2[...] + rs
        n1 = R.n1[...]
        dh1 = norm_back(dy1 * R.vfull[2:3], n1, R.r1[:, 0:1])
        R.dh1[...] = dh1
        da_all[me] = dh1.astype(BF)
        ag_start(da_all, 3)
        R.sv[2:3, :] = colsum(dy1 * n1)
        R.sv[3:4, :] = colsum(dy1)

    def sv_copy(e):
        to, at = dev(c32(e // 2), e % 2)
        return rcopy(R.sv.at[:, lanes(at, T)], R.sv_rcv.at[me], R.sv_s.at[e], R.sv_r.at[e], to)

    for e in far_first:
        sv_copy(e).start()
    R.sv_rcv[me] = R.sv[:, lanes(me, T)]
    z_one(1)
    z_two(0)

    def z_service(p):
        @pl.when(p == 1)
        def _():
            z_one(2)
            z_two(1)

        @pl.when(p == 3)
        def _():
            z_one(3)
            z_two(2)

    R.dk[...] = jnp.zeros_like(R.dk)
    R.dv[...] = jnp.zeros_like(R.dv)

    def attend_back_step(p, carry):
        ag_wait(da_all, 3, p)
        a, b, x = pair(da_all, p)
        qp = jnp.concatenate([R.q[a], R.q[b]], 0)
        dc = mm(x, R.wo_v[...], NT).astype(BF)
        vv = rows(R.v)
        outs = []
        for h in range(heads):
            dcm, qm = head_mask(h, dc), head_mask(h, qp)
            low = R.pt[h, p]
            pt = low.astype(F32)
            dpt = mm(vv, dcm, NT)
            ds = (pt * (dpt - jnp.sum(pt * dpt, 0, keepdims=True))).astype(BF)
            outs.append(mm(R.kt[h * HD:(h + 1) * HD, :], ds, NN))
            R.dk[...] += mm(ds, qm, NN)
            R.dv[...] += mm(low, dcm, NN)
        dq = jnp.concatenate(outs, 0).T.astype(BF) * 0.125
        R.dqkv[a, :, 0:W] = dq[:T]
        R.dqkv[b, :, 0:W] = dq[T:]
        z_service(p)
        return carry

    with jax.named_scope("attend_back"):
        lax.fori_loop(0, 4, attend_back_step, 0)
        R.dqkv[:, :, W:2 * W] = R.dk[...].astype(BF).reshape(8, T, W)
        R.dqkv[:, :, 2 * W:] = R.dv[...].astype(BF).reshape(8, T, W)

    def dqkv_copy(p, flip):
        to, at = dev(p, flip)
        return rcopy(R.dqkv_snd.at[at], R.zown_w.at[me], R.dqkv_s.at[p, flip], R.dqkv_r.at[p, flip], to)

    def dqkv_step(p, carry):
        a, b = dev(p, 0)[1], dev(p, 1)[1]
        x = jnp.concatenate([tok_all[:, :, lanes(a, T)], tok_all[:, :, lanes(b, T)]], 2).reshape(8 * T, 2 * T)
        g = mm(x, rows(R.dqkv), TN).astype(BF)
        R.dqkv_snd[b] = g[T:]
        dqkv_copy(p, 1).start()

        @pl.when(p == 0)
        def _():
            R.zown_w[me] = g[:T]

        @pl.when(p > 0)
        def _():
            R.dqkv_snd[a] = g[:T]
            dqkv_copy(p, 0).start()

        return carry

    with jax.named_scope("grad_qkv"):
        lax.fori_loop(0, 4, dqkv_step, 0)

    with jax.named_scope("grad_out"):
        for p in range(4):
            for flip in (0, 1):
                if (p, flip) != (0, 0):
                    din_copy(c32(p), flip).wait_recv()
        for c in range(Z_IN, Z_OUT):
            z_produce(c)
        R.zown_o[...] = mm(R.ctxt[...], rows(da_all), NN).astype(BF)
        z_produce(Z_OUT)
        z_one(4)
        z_two(3)

    def input_step(p, carry):
        a, b, x = pair(R.dqkv, p)
        rs_put(3, p, mm(x, rows(R.wqkv), NT))

        @pl.when(p > 1)
        def _():
            rs_combine(3, p - 1)

        return carry

    with jax.named_scope("input_back"):
        lax.fori_loop(0, 4, input_step, 0)
        rs_combine(3, c32(3))
        z_one(5)
        z_two(4)

    with jax.named_scope("small_grads"):
        for e in range(1, 8):
            sv_copy(e).wait_recv()
        acc = R.sv_rcv[0]
        for s in range(1, 8):
            acc = acc + R.sv_rcv[s]
        own = lanes(me, T)
        parts = [
            acc[0:4],
            colsum(rows(R.dqkv)[:, 0:W]),
            colsum(rows(R.dqkv)[:, 2 * W:]),
            colsum(da_all[:, :, own].reshape(8 * T, T)),
            colsum(df_all[:, :, own].reshape(8 * T, T)),
        ]
        dbi = colsum(rows(R.dz))
        parts += [dbi[:, i * T:(i + 1) * T] for i in range(FW // T)]
        parts.append(jnp.zeros((16 - 8 - FW // T, T), F32))
        R.zown_s[...] = jnp.concatenate(parts, 0).astype(BF)
        z_produce(Z_SMALL)
        rs_relay(3)

    with jax.named_scope("z_rest"):
        z_one(6)
        z_two(5)
        for p in range(4):
            for flip in (0, 1):
                if (p, flip) != (0, 0):
                    dqkv_copy(c32(p), flip).wait_recv()
        for c in range(Z_QKV, Z_ALL):
            z_produce(c)
    with jax.named_scope("input_grad"):
        R.igrad[...] = R.dh1[...] + rs_final(3)
    with jax.named_scope("z_last"):
        for c in range(7, Z_ALL):
            z_one(c)
            z_two(c - 1)
        z_two(Z_ALL - 1)

    with jax.named_scope("finish"):
        for c in range(Z_ALL):
            z_finish(c)
        for buf, r in ((tok_all, 0), (y1_all, 1), (df_all, 2), (da_all, 3)):
            ag_finish(buf, r)
        for e in range(1, 8):
            vec_copy(e).wait_send()
            win_copy(e).wait_send()
            sv_copy(e).wait_send()
            for j in range(3):
                qkv_copy(e, j).wait_send()
            din_copy(c32(e // 2), e % 2).wait_send()
            dqkv_copy(c32(e // 2), e % 2).wait_send()


def sharded_plan(
    tokens, segment_ids, cotangent,
    w_query, w_key, w_value, w_out, w_in, w_back,
    bias_query, bias_value, bias_out, bias_in, bias_back,
    first_gain, first_shift, second_gain, second_shift,
):
    tokens, cotangent = tokens[0], cotangent[0]
    T, D = tokens.shape
    W, FW = D // 8, w_in.shape[1] // 8
    ins = dict(
        tok=tokens, cot=cotangent, wq=w_query, wk=w_key, wv=w_value, wo=w_out, wi=w_in, wb=w_back, ids=segment_ids,
        bo=bias_out, bb=bias_back, g1=first_gain, s1=first_shift, g2=second_gain, s2=second_shift,
        bq=bias_query, bv=bias_value, bi=bias_in,
    )
    in_hbm = 8
    outs = dict(
        out=((T, D), BF), igrad=((T, D), F32), zsum_b=((4, T, D), BF), zsum_i=((8, T, FW), BF),
        zsum_o=((T, D), BF), zsum_w=((8, T, 3 * W), BF), zsum_s=((16, T), BF),
    )
    blocks = {k: ((8, T, D), BF) for k in ("tok_all", "y1_all", "df_all", "da_all")}
    scr = dict(
        **blocks,
        wqkv=((8, T, 3 * W), BF), win=((8, T, FW), BF), wb_v=(w_back.shape, BF), wo_v=(w_out.shape, BF),
        cot_v=((T, D), BF), vec=((8, T), F32), vec_all=((8, 8, T), F32), vfull=((8, D), F32), segk=((8, T, T), F32),
        q=((8, T, W), BF), k=((8, T, W), BF), v=((8, T, W), BF), vt=((W, 8 * T), BF), kt=((W, 8 * T), BF),
        pt=((W // HD, 4, 8 * T, 2 * T), BF), ctxt=((W, 8 * T), BF),
        hid=((8, T, FW), BF), slope=((8, T, FW), F32), dz=((8, T, FW), BF),
        n1=((T, D), F32), r1=((T, 128), F32), y1=((T, D), F32), dh2=((T, D), F32), dh1=((T, D), F32),
        sv=((8, D), F32), sv_rcv=((8, 8, T), F32),
        keep=((4, T, D), F32), snd_c=((4, T, D), BF), snd_l=((4, T, D), BF),
        rcv_c=((4, 4, T, D), BF), rcv_l=((4, 4, T, D), BF),
        dk=((8 * T, W), F32), dv=((8 * T, W), F32), dqkv=((8, T, 3 * W), BF),
        din_snd=((8, T, FW), BF), dqkv_snd=((8, T, 3 * W), BF),
        **{z + k[4:]: s for z in ("zown", "zmid") for k, s in outs.items() if k.startswith("zsum")},
    )
    sems = dict(
        ag_s=(4, 4, 2), ag_r=(4, 4, 2), ag_fs=(4, 4, 2), ag_f=(4, 4, 2),
        rs_cs=(4, 4), rs_cr=(4, 4), rs_ls=(4, 4, 2), rs_lr=(4, 4, 2),
        z_s=(18, 2), z_r=(18, 2), loc=(8,), vec_s=(8,), vec_r=(8,), qkv_s=(8, 3), qkv_r=(8, 3), win_s=(8,), win_r=(8,),
        sv_s=(8,), sv_r=(8,), din_s=(4, 2), din_r=(4, 2), dqkv_s=(4, 2), dqkv_r=(4, 2),
    )
    names = list(ins) + list(outs) + list(scr) + list(sems)
    res = pl.pallas_call(
        partial(layer_kernel, names),
        out_shape=[jax.ShapeDtypeStruct(*s) for s in outs.values()],
        in_specs=[pl.BlockSpec(memory_space=pl.ANY if i < in_hbm else pltpu.VMEM) for i in range(len(ins))],
        out_specs=[pl.BlockSpec(memory_space=pltpu.VMEM) for _ in outs],
        scratch_shapes=[pltpu.VMEM(*s) for s in scr.values()] + [pltpu.SemaphoreType.DMA(s) for s in sems.values()],
        compiler_params=pltpu.CompilerParams(collective_id=0, has_side_effects=True, vmem_limit_bytes=60 << 20),
        name="layer",
    )(*ins.values())
    grid = 4
    wide = pl.BlockSpec((T // grid, D), lambda i: (i, 0))

    def whole(n):
        return pl.BlockSpec((n,), lambda i: (0,))

    firsts = [(T, D), (T, D), (T, D), (T, D), (T, D), (T, D), w_in.shape, w_back.shape]
    types = [BF] + [F32] * 7
    return_specs = [wide, wide] + [pl.BlockSpec((T, 2 * T), lambda i: (0, i))] * 3 + [
        wide, pl.BlockSpec((T, 2 * FW), lambda i: (0, i)), pl.BlockSpec((T, D), lambda i: (i, 0)),
    ]
    sizes = [T, T, T, FW, T, T, T, T, T]
    final = pl.pallas_call(
        finish_kernel,
        grid=(grid,),
        out_shape=[jax.ShapeDtypeStruct(s, t) for s, t in zip(firsts, types)]
        + [jax.ShapeDtypeStruct((n,), F32) for n in sizes],
        in_specs=[
            wide, wide, pl.BlockSpec((1, T, D), lambda i: (i, 0, 0)), pl.BlockSpec((2, T, FW), lambda i: (i, 0, 0)),
            wide, pl.BlockSpec((2, T, 3 * W), lambda i: (i, 0, 0)), pl.BlockSpec((16, T), lambda i: (0, 0)),
        ],
        out_specs=return_specs + [whole(n) for n in sizes],
        name="finish",
    )(*res)
    return (final[0][None], final[1][None], *final[2:])


def finish_kernel(out, igrad, tb, ti, to, tw, ts, o_out, o_igrad, o_q, o_k, o_v, o_o, o_i, o_b, *o_small):
    o_out[...] = out[...]
    o_igrad[...] = igrad[...]
    o_b[...] = tb[0].astype(F32)
    o_o[...] = to[...].astype(F32)
    width = ti.shape[2]
    for j in range(2):
        o_i[:, j * width:(j + 1) * width] = ti[j].astype(F32)
    W = tw.shape[2] // 3
    for j, o in enumerate((o_q, o_k, o_v)):
        for s in range(2):
            o[:, s * W:(s + 1) * W] = tw[s, :, j * W:(j + 1) * W].astype(F32)

    @pl.when(pl.program_id(0) == 0)
    def _():
        v = ts[...].astype(F32)
        bq, bv, bo, bi, bb, g1, s1, g2, s2 = o_small
        for o, i in ((bq, 4), (bv, 5), (bo, 6), (bb, 7), (g1, 2), (s1, 3), (g2, 0), (s2, 1)):
            o[...] = v[i]
        n = v.shape[1]
        for i in range(bi.shape[0] // n):
            bi[i * n:(i + 1) * n] = v[8 + i]


def pick_plan(mesh):
    group = mesh.shape["blk"] * mesh.shape["head"]
    return sharded_plan if (mesh.shape["dp"], group) == (4, 8) else general_plan


def flat_dot(left_side, right_side):
    return jnp.dot(
        left_side.reshape(-1, left_side.shape[-1]), right_side, preferred_element_type=jnp.float32
    )


def inner_dot(left_side, right_side):
    return jnp.einsum(
        "ra,rb->ab",
        left_side.reshape(-1, left_side.shape[-1]),
        right_side.reshape(-1, right_side.shape[-1]),
        preferred_element_type=jnp.float32,
    )


def layer_norm(value_rows, gain_row, shift_row):
    centre = jnp.mean(value_rows, -1, keepdims=True)
    centred = value_rows - centre
    spread = jnp.mean(centred * centred, -1, keepdims=True)
    return centred * lax.rsqrt(spread + 1e-05) * gain_row + shift_row


def head_view(array_in):
    return array_in.reshape(array_in.shape[0], array_in.shape[1], -1, HD)


def allowed_pairs(query_ids, key_ids):
    same_doc = (query_ids[:, :, None] == key_ids[:, None, :]) & (key_ids[:, None, :] >= 0)
    return same_doc[:, None]


def forward_step(state_now, arrived, local_data):
    running_max, running_sum, weighted = state_now
    key_block, value_block, key_ids = arrived
    query_block, query_ids = local_data
    scores = jnp.einsum(
        "gqhd,gkhd->ghqk",
        head_view(query_block),
        head_view(key_block),
        preferred_element_type=jnp.float32,
    )
    allowed = allowed_pairs(query_ids, key_ids)
    masked = jnp.where(allowed, scores, -1e30)
    new_max = jnp.maximum(running_max, jnp.max(masked, -1))
    exponents = jnp.where(allowed, jnp.exp(masked - new_max[..., None]), 0.0)
    running_sum = jnp.sum(exponents, -1)
    weighted = jnp.einsum(
        "ghqk,gkhd->ghqd",
        exponents.astype(jnp.bfloat16),
        head_view(value_block),
        preferred_element_type=jnp.float32,
    )
    return (new_max, running_sum, weighted)


def probabilities(query_block, key_block, query_ids, key_ids, log_sums):
    scores = jnp.einsum(
        "gqhd,gkhd->ghqk",
        head_view(query_block),
        head_view(key_block),
        preferred_element_type=jnp.float32,
    )
    allowed = allowed_pairs(query_ids, key_ids)
    masked = jnp.where(allowed, scores, -1e30)
    return jnp.where(allowed, jnp.exp(masked - log_sums.transpose(0, 2, 1)[..., None]), 0.0)


def score_grads(weights_now, grad_block, value_block, deltas):
    grad_weights = jnp.einsum(
        "gqhd,gkhd->ghqk",
        head_view(grad_block),
        head_view(value_block),
        preferred_element_type=jnp.float32,
    )
    return (weights_now * (grad_weights - deltas.transpose(0, 2, 1)[..., None])).astype(
        jnp.bfloat16
    )


def heads_to_rows(array_in):
    return array_in.transpose(0, 2, 1, 3).reshape(array_in.shape[0], array_in.shape[2], -1)


def general_plan(
    tokens,
    segment_ids,
    cotangent,
    w_query,
    w_key,
    w_value,
    w_out,
    w_in,
    w_back,
    bias_query,
    bias_value,
    bias_out,
    bias_in,
    bias_back,
    first_gain,
    first_shift,
    second_gain,
    second_shift,
):
    (
        query_full,
        key_full,
        value_full,
        out_full,
        in_full,
        back_full,
        query_bias,
        value_bias,
        out_bias,
        in_bias,
        back_bias,
        gain_one,
        shift_one,
        gain_two,
        shift_two,
    ) = (
        lax.all_gather(w_query, GROUP, axis=0, tiled=True),
        lax.all_gather(w_key, GROUP, axis=0, tiled=True),
        lax.all_gather(w_value, GROUP, axis=0, tiled=True),
        lax.all_gather(w_out, GROUP, axis=0, tiled=True),
        lax.all_gather(w_in, GROUP, axis=0, tiled=True),
        lax.all_gather(w_back, GROUP, axis=0, tiled=True),
        lax.all_gather(bias_query, GROUP, axis=0, tiled=True),
        lax.all_gather(bias_value, GROUP, axis=0, tiled=True),
        lax.all_gather(bias_out, GROUP, axis=0, tiled=True),
        lax.all_gather(bias_in, GROUP, axis=0, tiled=True),
        lax.all_gather(bias_back, GROUP, axis=0, tiled=True),
        lax.all_gather(first_gain, GROUP, axis=0, tiled=True),
        lax.all_gather(first_shift, GROUP, axis=0, tiled=True),
        lax.all_gather(second_gain, GROUP, axis=0, tiled=True),
        lax.all_gather(second_shift, GROUP, axis=0, tiled=True),
    )
    query_bias = query_bias.astype(jnp.float32)
    value_bias = value_bias.astype(jnp.float32)
    out_bias = out_bias.astype(jnp.float32)
    in_bias = in_bias.astype(jnp.float32)
    back_bias = back_bias.astype(jnp.float32)
    gain_one = gain_one.astype(jnp.float32)
    shift_one = shift_one.astype(jnp.float32)
    gain_two = gain_two.astype(jnp.float32)
    shift_two = shift_two.astype(jnp.float32)
    seq_count = tokens.shape[0]
    query_tok = (
        ((flat_dot(tokens, query_full) + query_bias) * 0.125)
        .astype(jnp.bfloat16)
        .reshape(tokens.shape)
    )
    key_tok = flat_dot(tokens, key_full).astype(jnp.bfloat16).reshape(tokens.shape)
    value_tok = (
        (flat_dot(tokens, value_full) + value_bias).astype(jnp.bfloat16).reshape(tokens.shape)
    )
    query_heads, key_heads, value_heads = (
        lax.all_to_all(query_tok, "head", split_axis=2, concat_axis=1, tiled=True),
        lax.all_to_all(key_tok, "head", split_axis=2, concat_axis=1, tiled=True),
        lax.all_to_all(value_tok, "head", split_axis=2, concat_axis=1, tiled=True),
    )
    rows_here = query_heads.shape[1]
    width_heads = query_heads.shape[2]
    heads_here = width_heads // HD
    start_state = (
        jnp.full((seq_count, heads_here, rows_here), -1e30, jnp.float32),
        jnp.zeros((seq_count, heads_here, rows_here), jnp.float32),
        jnp.zeros((seq_count, heads_here, rows_here, HD), jnp.float32),
    )
    running_max, running_sum, weighted = forward_step(
        start_state,
        (
            lax.all_gather(key_heads, "blk", axis=1, tiled=True),
            lax.all_gather(value_heads, "blk", axis=1, tiled=True),
            lax.all_gather(segment_ids, "blk", axis=1, tiled=True),
        ),
        (query_heads, segment_ids),
    )
    floored = jnp.maximum(running_sum, 1.0)
    ctx_heads = heads_to_rows(weighted / floored[..., None])
    log_sums = (running_max + jnp.log(floored)).transpose(0, 2, 1)
    ctx_tok = lax.all_to_all(
        ctx_heads.astype(jnp.bfloat16), "head", split_axis=1, concat_axis=2, tiled=True
    )
    first_sum = tokens.astype(jnp.float32) + (flat_dot(ctx_tok, out_full) + out_bias).reshape(
        tokens.shape
    )
    first_norm = layer_norm(first_sum, gain_one, shift_one)
    first_low = first_norm.astype(jnp.bfloat16)
    inner_rows = flat_dot(first_low, in_full) + in_bias
    hidden_low = jax.nn.gelu(inner_rows, approximate=False).astype(jnp.bfloat16)
    second_sum = first_norm + (flat_dot(hidden_low, back_full) + back_bias).reshape(tokens.shape)
    output_now, second_pull = jax.vjp(layer_norm, second_sum, gain_two, shift_two)
    grad_second, grad_gain_two, grad_shift_two = second_pull(cotangent.astype(jnp.float32))
    grad_branch = grad_second.astype(jnp.bfloat16)
    grad_back_bias = jnp.sum(grad_branch.astype(jnp.float32), (0, 1))
    grad_back = inner_dot(hidden_low, grad_branch)
    grad_hidden = flat_dot(grad_branch, back_full.T)
    unused_value, gelu_pull = jax.vjp(partial(jax.nn.gelu, approximate=False), inner_rows)
    grad_inner = gelu_pull(grad_hidden)[0].astype(jnp.bfloat16)
    grad_in_bias = jnp.sum(grad_inner.astype(jnp.float32), 0)
    grad_in = inner_dot(first_low, grad_inner)
    grad_first_norm = grad_second + flat_dot(grad_inner, in_full.T).reshape(tokens.shape)
    unused_norm, first_pull = jax.vjp(layer_norm, first_sum, gain_one, shift_one)
    grad_first, grad_gain_one, grad_shift_one = first_pull(grad_first_norm)
    grad_attn = grad_first.astype(jnp.bfloat16)
    grad_out_bias = jnp.sum(grad_attn.astype(jnp.float32), (0, 1))
    grad_out = inner_dot(ctx_tok, grad_attn)
    grad_ctx_tok = flat_dot(grad_attn, out_full.T).astype(jnp.bfloat16).reshape(tokens.shape)
    grad_ctx = lax.all_to_all(grad_ctx_tok, "head", split_axis=2, concat_axis=1, tiled=True)
    deltas = jnp.sum(head_view(grad_ctx).astype(jnp.float32) * head_view(ctx_heads), -1)
    key_block = lax.all_gather(key_heads, "blk", axis=1, tiled=True)
    value_block = lax.all_gather(value_heads, "blk", axis=1, tiled=True)
    key_ids = lax.all_gather(segment_ids, "blk", axis=1, tiled=True)
    weights_now = probabilities(query_heads, key_block, segment_ids, key_ids, log_sums)
    dscores = score_grads(weights_now, grad_ctx, value_block, deltas)
    grad_query_heads = jnp.einsum(
        "ghqk,gkhd->ghqd", dscores, head_view(key_block), preferred_element_type=jnp.float32
    )
    key_part = jnp.einsum(
        "ghqk,gqhd->gkhd", dscores, head_view(query_heads), preferred_element_type=jnp.float32
    )
    value_part = jnp.einsum(
        "ghqk,gqhd->gkhd",
        weights_now.astype(jnp.bfloat16),
        head_view(grad_ctx),
        preferred_element_type=jnp.float32,
    )
    both_parts = jnp.concatenate(
        [
            key_part.reshape(key_part.shape[0], key_part.shape[1], -1),
            value_part.reshape(value_part.shape[0], value_part.shape[1], -1),
        ],
        2,
    )
    grad_query_heads, pair_grads = (grad_query_heads, both_parts)
    pair_home = lax.psum_scatter(
        pair_grads.astype(jnp.bfloat16), "blk", scatter_dimension=1, tiled=True
    ).astype(jnp.float32)
    grad_key_heads = pair_home[:, :, :width_heads].astype(jnp.bfloat16)
    grad_value_heads = pair_home[:, :, width_heads:].astype(jnp.bfloat16)
    grad_query_rows = heads_to_rows(grad_query_heads).astype(jnp.bfloat16)
    grad_query_tok, grad_key_tok, grad_value_tok = (
        lax.all_to_all(grad_query_rows, "head", split_axis=1, concat_axis=2, tiled=True),
        lax.all_to_all(grad_key_heads, "head", split_axis=1, concat_axis=2, tiled=True),
        lax.all_to_all(grad_value_heads, "head", split_axis=1, concat_axis=2, tiled=True),
    )
    grad_query_tok = grad_query_tok * 0.125
    grad_inputs = grad_first + (
        flat_dot(grad_query_tok, query_full.T)
        + flat_dot(grad_key_tok, key_full.T)
        + flat_dot(grad_value_tok, value_full.T)
    ).reshape(tokens.shape)
    (
        shard_wq,
        shard_wk,
        shard_wv,
        shard_wo,
        shard_wi,
        shard_wb,
        shard_bq,
        shard_bv,
        shard_bo,
        shard_bi,
        shard_bb,
        shard_g1,
        shard_s1,
        shard_g2,
        shard_s2,
    ) = (
        lax.psum_scatter(
            inner_dot(tokens, grad_query_tok), GROUP, scatter_dimension=0, tiled=True
        ),
        lax.psum_scatter(
            inner_dot(tokens, grad_key_tok), GROUP, scatter_dimension=0, tiled=True
        ),
        lax.psum_scatter(
            inner_dot(tokens, grad_value_tok), GROUP, scatter_dimension=0, tiled=True
        ),
        lax.psum_scatter(grad_out, GROUP, scatter_dimension=0, tiled=True),
        lax.psum_scatter(grad_in, GROUP, scatter_dimension=0, tiled=True),
        lax.psum_scatter(grad_back, GROUP, scatter_dimension=0, tiled=True),
        lax.psum_scatter(
            jnp.sum(grad_query_tok.astype(jnp.float32), (0, 1)),
            GROUP,
            scatter_dimension=0,
            tiled=True,
        ),
        lax.psum_scatter(
            jnp.sum(grad_value_tok.astype(jnp.float32), (0, 1)),
            GROUP,
            scatter_dimension=0,
            tiled=True,
        ),
        lax.psum_scatter(grad_out_bias, GROUP, scatter_dimension=0, tiled=True),
        lax.psum_scatter(grad_in_bias, GROUP, scatter_dimension=0, tiled=True),
        lax.psum_scatter(grad_back_bias, GROUP, scatter_dimension=0, tiled=True),
        lax.psum_scatter(grad_gain_one, GROUP, scatter_dimension=0, tiled=True),
        lax.psum_scatter(grad_shift_one, GROUP, scatter_dimension=0, tiled=True),
        lax.psum_scatter(grad_gain_two, GROUP, scatter_dimension=0, tiled=True),
        lax.psum_scatter(grad_shift_two, GROUP, scatter_dimension=0, tiled=True),
    )
    (
        total_wq,
        total_wk,
        total_wv,
        total_wo,
        total_wi,
        total_wb,
        total_bq,
        total_bv,
        total_bo,
        total_bi,
        total_bb,
        total_g1,
        total_s1,
        total_g2,
        total_s2,
    ) = (
        lax.psum(shard_wq.astype(jnp.bfloat16), "dp").astype(jnp.float32),
        lax.psum(shard_wk.astype(jnp.bfloat16), "dp").astype(jnp.float32),
        lax.psum(shard_wv.astype(jnp.bfloat16), "dp").astype(jnp.float32),
        lax.psum(shard_wo.astype(jnp.bfloat16), "dp").astype(jnp.float32),
        lax.psum(shard_wi.astype(jnp.bfloat16), "dp").astype(jnp.float32),
        lax.psum(shard_wb.astype(jnp.bfloat16), "dp").astype(jnp.float32),
        lax.psum(shard_bq.astype(jnp.bfloat16), "dp").astype(jnp.float32),
        lax.psum(shard_bv.astype(jnp.bfloat16), "dp").astype(jnp.float32),
        lax.psum(shard_bo.astype(jnp.bfloat16), "dp").astype(jnp.float32),
        lax.psum(shard_bi.astype(jnp.bfloat16), "dp").astype(jnp.float32),
        lax.psum(shard_bb.astype(jnp.bfloat16), "dp").astype(jnp.float32),
        lax.psum(shard_g1.astype(jnp.bfloat16), "dp").astype(jnp.float32),
        lax.psum(shard_s1.astype(jnp.bfloat16), "dp").astype(jnp.float32),
        lax.psum(shard_g2.astype(jnp.bfloat16), "dp").astype(jnp.float32),
        lax.psum(shard_s2.astype(jnp.bfloat16), "dp").astype(jnp.float32),
    )
    return (
        output_now.astype(jnp.bfloat16),
        grad_inputs,
        total_wq,
        total_wk,
        total_wv,
        total_wo,
        total_wi,
        total_wb,
        total_bq,
        total_bv,
        total_bo,
        total_bi,
        total_bb,
        total_g1,
        total_s1,
        total_g2,
        total_s2,
    )


def solution(mesh):
    in_specs = (
        P("dp", GROUP, None),
        P("dp", "blk"),
        P("dp", GROUP, None),
        P(GROUP, None),
        P(GROUP, None),
        P(GROUP, None),
        P(GROUP, None),
        P(GROUP, None),
        P(GROUP, None),
        P(GROUP),
        P(GROUP),
        P(GROUP),
        P(GROUP),
        P(GROUP),
        P(GROUP),
        P(GROUP),
        P(GROUP),
        P(GROUP),
    )
    out_specs = (
        P("dp", GROUP, None),
        P("dp", GROUP, None),
        P(GROUP, None),
        P(GROUP, None),
        P(GROUP, None),
        P(GROUP, None),
        P(GROUP, None),
        P(GROUP, None),
        P(GROUP),
        P(GROUP),
        P(GROUP),
        P(GROUP),
        P(GROUP),
        P(GROUP),
        P(GROUP),
        P(GROUP),
        P(GROUP),
    )
    plan = pick_plan(mesh)
    return jax.shard_map(
        plan, mesh=mesh, in_specs=in_specs, out_specs=out_specs, check_vma=False
    )
```

```python
from functools import partial
from types import SimpleNamespace

import jax
import jax.numpy as jnp
from jax import lax
from jax.experimental import pallas as pl
from jax.experimental.pallas import tpu as pltpu
from jax.sharding import PartitionSpec as P

HD = 64
BF = jnp.bfloat16
F32 = jnp.float32
GROUP = ("blk", "head")
MESH = pl.DeviceIdType.MESH
NN = ((1,), (0,))
NT = ((1,), (1,))
TN = ((0,), (0,))


def mm(a, b, dims):
    return lax.dot_general(a, b, (dims, ((), ())), preferred_element_type=F32)


def norm_parts(v):
    c = v - jnp.mean(v, -1, keepdims=True)
    r = lax.rsqrt(jnp.mean(c * c, -1, keepdims=True) + 1e-05)
    return c * r, r


def norm_back(e, n, r):
    return r * (e - jnp.mean(e, -1, keepdims=True) - n * jnp.mean(e * n, -1, keepdims=True))


def colsum(x):
    return jnp.sum(x.astype(F32), 0, keepdims=True)


def when(cond):
    if isinstance(cond, bool):
        return (lambda body: body()) if cond else (lambda body: None)
    return pl.when(cond)


def rows(ref):
    x = ref[...]
    return x.reshape(-1, x.shape[-1])


def layer_kernel(names, *refs):
    R = SimpleNamespace(**dict(zip(names, refs, strict=True)))
    dp, blk, head = [lax.axis_index(a) for a in ("dp", "blk", "head")]
    core, chip_x = lax.rem(blk, 2), lax.div(blk, 2)
    T, D = R.tok.shape
    W = R.q.shape[-1]
    FW = R.wi.shape[1] // 8

    def dev(p, flip):
        hh = lax.rem(head + lax.rem(p, 2), 2)
        bb = lax.rem(chip_x + lax.div(p, 2), 2) * 2 + lax.rem(core + flip, 2)
        return (dp, bb, hh), bb * 2 + hh

    def c32(i):
        return jnp.asarray(i, jnp.int32)

    me = blk * 2 + head
    partner, partner_at = dev(c32(0), 1)
    z_end = lax.rem(dp, 3) == 0
    z_other = jnp.where(dp == 0, 1, jnp.where(dp == 3, 2, jnp.where(dp == 1, 0, 3)))
    z_mid = jnp.where(dp == 1, 2, 1)

    def rcopy(src, dst, ssem, rsem, to):
        return pltpu.make_async_remote_copy(src, dst, ssem, rsem, device_id=to, device_id_type=MESH)

    def lanes(i, w):
        return pl.ds(pl.multiple_of(i * w, w), w)

    bar = pltpu.get_barrier_semaphore()
    for e in range(1, 8):
        to, _ = dev(c32(e // 2), e % 2)
        pl.semaphore_signal(bar, 1, device_id=to, device_id_type=MESH)
    for j in range(1, 4):
        pl.semaphore_signal(bar, 1, device_id=(lax.rem(dp + j, 4), blk, head), device_id_type=MESH)
    pl.semaphore_wait(bar, 10)

    half = (pl.ds(0, T // 2), pl.ds(T // 2, T // 2))
    by_y, by_x, by_both = 1, 2, 3

    def ag_direct(buf, r, p, h):
        to, _ = dev(c32(p), 0)
        part = buf.at[me, half[h]]
        return rcopy(part, part, R.ag_s.at[r, p, h], R.ag_r.at[r, p, h], to)

    def ag_relay(buf, r, h):
        via, over = (by_x, by_y) if h == 0 else (by_y, by_x)
        _, at = dev(c32(via), 0)
        to, _ = dev(c32(over), 0)
        part = buf.at[at, half[h]]
        return rcopy(part, part, R.ag_s.at[r, by_both, h], R.ag_r.at[r, by_both, h], to)

    def ag_home(buf, r):
        return rcopy(buf.at[me], buf.at[me], R.ag_fs.at[r, 0, 0], R.ag_f.at[r, 0, 0], partner)

    def ag_forward(buf, r, p, h):
        _, at = dev(c32(p), 0)
        part = buf.at[at, half[h]]
        return rcopy(part, part, R.ag_fs.at[r, p, h], R.ag_f.at[r, p, h], partner)

    def ag_start(buf, r):
        ag_direct(buf, r, by_x, 0).start()
        ag_direct(buf, r, by_y, 1).start()
        ag_direct(buf, r, by_x, 1).start()
        ag_direct(buf, r, by_y, 0).start()
        ag_home(buf, r).start()

    def ag_got(buf, r, p, h):
        (ag_relay(buf, r, h) if p == by_both else ag_direct(buf, r, p, h)).wait_recv()
        ag_forward(buf, r, p, h).start()

    def ag_wait(buf, r, p, relayed=lambda: None):
        @when(p == 0)
        def _():
            ag_home(buf, r).wait_recv()

        @when(p == by_y)
        def _():
            ag_got(buf, r, by_x, 0)
            ag_relay(buf, r, 0).start()
            ag_got(buf, r, by_y, 1)
            ag_relay(buf, r, 1).start()
            relayed()
            ag_got(buf, r, by_y, 0)
            ag_got(buf, r, by_x, 1)
            for h in (0, 1):
                ag_forward(buf, r, by_y, h).wait_recv()

        @when(p == by_x)
        def _():
            ag_got(buf, r, by_both, 0)
            ag_got(buf, r, by_both, 1)
            for h in (0, 1):
                ag_forward(buf, r, by_x, h).wait_recv()

        @when(p == by_both)
        def _():
            for h in (0, 1):
                ag_forward(buf, r, by_both, h).wait_recv()

    def ag_finish(buf, r):
        ag_home(buf, r).wait_send()
        for h in (0, 1):
            ag_direct(buf, r, by_x, h).wait_send()
            ag_direct(buf, r, by_y, h).wait_send()
            ag_relay(buf, r, h).wait_send()
            for p in (by_y, by_x, by_both):
                ag_forward(buf, r, p, h).wait_send()

    def pair(buf, p):
        a, b = dev(p, 0)[1], dev(p, 1)[1]
        return a, b, jnp.concatenate([buf[a], buf[b]], 0)

    def rs_chip(r, p):
        return rcopy(R.snd_c.at[p], R.rcv_c.at[r, p], R.rs_cs.at[r, p], R.rs_cr.at[r, p], partner)

    def rs_link(r, p, h):
        over = p if p != by_both else (by_x, by_y)[h]
        to, _ = dev(c32(over), 0)
        return rcopy(
            R.snd_l.at[p, half[h]], R.rcv_l.at[r, p, half[h]], R.rs_ls.at[r, p, h], R.rs_lr.at[r, p, h], to
        )

    def rs_put(r, p, part):
        R.snd_c[p] = part[T:].astype(BF)
        rs_chip(r, p).start()
        R.keep[p] = part[:T]

    def rs_combine(r, p):
        rs_chip(r, p).wait_recv()
        both = R.keep[p] + R.rcv_c[r, p].astype(F32)
        R.keep[p] = both
        R.snd_l[p] = both.astype(BF)

        @when(p == by_y)
        def _():
            rs_link(r, by_y, 1).start()

        @when(p == by_x)
        def _():
            rs_link(r, by_x, 0).start()

        @when(p == by_both)
        def _():
            rs_link(r, by_both, 0).start()
            rs_link(r, by_both, 1).start()

    def rs_relay(r):
        for p, h in ((by_y, 0), (by_x, 1)):
            rs_link(r, by_both, h).wait_recv()
            R.snd_l[p, half[h]] = (R.keep[p, half[h]] + R.rcv_l[r, by_both, half[h]].astype(F32)).astype(BF)
            rs_link(r, p, h).start()

    def rs_final(r):
        rs_chip(r, c32(0)).wait_recv()
        acc = R.keep[0] + R.rcv_c[r, 0].astype(F32)
        for p in (by_y, by_x):
            for h in (0, 1):
                rs_link(r, p, h).wait_recv()
            acc = acc + R.rcv_l[r, p].astype(F32)
        for p in range(4):
            rs_chip(r, c32(p)).wait_send()
            if p:
                for h in (0, 1):
                    rs_link(r, p, h).wait_send()
        return acc

    quarter = (pl.ds(0, T // 4), pl.ds(T // 4, T // 4))
    chunks = [("b", lambda x, q=q: x.at[0, q], T // 4) for q in quarter] + [("b", lambda x: x.at[0, half[1]], T // 2)]
    chunks += [("b", lambda x, i=i, h=h: x.at[i, h], T // 2) for i in range(1, 4) for h in half]
    chunks += [("i", lambda x, t=t: x.at[t], T // 2) for t in range(8)]
    chunks += [("o", lambda x, h=h: x.at[h], T // 2) for h in half] + [("s", lambda x: x, 1)]
    chunks += [("w", lambda x, t=t: x.at[t], 3 * T // 8) for t in range(7)]
    chunks += [("w", lambda x, h=h: x.at[7, h], 3 * T // 16) for h in half]
    Z_IN, Z_OUT, Z_SMALL, Z_QKV, Z_ALL = 9, 17, 19, 20, len(chunks)

    def zrefs(c):
        k, cut, _ = chunks[c]
        return cut(getattr(R, "zown_" + k)), cut(getattr(R, "zsum_" + k)), cut(getattr(R, "zmid_" + k))

    def z_up(c):
        own, tot, _ = zrefs(c)
        return rcopy(own, tot, R.z_s.at[c, 0], R.z_r.at[c, 0], (z_other, blk, head))

    def z_across(c):
        own, _, mid = zrefs(c)
        return rcopy(own, mid, R.z_s.at[c, 0], R.z_r.at[c, 1], (z_mid, blk, head))

    def z_down(c):
        _, tot, _ = zrefs(c)
        return rcopy(tot, tot, R.z_s.at[c, 1], R.z_r.at[c, 0], (z_other, blk, head))

    row_us, hop_us = 0.0432, 2.0
    steps, sent = [], 0.0
    for c, (_, _, n) in enumerate(chunks):
        sent += n * row_us
        steps += [(sent + hop_us, c, 0), (sent + n * row_us + 2.2 * hop_us, c, 1)]
    steps.sort()
    made = set()

    def z_until(us):
        while steps and steps[0][0] <= us and steps[0][1] in made:
            _, c, second = steps.pop(0)
            (z_two if second else z_one)(c)

    def z_produce(c):
        made.add(c)

        @pl.when(z_end)
        def _():
            z_up(c).start()

    def z_one(c):
        @pl.when(jnp.logical_not(z_end))
        def _():
            own, tot, _ = zrefs(c)
            z_up(c).wait_recv()
            own[...] = (own[...].astype(F32) + tot[...].astype(F32)).astype(BF)
            z_across(c).start()

    def z_two(c):
        @pl.when(jnp.logical_not(z_end))
        def _():
            own, tot, mid = zrefs(c)
            z_across(c).wait_recv()
            tot[...] = (own[...].astype(F32) + mid[...].astype(F32)).astype(BF)
            z_down(c).start()

    def z_finish(c):
        @pl.when(z_end)
        def _():
            z_up(c).wait_send()
            if not Z_IN <= c < Z_OUT:
                z_down(c).wait_recv()

        @pl.when(jnp.logical_not(z_end))
        def _():
            z_across(c).wait_send()
            z_down(c).wait_send()

    tok_all, y1_all, df_all, da_all = R.tok_all, R.y1_all, R.df_all, R.da_all
    local = [
        pltpu.make_async_copy(R.tok, tok_all.at[me], R.loc.at[0]),
        pltpu.make_async_copy(R.wb, R.wb_v, R.loc.at[1]),
        pltpu.make_async_copy(R.wo, R.wo_v, R.loc.at[2]),
        pltpu.make_async_copy(R.wi.at[:, lanes(me, FW)], R.win.at[me], R.loc.at[3]),
        pltpu.make_async_copy(R.cot, R.cot_v, R.loc.at[4]),
    ]
    for j, w in enumerate((R.wq, R.wk, R.wv)):
        local.append(pltpu.make_async_copy(w.at[:, lanes(me, W)], R.wqkv.at[me, :, pl.ds(j * W, W)], R.loc.at[5 + j]))
    for cp in local:
        cp.start()
    vecs = [x[...].astype(F32).reshape(1, T) for x in (R.bo, R.bb, R.g1, R.s1, R.g2, R.s2)]
    vecs.append(R.ids[0:1, lanes(head, T)].astype(F32))
    R.vec[...] = jnp.concatenate(vecs + [jnp.zeros((1, T), F32)], 0)
    R.vec_all[me] = R.vec[...]

    def vec_copy(e):
        to, _ = dev(c32(e // 2), e % 2)
        return rcopy(R.vec, R.vec_all.at[me], R.vec_s.at[e], R.vec_r.at[e], to)

    def qkv_copy(e, j):
        to, at = dev(c32(e // 2), e % 2)
        w = (R.wq, R.wk, R.wv)[j]
        return rcopy(w.at[:, lanes(at, W)], R.wqkv.at[me, :, pl.ds(j * W, W)], R.qkv_s.at[e, j], R.qkv_r.at[e, j], to)

    def win_copy(e):
        to, at = dev(c32(e // 2), e % 2)
        return rcopy(R.wi.at[:, lanes(at, FW)], R.win.at[me], R.win_s.at[e], R.win_r.at[e], to)

    far_first = (6, 7, 2, 3, 4, 5, 1)
    with jax.named_scope("start_copies"):
        for e in far_first:
            vec_copy(e).start()
        for e in far_first:
            for j in range(3):
                qkv_copy(e, j).start()
        local[0].wait()
        ag_start(tok_all, 0)

    with jax.named_scope("vectors"):
        for e in range(1, 8):
            vec_copy(e).wait_recv()
        for s in range(8):
            v = R.vec_all[s]
            R.vfull[:, s * T:(s + 1) * T] = v
            ids = jnp.broadcast_to(v[6:7], (T, T)).T
            R.segk[s] = jnp.where(ids < 0, -2.0, ids)

    with jax.named_scope("wait_qkv_weights"):
        for e in range(1, 8):
            for j in range(3):
                qkv_copy(e, j).wait_recv()
        for j in range(5, 8):
            local[j].wait()

    def qkv_step(p, carry):
        ag_wait(tok_all, 0, p)

        @when(p == by_y)
        def _():
            for e in far_first:
                win_copy(e).start()

        a, b, x = pair(tok_all, p)
        y = mm(x, rows(R.wqkv), NN)
        qq = ((y[:, :W] + R.bq[...].astype(F32).reshape(1, W)) * 0.125).astype(BF)
        kk = y[:, W:2 * W].astype(BF)
        vv = (y[:, 2 * W:] + R.bv[...].astype(F32).reshape(1, W)).astype(BF)
        for at, sl in ((a, slice(0, T)), (b, slice(T, 2 * T))):
            R.q[at], R.k[at], R.v[at] = qq[sl], kk[sl], vv[sl]
        return carry

    with jax.named_scope("project_qkv"):
        lax.fori_loop(0, 4, qkv_step, 0)
    for i in (1, 2, 3, 4):
        local[i].wait()

    def head_mask(h, like):
        lane = lax.broadcasted_iota(jnp.int32, like.shape, 1)
        return jnp.where(lax.div(lane, HD) == h, like, jnp.zeros_like(like))

    heads = W // HD

    def ids_of(a, b):
        return jnp.concatenate([R.vec_all[a, 6:7], R.vec_all[b, 6:7]], 1)

    def attend_step(i, carry):
        p = 3 - i
        a, b, qp = pair(R.q, p)
        segq = ids_of(a, b)
        segk = rows(R.segk)
        allowed = jnp.concatenate([segk, segk], 1) == segq
        kk = rows(R.k)
        outs = []
        scores = [mm(kk, head_mask(h, qp), NT) for h in range(heads)]
        for h in range(heads):
            s = jnp.where(allowed, scores[h], -1e30)
            ex = jnp.exp(s - jnp.max(s, 0, keepdims=True))
            total = jnp.maximum(jnp.sum(ex, 0, keepdims=True), 1.0)
            pt = (ex * jnp.where(segq >= 0, 1.0 / total, 0.0)).astype(BF)
            R.pt[h, p] = pt
            outs.append(mm(R.vt[h * HD:(h + 1) * HD, :], pt, NN))
            if h == 0:
                @pl.when(p < 3)
                def _():
                    rs_combine(0, p + 1)

        ct = jnp.concatenate(outs, 0).astype(BF)
        R.ctxt[:, lanes(a, T)] = ct[:, :T]
        R.ctxt[:, lanes(b, T)] = ct[:, T:]
        rs_put(0, p, mm(ct, R.wo_v[...], TN))
        return carry

    with jax.named_scope("attend"):
        R.vt[...] = rows(R.v).T
        lax.fori_loop(0, 4, attend_step, 0)

    with jax.named_scope("first_norm"):
        rs_relay(0)
        rs = rs_final(0)
        h1 = tok_all[me].astype(F32) + rs + R.vfull[0:1]
        n1, r1 = norm_parts(h1)
        y1 = n1 * R.vfull[2:3] + R.vfull[3:4]
        R.n1[...], R.y1[...] = n1, y1
        R.r1[...] = jnp.broadcast_to(r1, R.r1.shape)
        y1_all[me] = y1.astype(BF)
        ag_start(y1_all, 1)
    R.kt[...] = rows(R.k).T

    with jax.named_scope("wait_hidden_weights"):
        for e in range(1, 8):
            win_copy(e).wait_recv()

    def hidden_step(p, carry):
        ag_wait(y1_all, 1, p)

        @pl.when(p > 1)
        def _():
            rs_combine(1, p - 1)
        a, b, x = pair(y1_all, p)
        z = hidden_in(x)
        cdf = 0.5 * (1.0 + lax.erf(z * 0.7071067811865476))
        low = (z * cdf).astype(BF)
        slope = cdf + z * (jnp.exp(-0.5 * z * z) * 0.3989422804014327)
        R.hid[a], R.hid[b] = low[:T], low[T:]
        R.slope[a], R.slope[b] = slope[:T], slope[T:]
        rs_put(1, p, mm(low, R.wb_v[...], NN))

        return carry

    def hidden_in(x):
        return mm(x, rows(R.win), NN) + R.bi[...].astype(F32).reshape(1, FW)

    with jax.named_scope("hidden"):
        lax.fori_loop(0, 4, hidden_step, 0)
        rs_combine(1, c32(3))

    with jax.named_scope("second_norm"):
        rs_relay(1)
        rs = rs_final(1)
        h2 = R.y1[...] + rs + R.vfull[1:2]
        n2, r2 = norm_parts(h2)
        gain = R.vfull[4:5]
        R.out[...] = (n2 * gain + R.vfull[5:6]).astype(BF)
        cot = R.cot_v[...].astype(F32)
        dh2 = norm_back(cot * gain, n2, r2)
        R.dh2[...] = dh2
        df_all[me] = dh2.astype(BF)
        ag_start(df_all, 2)
        R.sv[0:1, :] = colsum(cot * n2)
        R.sv[1:2, :] = colsum(cot)

    def grad_back(i):
        x = R.hid[:, :, i * T:(i + 1) * T].reshape(8 * T, T)
        R.zown_b[i] = mm(x, rows(df_all), TN).astype(BF)
        for c in range(3) if i == 0 else (2 * i + 1, 2 * i + 2):
            z_produce(c)

    def hidden_back_step(p, carry):
        ag_wait(df_all, 2, p)

        @pl.when(p > 1)
        def _():
            rs_combine(2, p - 1)

        @when(p == by_both)
        def _():
            grad_back(0)

        a, b, x = pair(df_all, p)
        slope = jnp.concatenate([R.slope[a], R.slope[b]], 0)
        dz = (mm(x, R.wb_v[...], NT) * slope).astype(BF)
        R.dz[a], R.dz[b] = dz[:T], dz[T:]
        rs_put(2, p, mm(dz, rows(R.win), NT))

        return carry

    with jax.named_scope("hidden_back"):
        lax.fori_loop(0, 4, hidden_back_step, 0)
        rs_combine(2, c32(3))

    with jax.named_scope("grad_back"):
        for i in range(1, 4):
            grad_back(i)
        z_until(6.0)
        rs_relay(2)
        z_until(7.5)

    def grad_in(i):
        x = y1_all[:, :, 2 * i * T:(2 * i + 2) * T].reshape(8 * T, 2 * T)
        g = mm(x, rows(R.dz), TN).astype(BF)
        R.zown_i[2 * i], R.zown_i[2 * i + 1] = g[:T], g[T:]
        z_produce(Z_IN + 2 * i)
        z_produce(Z_IN + 2 * i + 1)

    def din_copy(t, s):
        return rcopy(R.zsum_i.at[t], R.grad_i.at[s], R.din_s.at[t], R.din_r.at[s], (dp, t // 2, t % 2))

    def z_deliver(t):
        @pl.when(z_end)
        def _():
            z_down(Z_IN + t).wait_recv()

        @pl.when(me != t)
        def _():
            din_copy(t, me).start()

        @pl.when(me == t)
        def _():
            R.grad_i[me] = R.zsum_i[t]

    with jax.named_scope("grad_in"):
        for i in range(4):
            grad_in(i)
            if i % 2:
                z_until(8.0 + i)

    with jax.named_scope("first_norm_back"):
        rs = rs_final(2)
        dy1 = R.dh2[...] + rs
        n1 = R.n1[...]
        dh1 = norm_back(dy1 * R.vfull[2:3], n1, R.r1[:, 0:1])
        R.dh1[...] = dh1
        da_all[me] = dh1.astype(BF)
        ag_start(da_all, 3)
        R.sv[2:3, :] = colsum(dy1 * n1)
        R.sv[3:4, :] = colsum(dy1)

    def sv_copy(e):
        to, at = dev(c32(e // 2), e % 2)
        return rcopy(R.sv.at[:, lanes(at, T)], R.sv_rcv.at[me], R.sv_s.at[e], R.sv_r.at[e], to)

    for e in far_first:
        sv_copy(e).start()
    R.sv_rcv[me] = R.sv[:, lanes(me, T)]

    z_until(12.0)

    R.dk[...] = jnp.zeros_like(R.dk)
    R.dv[...] = jnp.zeros_like(R.dv)

    def attend_back_step(p):
        ag_wait(da_all, 3, p, lambda: z_until(17.0))
        z_until((13.8, 20.0, 23.0, 25.8)[p])
        a, b, x = pair(da_all, c32(p))
        qp = jnp.concatenate([R.q[a], R.q[b]], 0)
        dc = mm(x, R.wo_v[...], NT).astype(BF)
        vv = rows(R.v)
        outs = []
        for h in range(heads):
            dcm, qm = head_mask(h, dc), head_mask(h, qp)
            low = R.pt[h, p]
            pt = low.astype(F32)
            dpt = mm(vv, dcm, NT)
            ds = (pt * (dpt - jnp.sum(pt * dpt, 0, keepdims=True))).astype(BF)
            outs.append(mm(R.kt[h * HD:(h + 1) * HD, :], ds, NN))
            R.dk[...] += mm(ds, qm, NN)
            R.dv[...] += mm(low, dcm, NN)
            z_until((14.8, 21.0, 24.0, 26.8)[p] + h)
        dq = jnp.concatenate(outs, 0).T.astype(BF) * 0.125
        R.dqkv[a, :, 0:W] = dq[:T]
        R.dqkv[b, :, 0:W] = dq[T:]

    with jax.named_scope("attend_back"):
        for p in range(4):
            attend_back_step(p)
        R.dqkv[:, :, W:2 * W] = R.dk[...].astype(BF).reshape(8, T, W)
        R.dqkv[:, :, 2 * W:] = R.dv[...].astype(BF).reshape(8, T, W)

    def dqkv_copy(p, flip):
        to, at = dev(p, flip)
        return rcopy(R.dqkv_snd.at[at], R.zown_w.at[me], R.dqkv_s.at[p, flip], R.dqkv_r.at[p, flip], to)

    def dqkv_step(p):
        a, b = dev(c32(p), 0)[1], dev(c32(p), 1)[1]
        x = jnp.concatenate([tok_all[:, :, lanes(a, T)], tok_all[:, :, lanes(b, T)]], 2).reshape(8 * T, 2 * T)
        g = mm(x, rows(R.dqkv), TN).astype(BF)
        R.dqkv_snd[b] = g[T:]
        dqkv_copy(c32(p), 1).start()
        if p == 0:
            R.zown_w[me] = g[:T]
        else:
            R.dqkv_snd[a] = g[:T]
            dqkv_copy(c32(p), 0).start()
        z_until(28.3 + 0.5 * p)

    with jax.named_scope("grad_qkv"):
        for p in range(4):
            dqkv_step(p)

    with jax.named_scope("grad_out"):
        R.zown_o[...] = mm(R.ctxt[...], rows(da_all), NN).astype(BF)
        z_produce(Z_OUT)
        z_produce(Z_OUT + 1)
        z_until(31.0)

    def input_step(p):
        if p > 1:
            rs_combine(3, p - 1)
        a, b, x = pair(R.dqkv, c32(p))
        rs_put(3, p, mm(x, rows(R.wqkv), NT))
        z_until((30.8, 31.4, 32.8, 34.4)[p])

    with jax.named_scope("input_back"):
        for p in range(4):
            input_step(p)
        rs_combine(3, c32(3))
        z_until(36.5)

    with jax.named_scope("small_grads"):
        for e in range(1, 8):
            sv_copy(e).wait_recv()
        acc = R.sv_rcv[0]
        for s in range(1, 8):
            acc = acc + R.sv_rcv[s]
        own = lanes(me, T)
        parts = [
            acc[0:4],
            colsum(rows(R.dqkv)[:, 0:W]),
            colsum(rows(R.dqkv)[:, 2 * W:]),
            colsum(da_all[:, :, own].reshape(8 * T, T)),
            colsum(df_all[:, :, own].reshape(8 * T, T)),
        ]
        dbi = colsum(rows(R.dz))
        parts += [dbi[:, i * T:(i + 1) * T] for i in range(FW // T)]
        parts.append(jnp.zeros((16 - 8 - FW // T, T), F32))
        R.zown_s[...] = jnp.concatenate(parts, 0).astype(BF)
        z_produce(Z_SMALL)
        z_until(39.0)

    with jax.named_scope("z_rest"):
        for p in range(4):
            for flip in (0, 1):
                if (p, flip) != (0, 0):
                    dqkv_copy(c32(p), flip).wait_recv()
        for c in range(Z_QKV, Z_ALL):
            z_produce(c)
        z_until(42.0)
        rs_relay(3)
        z_until(46.0)
    with jax.named_scope("input_grad"):
        R.igrad[...] = R.dh1[...] + rs_final(3)
    with jax.named_scope("z_last"):
        for t in range(8):
            z_until(49.0 + 2 * t)
            z_deliver(t)
        z_until(1000.0)

    with jax.named_scope("finish"):
        for c in range(Z_ALL):
            z_finish(c)
        for t in range(8):
            @pl.when(me != t)
            def _():
                din_copy(t, t).wait()
        for buf, r in ((tok_all, 0), (y1_all, 1), (df_all, 2), (da_all, 3)):
            ag_finish(buf, r)
        for e in range(1, 8):
            vec_copy(e).wait_send()
            win_copy(e).wait_send()
            sv_copy(e).wait_send()
            for j in range(3):
                qkv_copy(e, j).wait_send()
            dqkv_copy(c32(e // 2), e % 2).wait_send()


def sharded_plan(
    tokens, segment_ids, cotangent,
    w_query, w_key, w_value, w_out, w_in, w_back,
    bias_query, bias_value, bias_out, bias_in, bias_back,
    first_gain, first_shift, second_gain, second_shift,
):
    tokens, cotangent = tokens[0], cotangent[0]
    T, D = tokens.shape
    W, FW = D // 8, w_in.shape[1] // 8
    ins = dict(
        tok=tokens, cot=cotangent, wq=w_query, wk=w_key, wv=w_value, wo=w_out, wi=w_in, wb=w_back, ids=segment_ids,
        bo=bias_out, bb=bias_back, g1=first_gain, s1=first_shift, g2=second_gain, s2=second_shift,
        bq=bias_query, bv=bias_value, bi=bias_in,
    )
    in_hbm = 8
    outs = dict(
        out=((T, D), BF), igrad=((T, D), F32), zsum_b=((4, T, D), BF),
        grad_i=((8, T, FW), BF), zsum_o=((T, D), BF), zsum_w=((8, T, 3 * W), BF), zsum_s=((16, T), BF),
    )
    blocks = {k: ((8, T, D), BF) for k in ("tok_all", "y1_all", "df_all", "da_all")}
    scr = dict(
        **blocks,
        wqkv=((8, T, 3 * W), BF), win=((8, T, FW), BF), wb_v=(w_back.shape, BF), wo_v=(w_out.shape, BF),
        cot_v=((T, D), BF), vec=((8, T), F32), vec_all=((8, 8, T), F32), vfull=((8, D), F32), segk=((8, T, T), F32),
        q=((8, T, W), BF), k=((8, T, W), BF), v=((8, T, W), BF), vt=((W, 8 * T), BF), kt=((W, 8 * T), BF),
        pt=((W // HD, 4, 8 * T, 2 * T), BF), ctxt=((W, 8 * T), BF),
        hid=((8, T, FW), BF), slope=((8, T, FW), F32), dz=((8, T, FW), BF),
        n1=((T, D), F32), r1=((T, 128), F32), y1=((T, D), F32), dh2=((T, D), F32), dh1=((T, D), F32),
        sv=((8, D), F32), sv_rcv=((8, 8, T), F32),
        keep=((4, T, D), F32), snd_c=((4, T, D), BF), snd_l=((4, T, D), BF),
        rcv_c=((4, 4, T, D), BF), rcv_l=((4, 4, T, D), BF),
        dk=((8 * T, W), F32), dv=((8 * T, W), F32), dqkv=((8, T, 3 * W), BF),
        dqkv_snd=((8, T, 3 * W), BF),
        **{z + k[4:]: s for z in ("zown", "zmid") for k, s in outs.items() if k.startswith("zsum")},
        **{k: ((8, T, FW), BF) for k in ("zown_i", "zmid_i", "zsum_i")},
    )
    sems = dict(
        ag_s=(4, 4, 2), ag_r=(4, 4, 2), ag_fs=(4, 4, 2), ag_f=(4, 4, 2),
        rs_cs=(4, 4), rs_cr=(4, 4), rs_ls=(4, 4, 2), rs_lr=(4, 4, 2),
        z_s=(29, 2), z_r=(29, 2), loc=(8,), vec_s=(8,), vec_r=(8,), qkv_s=(8, 3), qkv_r=(8, 3), win_s=(8,), win_r=(8,),
        sv_s=(8,), sv_r=(8,), din_s=(8,), din_r=(8,), dqkv_s=(4, 2), dqkv_r=(4, 2),
    )
    names = list(ins) + list(outs) + list(scr) + list(sems)
    res = pl.pallas_call(
        partial(layer_kernel, names),
        out_shape=[jax.ShapeDtypeStruct(*s) for s in outs.values()],
        in_specs=[pl.BlockSpec(memory_space=pl.ANY if i < in_hbm else pltpu.VMEM) for i in range(len(ins))],
        out_specs=[pl.BlockSpec(memory_space=pltpu.VMEM) for _ in outs],
        scratch_shapes=[pltpu.VMEM(*s) for s in scr.values()] + [pltpu.SemaphoreType.DMA(s) for s in sems.values()],
        compiler_params=pltpu.CompilerParams(collective_id=0, has_side_effects=True, vmem_limit_bytes=60 << 20),
        name="layer",
    )(*ins.values())
    grid = 4
    wide = pl.BlockSpec((T // grid, D), lambda i: (i, 0))

    def whole(n):
        return pl.BlockSpec((n,), lambda i: (0,))

    firsts = [(T, D), (T, D), (T, D), (T, D), (T, D), (T, D), w_in.shape, w_back.shape]
    types = [BF] + [F32] * 7
    return_specs = [wide, wide] + [pl.BlockSpec((T, 2 * T), lambda i: (0, i))] * 3 + [
        wide, pl.BlockSpec((T, 2 * FW), lambda i: (0, i)), pl.BlockSpec((T, D), lambda i: (i, 0)),
    ]
    sizes = [T, T, T, FW, T, T, T, T, T]
    final = pl.pallas_call(
        finish_kernel,
        grid=(grid,),
        out_shape=[jax.ShapeDtypeStruct(s, t) for s, t in zip(firsts, types)]
        + [jax.ShapeDtypeStruct((n,), F32) for n in sizes],
        in_specs=[
            wide, wide, pl.BlockSpec((1, T, D), lambda i: (i, 0, 0)), pl.BlockSpec((2, T, FW), lambda i: (i, 0, 0)),
            wide, pl.BlockSpec((2, T, 3 * W), lambda i: (i, 0, 0)), pl.BlockSpec((16, T), lambda i: (0, 0)),
        ],
        out_specs=return_specs + [whole(n) for n in sizes],
        name="finish",
    )(*res)
    return (final[0][None], final[1][None], *final[2:])


def finish_kernel(out, igrad, tb, ti, to, tw, ts, o_out, o_igrad, o_q, o_k, o_v, o_o, o_i, o_b, *o_small):
    o_out[...] = out[...]
    o_igrad[...] = igrad[...]
    o_b[...] = tb[0].astype(F32)
    o_o[...] = to[...].astype(F32)
    width = ti.shape[2]
    for j in range(2):
        o_i[:, j * width:(j + 1) * width] = ti[j].astype(F32)
    W = tw.shape[2] // 3
    for j, o in enumerate((o_q, o_k, o_v)):
        for s in range(2):
            o[:, s * W:(s + 1) * W] = tw[s, :, j * W:(j + 1) * W].astype(F32)

    @pl.when(pl.program_id(0) == 0)
    def _():
        v = ts[...].astype(F32)
        bq, bv, bo, bi, bb, g1, s1, g2, s2 = o_small
        for o, i in ((bq, 4), (bv, 5), (bo, 6), (bb, 7), (g1, 2), (s1, 3), (g2, 0), (s2, 1)):
            o[...] = v[i]
        n = v.shape[1]
        for i in range(bi.shape[0] // n):
            bi[i * n:(i + 1) * n] = v[8 + i]


def pick_plan(mesh):
    group = mesh.shape["blk"] * mesh.shape["head"]
    return sharded_plan if (mesh.shape["dp"], group) == (4, 8) else general_plan


def flat_dot(left_side, right_side):
    return jnp.dot(
        left_side.reshape(-1, left_side.shape[-1]), right_side, preferred_element_type=jnp.float32
    )


def inner_dot(left_side, right_side):
    return jnp.einsum(
        "ra,rb->ab",
        left_side.reshape(-1, left_side.shape[-1]),
        right_side.reshape(-1, right_side.shape[-1]),
        preferred_element_type=jnp.float32,
    )


def layer_norm(value_rows, gain_row, shift_row):
    centre = jnp.mean(value_rows, -1, keepdims=True)
    centred = value_rows - centre
    spread = jnp.mean(centred * centred, -1, keepdims=True)
    return centred * lax.rsqrt(spread + 1e-05) * gain_row + shift_row


def head_view(array_in):
    return array_in.reshape(array_in.shape[0], array_in.shape[1], -1, HD)


def allowed_pairs(query_ids, key_ids):
    same_doc = (query_ids[:, :, None] == key_ids[:, None, :]) & (key_ids[:, None, :] >= 0)
    return same_doc[:, None]


def forward_step(state_now, arrived, local_data):
    running_max, running_sum, weighted = state_now
    key_block, value_block, key_ids = arrived
    query_block, query_ids = local_data
    scores = jnp.einsum(
        "gqhd,gkhd->ghqk",
        head_view(query_block),
        head_view(key_block),
        preferred_element_type=jnp.float32,
    )
    allowed = allowed_pairs(query_ids, key_ids)
    masked = jnp.where(allowed, scores, -1e30)
    new_max = jnp.maximum(running_max, jnp.max(masked, -1))
    exponents = jnp.where(allowed, jnp.exp(masked - new_max[..., None]), 0.0)
    running_sum = jnp.sum(exponents, -1)
    weighted = jnp.einsum(
        "ghqk,gkhd->ghqd",
        exponents.astype(jnp.bfloat16),
        head_view(value_block),
        preferred_element_type=jnp.float32,
    )
    return (new_max, running_sum, weighted)


def probabilities(query_block, key_block, query_ids, key_ids, log_sums):
    scores = jnp.einsum(
        "gqhd,gkhd->ghqk",
        head_view(query_block),
        head_view(key_block),
        preferred_element_type=jnp.float32,
    )
    allowed = allowed_pairs(query_ids, key_ids)
    masked = jnp.where(allowed, scores, -1e30)
    return jnp.where(allowed, jnp.exp(masked - log_sums.transpose(0, 2, 1)[..., None]), 0.0)


def score_grads(weights_now, grad_block, value_block, deltas):
    grad_weights = jnp.einsum(
        "gqhd,gkhd->ghqk",
        head_view(grad_block),
        head_view(value_block),
        preferred_element_type=jnp.float32,
    )
    return (weights_now * (grad_weights - deltas.transpose(0, 2, 1)[..., None])).astype(
        jnp.bfloat16
    )


def heads_to_rows(array_in):
    return array_in.transpose(0, 2, 1, 3).reshape(array_in.shape[0], array_in.shape[2], -1)


def general_plan(
    tokens,
    segment_ids,
    cotangent,
    w_query,
    w_key,
    w_value,
    w_out,
    w_in,
    w_back,
    bias_query,
    bias_value,
    bias_out,
    bias_in,
    bias_back,
    first_gain,
    first_shift,
    second_gain,
    second_shift,
):
    (
        query_full,
        key_full,
        value_full,
        out_full,
        in_full,
        back_full,
        query_bias,
        value_bias,
        out_bias,
        in_bias,
        back_bias,
        gain_one,
        shift_one,
        gain_two,
        shift_two,
    ) = (
        lax.all_gather(w_query, GROUP, axis=0, tiled=True),
        lax.all_gather(w_key, GROUP, axis=0, tiled=True),
        lax.all_gather(w_value, GROUP, axis=0, tiled=True),
        lax.all_gather(w_out, GROUP, axis=0, tiled=True),
        lax.all_gather(w_in, GROUP, axis=0, tiled=True),
        lax.all_gather(w_back, GROUP, axis=0, tiled=True),
        lax.all_gather(bias_query, GROUP, axis=0, tiled=True),
        lax.all_gather(bias_value, GROUP, axis=0, tiled=True),
        lax.all_gather(bias_out, GROUP, axis=0, tiled=True),
        lax.all_gather(bias_in, GROUP, axis=0, tiled=True),
        lax.all_gather(bias_back, GROUP, axis=0, tiled=True),
        lax.all_gather(first_gain, GROUP, axis=0, tiled=True),
        lax.all_gather(first_shift, GROUP, axis=0, tiled=True),
        lax.all_gather(second_gain, GROUP, axis=0, tiled=True),
        lax.all_gather(second_shift, GROUP, axis=0, tiled=True),
    )
    query_bias = query_bias.astype(jnp.float32)
    value_bias = value_bias.astype(jnp.float32)
    out_bias = out_bias.astype(jnp.float32)
    in_bias = in_bias.astype(jnp.float32)
    back_bias = back_bias.astype(jnp.float32)
    gain_one = gain_one.astype(jnp.float32)
    shift_one = shift_one.astype(jnp.float32)
    gain_two = gain_two.astype(jnp.float32)
    shift_two = shift_two.astype(jnp.float32)
    seq_count = tokens.shape[0]
    query_tok = (
        ((flat_dot(tokens, query_full) + query_bias) * 0.125)
        .astype(jnp.bfloat16)
        .reshape(tokens.shape)
    )
    key_tok = flat_dot(tokens, key_full).astype(jnp.bfloat16).reshape(tokens.shape)
    value_tok = (
        (flat_dot(tokens, value_full) + value_bias).astype(jnp.bfloat16).reshape(tokens.shape)
    )
    query_heads, key_heads, value_heads = (
        lax.all_to_all(query_tok, "head", split_axis=2, concat_axis=1, tiled=True),
        lax.all_to_all(key_tok, "head", split_axis=2, concat_axis=1, tiled=True),
        lax.all_to_all(value_tok, "head", split_axis=2, concat_axis=1, tiled=True),
    )
    rows_here = query_heads.shape[1]
    width_heads = query_heads.shape[2]
    heads_here = width_heads // HD
    start_state = (
        jnp.full((seq_count, heads_here, rows_here), -1e30, jnp.float32),
        jnp.zeros((seq_count, heads_here, rows_here), jnp.float32),
        jnp.zeros((seq_count, heads_here, rows_here, HD), jnp.float32),
    )
    running_max, running_sum, weighted = forward_step(
        start_state,
        (
            lax.all_gather(key_heads, "blk", axis=1, tiled=True),
            lax.all_gather(value_heads, "blk", axis=1, tiled=True),
            lax.all_gather(segment_ids, "blk", axis=1, tiled=True),
        ),
        (query_heads, segment_ids),
    )
    floored = jnp.maximum(running_sum, 1.0)
    ctx_heads = heads_to_rows(weighted / floored[..., None])
    log_sums = (running_max + jnp.log(floored)).transpose(0, 2, 1)
    ctx_tok = lax.all_to_all(
        ctx_heads.astype(jnp.bfloat16), "head", split_axis=1, concat_axis=2, tiled=True
    )
    first_sum = tokens.astype(jnp.float32) + (flat_dot(ctx_tok, out_full) + out_bias).reshape(
        tokens.shape
    )
    first_norm = layer_norm(first_sum, gain_one, shift_one)
    first_low = first_norm.astype(jnp.bfloat16)
    inner_rows = flat_dot(first_low, in_full) + in_bias
    hidden_low = jax.nn.gelu(inner_rows, approximate=False).astype(jnp.bfloat16)
    second_sum = first_norm + (flat_dot(hidden_low, back_full) + back_bias).reshape(tokens.shape)
    output_now, second_pull = jax.vjp(layer_norm, second_sum, gain_two, shift_two)
    grad_second, grad_gain_two, grad_shift_two = second_pull(cotangent.astype(jnp.float32))
    grad_branch = grad_second.astype(jnp.bfloat16)
    grad_back_bias = jnp.sum(grad_branch.astype(jnp.float32), (0, 1))
    grad_back = inner_dot(hidden_low, grad_branch)
    grad_hidden = flat_dot(grad_branch, back_full.T)
    unused_value, gelu_pull = jax.vjp(partial(jax.nn.gelu, approximate=False), inner_rows)
    grad_inner = gelu_pull(grad_hidden)[0].astype(jnp.bfloat16)
    grad_in_bias = jnp.sum(grad_inner.astype(jnp.float32), 0)
    grad_in = inner_dot(first_low, grad_inner)
    grad_first_norm = grad_second + flat_dot(grad_inner, in_full.T).reshape(tokens.shape)
    unused_norm, first_pull = jax.vjp(layer_norm, first_sum, gain_one, shift_one)
    grad_first, grad_gain_one, grad_shift_one = first_pull(grad_first_norm)
    grad_attn = grad_first.astype(jnp.bfloat16)
    grad_out_bias = jnp.sum(grad_attn.astype(jnp.float32), (0, 1))
    grad_out = inner_dot(ctx_tok, grad_attn)
    grad_ctx_tok = flat_dot(grad_attn, out_full.T).astype(jnp.bfloat16).reshape(tokens.shape)
    grad_ctx = lax.all_to_all(grad_ctx_tok, "head", split_axis=2, concat_axis=1, tiled=True)
    deltas = jnp.sum(head_view(grad_ctx).astype(jnp.float32) * head_view(ctx_heads), -1)
    key_block = lax.all_gather(key_heads, "blk", axis=1, tiled=True)
    value_block = lax.all_gather(value_heads, "blk", axis=1, tiled=True)
    key_ids = lax.all_gather(segment_ids, "blk", axis=1, tiled=True)
    weights_now = probabilities(query_heads, key_block, segment_ids, key_ids, log_sums)
    dscores = score_grads(weights_now, grad_ctx, value_block, deltas)
    grad_query_heads = jnp.einsum(
        "ghqk,gkhd->ghqd", dscores, head_view(key_block), preferred_element_type=jnp.float32
    )
    key_part = jnp.einsum(
        "ghqk,gqhd->gkhd", dscores, head_view(query_heads), preferred_element_type=jnp.float32
    )
    value_part = jnp.einsum(
        "ghqk,gqhd->gkhd",
        weights_now.astype(jnp.bfloat16),
        head_view(grad_ctx),
        preferred_element_type=jnp.float32,
    )
    both_parts = jnp.concatenate(
        [
            key_part.reshape(key_part.shape[0], key_part.shape[1], -1),
            value_part.reshape(value_part.shape[0], value_part.shape[1], -1),
        ],
        2,
    )
    grad_query_heads, pair_grads = (grad_query_heads, both_parts)
    pair_home = lax.psum_scatter(
        pair_grads.astype(jnp.bfloat16), "blk", scatter_dimension=1, tiled=True
    ).astype(jnp.float32)
    grad_key_heads = pair_home[:, :, :width_heads].astype(jnp.bfloat16)
    grad_value_heads = pair_home[:, :, width_heads:].astype(jnp.bfloat16)
    grad_query_rows = heads_to_rows(grad_query_heads).astype(jnp.bfloat16)
    grad_query_tok, grad_key_tok, grad_value_tok = (
        lax.all_to_all(grad_query_rows, "head", split_axis=1, concat_axis=2, tiled=True),
        lax.all_to_all(grad_key_heads, "head", split_axis=1, concat_axis=2, tiled=True),
        lax.all_to_all(grad_value_heads, "head", split_axis=1, concat_axis=2, tiled=True),
    )
    grad_query_tok = grad_query_tok * 0.125
    grad_inputs = grad_first + (
        flat_dot(grad_query_tok, query_full.T)
        + flat_dot(grad_key_tok, key_full.T)
        + flat_dot(grad_value_tok, value_full.T)
    ).reshape(tokens.shape)
    (
        shard_wq,
        shard_wk,
        shard_wv,
        shard_wo,
        shard_wi,
        shard_wb,
        shard_bq,
        shard_bv,
        shard_bo,
        shard_bi,
        shard_bb,
        shard_g1,
        shard_s1,
        shard_g2,
        shard_s2,
    ) = (
        lax.psum_scatter(
            inner_dot(tokens, grad_query_tok), GROUP, scatter_dimension=0, tiled=True
        ),
        lax.psum_scatter(
            inner_dot(tokens, grad_key_tok), GROUP, scatter_dimension=0, tiled=True
        ),
        lax.psum_scatter(
            inner_dot(tokens, grad_value_tok), GROUP, scatter_dimension=0, tiled=True
        ),
        lax.psum_scatter(grad_out, GROUP, scatter_dimension=0, tiled=True),
        lax.psum_scatter(grad_in, GROUP, scatter_dimension=0, tiled=True),
        lax.psum_scatter(grad_back, GROUP, scatter_dimension=0, tiled=True),
        lax.psum_scatter(
            jnp.sum(grad_query_tok.astype(jnp.float32), (0, 1)),
            GROUP,
            scatter_dimension=0,
            tiled=True,
        ),
        lax.psum_scatter(
            jnp.sum(grad_value_tok.astype(jnp.float32), (0, 1)),
            GROUP,
            scatter_dimension=0,
            tiled=True,
        ),
        lax.psum_scatter(grad_out_bias, GROUP, scatter_dimension=0, tiled=True),
        lax.psum_scatter(grad_in_bias, GROUP, scatter_dimension=0, tiled=True),
        lax.psum_scatter(grad_back_bias, GROUP, scatter_dimension=0, tiled=True),
        lax.psum_scatter(grad_gain_one, GROUP, scatter_dimension=0, tiled=True),
        lax.psum_scatter(grad_shift_one, GROUP, scatter_dimension=0, tiled=True),
        lax.psum_scatter(grad_gain_two, GROUP, scatter_dimension=0, tiled=True),
        lax.psum_scatter(grad_shift_two, GROUP, scatter_dimension=0, tiled=True),
    )
    (
        total_wq,
        total_wk,
        total_wv,
        total_wo,
        total_wi,
        total_wb,
        total_bq,
        total_bv,
        total_bo,
        total_bi,
        total_bb,
        total_g1,
        total_s1,
        total_g2,
        total_s2,
    ) = (
        lax.psum(shard_wq.astype(jnp.bfloat16), "dp").astype(jnp.float32),
        lax.psum(shard_wk.astype(jnp.bfloat16), "dp").astype(jnp.float32),
        lax.psum(shard_wv.astype(jnp.bfloat16), "dp").astype(jnp.float32),
        lax.psum(shard_wo.astype(jnp.bfloat16), "dp").astype(jnp.float32),
        lax.psum(shard_wi.astype(jnp.bfloat16), "dp").astype(jnp.float32),
        lax.psum(shard_wb.astype(jnp.bfloat16), "dp").astype(jnp.float32),
        lax.psum(shard_bq.astype(jnp.bfloat16), "dp").astype(jnp.float32),
        lax.psum(shard_bv.astype(jnp.bfloat16), "dp").astype(jnp.float32),
        lax.psum(shard_bo.astype(jnp.bfloat16), "dp").astype(jnp.float32),
        lax.psum(shard_bi.astype(jnp.bfloat16), "dp").astype(jnp.float32),
        lax.psum(shard_bb.astype(jnp.bfloat16), "dp").astype(jnp.float32),
        lax.psum(shard_g1.astype(jnp.bfloat16), "dp").astype(jnp.float32),
        lax.psum(shard_s1.astype(jnp.bfloat16), "dp").astype(jnp.float32),
        lax.psum(shard_g2.astype(jnp.bfloat16), "dp").astype(jnp.float32),
        lax.psum(shard_s2.astype(jnp.bfloat16), "dp").astype(jnp.float32),
    )
    return (
        output_now.astype(jnp.bfloat16),
        grad_inputs,
        total_wq,
        total_wk,
        total_wv,
        total_wo,
        total_wi,
        total_wb,
        total_bq,
        total_bv,
        total_bo,
        total_bi,
        total_bb,
        total_g1,
        total_s1,
        total_g2,
        total_s2,
    )


def solution(mesh):
    in_specs = (
        P("dp", GROUP, None),
        P("dp", "blk"),
        P("dp", GROUP, None),
        P(GROUP, None),
        P(GROUP, None),
        P(GROUP, None),
        P(GROUP, None),
        P(GROUP, None),
        P(GROUP, None),
        P(GROUP),
        P(GROUP),
        P(GROUP),
        P(GROUP),
        P(GROUP),
        P(GROUP),
        P(GROUP),
        P(GROUP),
        P(GROUP),
    )
    out_specs = (
        P("dp", GROUP, None),
        P("dp", GROUP, None),
        P(GROUP, None),
        P(GROUP, None),
        P(GROUP, None),
        P(GROUP, None),
        P(GROUP, None),
        P(GROUP, None),
        P(GROUP),
        P(GROUP),
        P(GROUP),
        P(GROUP),
        P(GROUP),
        P(GROUP),
        P(GROUP),
        P(GROUP),
        P(GROUP),
    )
    plan = pick_plan(mesh)
    return jax.shard_map(
        plan, mesh=mesh, in_specs=in_specs, out_specs=out_specs, check_vma=False
    )
```

```python
from functools import partial
from types import SimpleNamespace

import jax
import jax.numpy as jnp
from jax import lax
from jax.experimental import pallas as pl
from jax.experimental.pallas import tpu as pltpu
from jax.sharding import PartitionSpec as P

HD = 64
BF = jnp.bfloat16
F32 = jnp.float32
GROUP = ("blk", "head")
MESH = pl.DeviceIdType.MESH
NN = ((1,), (0,))
NT = ((1,), (1,))
TN = ((0,), (0,))


def mm(a, b, dims):
    return lax.dot_general(a, b, (dims, ((), ())), preferred_element_type=F32)


def norm_parts(v):
    c = v - jnp.mean(v, -1, keepdims=True)
    r = lax.rsqrt(jnp.mean(c * c, -1, keepdims=True) + 1e-05)
    return c * r, r


def norm_back(e, n, r):
    return r * (e - jnp.mean(e, -1, keepdims=True) - n * jnp.mean(e * n, -1, keepdims=True))


def colsum(x):
    return jnp.sum(x.astype(F32), 0, keepdims=True)


def when(cond):
    if isinstance(cond, bool):
        return (lambda body: body()) if cond else (lambda body: None)
    return pl.when(cond)


def rows(ref):
    x = ref[...]
    return x.reshape(-1, x.shape[-1])


def layer_kernel(names, *refs):
    R = SimpleNamespace(**dict(zip(names, refs, strict=True)))
    dp, blk, head = [lax.axis_index(a) for a in ("dp", "blk", "head")]
    core, chip_x = lax.rem(blk, 2), lax.div(blk, 2)
    T, D = R.tok.shape
    W = R.q.shape[-1]
    FW = R.wi.shape[1] // 8

    def dev(p, flip):
        hh = lax.rem(head + lax.rem(p, 2), 2)
        bb = lax.rem(chip_x + lax.div(p, 2), 2) * 2 + lax.rem(core + flip, 2)
        return (dp, bb, hh), bb * 2 + hh

    def c32(i):
        return jnp.asarray(i, jnp.int32)

    me = blk * 2 + head
    partner, partner_at = dev(c32(0), 1)
    z_end = lax.rem(dp, 3) == 0
    z_other = jnp.where(dp == 0, 1, jnp.where(dp == 3, 2, jnp.where(dp == 1, 0, 3)))
    z_mid = jnp.where(dp == 1, 2, 1)

    def rcopy(src, dst, ssem, rsem, to):
        return pltpu.make_async_remote_copy(src, dst, ssem, rsem, device_id=to, device_id_type=MESH)

    def all_of(ref, ssem, rsem):
        return rcopy(ref, ref, ssem, rsem, partner)

    seven = pl.ds(0, 7)

    def lanes(i, w):
        return pl.ds(pl.multiple_of(i * w, w), w)

    tok_all, y1_all, df_all, da_all = R.tok_all, R.y1_all, R.df_all, R.da_all
    small_in = (R.ids, R.bo, R.bb, R.g1, R.s1, R.g2, R.s2, R.bq, R.bv, R.bi)
    small_v = (R.ids_v, R.bo_v, R.bb_v, R.g1_v, R.s1_v, R.g2_v, R.s2_v, R.bq_v, R.bv_v, R.bi_v)
    local = [
        pltpu.make_async_copy(R.tok, tok_all.at[me], R.loc.at[0]),
        pltpu.make_async_copy(R.wb, R.wb_v, R.loc.at[1]),
        pltpu.make_async_copy(R.wo, R.wo_v, R.loc.at[2]),
        pltpu.make_async_copy(R.wi.at[:, lanes(me, FW)], R.win.at[me], R.loc.at[3]),
        pltpu.make_async_copy(R.cot, R.cot_v, R.loc.at[4]),
    ]
    for j, w in enumerate((R.wq, R.wk, R.wv)):
        local.append(pltpu.make_async_copy(w.at[:, lanes(me, W)], R.wqkv.at[me, :, pl.ds(j * W, W)], R.loc.at[5]))
    small = [
        pltpu.make_async_copy(x, y, R.small_s.at[i])
        for i, (x, y) in enumerate(zip(small_in, small_v, strict=True))
    ]
    for cp in local + small:
        cp.start()

    bar = pltpu.get_barrier_semaphore()
    for e in range(1, 8):
        to, _ = dev(c32(e // 2), e % 2)
        pl.semaphore_signal(bar, 1, device_id=to, device_id_type=MESH)
    for j in range(1, 4):
        pl.semaphore_signal(bar, 1, device_id=(lax.rem(dp + j, 4), blk, head), device_id_type=MESH)
    pl.semaphore_wait(bar, 10)

    put_out = pltpu.make_async_copy(R.out_v, R.out, R.put_s.at[0])
    put_igrad = pltpu.make_async_copy(R.igrad_v, R.igrad, R.put_s.at[1])

    half = (pl.ds(0, T // 2), pl.ds(T // 2, T // 2))
    by_y, by_x, by_both = 1, 2, 3

    def ag_direct(buf, r, p, h):
        to, _ = dev(c32(p), 0)
        part = buf.at[me, half[h]]
        return rcopy(part, part, R.ag_s.at[r], R.ag_r.at[p, h], to)

    def ag_relay(buf, r, h):
        via, over = (by_x, by_y) if h == 0 else (by_y, by_x)
        _, at = dev(c32(via), 0)
        to, _ = dev(c32(over), 0)
        part = buf.at[at, half[h]]
        return rcopy(part, part, R.ag_s.at[r], R.ag_r.at[by_both, h], to)

    def ag_home(buf, r):
        return rcopy(buf.at[me], buf.at[me], R.ag_s.at[r], R.ag_f.at[0, 0], partner)

    def ag_forward(buf, r, p, h):
        _, at = dev(c32(p), 0)
        part = buf.at[at, half[h]]
        return rcopy(part, part, R.ag_s.at[r], R.ag_f.at[p, h], partner)

    def ag_start(buf, r):
        ag_direct(buf, r, by_x, 0).start()
        ag_direct(buf, r, by_y, 1).start()
        ag_direct(buf, r, by_x, 1).start()
        ag_direct(buf, r, by_y, 0).start()
        ag_home(buf, r).start()

    def ag_got(buf, r, p, h):
        (ag_relay(buf, r, h) if p == by_both else ag_direct(buf, r, p, h)).wait_recv()
        ag_forward(buf, r, p, h).start()

    def ag_wait(buf, r, p, relayed=lambda: None):
        @when(p == 0)
        def _():
            ag_home(buf, r).wait_recv()

        @when(p == by_y)
        def _():
            ag_got(buf, r, by_x, 0)
            ag_relay(buf, r, 0).start()
            ag_got(buf, r, by_y, 1)
            ag_relay(buf, r, 1).start()
            relayed()
            ag_got(buf, r, by_y, 0)
            ag_got(buf, r, by_x, 1)
            for h in (0, 1):
                ag_forward(buf, r, by_y, h).wait_recv()

        @when(p == by_x)
        def _():
            ag_got(buf, r, by_both, 0)
            ag_got(buf, r, by_both, 1)
            for h in (0, 1):
                ag_forward(buf, r, by_x, h).wait_recv()

        @when(p == by_both)
        def _():
            for h in (0, 1):
                ag_forward(buf, r, by_both, h).wait_recv()

    def ag_finish(buf, r):
        all_of(buf.at[seven], R.ag_s.at[r], R.ag_r.at[0, 0]).wait_send()

    def pair(buf, p):
        a, b = dev(p, 0)[1], dev(p, 1)[1]
        return a, b, jnp.concatenate([buf[a], buf[b]], 0)

    def rs_chip(r, p):
        return rcopy(R.snd_c.at[p], R.rcv_c.at[r, p], R.rs_s.at[0], R.rs_cr.at[p], partner)

    def rs_link(r, p, h):
        over = p if p != by_both else (by_x, by_y)[h]
        to, _ = dev(c32(over), 0)
        return rcopy(
            R.snd_l.at[p, half[h]], R.rcv_l.at[r, p, half[h]], R.rs_s.at[1], R.rs_lr.at[p, h], to
        )

    def rs_put(r, p, part):
        R.snd_c[p] = part[T:].astype(BF)
        rs_chip(r, p).start()
        R.keep[p] = part[:T]

    def rs_combine(r, p):
        rs_chip(r, p).wait_recv()
        both = R.keep[p] + R.rcv_c[r, p].astype(F32)
        R.keep[p] = both
        R.snd_l[p] = both.astype(BF)

        @when(p == by_y)
        def _():
            rs_link(r, by_y, 1).start()

        @when(p == by_x)
        def _():
            rs_link(r, by_x, 0).start()

        @when(p == by_both)
        def _():
            rs_link(r, by_both, 0).start()
            rs_link(r, by_both, 1).start()

    def rs_relay(r):
        for p, h in ((by_y, 0), (by_x, 1)):
            rs_link(r, by_both, h).wait_recv()
            R.snd_l[p, half[h]] = (R.keep[p, half[h]] + R.rcv_l[r, by_both, half[h]].astype(F32)).astype(BF)
            rs_link(r, p, h).start()

    def rs_final(r):
        rs_chip(r, c32(0)).wait_recv()
        acc = R.keep[0] + R.rcv_c[r, 0].astype(F32)
        for p in (by_y, by_x):
            for h in (0, 1):
                rs_link(r, p, h).wait_recv()
            acc = acc + R.rcv_l[r, p].astype(F32)
        all_of(R.snd_c, R.rs_s.at[0], R.rs_cr.at[0]).wait_send()
        all_of(R.snd_l.at[pl.ds(1, 3)], R.rs_s.at[1], R.rs_cr.at[0]).wait_send()
        return acc

    quarter = (pl.ds(0, T // 4), pl.ds(T // 4, T // 4))
    chunks = [("b", lambda x, q=q: x.at[0, q], T // 4) for q in quarter] + [("b", lambda x: x.at[0, half[1]], T // 2)]
    chunks += [("b", lambda x, i=i, h=h: x.at[i, h], T // 2) for i in range(1, 4) for h in half]
    chunks += [("i", lambda x, t=t: x.at[t], T // 2) for t in range(8)]
    chunks += [("o", lambda x, h=h: x.at[h], T // 2) for h in half] + [("s", lambda x: x, 1)]
    chunks += [("w", lambda x, t=t: x.at[t], 3 * T // 8) for t in range(7)]
    chunks += [("w", lambda x, h=h: x.at[7, h], 3 * T // 16) for h in half]
    Z_IN, Z_OUT, Z_SMALL, Z_QKV, Z_ALL = 9, 17, 19, 20, len(chunks)

    def zrefs(c):
        k, cut, _ = chunks[c]
        return cut(getattr(R, "zown_" + k)), cut(getattr(R, "zsum_" + k)), cut(getattr(R, "zmid_" + k))

    kinds = "biosw"

    def z_sem(c, way):
        return R.z_s.at[kinds.index(chunks[c][0]), way]

    def z_up(c):
        own, tot, _ = zrefs(c)
        return rcopy(own, tot, z_sem(c, 0), R.z_r.at[c, 0], (z_other, blk, head))

    def z_across(c):
        own, _, mid = zrefs(c)
        return rcopy(own, mid, z_sem(c, 0), R.z_r.at[c, 1], (z_mid, blk, head))

    def z_down(c):
        _, tot, _ = zrefs(c)
        return rcopy(tot, tot, z_sem(c, 1), R.z_r.at[c, 0], (z_other, blk, head))

    row_us, hop_us = 0.0432, 2.0
    steps, sent = [], 0.0
    for c, (_, _, n) in enumerate(chunks):
        sent += n * row_us
        steps += [(sent + hop_us, c, 0), (sent + n * row_us + 2.2 * hop_us, c, 1)]
    steps.sort()
    made = set()

    def z_until(us):
        while steps and steps[0][0] <= us and steps[0][1] in made:
            _, c, second = steps.pop(0)
            (z_two if second else z_one)(c)

    def z_produce(c):
        made.add(c)

        @pl.when(z_end)
        def _():
            z_up(c).start()

    def z_one(c):
        @pl.when(jnp.logical_not(z_end))
        def _():
            own, tot, _ = zrefs(c)
            z_up(c).wait_recv()
            own[...] = (own[...].astype(F32) + tot[...].astype(F32)).astype(BF)
            z_across(c).start()

    def z_two(c):
        @pl.when(jnp.logical_not(z_end))
        def _():
            own, tot, mid = zrefs(c)
            z_across(c).wait_recv()
            tot[...] = (own[...].astype(F32) + mid[...].astype(F32)).astype(BF)
            z_down(c).start()

    def z_finish(c):
        @pl.when(z_end)
        def _():
            if not Z_IN <= c < Z_OUT:
                z_down(c).wait_recv()

    def z_sent():
        for i, k in enumerate(kinds):
            own, tot = getattr(R, "zown_" + k), getattr(R, "zsum_" + k)
            all_of(own, R.z_s.at[i, 0], R.z_r.at[0, 0]).wait_send()

            @pl.when(jnp.logical_not(z_end))
            def _():
                all_of(tot, R.z_s.at[i, 1], R.z_r.at[0, 0]).wait_send()

    def vec_copy(e):
        to, _ = dev(c32(e // 2), e % 2)
        return rcopy(R.vec, R.vec_all.at[me], R.vec_s.at[0], R.vec_s.at[1], to)

    def qkv_copy(e, j):
        to, at = dev(c32(e // 2), e % 2)
        w = (R.wq, R.wk, R.wv)[j]
        return rcopy(w.at[:, lanes(at, W)], R.wqkv.at[me, :, pl.ds(j * W, W)], R.qkv_s.at[0], R.qkv_s.at[1], to)

    def win_copy(e):
        to, at = dev(c32(e // 2), e % 2)
        return rcopy(R.wi.at[:, lanes(at, FW)], R.win.at[me], R.win_s.at[0], R.win_s.at[1], to)

    far_first = (6, 7, 2, 3, 4, 5, 1)
    with jax.named_scope("start_copies"):
        for e in far_first:
            for j in range(3):
                qkv_copy(e, j).start()
        local[0].wait()
        ag_start(tok_all, 0)
        for cp in small:
            cp.wait()
        vecs = [x[...].astype(F32).reshape(1, T) for x in small_v[1:7]]
        vecs.append(R.ids_v[0:1, lanes(head, T)].astype(F32))
        R.vec[...] = jnp.concatenate(vecs + [jnp.zeros((1, T), F32)], 0)
        R.vec_all[me] = R.vec[...]
        for e in far_first:
            vec_copy(e).start()

    with jax.named_scope("wait_qkv_weights"):
        all_of(R.wqkv.at[seven], R.qkv_s.at[0], R.qkv_s.at[1]).wait_recv()
        pltpu.make_async_copy(R.wqkv.at[me], R.wqkv.at[me], R.loc.at[5]).wait()

    def qkv_step(p, carry):
        ag_wait(tok_all, 0, p)

        @when(p == by_y)
        def _():
            for e in far_first:
                win_copy(e).start()

        a, b, x = pair(tok_all, p)
        y = mm(x, rows(R.wqkv), NN)
        qq = ((y[:, :W] + R.bq_v[...].astype(F32).reshape(1, W)) * 0.125).astype(BF)
        kk = y[:, W:2 * W].astype(BF)
        vv = (y[:, 2 * W:] + R.bv_v[...].astype(F32).reshape(1, W)).astype(BF)
        for at, sl in ((a, slice(0, T)), (b, slice(T, 2 * T))):
            R.q[at], R.k[at], R.v[at] = qq[sl], kk[sl], vv[sl]
        return carry

    with jax.named_scope("project_qkv"):
        lax.fori_loop(0, 4, qkv_step, 0)

    with jax.named_scope("vectors"):
        all_of(R.vec_all.at[seven], R.vec_s.at[0], R.vec_s.at[1]).wait_recv()
        for s in range(8):
            v = R.vec_all[s]
            R.vfull[:, s * T:(s + 1) * T] = v
            ids = jnp.broadcast_to(v[6:7], (T, T)).T
            R.segk[s] = jnp.where(ids < 0, -2.0, ids)

    for i in (1, 2, 3, 4):
        local[i].wait()

    def head_mask(h, like):
        lane = lax.broadcasted_iota(jnp.int32, like.shape, 1)
        return jnp.where(lax.div(lane, HD) == h, like, jnp.zeros_like(like))

    heads = W // HD

    def ids_of(a, b):
        return jnp.concatenate([R.vec_all[a, 6:7], R.vec_all[b, 6:7]], 1)

    def attend_step(i, carry):
        p = 3 - i
        a, b, qp = pair(R.q, p)
        segq = ids_of(a, b)
        segk = rows(R.segk)
        allowed = jnp.concatenate([segk, segk], 1) == segq
        kk = rows(R.k)
        outs = []
        scores = [mm(kk, head_mask(h, qp), NT) for h in range(heads)]
        for h in range(heads):
            s = jnp.where(allowed, scores[h], -1e30)
            ex = jnp.exp(s - jnp.max(s, 0, keepdims=True))
            total = jnp.maximum(jnp.sum(ex, 0, keepdims=True), 1.0)
            pt = (ex * jnp.where(segq >= 0, 1.0 / total, 0.0)).astype(BF)
            R.pt[h, p] = pt
            outs.append(mm(R.vt[h * HD:(h + 1) * HD, :], pt, NN))
            if h == 0:
                @pl.when(p < 3)
                def _():
                    rs_combine(0, p + 1)

        ct = jnp.concatenate(outs, 0).astype(BF)
        R.ctxt[:, lanes(a, T)] = ct[:, :T]
        R.ctxt[:, lanes(b, T)] = ct[:, T:]
        rs_put(0, p, mm(ct, R.wo_v[...], TN))
        return carry

    with jax.named_scope("attend"):
        R.vt[...] = rows(R.v).T
        lax.fori_loop(0, 4, attend_step, 0)

    with jax.named_scope("first_norm"):
        rs_relay(0)
        rs = rs_final(0)
        h1 = tok_all[me].astype(F32) + rs + R.vfull[0:1]
        n1, r1 = norm_parts(h1)
        y1 = n1 * R.vfull[2:3] + R.vfull[3:4]
        R.n1[...], R.y1[...] = n1, y1
        R.r1[...] = jnp.broadcast_to(r1, R.r1.shape)
        y1_all[me] = y1.astype(BF)
        ag_start(y1_all, 1)
    R.kt[...] = rows(R.k).T

    with jax.named_scope("wait_hidden_weights"):
        all_of(R.win.at[seven], R.win_s.at[0], R.win_s.at[1]).wait_recv()

    def hidden_step(p, carry):
        ag_wait(y1_all, 1, p)
        a, b, x = pair(y1_all, p)
        z = hidden_in(x)
        cdf = 0.5 * (1.0 + lax.erf(z * 0.7071067811865476))
        low = (z * cdf).astype(BF)
        slope = cdf + z * (jnp.exp(-0.5 * z * z) * 0.3989422804014327)
        R.hid[a], R.hid[b] = low[:T], low[T:]
        R.slope[a], R.slope[b] = slope[:T], slope[T:]

        @pl.when(p > 1)
        def _():
            rs_combine(1, p - 1)

        rs_put(1, p, mm(low, R.wb_v[...], NN))

        return carry

    def hidden_in(x):
        return mm(x, rows(R.win), NN) + R.bi_v[...].astype(F32).reshape(1, FW)

    with jax.named_scope("hidden"):
        lax.fori_loop(0, 4, hidden_step, 0)
        rs_combine(1, c32(3))

    with jax.named_scope("second_norm"):
        rs_relay(1)
        rs = rs_final(1)
        h2 = R.y1[...] + rs + R.vfull[1:2]
        n2, r2 = norm_parts(h2)
        gain = R.vfull[4:5]
        R.out_v[...] = (n2 * gain + R.vfull[5:6]).astype(BF)
        put_out.start()
        cot = R.cot_v[...].astype(F32)
        dh2 = norm_back(cot * gain, n2, r2)
        R.dh2[...] = dh2
        df_all[me] = dh2.astype(BF)
        ag_start(df_all, 2)
        R.sv[0:1, :] = colsum(cot * n2)
        R.sv[1:2, :] = colsum(cot)

    def grad_back(i):
        x = R.hid[:, :, i * T:(i + 1) * T].reshape(8 * T, T)
        R.zown_b[i] = mm(x, rows(df_all), TN).astype(BF)
        for c in range(3) if i == 0 else (2 * i + 1, 2 * i + 2):
            z_produce(c)

    def hidden_back_step(p, carry):
        ag_wait(df_all, 2, p)

        @when(p == by_both)
        def _():
            grad_back(0)

        a, b, x = pair(df_all, p)
        slope = jnp.concatenate([R.slope[a], R.slope[b]], 0)
        dz = (mm(x, R.wb_v[...], NT) * slope).astype(BF)
        R.dz[a], R.dz[b] = dz[:T], dz[T:]

        @pl.when(p > 1)
        def _():
            rs_combine(2, p - 1)

        rs_put(2, p, mm(dz, rows(R.win), NT))

        return carry

    with jax.named_scope("hidden_back"):
        lax.fori_loop(0, 4, hidden_back_step, 0)
        rs_combine(2, c32(3))

    with jax.named_scope("grad_back"):
        for i in range(1, 4):
            grad_back(i)
        z_until(6.0)
        rs_relay(2)
        z_until(7.5)

    def grad_in(i):
        x = y1_all[:, :, 2 * i * T:(2 * i + 2) * T].reshape(8 * T, 2 * T)
        g = mm(x, rows(R.dz), TN).astype(BF)
        R.zown_i[2 * i], R.zown_i[2 * i + 1] = g[:T], g[T:]
        z_produce(Z_IN + 2 * i)
        z_produce(Z_IN + 2 * i + 1)

    def din_copy(t, s):
        return rcopy(R.zsum_i.at[t], R.grad_i.at[s], R.din_s.at[0], R.din_s.at[1], (dp, t // 2, t % 2))

    def z_deliver(t):
        @pl.when(z_end)
        def _():
            z_down(Z_IN + t).wait_recv()

        @pl.when(me != t)
        def _():
            din_copy(t, me).start()

        @pl.when(me == t)
        def _():
            R.grad_i[me] = R.zsum_i[t]

    with jax.named_scope("grad_in"):
        for i in range(4):
            grad_in(i)
            if i % 2:
                z_until(8.0 + i)

    with jax.named_scope("first_norm_back"):
        rs = rs_final(2)
        dy1 = R.dh2[...] + rs
        n1 = R.n1[...]
        dh1 = norm_back(dy1 * R.vfull[2:3], n1, R.r1[:, 0:1])
        R.dh1[...] = dh1
        da_all[me] = dh1.astype(BF)
        ag_start(da_all, 3)
        R.sv[2:3, :] = colsum(dy1 * n1)
        R.sv[3:4, :] = colsum(dy1)

    def sv_copy(e):
        to, at = dev(c32(e // 2), e % 2)
        return rcopy(R.sv.at[:, lanes(at, T)], R.sv_rcv.at[me], R.sv_s.at[0], R.sv_s.at[1], to)

    for e in far_first:
        sv_copy(e).start()
    R.sv_rcv[me] = R.sv[:, lanes(me, T)]

    z_until(12.0)

    R.dk[...] = jnp.zeros_like(R.dk)
    R.dv[...] = jnp.zeros_like(R.dv)

    def attend_back_step(p):
        ag_wait(da_all, 3, p, lambda: z_until(17.0))
        z_until((13.8, 20.0, 23.0, 25.8)[p])
        a, b, x = pair(da_all, c32(p))
        qp = jnp.concatenate([R.q[a], R.q[b]], 0)
        dc = mm(x, R.wo_v[...], NT).astype(BF)
        vv = rows(R.v)
        outs = []
        for h in range(heads):
            dcm, qm = head_mask(h, dc), head_mask(h, qp)
            low = R.pt[h, p]
            pt = low.astype(F32)
            dpt = mm(vv, dcm, NT)
            ds = (pt * (dpt - jnp.sum(pt * dpt, 0, keepdims=True))).astype(BF)
            outs.append(mm(R.kt[h * HD:(h + 1) * HD, :], ds, NN))
            R.dk[...] += mm(ds, qm, NN)
            R.dv[...] += mm(low, dcm, NN)
            z_until((14.8, 21.0, 24.0, 26.8)[p] + h)
        dq = jnp.concatenate(outs, 0).T.astype(BF) * 0.125
        R.dqkv[a, :, 0:W] = dq[:T]
        R.dqkv[b, :, 0:W] = dq[T:]

    with jax.named_scope("attend_back"):
        for p in range(4):
            attend_back_step(p)
        R.dqkv[:, :, W:2 * W] = R.dk[...].astype(BF).reshape(8, T, W)
        R.dqkv[:, :, 2 * W:] = R.dv[...].astype(BF).reshape(8, T, W)

    def dqkv_copy(p, flip):
        to, at = dev(p, flip)
        return rcopy(R.dqkv_snd.at[at], R.zown_w.at[me], R.dqkv_s.at[0], R.dqkv_s.at[1], to)

    def dqkv_step(p):
        a, b = dev(c32(p), 0)[1], dev(c32(p), 1)[1]
        x = jnp.concatenate([tok_all[:, :, lanes(a, T)], tok_all[:, :, lanes(b, T)]], 2).reshape(8 * T, 2 * T)
        g = mm(x, rows(R.dqkv), TN).astype(BF)
        R.dqkv_snd[b] = g[T:]
        dqkv_copy(c32(p), 1).start()
        if p == 0:
            R.zown_w[me] = g[:T]
        else:
            R.dqkv_snd[a] = g[:T]
            dqkv_copy(c32(p), 0).start()
        z_until(28.3 + 0.5 * p)

    with jax.named_scope("grad_qkv"):
        for p in range(4):
            dqkv_step(p)

    with jax.named_scope("grad_out"):
        R.zown_o[...] = mm(R.ctxt[...], rows(da_all), NN).astype(BF)
        z_produce(Z_OUT)
        z_produce(Z_OUT + 1)
        z_until(31.0)

    def input_step(p):
        if p > 1:
            rs_combine(3, p - 1)
        a, b, x = pair(R.dqkv, c32(p))
        rs_put(3, p, mm(x, rows(R.wqkv), NT))
        z_until((30.8, 31.4, 32.8, 34.4)[p])

    with jax.named_scope("input_back"):
        for p in range(4):
            input_step(p)
        rs_combine(3, c32(3))
        z_until(36.5)

    with jax.named_scope("small_grads"):
        all_of(R.sv_rcv.at[seven], R.sv_s.at[0], R.sv_s.at[1]).wait_recv()
        acc = R.sv_rcv[0]
        for s in range(1, 8):
            acc = acc + R.sv_rcv[s]
        own = lanes(me, T)
        parts = [
            acc[0:4],
            colsum(rows(R.dqkv)[:, 0:W]),
            colsum(rows(R.dqkv)[:, 2 * W:]),
            colsum(da_all[:, :, own].reshape(8 * T, T)),
            colsum(df_all[:, :, own].reshape(8 * T, T)),
        ]
        dbi = colsum(rows(R.dz))
        parts += [dbi[:, i * T:(i + 1) * T] for i in range(FW // T)]
        parts.append(jnp.zeros((16 - 8 - FW // T, T), F32))
        R.zown_s[...] = jnp.concatenate(parts, 0).astype(BF)
        z_produce(Z_SMALL)
        z_until(39.0)

    with jax.named_scope("z_rest"):
        all_of(R.zown_w.at[seven], R.dqkv_s.at[0], R.dqkv_s.at[1]).wait_recv()
        for c in range(Z_QKV, Z_ALL):
            z_produce(c)
        z_until(42.0)
        rs_relay(3)
        z_until(46.0)
    with jax.named_scope("input_grad"):
        R.igrad_v[...] = R.dh1[...] + rs_final(3)
        put_igrad.start()
    with jax.named_scope("z_last"):
        for t in range(8):
            z_until(49.0 + 2 * t)
            z_deliver(t)
        z_until(1000.0)

    with jax.named_scope("finish"):
        puts = [put_out, put_igrad]

        def put(i, src, dst):
            puts.append(pltpu.make_async_copy(src, dst, R.put_s.at[i]))
            puts[-1].start()

        for c in range(Z_ALL):
            z_finish(c)
            if c == Z_IN - 1:
                put(2, R.zsum_b, R.gb)
            if c == Z_OUT - 1:
                all_of(R.grad_i.at[seven], R.din_s.at[0], R.din_s.at[1]).wait()
                put(3, R.grad_i, R.gi)
            if c == Z_SMALL:
                put(4, R.zsum_o, R.go)
                put(5, R.zsum_s, R.gs)
            if c >= Z_QKV and c - Z_QKV < 7:
                put(6 + c - Z_QKV, R.zsum_w.at[c - Z_QKV], R.gw.at[c - Z_QKV])
        put(13, R.zsum_w.at[7], R.gw.at[7])
        z_sent()
        for buf, r in ((tok_all, 0), (y1_all, 1), (df_all, 2), (da_all, 3)):
            ag_finish(buf, r)
        for ref, sem in (
            (R.vec_all, R.vec_s), (R.win, R.win_s), (R.sv_rcv, R.sv_s), (R.wqkv, R.qkv_s), (R.zown_w, R.dqkv_s),
        ):
            all_of(ref.at[seven], sem.at[0], sem.at[1]).wait_send()
        for cp in puts:
            cp.wait()


def sharded_plan(
    tokens, segment_ids, cotangent,
    w_query, w_key, w_value, w_out, w_in, w_back,
    bias_query, bias_value, bias_out, bias_in, bias_back,
    first_gain, first_shift, second_gain, second_shift,
):
    tokens, cotangent = tokens[0], cotangent[0]
    T, D = tokens.shape
    W, FW = D // 8, w_in.shape[1] // 8
    ins = dict(
        tok=tokens, cot=cotangent, wq=w_query, wk=w_key, wv=w_value, wo=w_out, wi=w_in, wb=w_back, ids=segment_ids,
        bo=bias_out, bb=bias_back, g1=first_gain, s1=first_shift, g2=second_gain, s2=second_shift,
        bq=bias_query, bv=bias_value, bi=bias_in,
    )
    in_hbm = 8
    outs = dict(
        out=((T, D), BF), igrad=((T, D), F32), gb=((4, T, D), BF), gi=((8, T, FW), BF), go=((T, D), BF),
        gw=((8, T, 3 * W), BF), gs=((16, T), BF),
    )
    sums = dict(b=outs["gb"], i=outs["gi"], o=outs["go"], w=outs["gw"], s=outs["gs"])
    blocks = {k: ((8, T, D), BF) for k in ("tok_all", "y1_all", "df_all", "da_all")}
    scr = dict(
        **blocks,
        wqkv=((8, T, 3 * W), BF), win=((8, T, FW), BF), wb_v=(w_back.shape, BF), wo_v=(w_out.shape, BF),
        cot_v=((T, D), BF), vec=((8, T), F32), vec_all=((8, 8, T), F32), vfull=((8, D), F32), segk=((8, T, T), F32),
        q=((8, T, W), BF), k=((8, T, W), BF), v=((8, T, W), BF), vt=((W, 8 * T), BF), kt=((W, 8 * T), BF),
        pt=((W // HD, 4, 8 * T, 2 * T), BF), ctxt=((W, 8 * T), BF),
        hid=((8, T, FW), BF), slope=((8, T, FW), F32), dz=((8, T, FW), BF),
        n1=((T, D), F32), r1=((T, 128), F32), y1=((T, D), F32), dh2=((T, D), F32), dh1=((T, D), F32),
        sv=((8, D), F32), sv_rcv=((8, 8, T), F32),
        keep=((4, T, D), F32), snd_c=((4, T, D), BF), snd_l=((4, T, D), BF),
        rcv_c=((4, 4, T, D), BF), rcv_l=((4, 4, T, D), BF),
        dk=((8 * T, W), F32), dv=((8 * T, W), F32), dqkv=((8, T, 3 * W), BF),
        dqkv_snd=((8, T, 3 * W), BF),
        **{z + k: v for z in ("zown_", "zsum_", "zmid_") for k, v in sums.items()}, grad_i=outs["gi"],
        out_v=outs["out"], igrad_v=outs["igrad"],
        **{k + "_v": (v.shape, v.dtype) for k, v in list(ins.items())[in_hbm:]},
    )
    sems = dict(
        ag_s=(4,), ag_r=(4, 2), ag_f=(4, 2), rs_s=(2,), rs_cr=(4,), rs_lr=(4, 2),

        z_s=(5, 2), z_r=(29, 2), loc=(6,), small_s=(10,), put_s=(14,), vec_s=(2,), qkv_s=(2,), win_s=(2,), sv_s=(2,), din_s=(2,), dqkv_s=(2,),
    )
    names = list(ins) + list(outs) + list(scr) + list(sems)
    res = pl.pallas_call(
        partial(layer_kernel, names),
        out_shape=[jax.ShapeDtypeStruct(*s) for s in outs.values()],
        in_specs=[pl.BlockSpec(memory_space=pltpu.HBM)] * len(ins),
        out_specs=[pl.BlockSpec(memory_space=pltpu.HBM)] * len(outs),
        scratch_shapes=[pltpu.VMEM(*s) for s in scr.values()] + [pltpu.SemaphoreType.DMA(s) for s in sems.values()],
        compiler_params=pltpu.CompilerParams(collective_id=0, has_side_effects=True, vmem_limit_bytes=60 << 20),
        name="layer",
    )(*ins.values())
    firsts = [(T, D)] * 6 + [w_in.shape, w_back.shape]
    sizes = [T, T, T, FW, T, T, T, T, T]
    shapes = [(n, t) for n, t in zip(firsts, [BF] + [F32] * 7)] + [((n,), F32) for n in sizes]
    loaded = list(outs.values())
    stored = [((3, T, D), F32), ((T, D), F32), (w_in.shape, F32), (w_back.shape, F32)] + shapes[8:]
    final = pl.pallas_call(
        finish_kernel,
        out_shape=[jax.ShapeDtypeStruct(*s) for s in shapes],
        in_specs=[pl.BlockSpec(memory_space=pltpu.HBM)] * len(loaded),
        out_specs=[pl.BlockSpec(memory_space=pltpu.HBM)] * len(shapes),
        scratch_shapes=[pltpu.VMEM(*s) for s in loaded + stored]
        + [pltpu.SemaphoreType.DMA((len(loaded) + 4,)), pltpu.SemaphoreType.DMA((len(shapes) + 6,))],
        compiler_params=pltpu.CompilerParams(vmem_limit_bytes=60 << 20),
        name="finish",
    )(*res)
    return (final[0][None], final[1][None], *final[2:])


def finish_kernel(*refs):
    ins, outs, rest = refs[:7], refs[7:24], refs[24:]
    loaded, stored, (load_s, store_s) = rest[:7], rest[7:20], rest[20:]
    out, igrad, gb, gi, go, gw, gs = loaded
    qkv, o_o, o_i, o_b, *o_small = stored
    order = (3, 2, 5, 4, 1, 0, 6)
    loads = {i: pltpu.make_async_copy(ins[i], loaded[i], load_s.at[i]) for i in order}
    for i in order:
        loads[i].start()
    stores = []

    def store(src, dst):
        stores.append(pltpu.make_async_copy(src, dst, store_s.at[len(stores)]))
        stores[-1].start()

    width = gi.shape[2]
    loads[3].wait()
    for j in range(8):
        o_i[:, j * width:(j + 1) * width] = gi[j].astype(F32)
    store(o_i, outs[6])
    loads[2].wait()
    T = gb.shape[1]
    for j in range(4):
        o_b[j * T:(j + 1) * T, :] = gb[j].astype(F32)
    store(o_b, outs[7])
    loads[5].wait()
    W = gw.shape[2] // 3
    for j in range(3):
        for s in range(8):
            qkv[j, :, s * W:(s + 1) * W] = gw[s, :, j * W:(j + 1) * W].astype(F32)
        store(qkv.at[j], outs[2 + j])
    loads[4].wait()
    o_o[...] = go[...].astype(F32)
    store(o_o, outs[5])
    loads[1].wait()
    store(igrad, outs[1])
    loads[0].wait()
    store(out, outs[0])
    loads[6].wait()
    v = gs[...].astype(F32)
    bq, bv, bo, bi, bb, g1, s1, g2, s2 = o_small
    for o, i in ((bq, 4), (bv, 5), (bo, 6), (bb, 7), (g1, 2), (s1, 3), (g2, 0), (s2, 1)):
        o[...] = v[i]
    n = v.shape[1]
    for i in range(bi.shape[0] // n):
        bi[i * n:(i + 1) * n] = v[8 + i]
    for i, o in enumerate(o_small):
        store(o, outs[8 + i])
    for cp in stores:
        cp.wait()


def pick_plan(mesh):
    group = mesh.shape["blk"] * mesh.shape["head"]
    return sharded_plan if (mesh.shape["dp"], group) == (4, 8) else general_plan


def flat_dot(left_side, right_side):
    return jnp.dot(
        left_side.reshape(-1, left_side.shape[-1]), right_side, preferred_element_type=jnp.float32
    )


def inner_dot(left_side, right_side):
    return jnp.einsum(
        "ra,rb->ab",
        left_side.reshape(-1, left_side.shape[-1]),
        right_side.reshape(-1, right_side.shape[-1]),
        preferred_element_type=jnp.float32,
    )


def layer_norm(value_rows, gain_row, shift_row):
    centre = jnp.mean(value_rows, -1, keepdims=True)
    centred = value_rows - centre
    spread = jnp.mean(centred * centred, -1, keepdims=True)
    return centred * lax.rsqrt(spread + 1e-05) * gain_row + shift_row


def head_view(array_in):
    return array_in.reshape(array_in.shape[0], array_in.shape[1], -1, HD)


def allowed_pairs(query_ids, key_ids):
    same_doc = (query_ids[:, :, None] == key_ids[:, None, :]) & (key_ids[:, None, :] >= 0)
    return same_doc[:, None]


def forward_step(state_now, arrived, local_data):
    running_max, running_sum, weighted = state_now
    key_block, value_block, key_ids = arrived
    query_block, query_ids = local_data
    scores = jnp.einsum(
        "gqhd,gkhd->ghqk",
        head_view(query_block),
        head_view(key_block),
        preferred_element_type=jnp.float32,
    )
    allowed = allowed_pairs(query_ids, key_ids)
    masked = jnp.where(allowed, scores, -1e30)
    new_max = jnp.maximum(running_max, jnp.max(masked, -1))
    exponents = jnp.where(allowed, jnp.exp(masked - new_max[..., None]), 0.0)
    running_sum = jnp.sum(exponents, -1)
    weighted = jnp.einsum(
        "ghqk,gkhd->ghqd",
        exponents.astype(jnp.bfloat16),
        head_view(value_block),
        preferred_element_type=jnp.float32,
    )
    return (new_max, running_sum, weighted)


def probabilities(query_block, key_block, query_ids, key_ids, log_sums):
    scores = jnp.einsum(
        "gqhd,gkhd->ghqk",
        head_view(query_block),
        head_view(key_block),
        preferred_element_type=jnp.float32,
    )
    allowed = allowed_pairs(query_ids, key_ids)
    masked = jnp.where(allowed, scores, -1e30)
    return jnp.where(allowed, jnp.exp(masked - log_sums.transpose(0, 2, 1)[..., None]), 0.0)


def score_grads(weights_now, grad_block, value_block, deltas):
    grad_weights = jnp.einsum(
        "gqhd,gkhd->ghqk",
        head_view(grad_block),
        head_view(value_block),
        preferred_element_type=jnp.float32,
    )
    return (weights_now * (grad_weights - deltas.transpose(0, 2, 1)[..., None])).astype(
        jnp.bfloat16
    )


def heads_to_rows(array_in):
    return array_in.transpose(0, 2, 1, 3).reshape(array_in.shape[0], array_in.shape[2], -1)


def general_plan(
    tokens,
    segment_ids,
    cotangent,
    w_query,
    w_key,
    w_value,
    w_out,
    w_in,
    w_back,
    bias_query,
    bias_value,
    bias_out,
    bias_in,
    bias_back,
    first_gain,
    first_shift,
    second_gain,
    second_shift,
):
    (
        query_full,
        key_full,
        value_full,
        out_full,
        in_full,
        back_full,
        query_bias,
        value_bias,
        out_bias,
        in_bias,
        back_bias,
        gain_one,
        shift_one,
        gain_two,
        shift_two,
    ) = (
        lax.all_gather(w_query, GROUP, axis=0, tiled=True),
        lax.all_gather(w_key, GROUP, axis=0, tiled=True),
        lax.all_gather(w_value, GROUP, axis=0, tiled=True),
        lax.all_gather(w_out, GROUP, axis=0, tiled=True),
        lax.all_gather(w_in, GROUP, axis=0, tiled=True),
        lax.all_gather(w_back, GROUP, axis=0, tiled=True),
        lax.all_gather(bias_query, GROUP, axis=0, tiled=True),
        lax.all_gather(bias_value, GROUP, axis=0, tiled=True),
        lax.all_gather(bias_out, GROUP, axis=0, tiled=True),
        lax.all_gather(bias_in, GROUP, axis=0, tiled=True),
        lax.all_gather(bias_back, GROUP, axis=0, tiled=True),
        lax.all_gather(first_gain, GROUP, axis=0, tiled=True),
        lax.all_gather(first_shift, GROUP, axis=0, tiled=True),
        lax.all_gather(second_gain, GROUP, axis=0, tiled=True),
        lax.all_gather(second_shift, GROUP, axis=0, tiled=True),
    )
    query_bias = query_bias.astype(jnp.float32)
    value_bias = value_bias.astype(jnp.float32)
    out_bias = out_bias.astype(jnp.float32)
    in_bias = in_bias.astype(jnp.float32)
    back_bias = back_bias.astype(jnp.float32)
    gain_one = gain_one.astype(jnp.float32)
    shift_one = shift_one.astype(jnp.float32)
    gain_two = gain_two.astype(jnp.float32)
    shift_two = shift_two.astype(jnp.float32)
    seq_count = tokens.shape[0]
    query_tok = (
        ((flat_dot(tokens, query_full) + query_bias) * 0.125)
        .astype(jnp.bfloat16)
        .reshape(tokens.shape)
    )
    key_tok = flat_dot(tokens, key_full).astype(jnp.bfloat16).reshape(tokens.shape)
    value_tok = (
        (flat_dot(tokens, value_full) + value_bias).astype(jnp.bfloat16).reshape(tokens.shape)
    )
    query_heads, key_heads, value_heads = (
        lax.all_to_all(query_tok, "head", split_axis=2, concat_axis=1, tiled=True),
        lax.all_to_all(key_tok, "head", split_axis=2, concat_axis=1, tiled=True),
        lax.all_to_all(value_tok, "head", split_axis=2, concat_axis=1, tiled=True),
    )
    rows_here = query_heads.shape[1]
    width_heads = query_heads.shape[2]
    heads_here = width_heads // HD
    start_state = (
        jnp.full((seq_count, heads_here, rows_here), -1e30, jnp.float32),
        jnp.zeros((seq_count, heads_here, rows_here), jnp.float32),
        jnp.zeros((seq_count, heads_here, rows_here, HD), jnp.float32),
    )
    running_max, running_sum, weighted = forward_step(
        start_state,
        (
            lax.all_gather(key_heads, "blk", axis=1, tiled=True),
            lax.all_gather(value_heads, "blk", axis=1, tiled=True),
            lax.all_gather(segment_ids, "blk", axis=1, tiled=True),
        ),
        (query_heads, segment_ids),
    )
    floored = jnp.maximum(running_sum, 1.0)
    ctx_heads = heads_to_rows(weighted / floored[..., None])
    log_sums = (running_max + jnp.log(floored)).transpose(0, 2, 1)
    ctx_tok = lax.all_to_all(
        ctx_heads.astype(jnp.bfloat16), "head", split_axis=1, concat_axis=2, tiled=True
    )
    first_sum = tokens.astype(jnp.float32) + (flat_dot(ctx_tok, out_full) + out_bias).reshape(
        tokens.shape
    )
    first_norm = layer_norm(first_sum, gain_one, shift_one)
    first_low = first_norm.astype(jnp.bfloat16)
    inner_rows = flat_dot(first_low, in_full) + in_bias
    hidden_low = jax.nn.gelu(inner_rows, approximate=False).astype(jnp.bfloat16)
    second_sum = first_norm + (flat_dot(hidden_low, back_full) + back_bias).reshape(tokens.shape)
    output_now, second_pull = jax.vjp(layer_norm, second_sum, gain_two, shift_two)
    grad_second, grad_gain_two, grad_shift_two = second_pull(cotangent.astype(jnp.float32))
    grad_branch = grad_second.astype(jnp.bfloat16)
    grad_back_bias = jnp.sum(grad_branch.astype(jnp.float32), (0, 1))
    grad_back = inner_dot(hidden_low, grad_branch)
    grad_hidden = flat_dot(grad_branch, back_full.T)
    unused_value, gelu_pull = jax.vjp(partial(jax.nn.gelu, approximate=False), inner_rows)
    grad_inner = gelu_pull(grad_hidden)[0].astype(jnp.bfloat16)
    grad_in_bias = jnp.sum(grad_inner.astype(jnp.float32), 0)
    grad_in = inner_dot(first_low, grad_inner)
    grad_first_norm = grad_second + flat_dot(grad_inner, in_full.T).reshape(tokens.shape)
    unused_norm, first_pull = jax.vjp(layer_norm, first_sum, gain_one, shift_one)
    grad_first, grad_gain_one, grad_shift_one = first_pull(grad_first_norm)
    grad_attn = grad_first.astype(jnp.bfloat16)
    grad_out_bias = jnp.sum(grad_attn.astype(jnp.float32), (0, 1))
    grad_out = inner_dot(ctx_tok, grad_attn)
    grad_ctx_tok = flat_dot(grad_attn, out_full.T).astype(jnp.bfloat16).reshape(tokens.shape)
    grad_ctx = lax.all_to_all(grad_ctx_tok, "head", split_axis=2, concat_axis=1, tiled=True)
    deltas = jnp.sum(head_view(grad_ctx).astype(jnp.float32) * head_view(ctx_heads), -1)
    key_block = lax.all_gather(key_heads, "blk", axis=1, tiled=True)
    value_block = lax.all_gather(value_heads, "blk", axis=1, tiled=True)
    key_ids = lax.all_gather(segment_ids, "blk", axis=1, tiled=True)
    weights_now = probabilities(query_heads, key_block, segment_ids, key_ids, log_sums)
    dscores = score_grads(weights_now, grad_ctx, value_block, deltas)
    grad_query_heads = jnp.einsum(
        "ghqk,gkhd->ghqd", dscores, head_view(key_block), preferred_element_type=jnp.float32
    )
    key_part = jnp.einsum(
        "ghqk,gqhd->gkhd", dscores, head_view(query_heads), preferred_element_type=jnp.float32
    )
    value_part = jnp.einsum(
        "ghqk,gqhd->gkhd",
        weights_now.astype(jnp.bfloat16),
        head_view(grad_ctx),
        preferred_element_type=jnp.float32,
    )
    both_parts = jnp.concatenate(
        [
            key_part.reshape(key_part.shape[0], key_part.shape[1], -1),
            value_part.reshape(value_part.shape[0], value_part.shape[1], -1),
        ],
        2,
    )
    grad_query_heads, pair_grads = (grad_query_heads, both_parts)
    pair_home = lax.psum_scatter(
        pair_grads.astype(jnp.bfloat16), "blk", scatter_dimension=1, tiled=True
    ).astype(jnp.float32)
    grad_key_heads = pair_home[:, :, :width_heads].astype(jnp.bfloat16)
    grad_value_heads = pair_home[:, :, width_heads:].astype(jnp.bfloat16)
    grad_query_rows = heads_to_rows(grad_query_heads).astype(jnp.bfloat16)
    grad_query_tok, grad_key_tok, grad_value_tok = (
        lax.all_to_all(grad_query_rows, "head", split_axis=1, concat_axis=2, tiled=True),
        lax.all_to_all(grad_key_heads, "head", split_axis=1, concat_axis=2, tiled=True),
        lax.all_to_all(grad_value_heads, "head", split_axis=1, concat_axis=2, tiled=True),
    )
    grad_query_tok = grad_query_tok * 0.125
    grad_inputs = grad_first + (
        flat_dot(grad_query_tok, query_full.T)
        + flat_dot(grad_key_tok, key_full.T)
        + flat_dot(grad_value_tok, value_full.T)
    ).reshape(tokens.shape)
    (
        shard_wq,
        shard_wk,
        shard_wv,
        shard_wo,
        shard_wi,
        shard_wb,
        shard_bq,
        shard_bv,
        shard_bo,
        shard_bi,
        shard_bb,
        shard_g1,
        shard_s1,
        shard_g2,
        shard_s2,
    ) = (
        lax.psum_scatter(
            inner_dot(tokens, grad_query_tok), GROUP, scatter_dimension=0, tiled=True
        ),
        lax.psum_scatter(
            inner_dot(tokens, grad_key_tok), GROUP, scatter_dimension=0, tiled=True
        ),
        lax.psum_scatter(
            inner_dot(tokens, grad_value_tok), GROUP, scatter_dimension=0, tiled=True
        ),
        lax.psum_scatter(grad_out, GROUP, scatter_dimension=0, tiled=True),
        lax.psum_scatter(grad_in, GROUP, scatter_dimension=0, tiled=True),
        lax.psum_scatter(grad_back, GROUP, scatter_dimension=0, tiled=True),
        lax.psum_scatter(
            jnp.sum(grad_query_tok.astype(jnp.float32), (0, 1)),
            GROUP,
            scatter_dimension=0,
            tiled=True,
        ),
        lax.psum_scatter(
            jnp.sum(grad_value_tok.astype(jnp.float32), (0, 1)),
            GROUP,
            scatter_dimension=0,
            tiled=True,
        ),
        lax.psum_scatter(grad_out_bias, GROUP, scatter_dimension=0, tiled=True),
        lax.psum_scatter(grad_in_bias, GROUP, scatter_dimension=0, tiled=True),
        lax.psum_scatter(grad_back_bias, GROUP, scatter_dimension=0, tiled=True),
        lax.psum_scatter(grad_gain_one, GROUP, scatter_dimension=0, tiled=True),
        lax.psum_scatter(grad_shift_one, GROUP, scatter_dimension=0, tiled=True),
        lax.psum_scatter(grad_gain_two, GROUP, scatter_dimension=0, tiled=True),
        lax.psum_scatter(grad_shift_two, GROUP, scatter_dimension=0, tiled=True),
    )
    (
        total_wq,
        total_wk,
        total_wv,
        total_wo,
        total_wi,
        total_wb,
        total_bq,
        total_bv,
        total_bo,
        total_bi,
        total_bb,
        total_g1,
        total_s1,
        total_g2,
        total_s2,
    ) = (
        lax.psum(shard_wq.astype(jnp.bfloat16), "dp").astype(jnp.float32),
        lax.psum(shard_wk.astype(jnp.bfloat16), "dp").astype(jnp.float32),
        lax.psum(shard_wv.astype(jnp.bfloat16), "dp").astype(jnp.float32),
        lax.psum(shard_wo.astype(jnp.bfloat16), "dp").astype(jnp.float32),
        lax.psum(shard_wi.astype(jnp.bfloat16), "dp").astype(jnp.float32),
        lax.psum(shard_wb.astype(jnp.bfloat16), "dp").astype(jnp.float32),
        lax.psum(shard_bq.astype(jnp.bfloat16), "dp").astype(jnp.float32),
        lax.psum(shard_bv.astype(jnp.bfloat16), "dp").astype(jnp.float32),
        lax.psum(shard_bo.astype(jnp.bfloat16), "dp").astype(jnp.float32),
        lax.psum(shard_bi.astype(jnp.bfloat16), "dp").astype(jnp.float32),
        lax.psum(shard_bb.astype(jnp.bfloat16), "dp").astype(jnp.float32),
        lax.psum(shard_g1.astype(jnp.bfloat16), "dp").astype(jnp.float32),
        lax.psum(shard_s1.astype(jnp.bfloat16), "dp").astype(jnp.float32),
        lax.psum(shard_g2.astype(jnp.bfloat16), "dp").astype(jnp.float32),
        lax.psum(shard_s2.astype(jnp.bfloat16), "dp").astype(jnp.float32),
    )
    return (
        output_now.astype(jnp.bfloat16),
        grad_inputs,
        total_wq,
        total_wk,
        total_wv,
        total_wo,
        total_wi,
        total_wb,
        total_bq,
        total_bv,
        total_bo,
        total_bi,
        total_bb,
        total_g1,
        total_s1,
        total_g2,
        total_s2,
    )


def solution(mesh):
    in_specs = (
        P("dp", GROUP, None),
        P("dp", "blk"),
        P("dp", GROUP, None),
        P(GROUP, None),
        P(GROUP, None),
        P(GROUP, None),
        P(GROUP, None),
        P(GROUP, None),
        P(GROUP, None),
        P(GROUP),
        P(GROUP),
        P(GROUP),
        P(GROUP),
        P(GROUP),
        P(GROUP),
        P(GROUP),
        P(GROUP),
        P(GROUP),
    )
    out_specs = (
        P("dp", GROUP, None),
        P("dp", GROUP, None),
        P(GROUP, None),
        P(GROUP, None),
        P(GROUP, None),
        P(GROUP, None),
        P(GROUP, None),
        P(GROUP, None),
        P(GROUP),
        P(GROUP),
        P(GROUP),
        P(GROUP),
        P(GROUP),
        P(GROUP),
        P(GROUP),
        P(GROUP),
        P(GROUP),
    )
    plan = pick_plan(mesh)
    return jax.shard_map(
        plan, mesh=mesh, in_specs=in_specs, out_specs=out_specs, check_vma=False
    )
```

```python
from functools import partial
from types import SimpleNamespace

import jax
import jax.numpy as jnp
from jax import lax
from jax.experimental import pallas as pl
from jax.experimental.pallas import tpu as pltpu
from jax.sharding import PartitionSpec as P

HD = 64
BF = jnp.bfloat16
F32 = jnp.float32
GROUP = ("blk", "head")
MESH = pl.DeviceIdType.MESH
NN = ((1,), (0,))
NT = ((1,), (1,))
TN = ((0,), (0,))


def mm(a, b, dims):
    return lax.dot_general(a, b, (dims, ((), ())), preferred_element_type=F32)


def norm_parts(v):
    c = v - jnp.mean(v, -1, keepdims=True)
    r = lax.rsqrt(jnp.mean(c * c, -1, keepdims=True) + 1e-05)
    return c * r, r


def norm_back(e, n, r):
    return r * (e - jnp.mean(e, -1, keepdims=True) - n * jnp.mean(e * n, -1, keepdims=True))


def colsum(x):
    return jnp.sum(x.astype(F32), 0, keepdims=True)


def when(cond):
    if isinstance(cond, bool):
        return (lambda body: body()) if cond else (lambda body: None)
    return pl.when(cond)


def rows(ref):
    x = ref[...]
    return x.reshape(-1, x.shape[-1])


def layer_kernel(names, *refs):
    R = SimpleNamespace(**dict(zip(names, refs, strict=True)))
    dp, blk, head = [lax.axis_index(a) for a in ("dp", "blk", "head")]
    core, chip_x = lax.rem(blk, 2), lax.div(blk, 2)
    T, D = R.tok.shape
    W = R.q.shape[-1]
    FW = R.wi.shape[1] // 8

    def dev(p, flip):
        hh = lax.rem(head + lax.rem(p, 2), 2)
        bb = lax.rem(chip_x + lax.div(p, 2), 2) * 2 + lax.rem(core + flip, 2)
        return (dp, bb, hh), bb * 2 + hh

    def c32(i):
        return jnp.asarray(i, jnp.int32)

    me = blk * 2 + head
    partner, partner_at = dev(c32(0), 1)
    z_end = lax.rem(dp, 3) == 0
    z_other = jnp.where(dp == 0, 1, jnp.where(dp == 3, 2, jnp.where(dp == 1, 0, 3)))
    z_mid = jnp.where(dp == 1, 2, 1)

    def rcopy(src, dst, ssem, rsem, to):
        return pltpu.make_async_remote_copy(src, dst, ssem, rsem, device_id=to, device_id_type=MESH)

    def all_of(ref, ssem, rsem):
        return rcopy(ref, ref, ssem, rsem, partner)

    seven = pl.ds(0, 7)

    def lanes(i, w):
        return pl.ds(pl.multiple_of(i * w, w), w)

    tok_all, y1_all, df_all, da_all = R.tok_all, R.y1_all, R.df_all, R.da_all
    small_in = (R.ids, R.bo, R.bb, R.g1, R.s1, R.g2, R.s2, R.bq, R.bv, R.bi)
    small_v = (R.ids_v, R.bo_v, R.bb_v, R.g1_v, R.s1_v, R.g2_v, R.s2_v, R.bq_v, R.bv_v, R.bi_v)
    local = [
        pltpu.make_async_copy(R.tok, tok_all.at[me], R.loc.at[0]),
        pltpu.make_async_copy(R.wb, R.wb_v, R.loc.at[1]),
        pltpu.make_async_copy(R.wo, R.wo_v, R.loc.at[2]),
        pltpu.make_async_copy(R.wi.at[:, lanes(me, FW)], R.win.at[me], R.loc.at[3]),
        pltpu.make_async_copy(R.cot, R.cot_v, R.loc.at[4]),
    ]
    for j, w in enumerate((R.wq, R.wk, R.wv)):
        local.append(pltpu.make_async_copy(w.at[:, lanes(me, W)], R.wqkv.at[me, :, pl.ds(j * W, W)], R.loc.at[5]))
    small = [
        pltpu.make_async_copy(x, y, R.small_s.at[i])
        for i, (x, y) in enumerate(zip(small_in, small_v, strict=True))
    ]
    for cp in local + small:
        cp.start()

    bar = pltpu.get_barrier_semaphore()
    for e in range(1, 8):
        to, _ = dev(c32(e // 2), e % 2)
        pl.semaphore_signal(bar, 1, device_id=to, device_id_type=MESH)
    for j in range(1, 4):
        pl.semaphore_signal(bar, 1, device_id=(lax.rem(dp + j, 4), blk, head), device_id_type=MESH)
    pl.semaphore_wait(bar, 10)

    put_out = pltpu.make_async_copy(R.out_v, R.out, R.put_s.at[0])
    put_igrad = pltpu.make_async_copy(R.igrad_v, R.igrad, R.put_s.at[1])

    half = (pl.ds(0, T // 2), pl.ds(T // 2, T // 2))
    by_y, by_x, by_both = 1, 2, 3

    def piece(st, q):
        return pl.ds((2 * st + q) * (T // 4), T // 4)

    def ag_direct(buf, r, st, p, q):
        to, _ = dev(c32(p), 0)
        part = buf.at[me, piece(st, q)]
        return rcopy(part, part, R.ag_s.at[r], R.ag_r.at[st, p, q], to)

    def ag_relay(buf, r, st, q):
        via, over = (by_x, by_y) if q == 0 else (by_y, by_x)
        _, at = dev(c32(via), 0)
        to, _ = dev(c32(over), 0)
        part = buf.at[at, piece(st, q)]
        return rcopy(part, part, R.ag_s.at[r], R.ag_r.at[st, by_both, q], to)

    def ag_home(buf, r, st):
        part = buf.at[me, half[st]]
        return rcopy(part, part, R.ag_s.at[r], R.ag_f.at[st, 0, 0], partner)

    def ag_forward(buf, r, st, p, q):
        _, at = dev(c32(p), 0)
        part = buf.at[at, piece(st, q)]
        return rcopy(part, part, R.ag_s.at[r], R.ag_f.at[st, p, q], partner)

    def ag_start(buf, r, st):
        for p, q in ((by_x, 0), (by_y, 1), (by_x, 1), (by_y, 0)):
            ag_direct(buf, r, st, p, q).start()
        ag_home(buf, r, st).start()

    def ag_got(buf, r, st, p, q):
        (ag_relay(buf, r, st, q) if p == by_both else ag_direct(buf, r, st, p, q)).wait_recv()
        ag_forward(buf, r, st, p, q).start()

    def ag_near(buf, r, st):
        for p, q in ((by_x, 0), (by_y, 1)):
            ag_got(buf, r, st, p, q)
            ag_relay(buf, r, st, q).start()
        for p, q in ((by_y, 0), (by_x, 1)):
            ag_got(buf, r, st, p, q)

    def ag_far(buf, r, st):
        for q in (0, 1):
            ag_got(buf, r, st, by_both, q)

    def ag_have(buf, r, st, p):
        if p == 0:
            ag_home(buf, r, st).wait_recv()
        else:
            for q in (0, 1):
                ag_forward(buf, r, st, p, q).wait_recv()

    def ag_wait(buf, r, p, between=lambda: None):
        for st in (0, 1):
            if p == by_y:
                ag_near(buf, r, st)
                between()
            if p == by_x:
                ag_far(buf, r, st)
        for st in (0, 1):
            ag_have(buf, r, st, p)

    def ag_finish(buf, r):
        all_of(buf.at[seven], R.ag_s.at[r], R.ag_r.at[0, 0, 0]).wait_send()

    def pair(buf, p):
        a, b = dev(p, 0)[1], dev(p, 1)[1]
        return a, b, jnp.concatenate([buf[a], buf[b]], 0)

    def half_pair(buf, p, st):
        a, b = dev(p, 0)[1], dev(p, 1)[1]
        return a, b, jnp.concatenate([buf[a, half[st]], buf[b, half[st]]], 0)

    def rs_chip(r, st, p):
        return rcopy(
            R.snd_c.at[p, half[st]], R.rcv_c.at[r, p, half[st]], R.rs_s.at[0], R.rs_cr.at[st, p], partner
        )

    def rs_link(r, st, p, q):
        over = p if p != by_both else (by_x, by_y)[q]
        to, _ = dev(c32(over), 0)
        return rcopy(
            R.snd_l.at[p, piece(st, q)], R.rcv_l.at[r, p, piece(st, q)], R.rs_s.at[1], R.rs_lr.at[st, p, q], to
        )

    def rs_put(r, st, p, same, other):
        R.snd_c[p, half[st]] = other.astype(BF)
        rs_chip(r, st, p).start()
        R.keep[p, half[st]] = same

    def rs_put_pair(r, p, part):
        for st in (0, 1):
            at = st * (T // 2)
            rs_put(r, st, p, part[at:at + T // 2], part[T + at:T + at + T // 2])

    def rs_combine(r, st, p):
        rs_chip(r, st, p).wait_recv()
        both = R.keep[p, half[st]] + R.rcv_c[r, p, half[st]].astype(F32)
        R.keep[p, half[st]] = both
        R.snd_l[p, half[st]] = both.astype(BF)
        for target, parts in ((by_y, (1,)), (by_x, (0,)), (by_both, (0, 1))):
            @when(p == target)
            def _():
                for q in parts:
                    rs_link(r, st, target, q).start()

    def rs_combine_pair(r, p):
        rs_combine(r, 0, p)
        rs_combine(r, 1, p)

    def rs_relay(r, st):
        for p, q in ((by_y, 0), (by_x, 1)):
            rs_link(r, st, by_both, q).wait_recv()
            rows_q = piece(st, q)
            R.snd_l[p, rows_q] = (R.keep[p, rows_q] + R.rcv_l[r, by_both, rows_q].astype(F32)).astype(BF)
            rs_link(r, st, p, q).start()

    def rs_final(r, st):
        rs_chip(r, st, c32(0)).wait_recv()
        acc = R.keep[0, half[st]] + R.rcv_c[r, 0, half[st]].astype(F32)
        for p in (by_y, by_x):
            for q in (0, 1):
                rs_link(r, st, p, q).wait_recv()
            acc = acc + R.rcv_l[r, p, half[st]].astype(F32)
        if st == 1:
            all_of(R.snd_c, R.rs_s.at[0], R.rs_cr.at[0, 0]).wait_send()
            all_of(R.snd_l.at[pl.ds(1, 3)], R.rs_s.at[1], R.rs_cr.at[0, 0]).wait_send()
        return acc

    def rs_whole(r):
        return jnp.concatenate([rs_final(r, 0), rs_final(r, 1)], 0)

    quarter = (pl.ds(0, T // 4), pl.ds(T // 4, T // 4))
    chunks = [("b", lambda x, q=q: x.at[0, q], T // 4) for q in quarter] + [("b", lambda x: x.at[0, half[1]], T // 2)]
    chunks += [("b", lambda x, i=i, h=h: x.at[i, h], T // 2) for i in range(1, 4) for h in half]
    chunks += [("i", lambda x, t=t: x.at[t], T // 2) for t in range(8)]
    chunks += [("o", lambda x, h=h: x.at[h], T // 2) for h in half] + [("s", lambda x: x, 1)]
    chunks += [("w", lambda x, t=t: x.at[t], 3 * T // 8) for t in range(7)]
    chunks += [("w", lambda x, h=h: x.at[7, h], 3 * T // 16) for h in half]
    Z_IN, Z_OUT, Z_SMALL, Z_QKV, Z_ALL = 9, 17, 19, 20, len(chunks)

    def zrefs(c):
        k, cut, _ = chunks[c]
        return cut(getattr(R, "zown_" + k)), cut(getattr(R, "zsum_" + k)), cut(getattr(R, "zmid_" + k))

    kinds = "biosw"

    def z_sem(c, way):
        return R.z_s.at[kinds.index(chunks[c][0]), way]

    def z_up(c):
        own, tot, _ = zrefs(c)
        return rcopy(own, tot, z_sem(c, 0), R.z_r.at[c, 0], (z_other, blk, head))

    def z_across(c):
        own, _, mid = zrefs(c)
        return rcopy(own, mid, z_sem(c, 0), R.z_r.at[c, 1], (z_mid, blk, head))

    def z_down(c):
        _, tot, _ = zrefs(c)
        return rcopy(tot, tot, z_sem(c, 1), R.z_r.at[c, 0], (z_other, blk, head))

    row_us, hop_us = 0.0432, 2.0
    steps, sent = [], 0.0
    for c, (_, _, n) in enumerate(chunks):
        sent += n * row_us
        steps += [(sent + hop_us, c, 0), (sent + n * row_us + 2.2 * hop_us, c, 1)]
    steps.sort()
    made = set()

    def z_until(us):
        while steps and steps[0][0] <= us and steps[0][1] in made:
            _, c, second = steps.pop(0)
            (z_two if second else z_one)(c)

    def z_produce(c):
        made.add(c)

        @pl.when(z_end)
        def _():
            z_up(c).start()

    def z_one(c):
        @pl.when(jnp.logical_not(z_end))
        def _():
            own, tot, _ = zrefs(c)
            z_up(c).wait_recv()
            own[...] = (own[...].astype(F32) + tot[...].astype(F32)).astype(BF)
            z_across(c).start()

    def z_two(c):
        @pl.when(jnp.logical_not(z_end))
        def _():
            own, tot, mid = zrefs(c)
            z_across(c).wait_recv()
            tot[...] = (own[...].astype(F32) + mid[...].astype(F32)).astype(BF)
            z_down(c).start()

    def z_finish(c):
        @pl.when(z_end)
        def _():
            if not Z_IN <= c < Z_OUT:
                z_down(c).wait_recv()

    def z_sent():
        for i, k in enumerate(kinds):
            own, tot = getattr(R, "zown_" + k), getattr(R, "zsum_" + k)
            all_of(own, R.z_s.at[i, 0], R.z_r.at[0, 0]).wait_send()

            @pl.when(jnp.logical_not(z_end))
            def _():
                all_of(tot, R.z_s.at[i, 1], R.z_r.at[0, 0]).wait_send()

    def vec_copy(e):
        to, _ = dev(c32(e // 2), e % 2)
        return rcopy(R.vec, R.vec_all.at[me], R.vec_s.at[0], R.vec_s.at[1], to)

    def qkv_copy(e, j):
        to, at = dev(c32(e // 2), e % 2)
        w = (R.wq, R.wk, R.wv)[j]
        return rcopy(w.at[:, lanes(at, W)], R.wqkv.at[me, :, pl.ds(j * W, W)], R.qkv_s.at[0], R.qkv_s.at[1], to)

    def win_copy(e):
        to, at = dev(c32(e // 2), e % 2)
        return rcopy(R.wi.at[:, lanes(at, FW)], R.win.at[me], R.win_s.at[0], R.win_s.at[1], to)

    far_first = (6, 7, 2, 3, 4, 5, 1)
    with jax.named_scope("start_copies"):
        for e in far_first:
            for j in range(3):
                qkv_copy(e, j).start()
        local[0].wait()
        for st in (0, 1):
            ag_start(tok_all, 0, st)
        for cp in small:
            cp.wait()
        vecs = [x[...].astype(F32).reshape(1, T) for x in small_v[1:7]]
        vecs.append(R.ids_v[0:1, lanes(head, T)].astype(F32))
        R.vec[...] = jnp.concatenate(vecs + [jnp.zeros((1, T), F32)], 0)
        R.vec_all[me] = R.vec[...]
        for e in far_first:
            vec_copy(e).start()

    with jax.named_scope("wait_qkv_weights"):
        all_of(R.wqkv.at[seven], R.qkv_s.at[0], R.qkv_s.at[1]).wait_recv()
        pltpu.make_async_copy(R.wqkv.at[me], R.wqkv.at[me], R.loc.at[5]).wait()

    def qkv_step(p):
        ag_wait(tok_all, 0, p)

        if p == by_y:
            for e in far_first:
                win_copy(e).start()
        a, b, x = pair(tok_all, c32(p))
        y = mm(x, rows(R.wqkv), NN)
        qq = ((y[:, :W] + R.bq_v[...].astype(F32).reshape(1, W)) * 0.125).astype(BF)
        kk = y[:, W:2 * W].astype(BF)
        vv = (y[:, 2 * W:] + R.bv_v[...].astype(F32).reshape(1, W)).astype(BF)
        for at, sl in ((a, slice(0, T)), (b, slice(T, 2 * T))):
            R.q[at], R.k[at], R.v[at] = qq[sl], kk[sl], vv[sl]

    with jax.named_scope("project_qkv"):
        for p in range(4):
            qkv_step(p)

    with jax.named_scope("vectors"):
        all_of(R.vec_all.at[seven], R.vec_s.at[0], R.vec_s.at[1]).wait_recv()
        for s in range(8):
            v = R.vec_all[s]
            R.vfull[:, s * T:(s + 1) * T] = v
            ids = jnp.broadcast_to(v[6:7], (T, T)).T
            R.segk[s] = jnp.where(ids < 0, -2.0, ids)

    for i in (1, 2, 3, 4):
        local[i].wait()

    def head_mask(h, like):
        lane = lax.broadcasted_iota(jnp.int32, like.shape, 1)
        return jnp.where(lax.div(lane, HD) == h, like, jnp.zeros_like(like))

    heads = W // HD

    def ids_of(a, b):
        return jnp.concatenate([R.vec_all[a, 6:7], R.vec_all[b, 6:7]], 1)

    def attend_step(i, carry):
        p = 3 - i
        a, b, qp = pair(R.q, p)
        segq = ids_of(a, b)
        segk = rows(R.segk)
        allowed = jnp.concatenate([segk, segk], 1) == segq
        kk = rows(R.k)
        outs = []
        scores = [mm(kk, head_mask(h, qp), NT) for h in range(heads)]
        for h in range(heads):
            s = jnp.where(allowed, scores[h], -1e30)
            ex = jnp.exp(s - jnp.max(s, 0, keepdims=True))
            total = jnp.maximum(jnp.sum(ex, 0, keepdims=True), 1.0)
            pt = (ex * jnp.where(segq >= 0, 1.0 / total, 0.0)).astype(BF)
            R.pt[h, p] = pt
            outs.append(mm(R.vt[h * HD:(h + 1) * HD, :], pt, NN))
            if h == 0:
                @pl.when(p < 3)
                def _():
                    rs_combine_pair(0, p + 1)

        ct = jnp.concatenate(outs, 0).astype(BF)
        R.ctxt[:, lanes(a, T)] = ct[:, :T]
        R.ctxt[:, lanes(b, T)] = ct[:, T:]
        rs_put_pair(0, p, mm(ct, R.wo_v[...], TN))
        return carry

    with jax.named_scope("attend"):
        R.vt[...] = rows(R.v).T
        lax.fori_loop(0, 4, attend_step, 0)

    with jax.named_scope("first_norm"):
        rs_relay(0, 0)
        rs_relay(0, 1)
        for st in (0, 1):
            rs = rs_final(0, st)
            h1 = tok_all[me, half[st]].astype(F32) + rs + R.vfull[0:1]
            n1, r1 = norm_parts(h1)
            y1 = n1 * R.vfull[2:3] + R.vfull[3:4]
            R.n1[half[st]], R.y1[half[st]] = n1, y1
            R.r1[half[st]] = jnp.broadcast_to(r1, (T // 2, 128))
            y1_all[me, half[st]] = y1.astype(BF)
            ag_start(y1_all, 1, st)
    R.kt[...] = rows(R.k).T

    with jax.named_scope("wait_hidden_weights"):
        all_of(R.win.at[seven], R.win_s.at[0], R.win_s.at[1]).wait_recv()

    def hidden_step(st, p):
        ag_have(y1_all, 1, st, p)
        a, b, x = half_pair(y1_all, c32(p), st)
        z = mm(x, rows(R.win), NN) + R.bi_v[...].astype(F32).reshape(1, FW)
        cdf = 0.5 * (1.0 + lax.erf(z * 0.7071067811865476))
        low = (z * cdf).astype(BF)
        slope = cdf + z * (jnp.exp(-0.5 * z * z) * 0.3989422804014327)
        R.hid[a, half[st]], R.hid[b, half[st]] = low[:T // 2], low[T // 2:]
        R.slope[a, half[st]], R.slope[b, half[st]] = slope[:T // 2], slope[T // 2:]
        if p > 1:
            rs_combine(1, st, p - 1)
        part = mm(low, R.wb_v[...], NN)
        rs_put(1, st, p, part[:T // 2], part[T // 2:])

    with jax.named_scope("hidden"):
        hidden_step(0, 0)
        ag_near(y1_all, 1, 0)
        hidden_step(0, 1)
        hidden_step(1, 0)
        ag_near(y1_all, 1, 1)
        hidden_step(0, 2)
        ag_far(y1_all, 1, 0)
        hidden_step(1, 1)
        hidden_step(0, 3)
        ag_far(y1_all, 1, 1)
        hidden_step(1, 2)
        rs_combine(1, 0, 3)
        hidden_step(1, 3)
        rs_combine(1, 1, 3)

    with jax.named_scope("second_norm"):
        rs_relay(1, 0)
        rs_relay(1, 1)
        for st in (0, 1):
            rs = rs_final(1, st)
            h2 = R.y1[half[st]] + rs + R.vfull[1:2]
            n2, r2 = norm_parts(h2)
            gain = R.vfull[4:5]
            R.out_v[half[st]] = (n2 * gain + R.vfull[5:6]).astype(BF)
            cot = R.cot_v[half[st]].astype(F32)
            dh2 = norm_back(cot * gain, n2, r2)
            R.dh2[half[st]] = dh2
            df_all[me, half[st]] = dh2.astype(BF)
            ag_start(df_all, 2, st)
            sums = jnp.concatenate([colsum(cot * n2), colsum(cot)], 0)
            R.sv[0:2, :] = sums if st == 0 else R.sv[0:2, :] + sums
        put_out.start()

    def grad_back(i):
        x = R.hid[:, :, i * T:(i + 1) * T].reshape(8 * T, T)
        R.zown_b[i] = mm(x, rows(df_all), TN).astype(BF)
        for c in range(3) if i == 0 else (2 * i + 1, 2 * i + 2):
            z_produce(c)

    def hidden_back_step(p):
        ag_wait(df_all, 2, p)
        if p == by_both:
            grad_back(0)
        a, b, x = pair(df_all, c32(p))
        slope = jnp.concatenate([R.slope[a], R.slope[b]], 0)
        dz = (mm(x, R.wb_v[...], NT) * slope).astype(BF)
        R.dz[a], R.dz[b] = dz[:T], dz[T:]
        if p > 1:
            rs_combine_pair(2, p - 1)
        rs_put_pair(2, p, mm(dz, rows(R.win), NT))

    with jax.named_scope("hidden_back"):
        for p in range(4):
            hidden_back_step(p)
        rs_combine_pair(2, 3)

    with jax.named_scope("grad_back"):
        for i in range(1, 4):
            grad_back(i)
        z_until(6.0)
        rs_relay(2, 0)
        rs_relay(2, 1)
        z_until(7.5)

    def grad_in(i):
        x = y1_all[:, :, 2 * i * T:(2 * i + 2) * T].reshape(8 * T, 2 * T)
        g = mm(x, rows(R.dz), TN).astype(BF)
        R.zown_i[2 * i], R.zown_i[2 * i + 1] = g[:T], g[T:]
        z_produce(Z_IN + 2 * i)
        z_produce(Z_IN + 2 * i + 1)

    def din_copy(t, s):
        return rcopy(R.zsum_i.at[t], R.grad_i.at[s], R.din_s.at[0], R.din_s.at[1], (dp, t // 2, t % 2))

    def z_deliver(t):
        @pl.when(z_end)
        def _():
            z_down(Z_IN + t).wait_recv()

        @pl.when(me != t)
        def _():
            din_copy(t, me).start()

        @pl.when(me == t)
        def _():
            R.grad_i[me] = R.zsum_i[t]

    with jax.named_scope("grad_in"):
        for i in range(4):
            grad_in(i)
            if i % 2:
                z_until(8.0 + i)

    with jax.named_scope("first_norm_back"):
        rs = rs_whole(2)
        dy1 = R.dh2[...] + rs
        n1 = R.n1[...]
        dh1 = norm_back(dy1 * R.vfull[2:3], n1, R.r1[:, 0:1])
        R.dh1[...] = dh1
        da_all[me] = dh1.astype(BF)
        for st in (0, 1):
            ag_start(da_all, 3, st)
        R.sv[2:3, :] = colsum(dy1 * n1)
        R.sv[3:4, :] = colsum(dy1)

    def sv_copy(e):
        to, at = dev(c32(e // 2), e % 2)
        return rcopy(R.sv.at[:, lanes(at, T)], R.sv_rcv.at[me], R.sv_s.at[0], R.sv_s.at[1], to)

    for e in far_first:
        sv_copy(e).start()
    R.sv_rcv[me] = R.sv[:, lanes(me, T)]

    z_until(12.0)

    R.dk[...] = jnp.zeros_like(R.dk)
    R.dv[...] = jnp.zeros_like(R.dv)

    def attend_back_step(p):
        ag_wait(da_all, 3, p, lambda: z_until(17.0))
        z_until((13.8, 20.0, 23.0, 25.8)[p])
        a, b, x = pair(da_all, c32(p))
        qp = jnp.concatenate([R.q[a], R.q[b]], 0)
        dc = mm(x, R.wo_v[...], NT).astype(BF)
        vv = rows(R.v)
        outs = []
        for h in range(heads):
            dcm, qm = head_mask(h, dc), head_mask(h, qp)
            low = R.pt[h, p]
            pt = low.astype(F32)
            dpt = mm(vv, dcm, NT)
            ds = (pt * (dpt - jnp.sum(pt * dpt, 0, keepdims=True))).astype(BF)
            outs.append(mm(R.kt[h * HD:(h + 1) * HD, :], ds, NN))
            R.dk[...] += mm(ds, qm, NN)
            R.dv[...] += mm(low, dcm, NN)
            z_until((14.8, 21.0, 24.0, 26.8)[p] + h)
        dq = jnp.concatenate(outs, 0).T.astype(BF) * 0.125
        R.dqkv[a, :, 0:W] = dq[:T]
        R.dqkv[b, :, 0:W] = dq[T:]

    with jax.named_scope("attend_back"):
        for p in range(4):
            attend_back_step(p)
        R.dqkv[:, :, W:2 * W] = R.dk[...].astype(BF).reshape(8, T, W)
        R.dqkv[:, :, 2 * W:] = R.dv[...].astype(BF).reshape(8, T, W)

    def dqkv_copy(p, flip):
        to, at = dev(p, flip)
        return rcopy(R.dqkv_snd.at[at], R.zown_w.at[me], R.dqkv_s.at[0], R.dqkv_s.at[1], to)

    def dqkv_step(p):
        a, b = dev(c32(p), 0)[1], dev(c32(p), 1)[1]
        x = jnp.concatenate([tok_all[:, :, lanes(a, T)], tok_all[:, :, lanes(b, T)]], 2).reshape(8 * T, 2 * T)
        g = mm(x, rows(R.dqkv), TN).astype(BF)
        R.dqkv_snd[b] = g[T:]
        dqkv_copy(c32(p), 1).start()
        if p == 0:
            R.zown_w[me] = g[:T]
        else:
            R.dqkv_snd[a] = g[:T]
            dqkv_copy(c32(p), 0).start()
        z_until(28.3 + 0.5 * p)

    with jax.named_scope("grad_qkv"):
        for p in range(4):
            dqkv_step(p)

    with jax.named_scope("grad_out"):
        R.zown_o[...] = mm(R.ctxt[...], rows(da_all), NN).astype(BF)
        z_produce(Z_OUT)
        z_produce(Z_OUT + 1)
        z_until(31.0)

    def input_step(p):
        if p > 1:
            rs_combine_pair(3, p - 1)
        a, b, x = pair(R.dqkv, c32(p))
        rs_put_pair(3, p, mm(x, rows(R.wqkv), NT))
        z_until((30.8, 31.4, 32.8, 34.4)[p])

    with jax.named_scope("input_back"):
        for p in range(4):
            input_step(p)
        rs_combine_pair(3, 3)
        z_until(36.5)

    with jax.named_scope("small_grads"):
        all_of(R.sv_rcv.at[seven], R.sv_s.at[0], R.sv_s.at[1]).wait_recv()
        acc = R.sv_rcv[0]
        for s in range(1, 8):
            acc = acc + R.sv_rcv[s]
        own = lanes(me, T)
        parts = [
            acc[0:4],
            colsum(rows(R.dqkv)[:, 0:W]),
            colsum(rows(R.dqkv)[:, 2 * W:]),
            colsum(da_all[:, :, own].reshape(8 * T, T)),
            colsum(df_all[:, :, own].reshape(8 * T, T)),
        ]
        dbi = colsum(rows(R.dz))
        parts += [dbi[:, i * T:(i + 1) * T] for i in range(FW // T)]
        parts.append(jnp.zeros((16 - 8 - FW // T, T), F32))
        R.zown_s[...] = jnp.concatenate(parts, 0).astype(BF)
        z_produce(Z_SMALL)
        z_until(39.0)

    with jax.named_scope("z_rest"):
        all_of(R.zown_w.at[seven], R.dqkv_s.at[0], R.dqkv_s.at[1]).wait_recv()
        for c in range(Z_QKV, Z_ALL):
            z_produce(c)
        z_until(42.0)
        rs_relay(3, 0)
        rs_relay(3, 1)
        z_until(46.0)
    with jax.named_scope("input_grad"):
        R.igrad_v[...] = R.dh1[...] + rs_whole(3)
        put_igrad.start()
    with jax.named_scope("z_last"):
        for t in range(8):
            z_until(49.0 + 2 * t)
            z_deliver(t)
        z_until(1000.0)

    with jax.named_scope("finish"):
        puts = [put_out, put_igrad]

        def put(i, src, dst):
            puts.append(pltpu.make_async_copy(src, dst, R.put_s.at[i]))
            puts[-1].start()

        for c in range(Z_ALL):
            z_finish(c)
            if c == Z_IN - 1:
                put(2, R.zsum_b, R.gb)
            if c == Z_OUT - 1:
                all_of(R.grad_i.at[seven], R.din_s.at[0], R.din_s.at[1]).wait()
                put(3, R.grad_i, R.gi)
            if c == Z_SMALL:
                put(4, R.zsum_o, R.go)
                put(5, R.zsum_s, R.gs)
            if c >= Z_QKV and c - Z_QKV < 7:
                put(6 + c - Z_QKV, R.zsum_w.at[c - Z_QKV], R.gw.at[c - Z_QKV])
        put(13, R.zsum_w.at[7], R.gw.at[7])
        z_sent()
        for buf, r in ((tok_all, 0), (y1_all, 1), (df_all, 2), (da_all, 3)):
            ag_finish(buf, r)
        for ref, sem in (
            (R.vec_all, R.vec_s), (R.win, R.win_s), (R.sv_rcv, R.sv_s), (R.wqkv, R.qkv_s), (R.zown_w, R.dqkv_s),
        ):
            all_of(ref.at[seven], sem.at[0], sem.at[1]).wait_send()
        for cp in puts:
            cp.wait()


def sharded_plan(
    tokens, segment_ids, cotangent,
    w_query, w_key, w_value, w_out, w_in, w_back,
    bias_query, bias_value, bias_out, bias_in, bias_back,
    first_gain, first_shift, second_gain, second_shift,
):
    tokens, cotangent = tokens[0], cotangent[0]
    T, D = tokens.shape
    W, FW = D // 8, w_in.shape[1] // 8
    ins = dict(
        tok=tokens, cot=cotangent, wq=w_query, wk=w_key, wv=w_value, wo=w_out, wi=w_in, wb=w_back, ids=segment_ids,
        bo=bias_out, bb=bias_back, g1=first_gain, s1=first_shift, g2=second_gain, s2=second_shift,
        bq=bias_query, bv=bias_value, bi=bias_in,
    )
    in_hbm = 8
    outs = dict(
        out=((T, D), BF), igrad=((T, D), F32), gb=((4, T, D), BF), gi=((8, T, FW), BF), go=((T, D), BF),
        gw=((8, T, 3 * W), BF), gs=((16, T), BF),
    )
    sums = dict(b=outs["gb"], i=outs["gi"], o=outs["go"], w=outs["gw"], s=outs["gs"])
    blocks = {k: ((8, T, D), BF) for k in ("tok_all", "y1_all", "df_all", "da_all")}
    scr = dict(
        **blocks,
        wqkv=((8, T, 3 * W), BF), win=((8, T, FW), BF), wb_v=(w_back.shape, BF), wo_v=(w_out.shape, BF),
        cot_v=((T, D), BF), vec=((8, T), F32), vec_all=((8, 8, T), F32), vfull=((8, D), F32), segk=((8, T, T), F32),
        q=((8, T, W), BF), k=((8, T, W), BF), v=((8, T, W), BF), vt=((W, 8 * T), BF), kt=((W, 8 * T), BF),
        pt=((W // HD, 4, 8 * T, 2 * T), BF), ctxt=((W, 8 * T), BF),
        hid=((8, T, FW), BF), slope=((8, T, FW), F32), dz=((8, T, FW), BF),
        n1=((T, D), F32), r1=((T, 128), F32), y1=((T, D), F32), dh2=((T, D), F32), dh1=((T, D), F32),
        sv=((8, D), F32), sv_rcv=((8, 8, T), F32),
        keep=((4, T, D), F32), snd_c=((4, T, D), BF), snd_l=((4, T, D), BF),
        rcv_c=((4, 4, T, D), BF), rcv_l=((4, 4, T, D), BF),
        dk=((8 * T, W), F32), dv=((8 * T, W), F32), dqkv=((8, T, 3 * W), BF),
        dqkv_snd=((8, T, 3 * W), BF),
        **{z + k: v for z in ("zown_", "zsum_", "zmid_") for k, v in sums.items()}, grad_i=outs["gi"],
        out_v=outs["out"], igrad_v=outs["igrad"],
        **{k + "_v": (v.shape, v.dtype) for k, v in list(ins.items())[in_hbm:]},
    )
    sems = dict(
        ag_s=(4,), ag_r=(2, 4, 2), ag_f=(2, 4, 2), rs_s=(2,), rs_cr=(2, 4), rs_lr=(2, 4, 2),
        z_s=(5, 2), z_r=(29, 2), loc=(6,), small_s=(10,), put_s=(14,), vec_s=(2,), qkv_s=(2,), win_s=(2,), sv_s=(2,), din_s=(2,), dqkv_s=(2,),
    )
    names = list(ins) + list(outs) + list(scr) + list(sems)
    res = pl.pallas_call(
        partial(layer_kernel, names),
        out_shape=[jax.ShapeDtypeStruct(*s) for s in outs.values()],
        in_specs=[pl.BlockSpec(memory_space=pltpu.HBM)] * len(ins),
        out_specs=[pl.BlockSpec(memory_space=pltpu.HBM)] * len(outs),
        scratch_shapes=[pltpu.VMEM(*s) for s in scr.values()] + [pltpu.SemaphoreType.DMA(s) for s in sems.values()],
        compiler_params=pltpu.CompilerParams(collective_id=0, has_side_effects=True, vmem_limit_bytes=60 << 20),
        name="layer",
    )(*ins.values())
    firsts = [(T, D)] * 6 + [w_in.shape, w_back.shape]
    sizes = [T, T, T, FW, T, T, T, T, T]
    shapes = [(n, t) for n, t in zip(firsts, [BF] + [F32] * 7)] + [((n,), F32) for n in sizes]
    loaded = list(outs.values())
    stored = [((3, T, D), F32), ((T, D), F32), (w_in.shape, F32), (w_back.shape, F32)] + shapes[8:]
    final = pl.pallas_call(
        finish_kernel,
        out_shape=[jax.ShapeDtypeStruct(*s) for s in shapes],
        in_specs=[pl.BlockSpec(memory_space=pltpu.HBM)] * len(loaded),
        out_specs=[pl.BlockSpec(memory_space=pltpu.HBM)] * len(shapes),
        scratch_shapes=[pltpu.VMEM(*s) for s in loaded + stored]
        + [pltpu.SemaphoreType.DMA((len(loaded) + 4,)), pltpu.SemaphoreType.DMA((len(shapes) + 6,))],
        compiler_params=pltpu.CompilerParams(vmem_limit_bytes=60 << 20),
        name="finish",
    )(*res)
    return (final[0][None], final[1][None], *final[2:])


def finish_kernel(*refs):
    ins, outs, rest = refs[:7], refs[7:24], refs[24:]
    loaded, stored, (load_s, store_s) = rest[:7], rest[7:20], rest[20:]
    out, igrad, gb, gi, go, gw, gs = loaded
    qkv, o_o, o_i, o_b, *o_small = stored
    order = (3, 2, 5, 4, 1, 0, 6)
    loads = {i: pltpu.make_async_copy(ins[i], loaded[i], load_s.at[i]) for i in order}
    for i in order:
        loads[i].start()
    stores = []

    def store(src, dst):
        stores.append(pltpu.make_async_copy(src, dst, store_s.at[len(stores)]))
        stores[-1].start()

    width = gi.shape[2]
    loads[3].wait()
    for j in range(8):
        o_i[:, j * width:(j + 1) * width] = gi[j].astype(F32)
    store(o_i, outs[6])
    loads[2].wait()
    T = gb.shape[1]
    for j in range(4):
        o_b[j * T:(j + 1) * T, :] = gb[j].astype(F32)
    store(o_b, outs[7])
    loads[5].wait()
    W = gw.shape[2] // 3
    for j in range(3):
        for s in range(8):
            qkv[j, :, s * W:(s + 1) * W] = gw[s, :, j * W:(j + 1) * W].astype(F32)
        store(qkv.at[j], outs[2 + j])
    loads[4].wait()
    o_o[...] = go[...].astype(F32)
    store(o_o, outs[5])
    loads[1].wait()
    store(igrad, outs[1])
    loads[0].wait()
    store(out, outs[0])
    loads[6].wait()
    v = gs[...].astype(F32)
    bq, bv, bo, bi, bb, g1, s1, g2, s2 = o_small
    for o, i in ((bq, 4), (bv, 5), (bo, 6), (bb, 7), (g1, 2), (s1, 3), (g2, 0), (s2, 1)):
        o[...] = v[i]
    n = v.shape[1]
    for i in range(bi.shape[0] // n):
        bi[i * n:(i + 1) * n] = v[8 + i]
    for i, o in enumerate(o_small):
        store(o, outs[8 + i])
    for cp in stores:
        cp.wait()


def pick_plan(mesh):
    group = mesh.shape["blk"] * mesh.shape["head"]
    return sharded_plan if (mesh.shape["dp"], group) == (4, 8) else general_plan


def flat_dot(left_side, right_side):
    return jnp.dot(
        left_side.reshape(-1, left_side.shape[-1]), right_side, preferred_element_type=jnp.float32
    )


def inner_dot(left_side, right_side):
    return jnp.einsum(
        "ra,rb->ab",
        left_side.reshape(-1, left_side.shape[-1]),
        right_side.reshape(-1, right_side.shape[-1]),
        preferred_element_type=jnp.float32,
    )


def layer_norm(value_rows, gain_row, shift_row):
    centre = jnp.mean(value_rows, -1, keepdims=True)
    centred = value_rows - centre
    spread = jnp.mean(centred * centred, -1, keepdims=True)
    return centred * lax.rsqrt(spread + 1e-05) * gain_row + shift_row


def head_view(array_in):
    return array_in.reshape(array_in.shape[0], array_in.shape[1], -1, HD)


def allowed_pairs(query_ids, key_ids):
    same_doc = (query_ids[:, :, None] == key_ids[:, None, :]) & (key_ids[:, None, :] >= 0)
    return same_doc[:, None]


def forward_step(state_now, arrived, local_data):
    running_max, running_sum, weighted = state_now
    key_block, value_block, key_ids = arrived
    query_block, query_ids = local_data
    scores = jnp.einsum(
        "gqhd,gkhd->ghqk",
        head_view(query_block),
        head_view(key_block),
        preferred_element_type=jnp.float32,
    )
    allowed = allowed_pairs(query_ids, key_ids)
    masked = jnp.where(allowed, scores, -1e30)
    new_max = jnp.maximum(running_max, jnp.max(masked, -1))
    exponents = jnp.where(allowed, jnp.exp(masked - new_max[..., None]), 0.0)
    running_sum = jnp.sum(exponents, -1)
    weighted = jnp.einsum(
        "ghqk,gkhd->ghqd",
        exponents.astype(jnp.bfloat16),
        head_view(value_block),
        preferred_element_type=jnp.float32,
    )
    return (new_max, running_sum, weighted)


def probabilities(query_block, key_block, query_ids, key_ids, log_sums):
    scores = jnp.einsum(
        "gqhd,gkhd->ghqk",
        head_view(query_block),
        head_view(key_block),
        preferred_element_type=jnp.float32,
    )
    allowed = allowed_pairs(query_ids, key_ids)
    masked = jnp.where(allowed, scores, -1e30)
    return jnp.where(allowed, jnp.exp(masked - log_sums.transpose(0, 2, 1)[..., None]), 0.0)


def score_grads(weights_now, grad_block, value_block, deltas):
    grad_weights = jnp.einsum(
        "gqhd,gkhd->ghqk",
        head_view(grad_block),
        head_view(value_block),
        preferred_element_type=jnp.float32,
    )
    return (weights_now * (grad_weights - deltas.transpose(0, 2, 1)[..., None])).astype(
        jnp.bfloat16
    )


def heads_to_rows(array_in):
    return array_in.transpose(0, 2, 1, 3).reshape(array_in.shape[0], array_in.shape[2], -1)


def general_plan(
    tokens,
    segment_ids,
    cotangent,
    w_query,
    w_key,
    w_value,
    w_out,
    w_in,
    w_back,
    bias_query,
    bias_value,
    bias_out,
    bias_in,
    bias_back,
    first_gain,
    first_shift,
    second_gain,
    second_shift,
):
    (
        query_full,
        key_full,
        value_full,
        out_full,
        in_full,
        back_full,
        query_bias,
        value_bias,
        out_bias,
        in_bias,
        back_bias,
        gain_one,
        shift_one,
        gain_two,
        shift_two,
    ) = (
        lax.all_gather(w_query, GROUP, axis=0, tiled=True),
        lax.all_gather(w_key, GROUP, axis=0, tiled=True),
        lax.all_gather(w_value, GROUP, axis=0, tiled=True),
        lax.all_gather(w_out, GROUP, axis=0, tiled=True),
        lax.all_gather(w_in, GROUP, axis=0, tiled=True),
        lax.all_gather(w_back, GROUP, axis=0, tiled=True),
        lax.all_gather(bias_query, GROUP, axis=0, tiled=True),
        lax.all_gather(bias_value, GROUP, axis=0, tiled=True),
        lax.all_gather(bias_out, GROUP, axis=0, tiled=True),
        lax.all_gather(bias_in, GROUP, axis=0, tiled=True),
        lax.all_gather(bias_back, GROUP, axis=0, tiled=True),
        lax.all_gather(first_gain, GROUP, axis=0, tiled=True),
        lax.all_gather(first_shift, GROUP, axis=0, tiled=True),
        lax.all_gather(second_gain, GROUP, axis=0, tiled=True),
        lax.all_gather(second_shift, GROUP, axis=0, tiled=True),
    )
    query_bias = query_bias.astype(jnp.float32)
    value_bias = value_bias.astype(jnp.float32)
    out_bias = out_bias.astype(jnp.float32)
    in_bias = in_bias.astype(jnp.float32)
    back_bias = back_bias.astype(jnp.float32)
    gain_one = gain_one.astype(jnp.float32)
    shift_one = shift_one.astype(jnp.float32)
    gain_two = gain_two.astype(jnp.float32)
    shift_two = shift_two.astype(jnp.float32)
    seq_count = tokens.shape[0]
    query_tok = (
        ((flat_dot(tokens, query_full) + query_bias) * 0.125)
        .astype(jnp.bfloat16)
        .reshape(tokens.shape)
    )
    key_tok = flat_dot(tokens, key_full).astype(jnp.bfloat16).reshape(tokens.shape)
    value_tok = (
        (flat_dot(tokens, value_full) + value_bias).astype(jnp.bfloat16).reshape(tokens.shape)
    )
    query_heads, key_heads, value_heads = (
        lax.all_to_all(query_tok, "head", split_axis=2, concat_axis=1, tiled=True),
        lax.all_to_all(key_tok, "head", split_axis=2, concat_axis=1, tiled=True),
        lax.all_to_all(value_tok, "head", split_axis=2, concat_axis=1, tiled=True),
    )
    rows_here = query_heads.shape[1]
    width_heads = query_heads.shape[2]
    heads_here = width_heads // HD
    start_state = (
        jnp.full((seq_count, heads_here, rows_here), -1e30, jnp.float32),
        jnp.zeros((seq_count, heads_here, rows_here), jnp.float32),
        jnp.zeros((seq_count, heads_here, rows_here, HD), jnp.float32),
    )
    running_max, running_sum, weighted = forward_step(
        start_state,
        (
            lax.all_gather(key_heads, "blk", axis=1, tiled=True),
            lax.all_gather(value_heads, "blk", axis=1, tiled=True),
            lax.all_gather(segment_ids, "blk", axis=1, tiled=True),
        ),
        (query_heads, segment_ids),
    )
    floored = jnp.maximum(running_sum, 1.0)
    ctx_heads = heads_to_rows(weighted / floored[..., None])
    log_sums = (running_max + jnp.log(floored)).transpose(0, 2, 1)
    ctx_tok = lax.all_to_all(
        ctx_heads.astype(jnp.bfloat16), "head", split_axis=1, concat_axis=2, tiled=True
    )
    first_sum = tokens.astype(jnp.float32) + (flat_dot(ctx_tok, out_full) + out_bias).reshape(
        tokens.shape
    )
    first_norm = layer_norm(first_sum, gain_one, shift_one)
    first_low = first_norm.astype(jnp.bfloat16)
    inner_rows = flat_dot(first_low, in_full) + in_bias
    hidden_low = jax.nn.gelu(inner_rows, approximate=False).astype(jnp.bfloat16)
    second_sum = first_norm + (flat_dot(hidden_low, back_full) + back_bias).reshape(tokens.shape)
    output_now, second_pull = jax.vjp(layer_norm, second_sum, gain_two, shift_two)
    grad_second, grad_gain_two, grad_shift_two = second_pull(cotangent.astype(jnp.float32))
    grad_branch = grad_second.astype(jnp.bfloat16)
    grad_back_bias = jnp.sum(grad_branch.astype(jnp.float32), (0, 1))
    grad_back = inner_dot(hidden_low, grad_branch)
    grad_hidden = flat_dot(grad_branch, back_full.T)
    unused_value, gelu_pull = jax.vjp(partial(jax.nn.gelu, approximate=False), inner_rows)
    grad_inner = gelu_pull(grad_hidden)[0].astype(jnp.bfloat16)
    grad_in_bias = jnp.sum(grad_inner.astype(jnp.float32), 0)
    grad_in = inner_dot(first_low, grad_inner)
    grad_first_norm = grad_second + flat_dot(grad_inner, in_full.T).reshape(tokens.shape)
    unused_norm, first_pull = jax.vjp(layer_norm, first_sum, gain_one, shift_one)
    grad_first, grad_gain_one, grad_shift_one = first_pull(grad_first_norm)
    grad_attn = grad_first.astype(jnp.bfloat16)
    grad_out_bias = jnp.sum(grad_attn.astype(jnp.float32), (0, 1))
    grad_out = inner_dot(ctx_tok, grad_attn)
    grad_ctx_tok = flat_dot(grad_attn, out_full.T).astype(jnp.bfloat16).reshape(tokens.shape)
    grad_ctx = lax.all_to_all(grad_ctx_tok, "head", split_axis=2, concat_axis=1, tiled=True)
    deltas = jnp.sum(head_view(grad_ctx).astype(jnp.float32) * head_view(ctx_heads), -1)
    key_block = lax.all_gather(key_heads, "blk", axis=1, tiled=True)
    value_block = lax.all_gather(value_heads, "blk", axis=1, tiled=True)
    key_ids = lax.all_gather(segment_ids, "blk", axis=1, tiled=True)
    weights_now = probabilities(query_heads, key_block, segment_ids, key_ids, log_sums)
    dscores = score_grads(weights_now, grad_ctx, value_block, deltas)
    grad_query_heads = jnp.einsum(
        "ghqk,gkhd->ghqd", dscores, head_view(key_block), preferred_element_type=jnp.float32
    )
    key_part = jnp.einsum(
        "ghqk,gqhd->gkhd", dscores, head_view(query_heads), preferred_element_type=jnp.float32
    )
    value_part = jnp.einsum(
        "ghqk,gqhd->gkhd",
        weights_now.astype(jnp.bfloat16),
        head_view(grad_ctx),
        preferred_element_type=jnp.float32,
    )
    both_parts = jnp.concatenate(
        [
            key_part.reshape(key_part.shape[0], key_part.shape[1], -1),
            value_part.reshape(value_part.shape[0], value_part.shape[1], -1),
        ],
        2,
    )
    grad_query_heads, pair_grads = (grad_query_heads, both_parts)
    pair_home = lax.psum_scatter(
        pair_grads.astype(jnp.bfloat16), "blk", scatter_dimension=1, tiled=True
    ).astype(jnp.float32)
    grad_key_heads = pair_home[:, :, :width_heads].astype(jnp.bfloat16)
    grad_value_heads = pair_home[:, :, width_heads:].astype(jnp.bfloat16)
    grad_query_rows = heads_to_rows(grad_query_heads).astype(jnp.bfloat16)
    grad_query_tok, grad_key_tok, grad_value_tok = (
        lax.all_to_all(grad_query_rows, "head", split_axis=1, concat_axis=2, tiled=True),
        lax.all_to_all(grad_key_heads, "head", split_axis=1, concat_axis=2, tiled=True),
        lax.all_to_all(grad_value_heads, "head", split_axis=1, concat_axis=2, tiled=True),
    )
    grad_query_tok = grad_query_tok * 0.125
    grad_inputs = grad_first + (
        flat_dot(grad_query_tok, query_full.T)
        + flat_dot(grad_key_tok, key_full.T)
        + flat_dot(grad_value_tok, value_full.T)
    ).reshape(tokens.shape)
    (
        shard_wq,
        shard_wk,
        shard_wv,
        shard_wo,
        shard_wi,
        shard_wb,
        shard_bq,
        shard_bv,
        shard_bo,
        shard_bi,
        shard_bb,
        shard_g1,
        shard_s1,
        shard_g2,
        shard_s2,
    ) = (
        lax.psum_scatter(
            inner_dot(tokens, grad_query_tok), GROUP, scatter_dimension=0, tiled=True
        ),
        lax.psum_scatter(
            inner_dot(tokens, grad_key_tok), GROUP, scatter_dimension=0, tiled=True
        ),
        lax.psum_scatter(
            inner_dot(tokens, grad_value_tok), GROUP, scatter_dimension=0, tiled=True
        ),
        lax.psum_scatter(grad_out, GROUP, scatter_dimension=0, tiled=True),
        lax.psum_scatter(grad_in, GROUP, scatter_dimension=0, tiled=True),
        lax.psum_scatter(grad_back, GROUP, scatter_dimension=0, tiled=True),
        lax.psum_scatter(
            jnp.sum(grad_query_tok.astype(jnp.float32), (0, 1)),
            GROUP,
            scatter_dimension=0,
            tiled=True,
        ),
        lax.psum_scatter(
            jnp.sum(grad_value_tok.astype(jnp.float32), (0, 1)),
            GROUP,
            scatter_dimension=0,
            tiled=True,
        ),
        lax.psum_scatter(grad_out_bias, GROUP, scatter_dimension=0, tiled=True),
        lax.psum_scatter(grad_in_bias, GROUP, scatter_dimension=0, tiled=True),
        lax.psum_scatter(grad_back_bias, GROUP, scatter_dimension=0, tiled=True),
        lax.psum_scatter(grad_gain_one, GROUP, scatter_dimension=0, tiled=True),
        lax.psum_scatter(grad_shift_one, GROUP, scatter_dimension=0, tiled=True),
        lax.psum_scatter(grad_gain_two, GROUP, scatter_dimension=0, tiled=True),
        lax.psum_scatter(grad_shift_two, GROUP, scatter_dimension=0, tiled=True),
    )
    (
        total_wq,
        total_wk,
        total_wv,
        total_wo,
        total_wi,
        total_wb,
        total_bq,
        total_bv,
        total_bo,
        total_bi,
        total_bb,
        total_g1,
        total_s1,
        total_g2,
        total_s2,
    ) = (
        lax.psum(shard_wq.astype(jnp.bfloat16), "dp").astype(jnp.float32),
        lax.psum(shard_wk.astype(jnp.bfloat16), "dp").astype(jnp.float32),
        lax.psum(shard_wv.astype(jnp.bfloat16), "dp").astype(jnp.float32),
        lax.psum(shard_wo.astype(jnp.bfloat16), "dp").astype(jnp.float32),
        lax.psum(shard_wi.astype(jnp.bfloat16), "dp").astype(jnp.float32),
        lax.psum(shard_wb.astype(jnp.bfloat16), "dp").astype(jnp.float32),
        lax.psum(shard_bq.astype(jnp.bfloat16), "dp").astype(jnp.float32),
        lax.psum(shard_bv.astype(jnp.bfloat16), "dp").astype(jnp.float32),
        lax.psum(shard_bo.astype(jnp.bfloat16), "dp").astype(jnp.float32),
        lax.psum(shard_bi.astype(jnp.bfloat16), "dp").astype(jnp.float32),
        lax.psum(shard_bb.astype(jnp.bfloat16), "dp").astype(jnp.float32),
        lax.psum(shard_g1.astype(jnp.bfloat16), "dp").astype(jnp.float32),
        lax.psum(shard_s1.astype(jnp.bfloat16), "dp").astype(jnp.float32),
        lax.psum(shard_g2.astype(jnp.bfloat16), "dp").astype(jnp.float32),
        lax.psum(shard_s2.astype(jnp.bfloat16), "dp").astype(jnp.float32),
    )
    return (
        output_now.astype(jnp.bfloat16),
        grad_inputs,
        total_wq,
        total_wk,
        total_wv,
        total_wo,
        total_wi,
        total_wb,
        total_bq,
        total_bv,
        total_bo,
        total_bi,
        total_bb,
        total_g1,
        total_s1,
        total_g2,
        total_s2,
    )


def solution(mesh):
    in_specs = (
        P("dp", GROUP, None),
        P("dp", "blk"),
        P("dp", GROUP, None),
        P(GROUP, None),
        P(GROUP, None),
        P(GROUP, None),
        P(GROUP, None),
        P(GROUP, None),
        P(GROUP, None),
        P(GROUP),
        P(GROUP),
        P(GROUP),
        P(GROUP),
        P(GROUP),
        P(GROUP),
        P(GROUP),
        P(GROUP),
        P(GROUP),
    )
    out_specs = (
        P("dp", GROUP, None),
        P("dp", GROUP, None),
        P(GROUP, None),
        P(GROUP, None),
        P(GROUP, None),
        P(GROUP, None),
        P(GROUP, None),
        P(GROUP, None),
        P(GROUP),
        P(GROUP),
        P(GROUP),
        P(GROUP),
        P(GROUP),
        P(GROUP),
        P(GROUP),
        P(GROUP),
        P(GROUP),
    )
    plan = pick_plan(mesh)
    return jax.shard_map(
        plan, mesh=mesh, in_specs=in_specs, out_specs=out_specs, check_vma=False
    )
```

```python
from functools import partial
from types import SimpleNamespace

import jax
import jax.numpy as jnp
from jax import lax
from jax.experimental import pallas as pl
from jax.experimental.pallas import tpu as pltpu
from jax.sharding import PartitionSpec as P

HD = 64
BF = jnp.bfloat16
F32 = jnp.float32
GROUP = ("blk", "head")
MESH = pl.DeviceIdType.MESH
NN = ((1,), (0,))
NT = ((1,), (1,))
TN = ((0,), (0,))


def mm(a, b, dims):
    return lax.dot_general(a, b, (dims, ((), ())), preferred_element_type=F32)


def norm_parts(v):
    c = v - jnp.mean(v, -1, keepdims=True)
    r = lax.rsqrt(jnp.mean(c * c, -1, keepdims=True) + 1e-05)
    return c * r, r


def norm_back(e, n, r):
    return r * (e - jnp.mean(e, -1, keepdims=True) - n * jnp.mean(e * n, -1, keepdims=True))


def colsum(x):
    return jnp.sum(x.astype(F32), 0, keepdims=True)


def when(cond):
    if isinstance(cond, bool):
        return (lambda body: body()) if cond else (lambda body: None)
    return pl.when(cond)


def rows(ref):
    x = ref[...]
    return x.reshape(-1, x.shape[-1])


def layer_kernel(names, *refs):
    R = SimpleNamespace(**dict(zip(names, refs, strict=True)))
    dp, blk, head = [lax.axis_index(a) for a in ("dp", "blk", "head")]
    core, chip_x = lax.rem(blk, 2), lax.div(blk, 2)
    T, D = R.tok.shape
    W = R.q.shape[-1]
    FW = R.wi.shape[1] // 8

    def dev(p, flip):
        hh = lax.rem(head + lax.rem(p, 2), 2)
        bb = lax.rem(chip_x + lax.div(p, 2), 2) * 2 + lax.rem(core + flip, 2)
        return (dp, bb, hh), bb * 2 + hh

    def c32(i):
        return jnp.asarray(i, jnp.int32)

    me = blk * 2 + head
    partner, partner_at = dev(c32(0), 1)
    z_end = lax.rem(dp, 3) == 0
    z_other = jnp.where(dp == 0, 1, jnp.where(dp == 3, 2, jnp.where(dp == 1, 0, 3)))
    z_mid = jnp.where(dp == 1, 2, 1)

    def rcopy(src, dst, ssem, rsem, to):
        return pltpu.make_async_remote_copy(src, dst, ssem, rsem, device_id=to, device_id_type=MESH)

    def all_of(ref, ssem, rsem):
        return rcopy(ref, ref, ssem, rsem, partner)

    seven = pl.ds(0, 7)

    def lanes(i, w):
        return pl.ds(pl.multiple_of(i * w, w), w)

    tok_all, y1_all, df_all, da_all = R.tok_all, R.y1_all, R.df_all, R.da_all
    half = (pl.ds(0, T // 2), pl.ds(T // 2, T // 2))

    def share(z):
        return pl.ds(pl.multiple_of(T // 2 + z * (T // 8), T // 8), T // 8)

    small_in = (R.ids, R.bo, R.bb, R.g1, R.s1, R.g2, R.s2, R.bq, R.bv, R.bi)
    small_v = (R.ids_v, R.bo_v, R.bb_v, R.g1_v, R.s1_v, R.g2_v, R.s2_v, R.bq_v, R.bv_v, R.bi_v)
    local = [
        pltpu.make_async_copy(R.tok, tok_all.at[me], R.loc.at[0]),
        pltpu.make_async_copy(R.wb, R.wb_v, R.loc.at[1]),
        pltpu.make_async_copy(R.wo, R.wo_v, R.loc.at[2]),
        pltpu.make_async_copy(R.wi.at[half[0], lanes(me, FW)], R.win.at[me, half[0]], R.loc.at[3]),
        pltpu.make_async_copy(R.cot, R.cot_v, R.loc.at[4]),
    ]
    local_share = pltpu.make_async_copy(R.wi.at[share(dp), lanes(me, FW)], R.win.at[me, share(dp)], R.loc.at[6])
    local_share.start()
    for j, w in enumerate((R.wq, R.wk, R.wv)):
        for part, at in ((half[0], 5), (share(dp), 7)):
            local.append(
                pltpu.make_async_copy(w.at[part, lanes(me, W)], R.wqkv.at[me, part, pl.ds(j * W, W)], R.loc.at[at])
            )
    small = [
        pltpu.make_async_copy(x, y, R.small_s.at[i])
        for i, (x, y) in enumerate(zip(small_in, small_v, strict=True))
    ]
    for cp in local + small:
        cp.start()

    bar = pltpu.get_barrier_semaphore()
    for e in range(1, 8):
        to, _ = dev(c32(e // 2), e % 2)
        pl.semaphore_signal(bar, 1, device_id=to, device_id_type=MESH)
    for j in range(1, 4):
        pl.semaphore_signal(bar, 1, device_id=(lax.rem(dp + j, 4), blk, head), device_id_type=MESH)
    pl.semaphore_wait(bar, 10)

    put_out = pltpu.make_async_copy(R.out_v, R.out, R.put_s.at[0])
    put_igrad = pltpu.make_async_copy(R.igrad_v, R.igrad, R.put_s.at[1])

    by_y, by_x, by_both = 1, 2, 3

    def piece(st, q):
        return pl.ds((2 * st + q) * (T // 4), T // 4)

    def ag_direct(buf, r, st, p, q):
        to, _ = dev(c32(p), 0)
        part = buf.at[me, piece(st, q)]
        return rcopy(part, part, R.ag_s.at[r], R.ag_r.at[st, p, q], to)

    def ag_relay(buf, r, st, q):
        via, over = (by_x, by_y) if q == 0 else (by_y, by_x)
        _, at = dev(c32(via), 0)
        to, _ = dev(c32(over), 0)
        part = buf.at[at, piece(st, q)]
        return rcopy(part, part, R.ag_s.at[r], R.ag_r.at[st, by_both, q], to)

    def ag_home(buf, r, st):
        part = buf.at[me, half[st]]
        return rcopy(part, part, R.ag_s.at[r], R.ag_f.at[st, 0, 0], partner)

    def ag_forward(buf, r, st, p, q):
        _, at = dev(c32(p), 0)
        part = buf.at[at, piece(st, q)]
        return rcopy(part, part, R.ag_s.at[r], R.ag_f.at[st, p, q], partner)

    def ag_start(buf, r, st):
        for p, q in ((by_x, 0), (by_y, 1), (by_x, 1), (by_y, 0)):
            ag_direct(buf, r, st, p, q).start()
        ag_home(buf, r, st).start()

    def ag_got(buf, r, st, p, q):
        (ag_relay(buf, r, st, q) if p == by_both else ag_direct(buf, r, st, p, q)).wait_recv()
        ag_forward(buf, r, st, p, q).start()

    def ag_near(buf, r, st):
        for p, q in ((by_x, 0), (by_y, 1)):
            ag_got(buf, r, st, p, q)
            ag_relay(buf, r, st, q).start()
        for p, q in ((by_y, 0), (by_x, 1)):
            ag_got(buf, r, st, p, q)

    def ag_far(buf, r, st):
        for q in (0, 1):
            ag_got(buf, r, st, by_both, q)

    def ag_have(buf, r, st, p):
        if p == 0:
            ag_home(buf, r, st).wait_recv()
        else:
            for q in (0, 1):
                ag_forward(buf, r, st, p, q).wait_recv()

    def ag_wait(buf, r, p, between=lambda st: None):
        for st in (0, 1):
            if p == by_y:
                ag_near(buf, r, st)
                between(st)
            if p == by_x:
                ag_far(buf, r, st)
        for st in (0, 1):
            ag_have(buf, r, st, p)

    def ag_finish(buf, r):
        all_of(buf.at[seven], R.ag_s.at[r], R.ag_r.at[0, 0, 0]).wait_send()

    def pair(buf, p):
        a, b = dev(p, 0)[1], dev(p, 1)[1]
        return a, b, jnp.concatenate([buf[a], buf[b]], 0)

    def half_pair(buf, p, st):
        a, b = dev(p, 0)[1], dev(p, 1)[1]
        return a, b, jnp.concatenate([buf[a, half[st]], buf[b, half[st]]], 0)

    def rs_chip(r, st, p):
        return rcopy(
            R.snd_c.at[p, half[st]], R.rcv_c.at[r, p, half[st]], R.rs_s.at[0], R.rs_cr.at[st, p], partner
        )

    def rs_link(r, st, p, q):
        over = p if p != by_both else (by_x, by_y)[q]
        to, _ = dev(c32(over), 0)
        return rcopy(
            R.snd_l.at[p, piece(st, q)], R.rcv_l.at[r, p, piece(st, q)], R.rs_s.at[1], R.rs_lr.at[st, p, q], to
        )

    def rs_put(r, st, p, same, other):
        R.snd_c[p, half[st]] = other.astype(BF)
        rs_chip(r, st, p).start()
        R.keep[p, half[st]] = same

    def rs_put_pair(r, p, part):
        for st in (0, 1):
            at = st * (T // 2)
            rs_put(r, st, p, part[at:at + T // 2], part[T + at:T + at + T // 2])

    def rs_combine(r, st, p):
        rs_chip(r, st, p).wait_recv()
        both = R.keep[p, half[st]] + R.rcv_c[r, p, half[st]].astype(F32)
        R.keep[p, half[st]] = both
        R.snd_l[p, half[st]] = both.astype(BF)
        for target, parts in ((by_y, (1,)), (by_x, (0,)), (by_both, (0, 1))):
            @when(p == target)
            def _():
                for q in parts:
                    rs_link(r, st, target, q).start()

    def rs_combine_pair(r, p):
        rs_combine(r, 0, p)
        rs_combine(r, 1, p)

    def rs_relay(r, st):
        for p, q in ((by_y, 0), (by_x, 1)):
            rs_link(r, st, by_both, q).wait_recv()
            rows_q = piece(st, q)
            R.snd_l[p, rows_q] = (R.keep[p, rows_q] + R.rcv_l[r, by_both, rows_q].astype(F32)).astype(BF)
            rs_link(r, st, p, q).start()

    def rs_final(r, st):
        rs_chip(r, st, c32(0)).wait_recv()
        acc = R.keep[0, half[st]] + R.rcv_c[r, 0, half[st]].astype(F32)
        for p in (by_y, by_x):
            for q in (0, 1):
                rs_link(r, st, p, q).wait_recv()
            acc = acc + R.rcv_l[r, p, half[st]].astype(F32)
        if st == 1:
            all_of(R.snd_c, R.rs_s.at[0], R.rs_cr.at[0, 0]).wait_send()
            all_of(R.snd_l.at[pl.ds(1, 3)], R.rs_s.at[1], R.rs_cr.at[0, 0]).wait_send()
        return acc

    def rs_whole(r):
        return jnp.concatenate([rs_final(r, 0), rs_final(r, 1)], 0)

    quarter = (pl.ds(0, T // 4), pl.ds(T // 4, T // 4))
    chunks = [("b", lambda x, q=q: x.at[0, q], T // 4) for q in quarter] + [("b", lambda x: x.at[0, half[1]], T // 2)]
    chunks += [("b", lambda x, i=i, h=h: x.at[i, h], T // 2) for i in range(1, 4) for h in half]
    chunks += [("i", lambda x, t=t: x.at[t], T // 2) for t in range(8)]
    chunks += [("o", lambda x, h=h: x.at[h], T // 2) for h in half] + [("s", lambda x: x, 1)]
    chunks += [("w", lambda x, t=t: x.at[t], 3 * T // 8) for t in range(7)]
    chunks += [("w", lambda x, h=h: x.at[7, h], 3 * T // 16) for h in half]
    Z_IN, Z_OUT, Z_SMALL, Z_QKV, Z_ALL = 9, 17, 19, 20, len(chunks)

    def zrefs(c):
        k, cut, _ = chunks[c]
        return cut(getattr(R, "zown_" + k)), cut(getattr(R, "zsum_" + k)), cut(getattr(R, "zmid_" + k))

    kinds = "biosw"

    def z_sem(c, way):
        return R.z_s.at[kinds.index(chunks[c][0]), way]

    def z_up(c):
        own, tot, _ = zrefs(c)
        return rcopy(own, tot, z_sem(c, 0), R.z_r.at[c, 0], (z_other, blk, head))

    def z_across(c):
        own, _, mid = zrefs(c)
        return rcopy(own, mid, z_sem(c, 0), R.z_r.at[c, 1], (z_mid, blk, head))

    def z_down(c):
        _, tot, _ = zrefs(c)
        return rcopy(tot, tot, z_sem(c, 1), R.z_r.at[c, 0], (z_other, blk, head))

    row_us, hop_us = 0.0432, 2.0
    steps, sent = [], 0.0
    for c, (_, _, n) in enumerate(chunks):
        sent += n * row_us
        steps += [(sent + hop_us, c, 0), (sent + n * row_us + 2.2 * hop_us, c, 1)]
    steps.sort()
    made = set()

    def z_until(us):
        while steps and steps[0][0] <= us and steps[0][1] in made:
            _, c, second = steps.pop(0)
            (z_two if second else z_one)(c)

    def z_produce(c):
        made.add(c)

        @pl.when(z_end)
        def _():
            z_up(c).start()

    def z_one(c):
        @pl.when(jnp.logical_not(z_end))
        def _():
            own, tot, _ = zrefs(c)
            z_up(c).wait_recv()
            own[...] = (own[...].astype(F32) + tot[...].astype(F32)).astype(BF)
            z_across(c).start()

    def z_two(c):
        @pl.when(jnp.logical_not(z_end))
        def _():
            own, tot, mid = zrefs(c)
            z_across(c).wait_recv()
            tot[...] = (own[...].astype(F32) + mid[...].astype(F32)).astype(BF)
            z_down(c).start()

    def z_finish(c):
        @pl.when(z_end)
        def _():
            if not Z_IN <= c < Z_OUT:
                z_down(c).wait_recv()

    def z_sent():
        for i, k in enumerate(kinds):
            own, tot = getattr(R, "zown_" + k), getattr(R, "zsum_" + k)
            all_of(own, R.z_s.at[i, 0], R.z_r.at[0, 0]).wait_send()

            @pl.when(jnp.logical_not(z_end))
            def _():
                all_of(tot, R.z_s.at[i, 1], R.z_r.at[0, 0]).wait_send()

    def vec_copy(e):
        to, _ = dev(c32(e // 2), e % 2)
        return rcopy(R.vec, R.vec_all.at[me], R.vec_s.at[0], R.vec_s.at[1], to)

    def qkv_copy(e, j, part, sems):
        to, at = dev(c32(e // 2), e % 2)
        w = (R.wq, R.wk, R.wv)[j]
        return rcopy(w.at[part, lanes(at, W)], R.wqkv.at[me, part, pl.ds(j * W, W)], sems.at[0], sems.at[1], to)

    def win_copy(e, part, sems):
        to, at = dev(c32(e // 2), e % 2)
        return rcopy(R.wi.at[part, lanes(at, FW)], R.win.at[me, part], sems.at[0], sems.at[1], to)

    def along(i, k, way):
        sign = 1 if way == 0 else -1
        q, to = dp - sign * k, dp + sign
        part = (R.wqkv, R.win)[i].at[:, share(q)]
        return rcopy(part, part, R.along_s.at[i, way, k], R.along_r.at[i, way, k], (to, blk, head))

    def along_do(i, k, act):
        for way, sends, gets in (
            (0, (dp <= 2) & (dp >= k), dp >= k + 1),
            (1, (dp >= 1) & (dp + k <= 3), dp + k <= 2),
        ):
            @pl.when(gets if act == 1 else sends)
            def _():
                step = along(i, k, way)
                (step.start, step.wait_recv, step.wait_send)[act]()

    def along_send(i, k):
        along_do(i, k, 0)

    def along_got(i, k):
        along_do(i, k, 1)

    def along_sent(i):
        for k in range(3):
            along_do(i, k, 2)

    far_first = (6, 7, 2, 3, 4, 5, 1)
    with jax.named_scope("start_copies"):
        for part, sems in ((share(dp), R.qshare_s), (half[0], R.qkv_s)):
            for e in far_first:
                for j in range(3):
                    qkv_copy(e, j, part, sems).start()
        local[0].wait()
        for st in (0, 1):
            ag_start(tok_all, 0, st)
        for cp in small:
            cp.wait()
        vecs = [x[...].astype(F32).reshape(1, T) for x in small_v[1:7]]
        vecs.append(R.ids_v[0:1, lanes(head, T)].astype(F32))
        R.vec[...] = jnp.concatenate(vecs + [jnp.zeros((1, T), F32)], 0)
        R.vec_all[me] = R.vec[...]
        for e in far_first:
            vec_copy(e).start()

    with jax.named_scope("wait_qkv_weights"):
        own = R.wqkv.at[me, pl.ds(0, T // 8)]
        pltpu.make_async_copy(own, own, R.loc.at[7]).wait()
        all_of(R.wqkv.at[seven, pl.ds(0, T // 8)], R.qshare_s.at[0], R.qshare_s.at[1]).wait()
        along_send(0, 0)
        along_got(0, 0)
        along_send(0, 1)
        ag_near(tok_all, 0, 0)
        along_got(0, 1)
        along_send(0, 2)
        ag_near(tok_all, 0, 1)
        ag_far(tok_all, 0, 0)
        for e in far_first:
            win_copy(e, share(dp), R.share_s).start()
        own = R.wqkv.at[me, half[0]]
        pltpu.make_async_copy(own, own, R.loc.at[5]).wait()
        all_of(R.wqkv.at[seven, half[0]], R.qkv_s.at[0], R.qkv_s.at[1]).wait()
        along_got(0, 2)
        along_sent(0)

    def qkv_step(p):
        if p == by_x:
            ag_far(tok_all, 0, 1)
            for e in far_first:
                win_copy(e, half[0], R.win_s).start()
        for st in (0, 1):
            ag_have(tok_all, 0, st, p)
        a, b, x = pair(tok_all, c32(p))
        y = mm(x, rows(R.wqkv), NN)
        qq = ((y[:, :W] + R.bq_v[...].astype(F32).reshape(1, W)) * 0.125).astype(BF)
        kk = y[:, W:2 * W].astype(BF)
        vv = (y[:, 2 * W:] + R.bv_v[...].astype(F32).reshape(1, W)).astype(BF)
        for at, sl in ((a, slice(0, T)), (b, slice(T, 2 * T))):
            R.q[at], R.k[at], R.v[at] = qq[sl], kk[sl], vv[sl]

    with jax.named_scope("project_qkv"):
        for p in range(4):
            qkv_step(p)

    with jax.named_scope("vectors"):
        all_of(R.vec_all.at[seven], R.vec_s.at[0], R.vec_s.at[1]).wait_recv()
        for s in range(8):
            v = R.vec_all[s]
            R.vfull[:, s * T:(s + 1) * T] = v
            ids = jnp.broadcast_to(v[6:7], (T, T)).T
            R.segk[s] = jnp.where(ids < 0, -2.0, ids)

    for i in (1, 2, 3, 4):
        local[i].wait()

    def head_mask(h, like):
        lane = lax.broadcasted_iota(jnp.int32, like.shape, 1)
        return jnp.where(lax.div(lane, HD) == h, like, jnp.zeros_like(like))

    heads = W // HD

    def ids_of(a, b):
        return jnp.concatenate([R.vec_all[a, 6:7], R.vec_all[b, 6:7]], 1)

    def attend_step(i, carry):
        p = 3 - i
        a, b, qp = pair(R.q, p)
        segq = ids_of(a, b)
        segk = rows(R.segk)
        allowed = jnp.concatenate([segk, segk], 1) == segq
        kk = rows(R.k)
        outs = []
        scores = [mm(kk, head_mask(h, qp), NT) for h in range(heads)]
        for h in range(heads):
            s = jnp.where(allowed, scores[h], -1e30)
            ex = jnp.exp(s - jnp.max(s, 0, keepdims=True))
            total = jnp.maximum(jnp.sum(ex, 0, keepdims=True), 1.0)
            pt = (ex * jnp.where(segq >= 0, 1.0 / total, 0.0)).astype(BF)
            R.pt[h, p] = pt
            outs.append(mm(R.vt[h * HD:(h + 1) * HD, :], pt, NN))
            if h == 0:
                @pl.when(p < 3)
                def _():
                    rs_combine_pair(0, p + 1)

                @pl.when(p == 3)
                def _():
                    local_share.wait()
                    all_of(R.win.at[seven, pl.ds(0, T // 8)], R.share_s.at[0], R.share_s.at[1]).wait()
                    along_send(1, 0)

                @pl.when(p == 1)
                def _():
                    along_got(1, 0)
                    along_send(1, 1)

        ct = jnp.concatenate(outs, 0).astype(BF)
        R.ctxt[:, lanes(a, T)] = ct[:, :T]
        R.ctxt[:, lanes(b, T)] = ct[:, T:]
        rs_put_pair(0, p, mm(ct, R.wo_v[...], TN))
        return carry

    with jax.named_scope("attend"):
        R.vt[...] = rows(R.v).T
        lax.fori_loop(0, 4, attend_step, 0)

    with jax.named_scope("first_norm"):
        rs_relay(0, 0)
        rs_relay(0, 1)
        along_got(1, 1)
        along_send(1, 2)
        for st in (0, 1):
            rs = rs_final(0, st)
            h1 = tok_all[me, half[st]].astype(F32) + rs + R.vfull[0:1]
            n1, r1 = norm_parts(h1)
            y1 = n1 * R.vfull[2:3] + R.vfull[3:4]
            R.n1[half[st]], R.y1[half[st]] = n1, y1
            R.r1[half[st]] = jnp.broadcast_to(r1, (T // 2, 128))
            y1_all[me, half[st]] = y1.astype(BF)
            ag_start(y1_all, 1, st)
    R.kt[...] = rows(R.k).T

    with jax.named_scope("wait_hidden_weights"):
        all_of(R.win.at[seven, half[0]], R.win_s.at[0], R.win_s.at[1]).wait()
        along_got(1, 2)
        along_sent(1)

    def hidden_step(*items):
        found = [half_pair(y1_all, c32(p), st) for st, p in items]
        z = mm(jnp.concatenate([x for _, _, x in found], 0), rows(R.win), NN) + R.bi_v[...].astype(F32).reshape(1, FW)
        cdf = 0.5 * (1.0 + lax.erf(z * 0.7071067811865476))
        low = (z * cdf).astype(BF)
        slope = cdf + z * (jnp.exp(-0.5 * z * z) * 0.3989422804014327)
        part = mm(low, R.wb_v[...], NN)
        for i, ((st, p), (a, b, _)) in enumerate(zip(items, found, strict=True)):
            same, other = slice(i * T, i * T + T // 2), slice(i * T + T // 2, (i + 1) * T)
            rs_put(1, st, p, part[same], part[other])
            R.hid[a, half[st]], R.hid[b, half[st]] = low[same], low[other]
            R.slope[a, half[st]], R.slope[b, half[st]] = slope[same], slope[other]

    with jax.named_scope("hidden"):
        for st in (0, 1):
            ag_have(y1_all, 1, st, 0)
        hidden_step((0, 0), (1, 0))
        ag_near(y1_all, 1, 0)
        for p in (by_y, by_x):
            ag_have(y1_all, 1, 0, p)
        hidden_step((0, by_y), (0, by_x))
        ag_near(y1_all, 1, 1)
        ag_far(y1_all, 1, 0)
        for p in (by_y, by_x):
            ag_have(y1_all, 1, 1, p)
            rs_combine(1, 0, p)
        hidden_step((1, by_y), (1, by_x))
        ag_far(y1_all, 1, 1)
        ag_have(y1_all, 1, 0, by_both)
        hidden_step((0, by_both))
        for p in (by_y, by_x):
            rs_combine(1, 1, p)
        ag_have(y1_all, 1, 1, by_both)
        hidden_step((1, by_both))
        rs_combine(1, 0, by_both)
        rs_combine(1, 1, by_both)

    with jax.named_scope("second_norm"):
        rs_relay(1, 0)
        rs_relay(1, 1)
        for st in (0, 1):
            rs = rs_final(1, st)
            h2 = R.y1[half[st]] + rs + R.vfull[1:2]
            n2, r2 = norm_parts(h2)
            gain = R.vfull[4:5]
            R.out_v[half[st]] = (n2 * gain + R.vfull[5:6]).astype(BF)
            cot = R.cot_v[half[st]].astype(F32)
            dh2 = norm_back(cot * gain, n2, r2)
            R.dh2[half[st]] = dh2
            df_all[me, half[st]] = dh2.astype(BF)
            ag_start(df_all, 2, st)
            sums = jnp.concatenate([colsum(cot * n2), colsum(cot)], 0)
            R.sv[0:2, :] = sums if st == 0 else R.sv[0:2, :] + sums
        put_out.start()

    def grad_back(i):
        x = R.hid[:, :, i * T:(i + 1) * T].reshape(8 * T, T)
        R.zown_b[i] = mm(x, rows(df_all), TN).astype(BF)
        for c in range(3) if i == 0 else (2 * i + 1, 2 * i + 2):
            z_produce(c)

    def hidden_back_step(p):
        ag_wait(df_all, 2, p)
        if p == by_both:
            grad_back(0)
        a, b, x = pair(df_all, c32(p))
        slope = jnp.concatenate([R.slope[a], R.slope[b]], 0)
        dz = (mm(x, R.wb_v[...], NT) * slope).astype(BF)
        R.dz[a], R.dz[b] = dz[:T], dz[T:]
        if p > 1:
            rs_combine_pair(2, p - 1)
        rs_put_pair(2, p, mm(dz, rows(R.win), NT))

    with jax.named_scope("hidden_back"):
        for p in range(4):
            hidden_back_step(p)
        rs_combine_pair(2, 3)

    with jax.named_scope("grad_back"):
        for i in range(1, 4):
            grad_back(i)
        z_until(7.5)
        rs_relay(2, 0)
        z_until(8.6)
        rs_relay(2, 1)
        z_until(9.8)

    def grad_in(i):
        x = y1_all[:, :, 2 * i * T:(2 * i + 2) * T].reshape(8 * T, 2 * T)
        g = mm(x, rows(R.dz), TN).astype(BF)
        R.zown_i[2 * i], R.zown_i[2 * i + 1] = g[:T], g[T:]
        z_produce(Z_IN + 2 * i)
        z_produce(Z_IN + 2 * i + 1)

    def din_copy(t, s):
        return rcopy(R.zsum_i.at[t], R.grad_i.at[s], R.din_s.at[0], R.din_s.at[1], (dp, t // 2, t % 2))

    def z_deliver(t):
        @pl.when(z_end)
        def _():
            z_down(Z_IN + t).wait_recv()

        @pl.when(me != t)
        def _():
            din_copy(t, me).start()

        @pl.when(me == t)
        def _():
            R.grad_i[me] = R.zsum_i[t]

    with jax.named_scope("grad_in"):
        for i in range(4):
            grad_in(i)
            if i % 2:
                z_until(10.0 + i)

    with jax.named_scope("first_norm_back"):
        rs = rs_whole(2)
        dy1 = R.dh2[...] + rs
        n1 = R.n1[...]
        dh1 = norm_back(dy1 * R.vfull[2:3], n1, R.r1[:, 0:1])
        R.dh1[...] = dh1
        da_all[me] = dh1.astype(BF)
        for st in (0, 1):
            ag_start(da_all, 3, st)
        R.sv[2:3, :] = colsum(dy1 * n1)
        R.sv[3:4, :] = colsum(dy1)

    def sv_copy(e):
        to, at = dev(c32(e // 2), e % 2)
        return rcopy(R.sv.at[:, lanes(at, T)], R.sv_rcv.at[me], R.sv_s.at[0], R.sv_s.at[1], to)

    for e in far_first:
        sv_copy(e).start()
    R.sv_rcv[me] = R.sv[:, lanes(me, T)]

    z_until(13.8)

    R.dk[...] = jnp.zeros_like(R.dk)
    R.dv[...] = jnp.zeros_like(R.dv)

    def attend_back_step(p):
        ag_wait(da_all, 3, p, lambda st: z_until(18.0 + 2.5 * st))
        z_until((14.6, 21.5, 25.0, 27.8)[p])
        a, b, x = pair(da_all, c32(p))
        qp = jnp.concatenate([R.q[a], R.q[b]], 0)
        dc = mm(x, R.wo_v[...], NT).astype(BF)
        vv = rows(R.v)
        outs = []
        for h in range(heads):
            dcm, qm = head_mask(h, dc), head_mask(h, qp)
            low = R.pt[h, p]
            pt = low.astype(F32)
            dpt = mm(vv, dcm, NT)
            ds = (pt * (dpt - jnp.sum(pt * dpt, 0, keepdims=True))).astype(BF)
            outs.append(mm(R.kt[h * HD:(h + 1) * HD, :], ds, NN))
            R.dk[...] += mm(ds, qm, NN)
            R.dv[...] += mm(low, dcm, NN)
            z_until((16.0, 22.8, 26.2, 28.8)[p] + 1.2 * h)
        dq = jnp.concatenate(outs, 0).T.astype(BF) * 0.125
        R.dqkv[a, :, 0:W] = dq[:T]
        R.dqkv[b, :, 0:W] = dq[T:]

    with jax.named_scope("attend_back"):
        for p in range(4):
            attend_back_step(p)
        R.dqkv[:, :, W:2 * W] = R.dk[...].astype(BF).reshape(8, T, W)
        R.dqkv[:, :, 2 * W:] = R.dv[...].astype(BF).reshape(8, T, W)

    def dqkv_copy(p, flip):
        to, at = dev(p, flip)
        return rcopy(R.dqkv_snd.at[at], R.zown_w.at[me], R.dqkv_s.at[0], R.dqkv_s.at[1], to)

    def dqkv_step(p):
        a, b = dev(c32(p), 0)[1], dev(c32(p), 1)[1]
        x = jnp.concatenate([tok_all[:, :, lanes(a, T)], tok_all[:, :, lanes(b, T)]], 2).reshape(8 * T, 2 * T)
        g = mm(x, rows(R.dqkv), TN).astype(BF)
        R.dqkv_snd[b] = g[T:]
        dqkv_copy(c32(p), 1).start()
        if p == 0:
            R.zown_w[me] = g[:T]
        else:
            R.dqkv_snd[a] = g[:T]
            dqkv_copy(c32(p), 0).start()
        z_until(30.5 + 0.5 * p)

    with jax.named_scope("grad_qkv"):
        for p in range(4):
            dqkv_step(p)

    with jax.named_scope("grad_out"):
        R.zown_o[...] = mm(R.ctxt[...], rows(da_all), NN).astype(BF)
        z_produce(Z_OUT)
        z_produce(Z_OUT + 1)
        z_until(33.0)

    def input_step(p):
        if p > 1:
            rs_combine_pair(3, p - 1)
        a, b, x = pair(R.dqkv, c32(p))
        rs_put_pair(3, p, mm(x, rows(R.wqkv), NT))
        z_until((33.5, 34.0, 35.5, 37.0)[p])

    with jax.named_scope("input_back"):
        for p in range(4):
            input_step(p)
        rs_combine_pair(3, 3)
        z_until(39.0)

    with jax.named_scope("small_grads"):
        all_of(R.sv_rcv.at[seven], R.sv_s.at[0], R.sv_s.at[1]).wait_recv()
        acc = R.sv_rcv[0]
        for s in range(1, 8):
            acc = acc + R.sv_rcv[s]
        own = lanes(me, T)
        parts = [
            acc[0:4],
            colsum(rows(R.dqkv)[:, 0:W]),
            colsum(rows(R.dqkv)[:, 2 * W:]),
            colsum(da_all[:, :, own].reshape(8 * T, T)),
            colsum(df_all[:, :, own].reshape(8 * T, T)),
        ]
        dbi = colsum(rows(R.dz))
        parts += [dbi[:, i * T:(i + 1) * T] for i in range(FW // T)]
        parts.append(jnp.zeros((16 - 8 - FW // T, T), F32))
        R.zown_s[...] = jnp.concatenate(parts, 0).astype(BF)
        z_produce(Z_SMALL)
        z_until(41.0)

    with jax.named_scope("z_rest"):
        all_of(R.zown_w.at[seven], R.dqkv_s.at[0], R.dqkv_s.at[1]).wait_recv()
        for c in range(Z_QKV, Z_ALL):
            z_produce(c)
        z_until(44.5)
        rs_relay(3, 0)
        z_until(47.0)
        rs_relay(3, 1)
        z_until(50.0)
    with jax.named_scope("input_grad"):
        R.igrad_v[...] = R.dh1[...] + rs_whole(3)
        put_igrad.start()
    with jax.named_scope("z_last"):
        for t in range(8):
            z_until(51.0 + 2 * t)
            z_deliver(t)
        z_until(1000.0)

    with jax.named_scope("finish"):
        puts = [put_out, put_igrad]

        def put(i, src, dst):
            puts.append(pltpu.make_async_copy(src, dst, R.put_s.at[i]))
            puts[-1].start()

        for c in range(Z_ALL):
            z_finish(c)
            if c == Z_IN - 1:
                put(2, R.zsum_b, R.gb)
            if c == Z_OUT - 1:
                all_of(R.grad_i.at[seven], R.din_s.at[0], R.din_s.at[1]).wait()
                put(3, R.grad_i, R.gi)
            if c == Z_SMALL:
                put(4, R.zsum_o, R.go)
                put(5, R.zsum_s, R.gs)
            if c >= Z_QKV and c - Z_QKV < 7:
                put(6 + c - Z_QKV, R.zsum_w.at[c - Z_QKV], R.gw.at[c - Z_QKV])
        put(13, R.zsum_w.at[7], R.gw.at[7])
        z_sent()
        for buf, r in ((tok_all, 0), (y1_all, 1), (df_all, 2), (da_all, 3)):
            ag_finish(buf, r)
        for ref, sem in (
            (R.vec_all, R.vec_s), (R.sv_rcv, R.sv_s), (R.zown_w, R.dqkv_s),
        ):
            all_of(ref.at[seven], sem.at[0], sem.at[1]).wait_send()
        for cp in puts:
            cp.wait()


def sharded_plan(
    tokens, segment_ids, cotangent,
    w_query, w_key, w_value, w_out, w_in, w_back,
    bias_query, bias_value, bias_out, bias_in, bias_back,
    first_gain, first_shift, second_gain, second_shift,
):
    tokens, cotangent = tokens[0], cotangent[0]
    T, D = tokens.shape
    W, FW = D // 8, w_in.shape[1] // 8
    ins = dict(
        tok=tokens, cot=cotangent, wq=w_query, wk=w_key, wv=w_value, wo=w_out, wi=w_in, wb=w_back, ids=segment_ids,
        bo=bias_out, bb=bias_back, g1=first_gain, s1=first_shift, g2=second_gain, s2=second_shift,
        bq=bias_query, bv=bias_value, bi=bias_in,
    )
    in_hbm = 8
    outs = dict(
        out=((T, D), BF), igrad=((T, D), F32), gb=((4, T, D), BF), gi=((8, T, FW), BF), go=((T, D), BF),
        gw=((8, T, 3 * W), BF), gs=((16, T), BF),
    )
    sums = dict(b=outs["gb"], i=outs["gi"], o=outs["go"], w=outs["gw"], s=outs["gs"])
    blocks = {k: ((8, T, D), BF) for k in ("tok_all", "y1_all", "df_all", "da_all")}
    scr = dict(
        **blocks,
        wqkv=((8, T, 3 * W), BF), win=((8, T, FW), BF), wb_v=(w_back.shape, BF), wo_v=(w_out.shape, BF),
        cot_v=((T, D), BF), vec=((8, T), F32), vec_all=((8, 8, T), F32), vfull=((8, D), F32), segk=((8, T, T), F32),
        q=((8, T, W), BF), k=((8, T, W), BF), v=((8, T, W), BF), vt=((W, 8 * T), BF), kt=((W, 8 * T), BF),
        pt=((W // HD, 4, 8 * T, 2 * T), BF), ctxt=((W, 8 * T), BF),
        hid=((8, T, FW), BF), slope=((8, T, FW), F32), dz=((8, T, FW), BF),
        n1=((T, D), F32), r1=((T, 128), F32), y1=((T, D), F32), dh2=((T, D), F32), dh1=((T, D), F32),
        sv=((8, D), F32), sv_rcv=((8, 8, T), F32),
        keep=((4, T, D), F32), snd_c=((4, T, D), BF), snd_l=((4, T, D), BF),
        rcv_c=((4, 4, T, D), BF), rcv_l=((4, 4, T, D), BF),
        dk=((8 * T, W), F32), dv=((8 * T, W), F32), dqkv=((8, T, 3 * W), BF),
        dqkv_snd=((8, T, 3 * W), BF),
        **{z + k: v for z in ("zown_", "zsum_", "zmid_") for k, v in sums.items()}, grad_i=outs["gi"],
        out_v=outs["out"], igrad_v=outs["igrad"],
        **{k + "_v": (v.shape, v.dtype) for k, v in list(ins.items())[in_hbm:]},
    )
    sems = dict(
        ag_s=(4,), ag_r=(2, 4, 2), ag_f=(2, 4, 2), rs_s=(2,), rs_cr=(2, 4), rs_lr=(2, 4, 2),
        z_s=(5, 2), z_r=(29, 2), loc=(8,), small_s=(10,), put_s=(14,), vec_s=(2,), qkv_s=(2,), win_s=(2,), share_s=(2,), qshare_s=(2,), along_s=(2, 2, 3), along_r=(2, 2, 3), sv_s=(2,), din_s=(2,), dqkv_s=(2,),
    )
    names = list(ins) + list(outs) + list(scr) + list(sems)
    res = pl.pallas_call(
        partial(layer_kernel, names),
        out_shape=[jax.ShapeDtypeStruct(*s) for s in outs.values()],
        in_specs=[pl.BlockSpec(memory_space=pltpu.HBM)] * len(ins),
        out_specs=[pl.BlockSpec(memory_space=pltpu.HBM)] * len(outs),
        scratch_shapes=[pltpu.VMEM(*s) for s in scr.values()] + [pltpu.SemaphoreType.DMA(s) for s in sems.values()],
        compiler_params=pltpu.CompilerParams(collective_id=0, has_side_effects=True, vmem_limit_bytes=60 << 20),
        name="layer",
    )(*ins.values())
    firsts = [(T, D)] * 6 + [w_in.shape, w_back.shape]
    sizes = [T, T, T, FW, T, T, T, T, T]
    shapes = [(n, t) for n, t in zip(firsts, [BF] + [F32] * 7)] + [((n,), F32) for n in sizes]
    loaded = list(outs.values())
    stored = [((3, T, D), F32), ((T, D), F32), (w_in.shape, F32), (w_back.shape, F32)] + shapes[8:]
    final = pl.pallas_call(
        finish_kernel,
        out_shape=[jax.ShapeDtypeStruct(*s) for s in shapes],
        in_specs=[pl.BlockSpec(memory_space=pltpu.HBM)] * len(loaded),
        out_specs=[pl.BlockSpec(memory_space=pltpu.HBM)] * len(shapes),
        scratch_shapes=[pltpu.VMEM(*s) for s in loaded + stored]
        + [pltpu.SemaphoreType.DMA((len(loaded) + 4,)), pltpu.SemaphoreType.DMA((len(shapes) + 6,))],
        compiler_params=pltpu.CompilerParams(vmem_limit_bytes=60 << 20),
        name="finish",
    )(*res)
    return (final[0][None], final[1][None], *final[2:])


def finish_kernel(*refs):
    ins, outs, rest = refs[:7], refs[7:24], refs[24:]
    loaded, stored, (load_s, store_s) = rest[:7], rest[7:20], rest[20:]
    out, igrad, gb, gi, go, gw, gs = loaded
    qkv, o_o, o_i, o_b, *o_small = stored
    order = (3, 2, 5, 4, 1, 0, 6)
    loads = {i: pltpu.make_async_copy(ins[i], loaded[i], load_s.at[i]) for i in order}
    for i in order:
        loads[i].start()
    stores = []

    def store(src, dst):
        stores.append(pltpu.make_async_copy(src, dst, store_s.at[len(stores)]))
        stores[-1].start()

    width = gi.shape[2]
    loads[3].wait()
    for j in range(8):
        o_i[:, j * width:(j + 1) * width] = gi[j].astype(F32)
    store(o_i, outs[6])
    loads[2].wait()
    T = gb.shape[1]
    for j in range(4):
        o_b[j * T:(j + 1) * T, :] = gb[j].astype(F32)
    store(o_b, outs[7])
    loads[5].wait()
    W = gw.shape[2] // 3
    for j in range(3):
        for s in range(8):
            qkv[j, :, s * W:(s + 1) * W] = gw[s, :, j * W:(j + 1) * W].astype(F32)
        store(qkv.at[j], outs[2 + j])
    loads[4].wait()
    o_o[...] = go[...].astype(F32)
    store(o_o, outs[5])
    loads[1].wait()
    store(igrad, outs[1])
    loads[0].wait()
    store(out, outs[0])
    loads[6].wait()
    v = gs[...].astype(F32)
    bq, bv, bo, bi, bb, g1, s1, g2, s2 = o_small
    for o, i in ((bq, 4), (bv, 5), (bo, 6), (bb, 7), (g1, 2), (s1, 3), (g2, 0), (s2, 1)):
        o[...] = v[i]
    n = v.shape[1]
    for i in range(bi.shape[0] // n):
        bi[i * n:(i + 1) * n] = v[8 + i]
    for i, o in enumerate(o_small):
        store(o, outs[8 + i])
    for cp in stores:
        cp.wait()


def pick_plan(mesh):
    group = mesh.shape["blk"] * mesh.shape["head"]
    return sharded_plan if (mesh.shape["dp"], group) == (4, 8) else general_plan


def flat_dot(left_side, right_side):
    return jnp.dot(
        left_side.reshape(-1, left_side.shape[-1]), right_side, preferred_element_type=jnp.float32
    )


def inner_dot(left_side, right_side):
    return jnp.einsum(
        "ra,rb->ab",
        left_side.reshape(-1, left_side.shape[-1]),
        right_side.reshape(-1, right_side.shape[-1]),
        preferred_element_type=jnp.float32,
    )


def layer_norm(value_rows, gain_row, shift_row):
    centre = jnp.mean(value_rows, -1, keepdims=True)
    centred = value_rows - centre
    spread = jnp.mean(centred * centred, -1, keepdims=True)
    return centred * lax.rsqrt(spread + 1e-05) * gain_row + shift_row


def head_view(array_in):
    return array_in.reshape(array_in.shape[0], array_in.shape[1], -1, HD)


def allowed_pairs(query_ids, key_ids):
    same_doc = (query_ids[:, :, None] == key_ids[:, None, :]) & (key_ids[:, None, :] >= 0)
    return same_doc[:, None]


def forward_step(state_now, arrived, local_data):
    running_max, running_sum, weighted = state_now
    key_block, value_block, key_ids = arrived
    query_block, query_ids = local_data
    scores = jnp.einsum(
        "gqhd,gkhd->ghqk",
        head_view(query_block),
        head_view(key_block),
        preferred_element_type=jnp.float32,
    )
    allowed = allowed_pairs(query_ids, key_ids)
    masked = jnp.where(allowed, scores, -1e30)
    new_max = jnp.maximum(running_max, jnp.max(masked, -1))
    exponents = jnp.where(allowed, jnp.exp(masked - new_max[..., None]), 0.0)
    running_sum = jnp.sum(exponents, -1)
    weighted = jnp.einsum(
        "ghqk,gkhd->ghqd",
        exponents.astype(jnp.bfloat16),
        head_view(value_block),
        preferred_element_type=jnp.float32,
    )
    return (new_max, running_sum, weighted)


def probabilities(query_block, key_block, query_ids, key_ids, log_sums):
    scores = jnp.einsum(
        "gqhd,gkhd->ghqk",
        head_view(query_block),
        head_view(key_block),
        preferred_element_type=jnp.float32,
    )
    allowed = allowed_pairs(query_ids, key_ids)
    masked = jnp.where(allowed, scores, -1e30)
    return jnp.where(allowed, jnp.exp(masked - log_sums.transpose(0, 2, 1)[..., None]), 0.0)


def score_grads(weights_now, grad_block, value_block, deltas):
    grad_weights = jnp.einsum(
        "gqhd,gkhd->ghqk",
        head_view(grad_block),
        head_view(value_block),
        preferred_element_type=jnp.float32,
    )
    return (weights_now * (grad_weights - deltas.transpose(0, 2, 1)[..., None])).astype(
        jnp.bfloat16
    )


def heads_to_rows(array_in):
    return array_in.transpose(0, 2, 1, 3).reshape(array_in.shape[0], array_in.shape[2], -1)


def general_plan(
    tokens,
    segment_ids,
    cotangent,
    w_query,
    w_key,
    w_value,
    w_out,
    w_in,
    w_back,
    bias_query,
    bias_value,
    bias_out,
    bias_in,
    bias_back,
    first_gain,
    first_shift,
    second_gain,
    second_shift,
):
    (
        query_full,
        key_full,
        value_full,
        out_full,
        in_full,
        back_full,
        query_bias,
        value_bias,
        out_bias,
        in_bias,
        back_bias,
        gain_one,
        shift_one,
        gain_two,
        shift_two,
    ) = (
        lax.all_gather(w_query, GROUP, axis=0, tiled=True),
        lax.all_gather(w_key, GROUP, axis=0, tiled=True),
        lax.all_gather(w_value, GROUP, axis=0, tiled=True),
        lax.all_gather(w_out, GROUP, axis=0, tiled=True),
        lax.all_gather(w_in, GROUP, axis=0, tiled=True),
        lax.all_gather(w_back, GROUP, axis=0, tiled=True),
        lax.all_gather(bias_query, GROUP, axis=0, tiled=True),
        lax.all_gather(bias_value, GROUP, axis=0, tiled=True),
        lax.all_gather(bias_out, GROUP, axis=0, tiled=True),
        lax.all_gather(bias_in, GROUP, axis=0, tiled=True),
        lax.all_gather(bias_back, GROUP, axis=0, tiled=True),
        lax.all_gather(first_gain, GROUP, axis=0, tiled=True),
        lax.all_gather(first_shift, GROUP, axis=0, tiled=True),
        lax.all_gather(second_gain, GROUP, axis=0, tiled=True),
        lax.all_gather(second_shift, GROUP, axis=0, tiled=True),
    )
    query_bias = query_bias.astype(jnp.float32)
    value_bias = value_bias.astype(jnp.float32)
    out_bias = out_bias.astype(jnp.float32)
    in_bias = in_bias.astype(jnp.float32)
    back_bias = back_bias.astype(jnp.float32)
    gain_one = gain_one.astype(jnp.float32)
    shift_one = shift_one.astype(jnp.float32)
    gain_two = gain_two.astype(jnp.float32)
    shift_two = shift_two.astype(jnp.float32)
    seq_count = tokens.shape[0]
    query_tok = (
        ((flat_dot(tokens, query_full) + query_bias) * 0.125)
        .astype(jnp.bfloat16)
        .reshape(tokens.shape)
    )
    key_tok = flat_dot(tokens, key_full).astype(jnp.bfloat16).reshape(tokens.shape)
    value_tok = (
        (flat_dot(tokens, value_full) + value_bias).astype(jnp.bfloat16).reshape(tokens.shape)
    )
    query_heads, key_heads, value_heads = (
        lax.all_to_all(query_tok, "head", split_axis=2, concat_axis=1, tiled=True),
        lax.all_to_all(key_tok, "head", split_axis=2, concat_axis=1, tiled=True),
        lax.all_to_all(value_tok, "head", split_axis=2, concat_axis=1, tiled=True),
    )
    rows_here = query_heads.shape[1]
    width_heads = query_heads.shape[2]
    heads_here = width_heads // HD
    start_state = (
        jnp.full((seq_count, heads_here, rows_here), -1e30, jnp.float32),
        jnp.zeros((seq_count, heads_here, rows_here), jnp.float32),
        jnp.zeros((seq_count, heads_here, rows_here, HD), jnp.float32),
    )
    running_max, running_sum, weighted = forward_step(
        start_state,
        (
            lax.all_gather(key_heads, "blk", axis=1, tiled=True),
            lax.all_gather(value_heads, "blk", axis=1, tiled=True),
            lax.all_gather(segment_ids, "blk", axis=1, tiled=True),
        ),
        (query_heads, segment_ids),
    )
    floored = jnp.maximum(running_sum, 1.0)
    ctx_heads = heads_to_rows(weighted / floored[..., None])
    log_sums = (running_max + jnp.log(floored)).transpose(0, 2, 1)
    ctx_tok = lax.all_to_all(
        ctx_heads.astype(jnp.bfloat16), "head", split_axis=1, concat_axis=2, tiled=True
    )
    first_sum = tokens.astype(jnp.float32) + (flat_dot(ctx_tok, out_full) + out_bias).reshape(
        tokens.shape
    )
    first_norm = layer_norm(first_sum, gain_one, shift_one)
    first_low = first_norm.astype(jnp.bfloat16)
    inner_rows = flat_dot(first_low, in_full) + in_bias
    hidden_low = jax.nn.gelu(inner_rows, approximate=False).astype(jnp.bfloat16)
    second_sum = first_norm + (flat_dot(hidden_low, back_full) + back_bias).reshape(tokens.shape)
    output_now, second_pull = jax.vjp(layer_norm, second_sum, gain_two, shift_two)
    grad_second, grad_gain_two, grad_shift_two = second_pull(cotangent.astype(jnp.float32))
    grad_branch = grad_second.astype(jnp.bfloat16)
    grad_back_bias = jnp.sum(grad_branch.astype(jnp.float32), (0, 1))
    grad_back = inner_dot(hidden_low, grad_branch)
    grad_hidden = flat_dot(grad_branch, back_full.T)
    unused_value, gelu_pull = jax.vjp(partial(jax.nn.gelu, approximate=False), inner_rows)
    grad_inner = gelu_pull(grad_hidden)[0].astype(jnp.bfloat16)
    grad_in_bias = jnp.sum(grad_inner.astype(jnp.float32), 0)
    grad_in = inner_dot(first_low, grad_inner)
    grad_first_norm = grad_second + flat_dot(grad_inner, in_full.T).reshape(tokens.shape)
    unused_norm, first_pull = jax.vjp(layer_norm, first_sum, gain_one, shift_one)
    grad_first, grad_gain_one, grad_shift_one = first_pull(grad_first_norm)
    grad_attn = grad_first.astype(jnp.bfloat16)
    grad_out_bias = jnp.sum(grad_attn.astype(jnp.float32), (0, 1))
    grad_out = inner_dot(ctx_tok, grad_attn)
    grad_ctx_tok = flat_dot(grad_attn, out_full.T).astype(jnp.bfloat16).reshape(tokens.shape)
    grad_ctx = lax.all_to_all(grad_ctx_tok, "head", split_axis=2, concat_axis=1, tiled=True)
    deltas = jnp.sum(head_view(grad_ctx).astype(jnp.float32) * head_view(ctx_heads), -1)
    key_block = lax.all_gather(key_heads, "blk", axis=1, tiled=True)
    value_block = lax.all_gather(value_heads, "blk", axis=1, tiled=True)
    key_ids = lax.all_gather(segment_ids, "blk", axis=1, tiled=True)
    weights_now = probabilities(query_heads, key_block, segment_ids, key_ids, log_sums)
    dscores = score_grads(weights_now, grad_ctx, value_block, deltas)
    grad_query_heads = jnp.einsum(
        "ghqk,gkhd->ghqd", dscores, head_view(key_block), preferred_element_type=jnp.float32
    )
    key_part = jnp.einsum(
        "ghqk,gqhd->gkhd", dscores, head_view(query_heads), preferred_element_type=jnp.float32
    )
    value_part = jnp.einsum(
        "ghqk,gqhd->gkhd",
        weights_now.astype(jnp.bfloat16),
        head_view(grad_ctx),
        preferred_element_type=jnp.float32,
    )
    both_parts = jnp.concatenate(
        [
            key_part.reshape(key_part.shape[0], key_part.shape[1], -1),
            value_part.reshape(value_part.shape[0], value_part.shape[1], -1),
        ],
        2,
    )
    grad_query_heads, pair_grads = (grad_query_heads, both_parts)
    pair_home = lax.psum_scatter(
        pair_grads.astype(jnp.bfloat16), "blk", scatter_dimension=1, tiled=True
    ).astype(jnp.float32)
    grad_key_heads = pair_home[:, :, :width_heads].astype(jnp.bfloat16)
    grad_value_heads = pair_home[:, :, width_heads:].astype(jnp.bfloat16)
    grad_query_rows = heads_to_rows(grad_query_heads).astype(jnp.bfloat16)
    grad_query_tok, grad_key_tok, grad_value_tok = (
        lax.all_to_all(grad_query_rows, "head", split_axis=1, concat_axis=2, tiled=True),
        lax.all_to_all(grad_key_heads, "head", split_axis=1, concat_axis=2, tiled=True),
        lax.all_to_all(grad_value_heads, "head", split_axis=1, concat_axis=2, tiled=True),
    )
    grad_query_tok = grad_query_tok * 0.125
    grad_inputs = grad_first + (
        flat_dot(grad_query_tok, query_full.T)
        + flat_dot(grad_key_tok, key_full.T)
        + flat_dot(grad_value_tok, value_full.T)
    ).reshape(tokens.shape)
    (
        shard_wq,
        shard_wk,
        shard_wv,
        shard_wo,
        shard_wi,
        shard_wb,
        shard_bq,
        shard_bv,
        shard_bo,
        shard_bi,
        shard_bb,
        shard_g1,
        shard_s1,
        shard_g2,
        shard_s2,
    ) = (
        lax.psum_scatter(
            inner_dot(tokens, grad_query_tok), GROUP, scatter_dimension=0, tiled=True
        ),
        lax.psum_scatter(
            inner_dot(tokens, grad_key_tok), GROUP, scatter_dimension=0, tiled=True
        ),
        lax.psum_scatter(
            inner_dot(tokens, grad_value_tok), GROUP, scatter_dimension=0, tiled=True
        ),
        lax.psum_scatter(grad_out, GROUP, scatter_dimension=0, tiled=True),
        lax.psum_scatter(grad_in, GROUP, scatter_dimension=0, tiled=True),
        lax.psum_scatter(grad_back, GROUP, scatter_dimension=0, tiled=True),
        lax.psum_scatter(
            jnp.sum(grad_query_tok.astype(jnp.float32), (0, 1)),
            GROUP,
            scatter_dimension=0,
            tiled=True,
        ),
        lax.psum_scatter(
            jnp.sum(grad_value_tok.astype(jnp.float32), (0, 1)),
            GROUP,
            scatter_dimension=0,
            tiled=True,
        ),
        lax.psum_scatter(grad_out_bias, GROUP, scatter_dimension=0, tiled=True),
        lax.psum_scatter(grad_in_bias, GROUP, scatter_dimension=0, tiled=True),
        lax.psum_scatter(grad_back_bias, GROUP, scatter_dimension=0, tiled=True),
        lax.psum_scatter(grad_gain_one, GROUP, scatter_dimension=0, tiled=True),
        lax.psum_scatter(grad_shift_one, GROUP, scatter_dimension=0, tiled=True),
        lax.psum_scatter(grad_gain_two, GROUP, scatter_dimension=0, tiled=True),
        lax.psum_scatter(grad_shift_two, GROUP, scatter_dimension=0, tiled=True),
    )
    (
        total_wq,
        total_wk,
        total_wv,
        total_wo,
        total_wi,
        total_wb,
        total_bq,
        total_bv,
        total_bo,
        total_bi,
        total_bb,
        total_g1,
        total_s1,
        total_g2,
        total_s2,
    ) = (
        lax.psum(shard_wq.astype(jnp.bfloat16), "dp").astype(jnp.float32),
        lax.psum(shard_wk.astype(jnp.bfloat16), "dp").astype(jnp.float32),
        lax.psum(shard_wv.astype(jnp.bfloat16), "dp").astype(jnp.float32),
        lax.psum(shard_wo.astype(jnp.bfloat16), "dp").astype(jnp.float32),
        lax.psum(shard_wi.astype(jnp.bfloat16), "dp").astype(jnp.float32),
        lax.psum(shard_wb.astype(jnp.bfloat16), "dp").astype(jnp.float32),
        lax.psum(shard_bq.astype(jnp.bfloat16), "dp").astype(jnp.float32),
        lax.psum(shard_bv.astype(jnp.bfloat16), "dp").astype(jnp.float32),
        lax.psum(shard_bo.astype(jnp.bfloat16), "dp").astype(jnp.float32),
        lax.psum(shard_bi.astype(jnp.bfloat16), "dp").astype(jnp.float32),
        lax.psum(shard_bb.astype(jnp.bfloat16), "dp").astype(jnp.float32),
        lax.psum(shard_g1.astype(jnp.bfloat16), "dp").astype(jnp.float32),
        lax.psum(shard_s1.astype(jnp.bfloat16), "dp").astype(jnp.float32),
        lax.psum(shard_g2.astype(jnp.bfloat16), "dp").astype(jnp.float32),
        lax.psum(shard_s2.astype(jnp.bfloat16), "dp").astype(jnp.float32),
    )
    return (
        output_now.astype(jnp.bfloat16),
        grad_inputs,
        total_wq,
        total_wk,
        total_wv,
        total_wo,
        total_wi,
        total_wb,
        total_bq,
        total_bv,
        total_bo,
        total_bi,
        total_bb,
        total_g1,
        total_s1,
        total_g2,
        total_s2,
    )


def solution(mesh):
    in_specs = (
        P("dp", GROUP, None),
        P("dp", "blk"),
        P("dp", GROUP, None),
        P(GROUP, None),
        P(GROUP, None),
        P(GROUP, None),
        P(GROUP, None),
        P(GROUP, None),
        P(GROUP, None),
        P(GROUP),
        P(GROUP),
        P(GROUP),
        P(GROUP),
        P(GROUP),
        P(GROUP),
        P(GROUP),
        P(GROUP),
        P(GROUP),
    )
    out_specs = (
        P("dp", GROUP, None),
        P("dp", GROUP, None),
        P(GROUP, None),
        P(GROUP, None),
        P(GROUP, None),
        P(GROUP, None),
        P(GROUP, None),
        P(GROUP, None),
        P(GROUP),
        P(GROUP),
        P(GROUP),
        P(GROUP),
        P(GROUP),
        P(GROUP),
        P(GROUP),
        P(GROUP),
        P(GROUP),
    )
    plan = pick_plan(mesh)
    return jax.shard_map(
        plan, mesh=mesh, in_specs=in_specs, out_specs=out_specs, check_vma=False
    )
```

```python
from functools import partial
from types import SimpleNamespace

import jax
import jax.numpy as jnp
from jax import lax
from jax.experimental import pallas as pl
from jax.experimental.pallas import tpu as pltpu
from jax.sharding import PartitionSpec as P

HD = 64
BF = jnp.bfloat16
F32 = jnp.float32
GROUP = ("blk", "head")
MESH = pl.DeviceIdType.MESH
NN = ((1,), (0,))
NT = ((1,), (1,))
TN = ((0,), (0,))


def mm(a, b, dims):
    return lax.dot_general(a, b, (dims, ((), ())), preferred_element_type=F32)


def norm_parts(v):
    c = v - jnp.mean(v, -1, keepdims=True)
    r = lax.rsqrt(jnp.mean(c * c, -1, keepdims=True) + 1e-05)
    return c * r, r


def norm_back(e, n, r):
    return r * (e - jnp.mean(e, -1, keepdims=True) - n * jnp.mean(e * n, -1, keepdims=True))


def colsum(x):
    return jnp.sum(x.astype(F32), 0, keepdims=True)


def when(cond):
    if isinstance(cond, bool):
        return (lambda body: body()) if cond else (lambda body: None)
    return pl.when(cond)


def rows(ref):
    x = ref[...]
    return x.reshape(-1, x.shape[-1])


def layer_kernel(names, *refs):
    R = SimpleNamespace(**dict(zip(names, refs, strict=True)))
    dp, blk, head = [lax.axis_index(a) for a in ("dp", "blk", "head")]
    core, chip_x = lax.rem(blk, 2), lax.div(blk, 2)
    T, D = R.tok.shape
    W = R.q.shape[-1]
    FW = R.wi.shape[1] // 8

    def dev(p, flip):
        hh = lax.rem(head + lax.rem(p, 2), 2)
        bb = lax.rem(chip_x + lax.div(p, 2), 2) * 2 + lax.rem(core + flip, 2)
        return (dp, bb, hh), bb * 2 + hh

    def c32(i):
        return jnp.asarray(i, jnp.int32)

    me = blk * 2 + head
    partner, partner_at = dev(c32(0), 1)
    z_end = lax.rem(dp, 3) == 0
    z_other = jnp.where(dp == 0, 1, jnp.where(dp == 3, 2, jnp.where(dp == 1, 0, 3)))
    z_mid = jnp.where(dp == 1, 2, 1)

    def rcopy(src, dst, ssem, rsem, to):
        return pltpu.make_async_remote_copy(src, dst, ssem, rsem, device_id=to, device_id_type=MESH)

    def all_of(ref, ssem, rsem):
        return rcopy(ref, ref, ssem, rsem, partner)

    seven = pl.ds(0, 7)

    def lanes(i, w):
        return pl.ds(pl.multiple_of(i * w, w), w)

    tok_all, y1_all, df_all, da_all = R.tok_all, R.y1_all, R.df_all, R.da_all
    half = (pl.ds(0, T // 2), pl.ds(T // 2, T // 2))

    def share(z):
        return pl.ds(pl.multiple_of(T // 2 + z * (T // 8), T // 8), T // 8)

    small_in = (R.ids, R.bo, R.bb, R.g1, R.s1, R.g2, R.s2, R.bq, R.bv, R.bi)
    small_v = (R.ids_v, R.bo_v, R.bb_v, R.g1_v, R.s1_v, R.g2_v, R.s2_v, R.bq_v, R.bv_v, R.bi_v)
    local = [
        pltpu.make_async_copy(R.tok, tok_all.at[me], R.loc.at[0]),
        pltpu.make_async_copy(R.wb, R.wb_v, R.loc.at[1]),
        pltpu.make_async_copy(R.wo, R.wo_v, R.loc.at[2]),
        pltpu.make_async_copy(R.wi.at[half[0], lanes(me, FW)], R.win.at[me, half[0]], R.loc.at[3]),
        pltpu.make_async_copy(R.cot, R.cot_v, R.loc.at[4]),
    ]
    local_share = pltpu.make_async_copy(R.wi.at[share(dp), lanes(me, FW)], R.win.at[me, share(dp)], R.loc.at[6])
    local_share.start()
    for j, w in enumerate((R.wq, R.wk, R.wv)):
        for part, at in ((half[0], 5), (share(dp), 7)):
            local.append(
                pltpu.make_async_copy(w.at[part, lanes(me, W)], R.wqkv.at[me, part, pl.ds(j * W, W)], R.loc.at[at])
            )
    small = [
        pltpu.make_async_copy(x, y, R.small_s.at[i])
        for i, (x, y) in enumerate(zip(small_in, small_v, strict=True))
    ]
    for cp in local + small:
        cp.start()

    bar = pltpu.get_barrier_semaphore()
    for e in range(1, 8):
        to, _ = dev(c32(e // 2), e % 2)
        pl.semaphore_signal(bar, 1, device_id=to, device_id_type=MESH)
    for j in range(1, 4):
        pl.semaphore_signal(bar, 1, device_id=(lax.rem(dp + j, 4), blk, head), device_id_type=MESH)
    pl.semaphore_wait(bar, 10)

    put_out = pltpu.make_async_copy(R.out_v, R.out, R.put_s.at[0])
    put_igrad = pltpu.make_async_copy(R.igrad_v, R.igrad, R.put_s.at[1])

    by_y, by_x, by_both = 1, 2, 3

    def piece(st, q):
        return pl.ds((2 * st + q) * (T // 4), T // 4)

    def ag_direct(buf, r, st, p, q):
        to, _ = dev(c32(p), 0)
        part = buf.at[me, piece(st, q)]
        return rcopy(part, part, R.ag_s.at[r], R.ag_r.at[st, p, q], to)

    def ag_relay(buf, r, st, q):
        via, over = (by_x, by_y) if q == 0 else (by_y, by_x)
        _, at = dev(c32(via), 0)
        to, _ = dev(c32(over), 0)
        part = buf.at[at, piece(st, q)]
        return rcopy(part, part, R.ag_s.at[r], R.ag_r.at[st, by_both, q], to)

    def ag_home(buf, r, st):
        part = buf.at[me, half[st]]
        return rcopy(part, part, R.ag_s.at[r], R.ag_f.at[st, 0, 0], partner)

    def ag_forward(buf, r, st, p, q):
        _, at = dev(c32(p), 0)
        part = buf.at[at, piece(st, q)]
        return rcopy(part, part, R.ag_s.at[r], R.ag_f.at[st, p, q], partner)

    def ag_start(buf, r, st):
        for p, q in ((by_x, 0), (by_y, 1), (by_x, 1), (by_y, 0)):
            ag_direct(buf, r, st, p, q).start()
        ag_home(buf, r, st).start()

    def ag_got(buf, r, st, p, q):
        (ag_relay(buf, r, st, q) if p == by_both else ag_direct(buf, r, st, p, q)).wait_recv()
        ag_forward(buf, r, st, p, q).start()

    def ag_near(buf, r, st):
        for p, q in ((by_x, 0), (by_y, 1)):
            ag_got(buf, r, st, p, q)
            ag_relay(buf, r, st, q).start()
        for p, q in ((by_y, 0), (by_x, 1)):
            ag_got(buf, r, st, p, q)

    def ag_far(buf, r, st):
        for q in (0, 1):
            ag_got(buf, r, st, by_both, q)

    def ag_have(buf, r, st, p):
        if p == 0:
            ag_home(buf, r, st).wait_recv()
        else:
            for q in (0, 1):
                ag_forward(buf, r, st, p, q).wait_recv()

    def ag_wait(buf, r, p, between=lambda st: None):
        for st in (0, 1):
            if p == by_y:
                ag_near(buf, r, st)
                between(st)
            if p == by_x:
                ag_far(buf, r, st)
        for st in (0, 1):
            ag_have(buf, r, st, p)

    def ag_finish(buf, r):
        all_of(buf.at[seven], R.ag_s.at[r], R.ag_r.at[0, 0, 0]).wait_send()

    def pair(buf, p):
        a, b = dev(p, 0)[1], dev(p, 1)[1]
        return a, b, jnp.concatenate([buf[a], buf[b]], 0)

    def half_pair(buf, p, st):
        a, b = dev(p, 0)[1], dev(p, 1)[1]
        return a, b, jnp.concatenate([buf[a, half[st]], buf[b, half[st]]], 0)

    def rs_chip(r, st, p):
        return rcopy(
            R.snd_c.at[p, half[st]], R.rcv_c.at[r, p, half[st]], R.rs_s.at[0], R.rs_cr.at[st, p], partner
        )

    def rs_link(r, st, p, q):
        over = p if p != by_both else (by_x, by_y)[q]
        to, _ = dev(c32(over), 0)
        return rcopy(
            R.snd_l.at[p, piece(st, q)], R.rcv_l.at[r, p, piece(st, q)], R.rs_s.at[1], R.rs_lr.at[st, p, q], to
        )

    def rs_put(r, st, p, same, other):
        R.snd_c[p, half[st]] = other.astype(BF)
        rs_chip(r, st, p).start()
        R.keep[p, half[st]] = same

    def rs_put_pair(r, p, part):
        for st in (0, 1):
            at = st * (T // 2)
            rs_put(r, st, p, part[at:at + T // 2], part[T + at:T + at + T // 2])

    def rs_combine(r, st, p):
        rs_chip(r, st, p).wait_recv()
        both = R.keep[p, half[st]] + R.rcv_c[r, p, half[st]].astype(F32)
        R.keep[p, half[st]] = both
        R.snd_l[p, half[st]] = both.astype(BF)
        for target, parts in ((by_y, (1,)), (by_x, (0,)), (by_both, (0, 1))):
            @when(p == target)
            def _():
                for q in parts:
                    rs_link(r, st, target, q).start()

    def rs_combine_pair(r, p):
        rs_combine(r, 0, p)
        rs_combine(r, 1, p)

    def rs_relay(r, st):
        for p, q in ((by_y, 0), (by_x, 1)):
            rs_link(r, st, by_both, q).wait_recv()
            rows_q = piece(st, q)
            R.snd_l[p, rows_q] = (R.keep[p, rows_q] + R.rcv_l[r, by_both, rows_q].astype(F32)).astype(BF)
            rs_link(r, st, p, q).start()

    def rs_final(r, st):
        rs_chip(r, st, c32(0)).wait_recv()
        acc = R.keep[0, half[st]] + R.rcv_c[r, 0, half[st]].astype(F32)
        for p in (by_y, by_x):
            for q in (0, 1):
                rs_link(r, st, p, q).wait_recv()
            acc = acc + R.rcv_l[r, p, half[st]].astype(F32)
        if st == 1:
            all_of(R.snd_c, R.rs_s.at[0], R.rs_cr.at[0, 0]).wait_send()
            all_of(R.snd_l.at[pl.ds(1, 3)], R.rs_s.at[1], R.rs_cr.at[0, 0]).wait_send()
        return acc

    def rs_whole(r):
        return jnp.concatenate([rs_final(r, 0), rs_final(r, 1)], 0)

    first = ((0, T // 8), (T // 8, T // 8), (T // 4, T // 4), (T // 2, T // 2))
    chunks = [("b", lambda x, i=i, n=n: x.at[0, pl.ds(i, n)], n) for i, n in first]
    chunks += [("b", lambda x, i=i, h=h: x.at[i, h], T // 2) for i in range(1, 4) for h in half]
    chunks += [("i", lambda x, t=t: x.at[t], T // 2) for t in range(8)]
    chunks += [("o", lambda x, h=h: x.at[h], T // 2) for h in half] + [("s", lambda x: x, 1)]
    chunks += [("w", lambda x, t=t: x.at[t], 3 * T // 8) for t in range(7)]
    chunks += [("w", lambda x, h=h: x.at[7, h], 3 * T // 16) for h in half]
    Z_IN, Z_OUT, Z_SMALL, Z_QKV, Z_ALL = 10, 18, 20, 21, len(chunks)

    def zrefs(c):
        k, cut, _ = chunks[c]
        return cut(getattr(R, "zown_" + k)), cut(getattr(R, "zsum_" + k)), cut(getattr(R, "zmid_" + k))

    kinds = "biosw"

    def z_sem(c, way):
        return R.z_s.at[kinds.index(chunks[c][0]), way]

    def z_up(c):
        own, tot, _ = zrefs(c)
        return rcopy(own, tot, z_sem(c, 0), R.z_r.at[c, 0], (z_other, blk, head))

    def z_across(c):
        own, _, mid = zrefs(c)
        return rcopy(own, mid, z_sem(c, 0), R.z_r.at[c, 1], (z_mid, blk, head))

    def z_down(c):
        _, tot, _ = zrefs(c)
        return rcopy(tot, tot, z_sem(c, 1), R.z_r.at[c, 0], (z_other, blk, head))

    row_us, hop_us = 0.0432, 2.0
    steps, sent = [], 0.0
    for c, (_, _, n) in enumerate(chunks):
        sent += n * row_us
        steps += [(sent + hop_us, c, 0), (sent + n * row_us + 2.2 * hop_us, c, 1)]
    steps.sort()
    made = set()

    def z_until(us):
        while steps and steps[0][0] <= us and steps[0][1] in made:
            _, c, second = steps.pop(0)
            (z_two if second else z_one)(c)

    def z_produce(c):
        made.add(c)

        @pl.when(z_end)
        def _():
            z_up(c).start()

    def z_one(c):
        @pl.when(jnp.logical_not(z_end))
        def _():
            own, tot, _ = zrefs(c)
            z_up(c).wait_recv()
            own[...] = (own[...].astype(F32) + tot[...].astype(F32)).astype(BF)
            z_across(c).start()

    def z_two(c):
        @pl.when(jnp.logical_not(z_end))
        def _():
            own, tot, mid = zrefs(c)
            z_across(c).wait_recv()
            tot[...] = (own[...].astype(F32) + mid[...].astype(F32)).astype(BF)
            z_down(c).start()

    def z_finish(c):
        @pl.when(z_end)
        def _():
            if not Z_IN <= c < Z_OUT:
                z_down(c).wait_recv()

    def z_sent():
        for i, k in enumerate(kinds):
            own, tot = getattr(R, "zown_" + k), getattr(R, "zsum_" + k)
            all_of(own, R.z_s.at[i, 0], R.z_r.at[0, 0]).wait_send()

            @pl.when(jnp.logical_not(z_end))
            def _():
                all_of(tot, R.z_s.at[i, 1], R.z_r.at[0, 0]).wait_send()

    def vec_copy(e):
        to, _ = dev(c32(e // 2), e % 2)
        return rcopy(R.vec, R.vec_all.at[me], R.vec_s.at[0], R.vec_s.at[1], to)

    def qkv_copy(e, j, part, sems):
        to, at = dev(c32(e // 2), e % 2)
        w = (R.wq, R.wk, R.wv)[j]
        return rcopy(w.at[part, lanes(at, W)], R.wqkv.at[me, part, pl.ds(j * W, W)], sems.at[0], sems.at[1], to)

    def win_copy(e, part, sems):
        to, at = dev(c32(e // 2), e % 2)
        return rcopy(R.wi.at[part, lanes(at, FW)], R.win.at[me, part], sems.at[0], sems.at[1], to)

    def along(i, k, way):
        sign = 1 if way == 0 else -1
        q, to = dp - sign * k, dp + sign
        part = (R.wqkv, R.win)[i].at[:, share(q)]
        return rcopy(part, part, R.along_s.at[i, way, k], R.along_r.at[i, way, k], (to, blk, head))

    def along_do(i, k, act):
        for way, sends, gets in (
            (0, (dp <= 2) & (dp >= k), dp >= k + 1),
            (1, (dp >= 1) & (dp + k <= 3), dp + k <= 2),
        ):
            @pl.when(gets if act == 1 else sends)
            def _():
                step = along(i, k, way)
                (step.start, step.wait_recv, step.wait_send)[act]()

    def along_send(i, k):
        along_do(i, k, 0)

    def along_got(i, k):
        along_do(i, k, 1)

    def along_sent(i):
        for k in range(3):
            along_do(i, k, 2)

    far_first = (6, 7, 2, 3, 4, 5, 1)
    with jax.named_scope("start_copies"):
        for part, sems in ((share(dp), R.qshare_s), (half[0], R.qkv_s)):
            for e in far_first:
                for j in range(3):
                    qkv_copy(e, j, part, sems).start()
        local[0].wait()
        for st in (0, 1):
            ag_start(tok_all, 0, st)
        for cp in small:
            cp.wait()
        vecs = [x[...].astype(F32).reshape(1, T) for x in small_v[1:7]]
        vecs.append(R.ids_v[0:1, lanes(head, T)].astype(F32))
        R.vec[...] = jnp.concatenate(vecs + [jnp.zeros((1, T), F32)], 0)
        R.vec_all[me] = R.vec[...]
        for e in far_first:
            vec_copy(e).start()

    with jax.named_scope("wait_qkv_weights"):
        own = R.wqkv.at[me, pl.ds(0, T // 8)]
        pltpu.make_async_copy(own, own, R.loc.at[7]).wait()
        all_of(R.wqkv.at[seven, pl.ds(0, T // 8)], R.qshare_s.at[0], R.qshare_s.at[1]).wait()
        along_send(0, 0)
        along_got(0, 0)
        along_send(0, 1)
        ag_near(tok_all, 0, 0)
        along_got(0, 1)
        along_send(0, 2)
        ag_near(tok_all, 0, 1)
        ag_far(tok_all, 0, 0)
        for e in far_first:
            win_copy(e, share(dp), R.share_s).start()
        own = R.wqkv.at[me, half[0]]
        pltpu.make_async_copy(own, own, R.loc.at[5]).wait()
        all_of(R.wqkv.at[seven, half[0]], R.qkv_s.at[0], R.qkv_s.at[1]).wait()
        along_got(0, 2)
        along_sent(0)

    def qkv_step(p):
        if p == by_x:
            ag_far(tok_all, 0, 1)
            for e in far_first:
                win_copy(e, half[0], R.win_s).start()
        for st in (0, 1):
            ag_have(tok_all, 0, st, p)
        a, b, x = pair(tok_all, c32(p))
        y = mm(x, rows(R.wqkv), NN)
        qq = ((y[:, :W] + R.bq_v[...].astype(F32).reshape(1, W)) * 0.125).astype(BF)
        kk = y[:, W:2 * W].astype(BF)
        vv = (y[:, 2 * W:] + R.bv_v[...].astype(F32).reshape(1, W)).astype(BF)
        for at, sl in ((a, slice(0, T)), (b, slice(T, 2 * T))):
            R.q[at], R.k[at], R.v[at] = qq[sl], kk[sl], vv[sl]

    with jax.named_scope("project_qkv"):
        for p in range(4):
            qkv_step(p)

    with jax.named_scope("vectors"):
        all_of(R.vec_all.at[seven], R.vec_s.at[0], R.vec_s.at[1]).wait_recv()
        for s in range(8):
            v = R.vec_all[s]
            R.vfull[:, s * T:(s + 1) * T] = v
            ids = jnp.broadcast_to(v[6:7], (T, T)).T
            R.segk[s] = jnp.where(ids < 0, -2.0, ids)

    for i in (1, 2, 3, 4):
        local[i].wait()

    def head_mask(h, like):
        lane = lax.broadcasted_iota(jnp.int32, like.shape, 1)
        return jnp.where(lax.div(lane, HD) == h, like, jnp.zeros_like(like))

    heads = W // HD

    far, near_a, near_b, here = [
        [(0, by_both), (1, by_both)], [(0, by_y), (0, by_x)], [(1, by_y), (1, by_x)], [(0, 0), (1, 0)],
    ]

    def rows_of(buf, items):
        found = [half_pair(buf, c32(p), st) for st, p in items]
        return [(a, b) for a, b, _ in found], jnp.concatenate([x for _, _, x in found], 0)

    def put_rows(buf, items, places, value, lane=slice(None)):
        for i, ((st, _), (a, b)) in enumerate(zip(items, places, strict=True)):
            buf[a, half[st], lane] = value[i * T:i * T + T // 2]
            buf[b, half[st], lane] = value[i * T + T // 2:(i + 1) * T]

    def put_parts(r, items, part):
        for i, (st, p) in enumerate(items):
            rs_put(r, st, p, part[i * T:i * T + T // 2], part[i * T + T // 2:(i + 1) * T])

    def ids_of(items, places):
        return jnp.concatenate(
            [
                R.vec_all[at, 6:7, st * (T // 2):(st + 1) * (T // 2)]
                for (st, _), both in zip(items, places, strict=True)
                for at in both
            ],
            1,
        )

    def attend_step(slot, items, between):
        places, qp = rows_of(R.q, items)
        segq = ids_of(items, places)
        segk = rows(R.segk)
        allowed = jnp.concatenate([segk, segk], 1) == segq
        kk = rows(R.k)
        outs = []
        scores = [mm(kk, head_mask(h, qp), NT) for h in range(heads)]
        for h in range(heads):
            s = jnp.where(allowed, scores[h], -1e30)
            ex = jnp.exp(s - jnp.max(s, 0, keepdims=True))
            total = jnp.maximum(jnp.sum(ex, 0, keepdims=True), 1.0)
            pt = (ex * jnp.where(segq >= 0, 1.0 / total, 0.0)).astype(BF)
            R.pt[h, slot] = pt
            outs.append(mm(R.vt[h * HD:(h + 1) * HD, :], pt, NN))
            if h == 0:
                between()
        ct = jnp.concatenate(outs, 0).T.astype(BF)
        put_rows(R.ctx, items, places, ct)
        put_parts(0, items, mm(ct, R.wo_v[...], NN))

    def after_far():
        local_share.wait()
        all_of(R.win.at[seven, pl.ds(0, T // 8)], R.share_s.at[0], R.share_s.at[1]).wait()
        along_send(1, 0)

    def after_near_a():
        rs_combine_pair(0, by_both)

    def after_near_b():
        rs_combine(0, 0, by_y)
        rs_combine(0, 0, by_x)
        along_got(1, 0)
        along_send(1, 1)

    def after_here():
        rs_combine(0, 1, by_y)
        rs_combine(0, 1, by_x)
        rs_relay(0, 1)

    with jax.named_scope("attend"):
        R.vt[...] = rows(R.v).T
        attend_step(0, far, after_far)
        attend_step(1, near_a, after_near_a)
        attend_step(2, near_b, after_near_b)
        rs_relay(0, 0)
        attend_step(3, here, after_here)
        along_got(1, 1)
        along_send(1, 2)

    with jax.named_scope("first_norm"):
        for st in (0, 1):
            rs = rs_final(0, st)
            h1 = tok_all[me, half[st]].astype(F32) + rs + R.vfull[0:1]
            n1, r1 = norm_parts(h1)
            y1 = n1 * R.vfull[2:3] + R.vfull[3:4]
            R.n1[half[st]], R.y1[half[st]] = n1, y1
            R.r1[half[st]] = jnp.broadcast_to(r1, (T // 2, 128))
            y1_all[me, half[st]] = y1.astype(BF)
            ag_start(y1_all, 1, st)
    R.kt[...] = rows(R.k).T

    with jax.named_scope("wait_hidden_weights"):
        all_of(R.win.at[seven, half[0]], R.win_s.at[0], R.win_s.at[1]).wait()
        along_got(1, 2)
        along_sent(1)

    def hidden_step(items):
        places, x = rows_of(y1_all, items)
        z = mm(x, rows(R.win), NN) + R.bi_v[...].astype(F32).reshape(1, FW)
        cdf = 0.5 * (1.0 + lax.erf(z * 0.7071067811865476))
        low = (z * cdf).astype(BF)
        slope = cdf + z * (jnp.exp(-0.5 * z * z) * 0.3989422804014327)
        put_parts(1, items, mm(low, R.wb_v[...], NN))
        put_rows(R.hid, items, places, low)
        put_rows(R.slope, items, places, slope)

    with jax.named_scope("hidden"):
        ag_near(y1_all, 1, 0)
        for st in (0, 1):
            ag_have(y1_all, 1, st, 0)
        hidden_step(here)
        for p in (by_y, by_x):
            ag_have(y1_all, 1, 0, p)
        hidden_step(near_a)
        ag_near(y1_all, 1, 1)
        ag_far(y1_all, 1, 0)
        for p in (by_y, by_x):
            ag_have(y1_all, 1, 1, p)
            rs_combine(1, 0, p)
        hidden_step(near_b)
        ag_far(y1_all, 1, 1)
        ag_have(y1_all, 1, 0, by_both)
        hidden_step(far[:1])
        for p in (by_y, by_x):
            rs_combine(1, 1, p)
        ag_have(y1_all, 1, 1, by_both)
        rs_combine(1, 0, by_both)
        hidden_step(far[1:])
        rs_combine(1, 1, by_both)

    with jax.named_scope("second_norm"):
        rs_relay(1, 0)
        rs_relay(1, 1)
        for st in (0, 1):
            rs = rs_final(1, st)
            h2 = R.y1[half[st]] + rs + R.vfull[1:2]
            n2, r2 = norm_parts(h2)
            gain = R.vfull[4:5]
            R.out_v[half[st]] = (n2 * gain + R.vfull[5:6]).astype(BF)
            cot = R.cot_v[half[st]].astype(F32)
            dh2 = norm_back(cot * gain, n2, r2)
            R.dh2[half[st]] = dh2
            df_all[me, half[st]] = dh2.astype(BF)
            ag_start(df_all, 2, st)
            sums = jnp.concatenate([colsum(cot * n2), colsum(cot)], 0)
            R.sv[0:2, :] = sums if st == 0 else R.sv[0:2, :] + sums
        put_out.start()

    def grad_back(i):
        x = R.hid[:, :, i * T:(i + 1) * T].reshape(8 * T, T)
        R.zown_b[i] = mm(x, rows(df_all), TN).astype(BF)
        for c in range(4) if i == 0 else (2 * i + 2, 2 * i + 3):
            z_produce(c)

    def hidden_back_step(p):
        ag_wait(df_all, 2, p)
        if p == by_both:
            grad_back(0)
        a, b, x = pair(df_all, c32(p))
        slope = jnp.concatenate([R.slope[a], R.slope[b]], 0)
        dz = (mm(x, R.wb_v[...], NT) * slope).astype(BF)
        R.dz[a], R.dz[b] = dz[:T], dz[T:]
        if p > 1:
            rs_combine_pair(2, p - 1)
        rs_put_pair(2, p, mm(dz, rows(R.win), NT))

    with jax.named_scope("hidden_back"):
        for p in range(4):
            hidden_back_step(p)
        z_until(2.8)
        rs_combine_pair(2, 3)
        z_until(3.5)

    with jax.named_scope("grad_back"):
        for i in range(1, 4):
            grad_back(i)
        z_until(7.5)
        rs_relay(2, 0)
        z_until(8.6)
        rs_relay(2, 1)
        z_until(9.8)

    def grad_in(i):
        x = y1_all[:, :, 2 * i * T:(2 * i + 2) * T].reshape(8 * T, 2 * T)
        g = mm(x, rows(R.dz), TN).astype(BF)
        R.zown_i[2 * i], R.zown_i[2 * i + 1] = g[:T], g[T:]
        z_produce(Z_IN + 2 * i)
        z_produce(Z_IN + 2 * i + 1)

    def din_copy(t, s):
        return rcopy(R.zsum_i.at[t], R.grad_i.at[s], R.din_s.at[0], R.din_s.at[1], (dp, t // 2, t % 2))

    def z_deliver(t):
        @pl.when(z_end)
        def _():
            z_down(Z_IN + t).wait_recv()

        @pl.when(me != t)
        def _():
            din_copy(t, me).start()

        @pl.when(me == t)
        def _():
            R.grad_i[me] = R.zsum_i[t]

    with jax.named_scope("grad_in"):
        for i in range(4):
            grad_in(i)
            if i % 2:
                z_until(10.0 + i)

    with jax.named_scope("first_norm_back"):
        rs = rs_whole(2)
        dy1 = R.dh2[...] + rs
        n1 = R.n1[...]
        dh1 = norm_back(dy1 * R.vfull[2:3], n1, R.r1[:, 0:1])
        R.dh1[...] = dh1
        da_all[me] = dh1.astype(BF)
        for st in (0, 1):
            ag_start(da_all, 3, st)
        R.sv[2:3, :] = colsum(dy1 * n1)
        R.sv[3:4, :] = colsum(dy1)

    def sv_copy(e):
        to, at = dev(c32(e // 2), e % 2)
        return rcopy(R.sv.at[:, lanes(at, T)], R.sv_rcv.at[me], R.sv_s.at[0], R.sv_s.at[1], to)

    for e in far_first:
        sv_copy(e).start()
    R.sv_rcv[me] = R.sv[:, lanes(me, T)]

    z_until(13.8)

    R.dk[...] = jnp.zeros_like(R.dk)
    R.dv[...] = jnp.zeros_like(R.dv)

    def attend_back_step(slot, items, times):
        z_until(times[0])
        places, x = rows_of(da_all, items)
        _, qp = rows_of(R.q, items)
        dc = mm(x, R.wo_v[...], NT).astype(BF)
        vv = rows(R.v)
        outs = []
        for h in range(heads):
            dcm, qm = head_mask(h, dc), head_mask(h, qp)
            low = R.pt[h, slot]
            pt = low.astype(F32)
            dpt = mm(vv, dcm, NT)
            ds = (pt * (dpt - jnp.sum(pt * dpt, 0, keepdims=True))).astype(BF)
            outs.append(mm(R.kt[h * HD:(h + 1) * HD, :], ds, NN))
            R.dk[...] += mm(ds, qm, NN)
            R.dv[...] += mm(low, dcm, NN)
            z_until(times[1 + h])
        dq = jnp.concatenate(outs, 0).T.astype(BF) * 0.125
        put_rows(R.dqkv, items, places, dq, slice(0, W))

    with jax.named_scope("attend_back"):
        for st in (0, 1):
            ag_have(da_all, 3, st, 0)
        attend_back_step(3, here, (14.6, 16.0, 17.2))
        for st, slot, items, times in ((0, 1, near_a, (20.2, 21.4, 22.6)), (1, 2, near_b, (24.6, 25.8, 27.0))):
            ag_near(da_all, 3, st)
            z_until((18.0, 23.4)[st])
            if st == 1:
                ag_far(da_all, 3, 0)
            for p in (by_y, by_x):
                ag_have(da_all, 3, st, p)
            attend_back_step(slot, items, times)
        ag_far(da_all, 3, 1)
        for st in (0, 1):
            ag_have(da_all, 3, st, by_both)
        attend_back_step(0, far, (28.0, 29.2, 30.4))
        R.dqkv[:, :, W:2 * W] = R.dk[...].astype(BF).reshape(8, T, W)
        R.dqkv[:, :, 2 * W:] = R.dv[...].astype(BF).reshape(8, T, W)

    def dqkv_copy(p, flip):
        to, at = dev(p, flip)
        return rcopy(R.dqkv_snd.at[at], R.zown_w.at[me], R.dqkv_s.at[0], R.dqkv_s.at[1], to)

    def dqkv_step(p):
        a, b = dev(c32(p), 0)[1], dev(c32(p), 1)[1]
        x = jnp.concatenate([tok_all[:, :, lanes(a, T)], tok_all[:, :, lanes(b, T)]], 2).reshape(8 * T, 2 * T)
        g = mm(x, rows(R.dqkv), TN).astype(BF)
        R.dqkv_snd[b] = g[T:]
        dqkv_copy(c32(p), 1).start()
        if p == 0:
            R.zown_w[me] = g[:T]
        else:
            R.dqkv_snd[a] = g[:T]
            dqkv_copy(c32(p), 0).start()
        z_until(30.5 + 0.5 * p)

    with jax.named_scope("grad_qkv"):
        for p in range(4):
            dqkv_step(p)

    with jax.named_scope("grad_out"):
        R.zown_o[...] = mm(rows(R.ctx), rows(da_all), TN).astype(BF)
        z_produce(Z_OUT)
        z_produce(Z_OUT + 1)
        z_until(33.0)

    def input_step(p):
        if p > 1:
            rs_combine_pair(3, p - 1)
        a, b, x = pair(R.dqkv, c32(p))
        rs_put_pair(3, p, mm(x, rows(R.wqkv), NT))
        z_until((33.5, 34.0, 35.5, 37.0)[p])

    with jax.named_scope("input_back"):
        for p in range(4):
            input_step(p)
        rs_combine_pair(3, 3)
        z_until(39.0)

    with jax.named_scope("small_grads"):
        all_of(R.sv_rcv.at[seven], R.sv_s.at[0], R.sv_s.at[1]).wait_recv()
        acc = R.sv_rcv[0]
        for s in range(1, 8):
            acc = acc + R.sv_rcv[s]
        own = lanes(me, T)
        parts = [
            acc[0:4],
            colsum(rows(R.dqkv)[:, 0:W]),
            colsum(rows(R.dqkv)[:, 2 * W:]),
            colsum(da_all[:, :, own].reshape(8 * T, T)),
            colsum(df_all[:, :, own].reshape(8 * T, T)),
        ]
        dbi = colsum(rows(R.dz))
        parts += [dbi[:, i * T:(i + 1) * T] for i in range(FW // T)]
        parts.append(jnp.zeros((16 - 8 - FW // T, T), F32))
        R.zown_s[...] = jnp.concatenate(parts, 0).astype(BF)
        z_produce(Z_SMALL)
        z_until(41.0)

    with jax.named_scope("z_rest"):
        all_of(R.zown_w.at[seven], R.dqkv_s.at[0], R.dqkv_s.at[1]).wait_recv()
        for c in range(Z_QKV, Z_ALL):
            z_produce(c)
        z_until(44.5)
        rs_relay(3, 0)
        z_until(47.0)
        rs_relay(3, 1)
        z_until(50.0)
    with jax.named_scope("input_grad"):
        R.igrad_v[...] = R.dh1[...] + rs_whole(3)
        put_igrad.start()
    puts = [put_out, put_igrad]

    def put(i, src, dst):
        puts.append(pltpu.make_async_copy(src, dst, R.put_s.at[i]))
        puts[-1].start()

    def z_through(c):
        while any(second and at <= c for _, at, second in steps):
            z_until(steps[0][0])
        z_finish(c)

    with jax.named_scope("z_last"):
        for t in range(8):
            z_until(51.0 + 2 * t)
            z_deliver(t)
            if t == 1:
                for c in range(Z_IN):
                    z_through(c)
                put(2, R.zsum_b, R.gb)
        for c in range(Z_OUT, Z_QKV):
            z_through(c)
        put(4, R.zsum_o, R.go)
        put(5, R.zsum_s, R.gs)
        for t in range(7):
            z_through(Z_QKV + t)
            put(6 + t, R.zsum_w.at[t], R.gw.at[t])
        all_of(R.grad_i.at[seven], R.din_s.at[0], R.din_s.at[1]).wait()
        put(3, R.grad_i, R.gi)
        for c in (Z_ALL - 2, Z_ALL - 1):
            z_through(c)
        put(13, R.zsum_w.at[7], R.gw.at[7])

    with jax.named_scope("finish"):
        z_sent()
        for buf, r in ((tok_all, 0), (y1_all, 1), (df_all, 2), (da_all, 3)):
            ag_finish(buf, r)
        for ref, sem in (
            (R.vec_all, R.vec_s), (R.sv_rcv, R.sv_s), (R.zown_w, R.dqkv_s),
        ):
            all_of(ref.at[seven], sem.at[0], sem.at[1]).wait_send()
        for cp in puts:
            cp.wait()


def sharded_plan(
    tokens, segment_ids, cotangent,
    w_query, w_key, w_value, w_out, w_in, w_back,
    bias_query, bias_value, bias_out, bias_in, bias_back,
    first_gain, first_shift, second_gain, second_shift,
):
    tokens, cotangent = tokens[0], cotangent[0]
    T, D = tokens.shape
    W, FW = D // 8, w_in.shape[1] // 8
    ins = dict(
        tok=tokens, cot=cotangent, wq=w_query, wk=w_key, wv=w_value, wo=w_out, wi=w_in, wb=w_back, ids=segment_ids,
        bo=bias_out, bb=bias_back, g1=first_gain, s1=first_shift, g2=second_gain, s2=second_shift,
        bq=bias_query, bv=bias_value, bi=bias_in,
    )
    in_hbm = 8
    outs = dict(
        out=((T, D), BF), igrad=((T, D), F32), gb=((4, T, D), BF), gi=((8, T, FW), BF), go=((T, D), BF),
        gw=((8, T, 3 * W), BF), gs=((16, T), BF),
    )
    sums = dict(b=outs["gb"], i=outs["gi"], o=outs["go"], w=outs["gw"], s=outs["gs"])
    blocks = {k: ((8, T, D), BF) for k in ("tok_all", "y1_all", "df_all", "da_all")}
    scr = dict(
        **blocks,
        wqkv=((8, T, 3 * W), BF), win=((8, T, FW), BF), wb_v=(w_back.shape, BF), wo_v=(w_out.shape, BF),
        cot_v=((T, D), BF), vec=((8, T), F32), vec_all=((8, 8, T), F32), vfull=((8, D), F32), segk=((8, T, T), F32),
        q=((8, T, W), BF), k=((8, T, W), BF), v=((8, T, W), BF), vt=((W, 8 * T), BF), kt=((W, 8 * T), BF),
        pt=((W // HD, 4, 8 * T, 2 * T), BF), ctx=((8, T, W), BF),
        hid=((8, T, FW), BF), slope=((8, T, FW), F32), dz=((8, T, FW), BF),
        n1=((T, D), F32), r1=((T, 128), F32), y1=((T, D), F32), dh2=((T, D), F32), dh1=((T, D), F32),
        sv=((8, D), F32), sv_rcv=((8, 8, T), F32),
        keep=((4, T, D), F32), snd_c=((4, T, D), BF), snd_l=((4, T, D), BF),
        rcv_c=((4, 4, T, D), BF), rcv_l=((4, 4, T, D), BF),
        dk=((8 * T, W), F32), dv=((8 * T, W), F32), dqkv=((8, T, 3 * W), BF),
        dqkv_snd=((8, T, 3 * W), BF),
        **{z + k: v for z in ("zown_", "zsum_", "zmid_") for k, v in sums.items()}, grad_i=outs["gi"],
        out_v=outs["out"], igrad_v=outs["igrad"],
        **{k + "_v": (v.shape, v.dtype) for k, v in list(ins.items())[in_hbm:]},
    )
    sems = dict(
        ag_s=(4,), ag_r=(2, 4, 2), ag_f=(2, 4, 2), rs_s=(2,), rs_cr=(2, 4), rs_lr=(2, 4, 2),
        z_s=(5, 2), z_r=(30, 2), loc=(8,), small_s=(10,), put_s=(14,), vec_s=(2,), qkv_s=(2,), win_s=(2,), share_s=(2,), qshare_s=(2,), along_s=(2, 2, 3), along_r=(2, 2, 3), sv_s=(2,), din_s=(2,), dqkv_s=(2,),
    )
    names = list(ins) + list(outs) + list(scr) + list(sems)
    res = pl.pallas_call(
        partial(layer_kernel, names),
        out_shape=[jax.ShapeDtypeStruct(*s) for s in outs.values()],
        in_specs=[pl.BlockSpec(memory_space=pltpu.HBM)] * len(ins),
        out_specs=[pl.BlockSpec(memory_space=pltpu.HBM)] * len(outs),
        scratch_shapes=[pltpu.VMEM(*s) for s in scr.values()] + [pltpu.SemaphoreType.DMA(s) for s in sems.values()],
        compiler_params=pltpu.CompilerParams(collective_id=0, has_side_effects=True, vmem_limit_bytes=60 << 20),
        name="layer",
    )(*ins.values())
    firsts = [(T, D)] * 6 + [w_in.shape, w_back.shape]
    sizes = [T, T, T, FW, T, T, T, T, T]
    shapes = [(n, t) for n, t in zip(firsts, [BF] + [F32] * 7)] + [((n,), F32) for n in sizes]
    loaded = list(outs.values())
    stored = [((3, T, D), F32), ((T, D), F32), (w_in.shape, F32), (w_back.shape, F32)] + shapes[8:]
    final = pl.pallas_call(
        finish_kernel,
        out_shape=[jax.ShapeDtypeStruct(*s) for s in shapes],
        in_specs=[pl.BlockSpec(memory_space=pltpu.HBM)] * len(loaded),
        out_specs=[pl.BlockSpec(memory_space=pltpu.HBM)] * len(shapes),
        scratch_shapes=[pltpu.VMEM(*s) for s in loaded + stored]
        + [pltpu.SemaphoreType.DMA((len(loaded) + 4,)), pltpu.SemaphoreType.DMA((len(shapes) + 6,))],
        compiler_params=pltpu.CompilerParams(vmem_limit_bytes=60 << 20),
        name="finish",
    )(*res)
    return (final[0][None], final[1][None], *final[2:])


def finish_kernel(*refs):
    ins, outs, rest = refs[:7], refs[7:24], refs[24:]
    loaded, stored, (load_s, store_s) = rest[:7], rest[7:20], rest[20:]
    out, igrad, gb, gi, go, gw, gs = loaded
    qkv, o_o, o_i, o_b, *o_small = stored
    order = (3, 2, 5, 4, 1, 0, 6)
    loads = {i: pltpu.make_async_copy(ins[i], loaded[i], load_s.at[i]) for i in order}
    for i in order:
        loads[i].start()
    stores = []

    def store(src, dst):
        stores.append(pltpu.make_async_copy(src, dst, store_s.at[len(stores)]))
        stores[-1].start()

    width = gi.shape[2]
    loads[3].wait()
    for j in range(8):
        o_i[:, j * width:(j + 1) * width] = gi[j].astype(F32)
    store(o_i, outs[6])
    loads[2].wait()
    T = gb.shape[1]
    for j in range(4):
        o_b[j * T:(j + 1) * T, :] = gb[j].astype(F32)
    store(o_b, outs[7])
    loads[5].wait()
    W = gw.shape[2] // 3
    for j in range(3):
        for s in range(8):
            qkv[j, :, s * W:(s + 1) * W] = gw[s, :, j * W:(j + 1) * W].astype(F32)
        store(qkv.at[j], outs[2 + j])
    loads[4].wait()
    o_o[...] = go[...].astype(F32)
    store(o_o, outs[5])
    loads[1].wait()
    store(igrad, outs[1])
    loads[0].wait()
    store(out, outs[0])
    loads[6].wait()
    v = gs[...].astype(F32)
    bq, bv, bo, bi, bb, g1, s1, g2, s2 = o_small
    for o, i in ((bq, 4), (bv, 5), (bo, 6), (bb, 7), (g1, 2), (s1, 3), (g2, 0), (s2, 1)):
        o[...] = v[i]
    n = v.shape[1]
    for i in range(bi.shape[0] // n):
        bi[i * n:(i + 1) * n] = v[8 + i]
    for i, o in enumerate(o_small):
        store(o, outs[8 + i])
    for cp in stores:
        cp.wait()


def pick_plan(mesh):
    group = mesh.shape["blk"] * mesh.shape["head"]
    return sharded_plan if (mesh.shape["dp"], group) == (4, 8) else general_plan


def flat_dot(left_side, right_side):
    return jnp.dot(
        left_side.reshape(-1, left_side.shape[-1]), right_side, preferred_element_type=jnp.float32
    )


def inner_dot(left_side, right_side):
    return jnp.einsum(
        "ra,rb->ab",
        left_side.reshape(-1, left_side.shape[-1]),
        right_side.reshape(-1, right_side.shape[-1]),
        preferred_element_type=jnp.float32,
    )


def layer_norm(value_rows, gain_row, shift_row):
    centre = jnp.mean(value_rows, -1, keepdims=True)
    centred = value_rows - centre
    spread = jnp.mean(centred * centred, -1, keepdims=True)
    return centred * lax.rsqrt(spread + 1e-05) * gain_row + shift_row


def head_view(array_in):
    return array_in.reshape(array_in.shape[0], array_in.shape[1], -1, HD)


def allowed_pairs(query_ids, key_ids):
    same_doc = (query_ids[:, :, None] == key_ids[:, None, :]) & (key_ids[:, None, :] >= 0)
    return same_doc[:, None]


def forward_step(state_now, arrived, local_data):
    running_max, running_sum, weighted = state_now
    key_block, value_block, key_ids = arrived
    query_block, query_ids = local_data
    scores = jnp.einsum(
        "gqhd,gkhd->ghqk",
        head_view(query_block),
        head_view(key_block),
        preferred_element_type=jnp.float32,
    )
    allowed = allowed_pairs(query_ids, key_ids)
    masked = jnp.where(allowed, scores, -1e30)
    new_max = jnp.maximum(running_max, jnp.max(masked, -1))
    exponents = jnp.where(allowed, jnp.exp(masked - new_max[..., None]), 0.0)
    running_sum = jnp.sum(exponents, -1)
    weighted = jnp.einsum(
        "ghqk,gkhd->ghqd",
        exponents.astype(jnp.bfloat16),
        head_view(value_block),
        preferred_element_type=jnp.float32,
    )
    return (new_max, running_sum, weighted)


def probabilities(query_block, key_block, query_ids, key_ids, log_sums):
    scores = jnp.einsum(
        "gqhd,gkhd->ghqk",
        head_view(query_block),
        head_view(key_block),
        preferred_element_type=jnp.float32,
    )
    allowed = allowed_pairs(query_ids, key_ids)
    masked = jnp.where(allowed, scores, -1e30)
    return jnp.where(allowed, jnp.exp(masked - log_sums.transpose(0, 2, 1)[..., None]), 0.0)


def score_grads(weights_now, grad_block, value_block, deltas):
    grad_weights = jnp.einsum(
        "gqhd,gkhd->ghqk",
        head_view(grad_block),
        head_view(value_block),
        preferred_element_type=jnp.float32,
    )
    return (weights_now * (grad_weights - deltas.transpose(0, 2, 1)[..., None])).astype(
        jnp.bfloat16
    )


def heads_to_rows(array_in):
    return array_in.transpose(0, 2, 1, 3).reshape(array_in.shape[0], array_in.shape[2], -1)


def general_plan(
    tokens,
    segment_ids,
    cotangent,
    w_query,
    w_key,
    w_value,
    w_out,
    w_in,
    w_back,
    bias_query,
    bias_value,
    bias_out,
    bias_in,
    bias_back,
    first_gain,
    first_shift,
    second_gain,
    second_shift,
):
    (
        query_full,
        key_full,
        value_full,
        out_full,
        in_full,
        back_full,
        query_bias,
        value_bias,
        out_bias,
        in_bias,
        back_bias,
        gain_one,
        shift_one,
        gain_two,
        shift_two,
    ) = (
        lax.all_gather(w_query, GROUP, axis=0, tiled=True),
        lax.all_gather(w_key, GROUP, axis=0, tiled=True),
        lax.all_gather(w_value, GROUP, axis=0, tiled=True),
        lax.all_gather(w_out, GROUP, axis=0, tiled=True),
        lax.all_gather(w_in, GROUP, axis=0, tiled=True),
        lax.all_gather(w_back, GROUP, axis=0, tiled=True),
        lax.all_gather(bias_query, GROUP, axis=0, tiled=True),
        lax.all_gather(bias_value, GROUP, axis=0, tiled=True),
        lax.all_gather(bias_out, GROUP, axis=0, tiled=True),
        lax.all_gather(bias_in, GROUP, axis=0, tiled=True),
        lax.all_gather(bias_back, GROUP, axis=0, tiled=True),
        lax.all_gather(first_gain, GROUP, axis=0, tiled=True),
        lax.all_gather(first_shift, GROUP, axis=0, tiled=True),
        lax.all_gather(second_gain, GROUP, axis=0, tiled=True),
        lax.all_gather(second_shift, GROUP, axis=0, tiled=True),
    )
    query_bias = query_bias.astype(jnp.float32)
    value_bias = value_bias.astype(jnp.float32)
    out_bias = out_bias.astype(jnp.float32)
    in_bias = in_bias.astype(jnp.float32)
    back_bias = back_bias.astype(jnp.float32)
    gain_one = gain_one.astype(jnp.float32)
    shift_one = shift_one.astype(jnp.float32)
    gain_two = gain_two.astype(jnp.float32)
    shift_two = shift_two.astype(jnp.float32)
    seq_count = tokens.shape[0]
    query_tok = (
        ((flat_dot(tokens, query_full) + query_bias) * 0.125)
        .astype(jnp.bfloat16)
        .reshape(tokens.shape)
    )
    key_tok = flat_dot(tokens, key_full).astype(jnp.bfloat16).reshape(tokens.shape)
    value_tok = (
        (flat_dot(tokens, value_full) + value_bias).astype(jnp.bfloat16).reshape(tokens.shape)
    )
    query_heads, key_heads, value_heads = (
        lax.all_to_all(query_tok, "head", split_axis=2, concat_axis=1, tiled=True),
        lax.all_to_all(key_tok, "head", split_axis=2, concat_axis=1, tiled=True),
        lax.all_to_all(value_tok, "head", split_axis=2, concat_axis=1, tiled=True),
    )
    rows_here = query_heads.shape[1]
    width_heads = query_heads.shape[2]
    heads_here = width_heads // HD
    start_state = (
        jnp.full((seq_count, heads_here, rows_here), -1e30, jnp.float32),
        jnp.zeros((seq_count, heads_here, rows_here), jnp.float32),
        jnp.zeros((seq_count, heads_here, rows_here, HD), jnp.float32),
    )
    running_max, running_sum, weighted = forward_step(
        start_state,
        (
            lax.all_gather(key_heads, "blk", axis=1, tiled=True),
            lax.all_gather(value_heads, "blk", axis=1, tiled=True),
            lax.all_gather(segment_ids, "blk", axis=1, tiled=True),
        ),
        (query_heads, segment_ids),
    )
    floored = jnp.maximum(running_sum, 1.0)
    ctx_heads = heads_to_rows(weighted / floored[..., None])
    log_sums = (running_max + jnp.log(floored)).transpose(0, 2, 1)
    ctx_tok = lax.all_to_all(
        ctx_heads.astype(jnp.bfloat16), "head", split_axis=1, concat_axis=2, tiled=True
    )
    first_sum = tokens.astype(jnp.float32) + (flat_dot(ctx_tok, out_full) + out_bias).reshape(
        tokens.shape
    )
    first_norm = layer_norm(first_sum, gain_one, shift_one)
    first_low = first_norm.astype(jnp.bfloat16)
    inner_rows = flat_dot(first_low, in_full) + in_bias
    hidden_low = jax.nn.gelu(inner_rows, approximate=False).astype(jnp.bfloat16)
    second_sum = first_norm + (flat_dot(hidden_low, back_full) + back_bias).reshape(tokens.shape)
    output_now, second_pull = jax.vjp(layer_norm, second_sum, gain_two, shift_two)
    grad_second, grad_gain_two, grad_shift_two = second_pull(cotangent.astype(jnp.float32))
    grad_branch = grad_second.astype(jnp.bfloat16)
    grad_back_bias = jnp.sum(grad_branch.astype(jnp.float32), (0, 1))
    grad_back = inner_dot(hidden_low, grad_branch)
    grad_hidden = flat_dot(grad_branch, back_full.T)
    unused_value, gelu_pull = jax.vjp(partial(jax.nn.gelu, approximate=False), inner_rows)
    grad_inner = gelu_pull(grad_hidden)[0].astype(jnp.bfloat16)
    grad_in_bias = jnp.sum(grad_inner.astype(jnp.float32), 0)
    grad_in = inner_dot(first_low, grad_inner)
    grad_first_norm = grad_second + flat_dot(grad_inner, in_full.T).reshape(tokens.shape)
    unused_norm, first_pull = jax.vjp(layer_norm, first_sum, gain_one, shift_one)
    grad_first, grad_gain_one, grad_shift_one = first_pull(grad_first_norm)
    grad_attn = grad_first.astype(jnp.bfloat16)
    grad_out_bias = jnp.sum(grad_attn.astype(jnp.float32), (0, 1))
    grad_out = inner_dot(ctx_tok, grad_attn)
    grad_ctx_tok = flat_dot(grad_attn, out_full.T).astype(jnp.bfloat16).reshape(tokens.shape)
    grad_ctx = lax.all_to_all(grad_ctx_tok, "head", split_axis=2, concat_axis=1, tiled=True)
    deltas = jnp.sum(head_view(grad_ctx).astype(jnp.float32) * head_view(ctx_heads), -1)
    key_block = lax.all_gather(key_heads, "blk", axis=1, tiled=True)
    value_block = lax.all_gather(value_heads, "blk", axis=1, tiled=True)
    key_ids = lax.all_gather(segment_ids, "blk", axis=1, tiled=True)
    weights_now = probabilities(query_heads, key_block, segment_ids, key_ids, log_sums)
    dscores = score_grads(weights_now, grad_ctx, value_block, deltas)
    grad_query_heads = jnp.einsum(
        "ghqk,gkhd->ghqd", dscores, head_view(key_block), preferred_element_type=jnp.float32
    )
    key_part = jnp.einsum(
        "ghqk,gqhd->gkhd", dscores, head_view(query_heads), preferred_element_type=jnp.float32
    )
    value_part = jnp.einsum(
        "ghqk,gqhd->gkhd",
        weights_now.astype(jnp.bfloat16),
        head_view(grad_ctx),
        preferred_element_type=jnp.float32,
    )
    both_parts = jnp.concatenate(
        [
            key_part.reshape(key_part.shape[0], key_part.shape[1], -1),
            value_part.reshape(value_part.shape[0], value_part.shape[1], -1),
        ],
        2,
    )
    grad_query_heads, pair_grads = (grad_query_heads, both_parts)
    pair_home = lax.psum_scatter(
        pair_grads.astype(jnp.bfloat16), "blk", scatter_dimension=1, tiled=True
    ).astype(jnp.float32)
    grad_key_heads = pair_home[:, :, :width_heads].astype(jnp.bfloat16)
    grad_value_heads = pair_home[:, :, width_heads:].astype(jnp.bfloat16)
    grad_query_rows = heads_to_rows(grad_query_heads).astype(jnp.bfloat16)
    grad_query_tok, grad_key_tok, grad_value_tok = (
        lax.all_to_all(grad_query_rows, "head", split_axis=1, concat_axis=2, tiled=True),
        lax.all_to_all(grad_key_heads, "head", split_axis=1, concat_axis=2, tiled=True),
        lax.all_to_all(grad_value_heads, "head", split_axis=1, concat_axis=2, tiled=True),
    )
    grad_query_tok = grad_query_tok * 0.125
    grad_inputs = grad_first + (
        flat_dot(grad_query_tok, query_full.T)
        + flat_dot(grad_key_tok, key_full.T)
        + flat_dot(grad_value_tok, value_full.T)
    ).reshape(tokens.shape)
    (
        shard_wq,
        shard_wk,
        shard_wv,
        shard_wo,
        shard_wi,
        shard_wb,
        shard_bq,
        shard_bv,
        shard_bo,
        shard_bi,
        shard_bb,
        shard_g1,
        shard_s1,
        shard_g2,
        shard_s2,
    ) = (
        lax.psum_scatter(
            inner_dot(tokens, grad_query_tok), GROUP, scatter_dimension=0, tiled=True
        ),
        lax.psum_scatter(
            inner_dot(tokens, grad_key_tok), GROUP, scatter_dimension=0, tiled=True
        ),
        lax.psum_scatter(
            inner_dot(tokens, grad_value_tok), GROUP, scatter_dimension=0, tiled=True
        ),
        lax.psum_scatter(grad_out, GROUP, scatter_dimension=0, tiled=True),
        lax.psum_scatter(grad_in, GROUP, scatter_dimension=0, tiled=True),
        lax.psum_scatter(grad_back, GROUP, scatter_dimension=0, tiled=True),
        lax.psum_scatter(
            jnp.sum(grad_query_tok.astype(jnp.float32), (0, 1)),
            GROUP,
            scatter_dimension=0,
            tiled=True,
        ),
        lax.psum_scatter(
            jnp.sum(grad_value_tok.astype(jnp.float32), (0, 1)),
            GROUP,
            scatter_dimension=0,
            tiled=True,
        ),
        lax.psum_scatter(grad_out_bias, GROUP, scatter_dimension=0, tiled=True),
        lax.psum_scatter(grad_in_bias, GROUP, scatter_dimension=0, tiled=True),
        lax.psum_scatter(grad_back_bias, GROUP, scatter_dimension=0, tiled=True),
        lax.psum_scatter(grad_gain_one, GROUP, scatter_dimension=0, tiled=True),
        lax.psum_scatter(grad_shift_one, GROUP, scatter_dimension=0, tiled=True),
        lax.psum_scatter(grad_gain_two, GROUP, scatter_dimension=0, tiled=True),
        lax.psum_scatter(grad_shift_two, GROUP, scatter_dimension=0, tiled=True),
    )
    (
        total_wq,
        total_wk,
        total_wv,
        total_wo,
        total_wi,
        total_wb,
        total_bq,
        total_bv,
        total_bo,
        total_bi,
        total_bb,
        total_g1,
        total_s1,
        total_g2,
        total_s2,
    ) = (
        lax.psum(shard_wq.astype(jnp.bfloat16), "dp").astype(jnp.float32),
        lax.psum(shard_wk.astype(jnp.bfloat16), "dp").astype(jnp.float32),
        lax.psum(shard_wv.astype(jnp.bfloat16), "dp").astype(jnp.float32),
        lax.psum(shard_wo.astype(jnp.bfloat16), "dp").astype(jnp.float32),
        lax.psum(shard_wi.astype(jnp.bfloat16), "dp").astype(jnp.float32),
        lax.psum(shard_wb.astype(jnp.bfloat16), "dp").astype(jnp.float32),
        lax.psum(shard_bq.astype(jnp.bfloat16), "dp").astype(jnp.float32),
        lax.psum(shard_bv.astype(jnp.bfloat16), "dp").astype(jnp.float32),
        lax.psum(shard_bo.astype(jnp.bfloat16), "dp").astype(jnp.float32),
        lax.psum(shard_bi.astype(jnp.bfloat16), "dp").astype(jnp.float32),
        lax.psum(shard_bb.astype(jnp.bfloat16), "dp").astype(jnp.float32),
        lax.psum(shard_g1.astype(jnp.bfloat16), "dp").astype(jnp.float32),
        lax.psum(shard_s1.astype(jnp.bfloat16), "dp").astype(jnp.float32),
        lax.psum(shard_g2.astype(jnp.bfloat16), "dp").astype(jnp.float32),
        lax.psum(shard_s2.astype(jnp.bfloat16), "dp").astype(jnp.float32),
    )
    return (
        output_now.astype(jnp.bfloat16),
        grad_inputs,
        total_wq,
        total_wk,
        total_wv,
        total_wo,
        total_wi,
        total_wb,
        total_bq,
        total_bv,
        total_bo,
        total_bi,
        total_bb,
        total_g1,
        total_s1,
        total_g2,
        total_s2,
    )


def solution(mesh):
    in_specs = (
        P("dp", GROUP, None),
        P("dp", "blk"),
        P("dp", GROUP, None),
        P(GROUP, None),
        P(GROUP, None),
        P(GROUP, None),
        P(GROUP, None),
        P(GROUP, None),
        P(GROUP, None),
        P(GROUP),
        P(GROUP),
        P(GROUP),
        P(GROUP),
        P(GROUP),
        P(GROUP),
        P(GROUP),
        P(GROUP),
        P(GROUP),
    )
    out_specs = (
        P("dp", GROUP, None),
        P("dp", GROUP, None),
        P(GROUP, None),
        P(GROUP, None),
        P(GROUP, None),
        P(GROUP, None),
        P(GROUP, None),
        P(GROUP, None),
        P(GROUP),
        P(GROUP),
        P(GROUP),
        P(GROUP),
        P(GROUP),
        P(GROUP),
        P(GROUP),
        P(GROUP),
        P(GROUP),
    )
    plan = pick_plan(mesh)
    return jax.shard_map(
        plan, mesh=mesh, in_specs=in_specs, out_specs=out_specs, check_vma=False
    )
```

```python
from functools import partial
from types import SimpleNamespace

import jax
import jax.numpy as jnp
from jax import lax
from jax.experimental import pallas as pl
from jax.experimental.pallas import tpu as pltpu
from jax.sharding import PartitionSpec as P

HD = 64
BF = jnp.bfloat16
F32 = jnp.float32
GROUP = ("blk", "head")
MESH = pl.DeviceIdType.MESH
NN = ((1,), (0,))
NT = ((1,), (1,))
TN = ((0,), (0,))


def mm(a, b, dims):
    return lax.dot_general(a, b, (dims, ((), ())), preferred_element_type=F32)


def norm_parts(v):
    c = v - jnp.mean(v, -1, keepdims=True)
    r = lax.rsqrt(jnp.mean(c * c, -1, keepdims=True) + 1e-05)
    return c * r, r


def norm_back(e, n, r):
    return r * (e - jnp.mean(e, -1, keepdims=True) - n * jnp.mean(e * n, -1, keepdims=True))


def colsum(x):
    return jnp.sum(x.astype(F32), 0, keepdims=True)


def when(cond):
    if isinstance(cond, bool):
        return (lambda body: body()) if cond else (lambda body: None)
    return pl.when(cond)


def rows(ref):
    x = ref[...]
    return x.reshape(-1, x.shape[-1])


def layer_kernel(names, *refs):
    R = SimpleNamespace(**dict(zip(names, refs, strict=True)))
    dp, blk, head = [lax.axis_index(a) for a in ("dp", "blk", "head")]
    core, chip_x = lax.rem(blk, 2), lax.div(blk, 2)
    T, D = R.tok.shape
    W = R.q.shape[-1]
    FW = R.wi.shape[1] // 8

    def dev(p, flip):
        hh = lax.rem(head + lax.rem(p, 2), 2)
        bb = lax.rem(chip_x + lax.div(p, 2), 2) * 2 + lax.rem(core + flip, 2)
        return (dp, bb, hh), bb * 2 + hh

    def c32(i):
        return jnp.asarray(i, jnp.int32)

    me = blk * 2 + head
    partner, partner_at = dev(c32(0), 1)
    z_end = lax.rem(dp, 3) == 0
    z_other = jnp.where(dp == 0, 1, jnp.where(dp == 3, 2, jnp.where(dp == 1, 0, 3)))
    z_mid = jnp.where(dp == 1, 2, 1)

    def rcopy(src, dst, ssem, rsem, to):
        return pltpu.make_async_remote_copy(src, dst, ssem, rsem, device_id=to, device_id_type=MESH)

    def all_of(ref, ssem, rsem):
        return rcopy(ref, ref, ssem, rsem, partner)

    seven = pl.ds(0, 7)

    def lanes(i, w):
        return pl.ds(pl.multiple_of(i * w, w), w)

    tok_all, y1_all, df_all, da_all = R.tok_all, R.y1_all, R.df_all, R.da_all
    half = (pl.ds(0, T // 2), pl.ds(T // 2, T // 2))

    def share(z):
        return pl.ds(pl.multiple_of(T // 2 + z * (T // 8), T // 8), T // 8)

    small_in = (R.ids, R.bo, R.bb, R.g1, R.s1, R.g2, R.s2, R.bq, R.bv, R.bi)
    small_v = (R.ids_v, R.bo_v, R.bb_v, R.g1_v, R.s1_v, R.g2_v, R.s2_v, R.bq_v, R.bv_v, R.bi_v)
    local = [
        pltpu.make_async_copy(R.tok, tok_all.at[me], R.loc.at[0]),
        pltpu.make_async_copy(R.wb, R.wb_v, R.loc.at[1]),
        pltpu.make_async_copy(R.wo, R.wo_v, R.loc.at[2]),
        pltpu.make_async_copy(R.wi.at[half[0], lanes(me, FW)], R.win.at[me, half[0]], R.loc.at[3]),
        pltpu.make_async_copy(R.cot, R.cot_v, R.loc.at[4]),
    ]
    local_share = pltpu.make_async_copy(R.wi.at[share(dp), lanes(me, FW)], R.win.at[me, share(dp)], R.loc.at[6])
    local_share.start()
    for j, w in enumerate((R.wq, R.wk, R.wv)):
        for part, at in ((half[0], 5), (share(dp), 7)):
            local.append(
                pltpu.make_async_copy(w.at[part, lanes(me, W)], R.wqkv.at[me, part, pl.ds(j * W, W)], R.loc.at[at])
            )
    small = [
        pltpu.make_async_copy(x, y, R.small_s.at[i])
        for i, (x, y) in enumerate(zip(small_in, small_v, strict=True))
    ]
    for cp in local + small:
        cp.start()

    bar = pltpu.get_barrier_semaphore()
    for e in range(1, 8):
        to, _ = dev(c32(e // 2), e % 2)
        pl.semaphore_signal(bar, 1, device_id=to, device_id_type=MESH)
    for j in range(1, 4):
        pl.semaphore_signal(bar, 1, device_id=(lax.rem(dp + j, 4), blk, head), device_id_type=MESH)
    pl.semaphore_wait(bar, 10)

    put_out = pltpu.make_async_copy(R.out_v, R.out, R.put_s.at[0])
    put_igrad = pltpu.make_async_copy(R.igrad_v, R.igrad, R.put_s.at[1])

    by_y, by_x, by_both = 1, 2, 3

    def piece(st, q):
        return pl.ds((2 * st + q) * (T // 4), T // 4)

    def ag_direct(buf, r, st, p, q):
        to, _ = dev(c32(p), 0)
        part = buf.at[me, piece(st, q)]
        return rcopy(part, part, R.ag_s.at[r], R.ag_r.at[st, p, q], to)

    def ag_relay(buf, r, st, q):
        via, over = (by_x, by_y) if q == 0 else (by_y, by_x)
        _, at = dev(c32(via), 0)
        to, _ = dev(c32(over), 0)
        part = buf.at[at, piece(st, q)]
        return rcopy(part, part, R.ag_s.at[r], R.ag_r.at[st, by_both, q], to)

    def ag_home(buf, r, st):
        part = buf.at[me, half[st]]
        return rcopy(part, part, R.ag_s.at[r], R.ag_f.at[st, 0, 0], partner)

    def ag_forward(buf, r, st, p, q):
        _, at = dev(c32(p), 0)
        part = buf.at[at, piece(st, q)]
        return rcopy(part, part, R.ag_s.at[r], R.ag_f.at[st, p, q], partner)

    def ag_start(buf, r, st):
        for p, q in ((by_x, 0), (by_y, 1), (by_x, 1), (by_y, 0)):
            ag_direct(buf, r, st, p, q).start()
        ag_home(buf, r, st).start()

    def ag_got(buf, r, st, p, q):
        (ag_relay(buf, r, st, q) if p == by_both else ag_direct(buf, r, st, p, q)).wait_recv()
        ag_forward(buf, r, st, p, q).start()

    def ag_near(buf, r, st):
        for p, q in ((by_x, 0), (by_y, 1)):
            ag_got(buf, r, st, p, q)
            ag_relay(buf, r, st, q).start()
        for p, q in ((by_y, 0), (by_x, 1)):
            ag_got(buf, r, st, p, q)

    def ag_far(buf, r, st):
        for q in (0, 1):
            ag_got(buf, r, st, by_both, q)

    def ag_have(buf, r, st, p):
        if p == 0:
            ag_home(buf, r, st).wait_recv()
        else:
            for q in (0, 1):
                ag_forward(buf, r, st, p, q).wait_recv()

    def ag_wait(buf, r, p, between=lambda st: None):
        for st in (0, 1):
            if p == by_y:
                ag_near(buf, r, st)
                between(st)
            if p == by_x:
                ag_far(buf, r, st)
        for st in (0, 1):
            ag_have(buf, r, st, p)

    def ag_finish(buf, r):
        all_of(buf.at[seven], R.ag_s.at[r], R.ag_r.at[0, 0, 0]).wait_send()

    def pair(buf, p):
        a, b = dev(p, 0)[1], dev(p, 1)[1]
        return a, b, jnp.concatenate([buf[a], buf[b]], 0)

    def half_pair(buf, p, st):
        a, b = dev(p, 0)[1], dev(p, 1)[1]
        return a, b, jnp.concatenate([buf[a, half[st]], buf[b, half[st]]], 0)

    def rs_chip(r, st, p):
        return rcopy(
            R.snd_c.at[p, half[st]], R.rcv_c.at[r, p, half[st]], R.rs_s.at[0], R.rs_cr.at[st, p], partner
        )

    def rs_link(r, st, p, q):
        over = p if p != by_both else (by_x, by_y)[q]
        to, _ = dev(c32(over), 0)
        return rcopy(
            R.snd_l.at[p, piece(st, q)], R.rcv_l.at[r, p, piece(st, q)], R.rs_s.at[1], R.rs_lr.at[st, p, q], to
        )

    def rs_put(r, st, p, same, other):
        R.snd_c[p, half[st]] = other.astype(BF)
        rs_chip(r, st, p).start()
        R.keep[p, half[st]] = same

    def rs_put_pair(r, p, part):
        for st in (0, 1):
            at = st * (T // 2)
            rs_put(r, st, p, part[at:at + T // 2], part[T + at:T + at + T // 2])

    def rs_combine(r, st, p):
        rs_chip(r, st, p).wait_recv()
        both = R.keep[p, half[st]] + R.rcv_c[r, p, half[st]].astype(F32)
        R.keep[p, half[st]] = both
        R.snd_l[p, half[st]] = both.astype(BF)
        for target, parts in ((by_y, (1,)), (by_x, (0,)), (by_both, (0, 1))):
            @when(p == target)
            def _():
                for q in parts:
                    rs_link(r, st, target, q).start()

    def rs_combine_pair(r, p):
        rs_combine(r, 0, p)
        rs_combine(r, 1, p)

    def rs_relay(r, st):
        for p, q in ((by_y, 0), (by_x, 1)):
            rs_link(r, st, by_both, q).wait_recv()
            rows_q = piece(st, q)
            R.snd_l[p, rows_q] = (R.keep[p, rows_q] + R.rcv_l[r, by_both, rows_q].astype(F32)).astype(BF)
            rs_link(r, st, p, q).start()

    def rs_final(r, st):
        rs_chip(r, st, c32(0)).wait_recv()
        acc = R.keep[0, half[st]] + R.rcv_c[r, 0, half[st]].astype(F32)
        for p in (by_y, by_x):
            for q in (0, 1):
                rs_link(r, st, p, q).wait_recv()
            acc = acc + R.rcv_l[r, p, half[st]].astype(F32)
        if st == 1:
            all_of(R.snd_c, R.rs_s.at[0], R.rs_cr.at[0, 0]).wait_send()
            all_of(R.snd_l.at[pl.ds(1, 3)], R.rs_s.at[1], R.rs_cr.at[0, 0]).wait_send()
        return acc

    def rs_whole(r):
        return jnp.concatenate([rs_final(r, 0), rs_final(r, 1)], 0)

    first = ((0, T // 8), (T // 8, T // 8), (T // 4, T // 4), (T // 2, T // 2))
    chunks = [("b", lambda x, i=i, n=n: x.at[0, pl.ds(i, n)], n) for i, n in first]
    chunks += [("b", lambda x, i=i, h=h: x.at[i, h], T // 2) for i in range(1, 4) for h in half]
    chunks += [("i", lambda x, t=t: x.at[t], T // 2) for t in range(8)]
    chunks += [("o", lambda x, h=h: x.at[h], T // 2) for h in half] + [("s", lambda x: x, 1)]
    chunks += [("w", lambda x, t=t: x.at[t], 3 * T // 8) for t in range(7)]
    chunks += [("w", lambda x, h=h: x.at[7, h], 3 * T // 16) for h in half]
    Z_IN, Z_OUT, Z_SMALL, Z_QKV, Z_ALL = 10, 18, 20, 21, len(chunks)

    def zrefs(c):
        k, cut, _ = chunks[c]
        return cut(getattr(R, "zown_" + k)), cut(getattr(R, "zsum_" + k)), cut(getattr(R, "zmid_" + k))

    kinds = "biosw"

    def z_sem(c, way):
        return R.z_s.at[kinds.index(chunks[c][0]), way]

    def z_up(c):
        own, tot, _ = zrefs(c)
        return rcopy(own, tot, z_sem(c, 0), R.z_r.at[c, 0], (z_other, blk, head))

    def z_across(c):
        own, _, mid = zrefs(c)
        return rcopy(own, mid, z_sem(c, 0), R.z_r.at[c, 1], (z_mid, blk, head))

    def z_down(c):
        _, tot, _ = zrefs(c)
        return rcopy(tot, tot, z_sem(c, 1), R.z_r.at[c, 0], (z_other, blk, head))

    row_us, hop_us = 0.0432, 2.0
    steps, sent = [], 0.0
    for c, (_, _, n) in enumerate(chunks):
        sent += n * row_us
        steps += [(sent + hop_us, c, 0), (sent + n * row_us + 2.2 * hop_us, c, 1)]
    steps.sort()
    made = set()

    def z_until(us):
        while steps and steps[0][0] <= us and steps[0][1] in made:
            _, c, second = steps.pop(0)
            (z_two if second else z_one)(c)

    def z_produce(c):
        made.add(c)

        @pl.when(z_end)
        def _():
            z_up(c).start()

    def z_one(c):
        @pl.when(jnp.logical_not(z_end))
        def _():
            own, tot, _ = zrefs(c)
            z_up(c).wait_recv()
            own[...] = (own[...].astype(F32) + tot[...].astype(F32)).astype(BF)
            z_across(c).start()

    def z_two(c):
        @pl.when(jnp.logical_not(z_end))
        def _():
            own, tot, mid = zrefs(c)
            z_across(c).wait_recv()
            tot[...] = (own[...].astype(F32) + mid[...].astype(F32)).astype(BF)
            z_down(c).start()

    def z_finish(c):
        @pl.when(z_end)
        def _():
            if not Z_IN <= c < Z_OUT:
                z_down(c).wait_recv()

    def z_sent():
        for i, k in enumerate(kinds):
            own, tot = getattr(R, "zown_" + k), getattr(R, "zsum_" + k)
            all_of(own, R.z_s.at[i, 0], R.z_r.at[0, 0]).wait_send()

            @pl.when(jnp.logical_not(z_end))
            def _():
                all_of(tot, R.z_s.at[i, 1], R.z_r.at[0, 0]).wait_send()

    def vec_copy(e):
        to, _ = dev(c32(e // 2), e % 2)
        return rcopy(R.vec, R.vec_all.at[me], R.vec_s.at[0], R.vec_s.at[1], to)

    def qkv_copy(e, j, part, sems):
        to, at = dev(c32(e // 2), e % 2)
        w = (R.wq, R.wk, R.wv)[j]
        return rcopy(w.at[part, lanes(at, W)], R.wqkv.at[me, part, pl.ds(j * W, W)], sems.at[0], sems.at[1], to)

    def win_copy(e, part, sems):
        to, at = dev(c32(e // 2), e % 2)
        return rcopy(R.wi.at[part, lanes(at, FW)], R.win.at[me, part], sems.at[0], sems.at[1], to)

    def along(i, k, way):
        sign = 1 if way == 0 else -1
        q, to = dp - sign * k, lax.rem(dp + sign + 4, 4)
        part = (R.wqkv, R.win)[i].at[:, share(q)]
        return rcopy(part, part, R.along_s.at[i, way, k], R.along_r.at[i, way, k], (to, blk, head))

    def along_do(i, k, act):
        for way, sends, gets in (
            (0, (dp <= 2) & (dp >= k), dp >= k + 1),
            (1, (dp >= 1) & (dp + k <= 3), dp + k <= 2),
        ):
            @pl.when(gets if act == 1 else sends)
            def _():
                step = along(i, k, way)
                (step.start, step.wait_recv, step.wait_send)[act]()

    def along_send(i, k):
        along_do(i, k, 0)

    def along_got(i, k):
        along_do(i, k, 1)

    def along_sent(i):
        for k in range(3):
            along_do(i, k, 2)

    far_first = (6, 7, 2, 3, 4, 5, 1)
    with jax.named_scope("start_copies"):
        for part, sems in ((share(dp), R.qshare_s), (half[0], R.qkv_s)):
            for e in far_first:
                for j in range(3):
                    qkv_copy(e, j, part, sems).start()
        local[0].wait()
        for st in (0, 1):
            ag_start(tok_all, 0, st)
        for cp in small:
            cp.wait()
        vecs = [x[...].astype(F32).reshape(1, T) for x in small_v[1:7]]
        vecs.append(R.ids_v[0:1, lanes(head, T)].astype(F32))
        R.vec[...] = jnp.concatenate(vecs + [jnp.zeros((1, T), F32)], 0)
        R.vec_all[me] = R.vec[...]
        for e in far_first:
            vec_copy(e).start()

    with jax.named_scope("wait_qkv_weights"):
        own = R.wqkv.at[me, pl.ds(0, T // 8)]
        pltpu.make_async_copy(own, own, R.loc.at[7]).wait()
        all_of(R.wqkv.at[seven, pl.ds(0, T // 8)], R.qshare_s.at[0], R.qshare_s.at[1]).wait()
        along_send(0, 0)
        along_got(0, 0)
        along_send(0, 1)
        ag_near(tok_all, 0, 0)
        along_got(0, 1)
        along_send(0, 2)
        ag_near(tok_all, 0, 1)
        ag_far(tok_all, 0, 0)
        for e in far_first:
            win_copy(e, share(dp), R.share_s).start()
        own = R.wqkv.at[me, half[0]]
        pltpu.make_async_copy(own, own, R.loc.at[5]).wait()
        all_of(R.wqkv.at[seven, half[0]], R.qkv_s.at[0], R.qkv_s.at[1]).wait()
        along_got(0, 2)
        along_sent(0)

    def qkv_step(p):
        if p == by_x:
            ag_far(tok_all, 0, 1)
            for e in far_first:
                win_copy(e, half[0], R.win_s).start()
        for st in (0, 1):
            ag_have(tok_all, 0, st, p)
        a, b, x = pair(tok_all, c32(p))
        y = mm(x, rows(R.wqkv), NN)
        qq = ((y[:, :W] + R.bq_v[...].astype(F32).reshape(1, W)) * 0.125).astype(BF)
        kk = y[:, W:2 * W].astype(BF)
        vv = (y[:, 2 * W:] + R.bv_v[...].astype(F32).reshape(1, W)).astype(BF)
        for at, sl in ((a, slice(0, T)), (b, slice(T, 2 * T))):
            R.q[at], R.k[at], R.v[at] = qq[sl], kk[sl], vv[sl]

    with jax.named_scope("project_qkv"):
        for p in range(4):
            qkv_step(p)

    with jax.named_scope("vectors"):
        all_of(R.vec_all.at[seven], R.vec_s.at[0], R.vec_s.at[1]).wait_recv()
        for s in range(8):
            v = R.vec_all[s]
            R.vfull[:, s * T:(s + 1) * T] = v
            ids = jnp.broadcast_to(v[6:7], (T, T)).T
            R.segk[s] = jnp.where(ids < 0, -2.0, ids)

    for i in (1, 2, 3, 4):
        local[i].wait()

    def head_mask(h, like):
        lane = lax.broadcasted_iota(jnp.int32, like.shape, 1)
        return jnp.where(lax.div(lane, HD) == h, like, jnp.zeros_like(like))

    heads = W // HD

    far, near_a, near_b, here = [
        [(0, by_both), (1, by_both)], [(0, by_y), (0, by_x)], [(1, by_y), (1, by_x)], [(0, 0), (1, 0)],
    ]

    def rows_of(buf, items):
        found = [half_pair(buf, c32(p), st) for st, p in items]
        return [(a, b) for a, b, _ in found], jnp.concatenate([x for _, _, x in found], 0)

    def put_rows(buf, items, places, value, lane=slice(None)):
        for i, ((st, _), (a, b)) in enumerate(zip(items, places, strict=True)):
            buf[a, half[st], lane] = value[i * T:i * T + T // 2]
            buf[b, half[st], lane] = value[i * T + T // 2:(i + 1) * T]

    def put_parts(r, items, part):
        for i, (st, p) in enumerate(items):
            rs_put(r, st, p, part[i * T:i * T + T // 2], part[i * T + T // 2:(i + 1) * T])

    def ids_of(items, places):
        return jnp.concatenate(
            [
                R.vec_all[at, 6:7, st * (T // 2):(st + 1) * (T // 2)]
                for (st, _), both in zip(items, places, strict=True)
                for at in both
            ],
            1,
        )

    def attend_step(slot, items, between):
        places, qp = rows_of(R.q, items)
        segq = ids_of(items, places)
        segk = rows(R.segk)
        allowed = jnp.concatenate([segk, segk], 1) == segq
        kk = rows(R.k)
        outs = []
        scores = [mm(kk, head_mask(h, qp), NT) for h in range(heads)]
        for h in range(heads):
            s = jnp.where(allowed, scores[h], -1e30)
            ex = jnp.exp(s - jnp.max(s, 0, keepdims=True))
            total = jnp.maximum(jnp.sum(ex, 0, keepdims=True), 1.0)
            pt = (ex * jnp.where(segq >= 0, 1.0 / total, 0.0)).astype(BF)
            R.pt[h, slot] = pt
            outs.append(mm(R.vt[h * HD:(h + 1) * HD, :], pt, NN))
            if h == 0:
                between()
        ct = jnp.concatenate(outs, 0).T.astype(BF)
        put_rows(R.ctx, items, places, ct)
        put_parts(0, items, mm(ct, R.wo_v[...], NN))

    def after_far():
        local_share.wait()
        all_of(R.win.at[seven, pl.ds(0, T // 8)], R.share_s.at[0], R.share_s.at[1]).wait()
        along_send(1, 0)

    def after_near_a():
        rs_combine_pair(0, by_both)

    def after_near_b():
        rs_combine(0, 0, by_y)
        rs_combine(0, 0, by_x)
        along_got(1, 0)
        along_send(1, 1)

    def after_here():
        rs_combine(0, 1, by_y)
        rs_combine(0, 1, by_x)
        rs_relay(0, 1)

    with jax.named_scope("attend"):
        R.vt[...] = rows(R.v).T
        attend_step(0, far, after_far)
        attend_step(1, near_a, after_near_a)
        attend_step(2, near_b, after_near_b)
        rs_relay(0, 0)
        attend_step(3, here, after_here)
        along_got(1, 1)
        along_send(1, 2)

    with jax.named_scope("first_norm"):
        for st in (0, 1):
            rs = rs_final(0, st)
            h1 = tok_all[me, half[st]].astype(F32) + rs + R.vfull[0:1]
            n1, r1 = norm_parts(h1)
            y1 = n1 * R.vfull[2:3] + R.vfull[3:4]
            R.n1[half[st]], R.y1[half[st]] = n1, y1
            R.r1[half[st]] = jnp.broadcast_to(r1, (T // 2, 128))
            y1_all[me, half[st]] = y1.astype(BF)
            ag_start(y1_all, 1, st)

    with jax.named_scope("wait_hidden_weights"):
        all_of(R.win.at[seven, half[0]], R.win_s.at[0], R.win_s.at[1]).wait()
        along_got(1, 2)
        along_sent(1)

    def hidden_step(items):
        places, x = rows_of(y1_all, items)
        z = mm(x, rows(R.win), NN) + R.bi_v[...].astype(F32).reshape(1, FW)
        cdf = 0.5 * (1.0 + lax.erf(z * 0.7071067811865476))
        low = (z * cdf).astype(BF)
        slope = cdf + z * (jnp.exp(-0.5 * z * z) * 0.3989422804014327)
        put_parts(1, items, mm(low, R.wb_v[...], NN))
        put_rows(R.hid, items, places, low)
        put_rows(R.slope, items, places, slope)

    with jax.named_scope("hidden"):
        ag_near(y1_all, 1, 0)
        for st in (0, 1):
            ag_have(y1_all, 1, st, 0)
        hidden_step(here)
        for p in (by_y, by_x):
            ag_have(y1_all, 1, 0, p)
        hidden_step(near_a)
        ag_near(y1_all, 1, 1)
        ag_far(y1_all, 1, 0)
        for p in (by_y, by_x):
            ag_have(y1_all, 1, 1, p)
            rs_combine(1, 0, p)
        hidden_step(near_b)
        ag_far(y1_all, 1, 1)
        ag_have(y1_all, 1, 0, by_both)
        hidden_step(far[:1])
        for p in (by_y, by_x):
            rs_combine(1, 1, p)
        ag_have(y1_all, 1, 1, by_both)
        rs_combine(1, 0, by_both)
        hidden_step(far[1:])
        R.kt[...] = rows(R.k).T
        rs_combine(1, 1, by_both)

    with jax.named_scope("second_norm"):
        rs_relay(1, 0)
        rs_relay(1, 1)
        for st in (0, 1):
            rs = rs_final(1, st)
            h2 = R.y1[half[st]] + rs + R.vfull[1:2]
            n2, r2 = norm_parts(h2)
            gain = R.vfull[4:5]
            R.out_v[half[st]] = (n2 * gain + R.vfull[5:6]).astype(BF)
            cot = R.cot_v[half[st]].astype(F32)
            dh2 = norm_back(cot * gain, n2, r2)
            R.dh2[half[st]] = dh2
            df_all[me, half[st]] = dh2.astype(BF)
            ag_start(df_all, 2, st)
            sums = jnp.concatenate([colsum(cot * n2), colsum(cot)], 0)
            R.sv[0:2, :] = sums if st == 0 else R.sv[0:2, :] + sums
        put_out.start()

    def grad_back(i):
        x = R.hid[:, :, i * T:(i + 1) * T].reshape(8 * T, T)
        R.zown_b[i] = mm(x, rows(df_all), TN).astype(BF)
        for c in range(4) if i == 0 else (2 * i + 2, 2 * i + 3):
            z_produce(c)

    def hidden_back_step(p):
        ag_wait(df_all, 2, p)
        if p == by_both:
            grad_back(0)
        a, b, x = pair(df_all, c32(p))
        slope = jnp.concatenate([R.slope[a], R.slope[b]], 0)
        dz = (mm(x, R.wb_v[...], NT) * slope).astype(BF)
        R.dz[a], R.dz[b] = dz[:T], dz[T:]
        if p > 1:
            rs_combine_pair(2, p - 1)
        rs_put_pair(2, p, mm(dz, rows(R.win), NT))

    with jax.named_scope("hidden_back"):
        for p in range(4):
            hidden_back_step(p)
        z_until(2.8)
        rs_combine_pair(2, 3)
        z_until(3.5)

    with jax.named_scope("grad_back"):
        for i in range(1, 4):
            grad_back(i)
        z_until(7.5)
        rs_relay(2, 0)
        z_until(8.6)
        rs_relay(2, 1)
        z_until(9.8)

    def grad_in(i):
        x = y1_all[:, :, 2 * i * T:(2 * i + 2) * T].reshape(8 * T, 2 * T)
        g = mm(x, rows(R.dz), TN).astype(BF)
        R.zown_i[2 * i], R.zown_i[2 * i + 1] = g[:T], g[T:]
        z_produce(Z_IN + 2 * i)
        z_produce(Z_IN + 2 * i + 1)

    def din_copy(t, s):
        return rcopy(R.zsum_i.at[t], R.grad_i.at[s], R.din_s.at[0], R.din_s.at[1], (dp, t // 2, t % 2))

    def z_deliver(t):
        @pl.when(z_end)
        def _():
            z_down(Z_IN + t).wait_recv()

        @pl.when(me != t)
        def _():
            din_copy(t, me).start()

        @pl.when(me == t)
        def _():
            R.grad_i[me] = R.zsum_i[t]

    with jax.named_scope("grad_in"):
        for i in range(4):
            grad_in(i)
            if i % 2:
                z_until(10.0 + i)

    with jax.named_scope("first_norm_back"):
        rs = rs_whole(2)
        dy1 = R.dh2[...] + rs
        n1 = R.n1[...]
        dh1 = norm_back(dy1 * R.vfull[2:3], n1, R.r1[:, 0:1])
        R.dh1[...] = dh1
        da_all[me] = dh1.astype(BF)
        for st in (0, 1):
            ag_start(da_all, 3, st)
        R.sv[2:3, :] = colsum(dy1 * n1)
        R.sv[3:4, :] = colsum(dy1)

    def sv_copy(e):
        to, at = dev(c32(e // 2), e % 2)
        return rcopy(R.sv.at[:, lanes(at, T)], R.sv_rcv.at[me], R.sv_s.at[0], R.sv_s.at[1], to)

    for e in far_first:
        sv_copy(e).start()
    R.sv_rcv[me] = R.sv[:, lanes(me, T)]

    z_until(13.8)

    R.dk[...] = jnp.zeros_like(R.dk)
    R.dv[...] = jnp.zeros_like(R.dv)

    def attend_back_step(slot, items, times):
        z_until(times[0])
        places, x = rows_of(da_all, items)
        _, qp = rows_of(R.q, items)
        dc = mm(x, R.wo_v[...], NT).astype(BF)
        vv = rows(R.v)
        outs = []
        for h in range(heads):
            dcm, qm = head_mask(h, dc), head_mask(h, qp)
            low = R.pt[h, slot]
            pt = low.astype(F32)
            dpt = mm(vv, dcm, NT)
            ds = (pt * (dpt - jnp.sum(pt * dpt, 0, keepdims=True))).astype(BF)
            outs.append(mm(R.kt[h * HD:(h + 1) * HD, :], ds, NN))
            R.dk[...] += mm(ds, qm, NN)
            R.dv[...] += mm(low, dcm, NN)
            z_until(times[1 + h])
        dq = jnp.concatenate(outs, 0).T.astype(BF) * 0.125
        put_rows(R.dqkv, items, places, dq, slice(0, W))

    with jax.named_scope("attend_back"):
        for st in (0, 1):
            ag_have(da_all, 3, st, 0)
        attend_back_step(3, here, (14.6, 16.0, 17.2))
        for st, slot, items, times in ((0, 1, near_a, (20.2, 21.4, 22.6)), (1, 2, near_b, (24.6, 25.8, 27.0))):
            ag_near(da_all, 3, st)
            z_until((18.0, 23.4)[st])
            if st == 1:
                ag_far(da_all, 3, 0)
            for p in (by_y, by_x):
                ag_have(da_all, 3, st, p)
            attend_back_step(slot, items, times)
        ag_far(da_all, 3, 1)
        for st in (0, 1):
            ag_have(da_all, 3, st, by_both)
        attend_back_step(0, far, (28.0, 29.2, 30.4))
        R.dqkv[:, :, W:2 * W] = R.dk[...].astype(BF).reshape(8, T, W)
        R.dqkv[:, :, 2 * W:] = R.dv[...].astype(BF).reshape(8, T, W)

    def dqkv_copy(p, flip):
        to, at = dev(p, flip)
        return rcopy(R.dqkv_snd.at[at], R.zown_w.at[me], R.dqkv_s.at[0], R.dqkv_s.at[1], to)

    def dqkv_step(p):
        a, b = dev(c32(p), 0)[1], dev(c32(p), 1)[1]
        x = jnp.concatenate([tok_all[:, :, lanes(a, T)], tok_all[:, :, lanes(b, T)]], 2).reshape(8 * T, 2 * T)
        g = mm(x, rows(R.dqkv), TN).astype(BF)
        R.dqkv_snd[b] = g[T:]
        dqkv_copy(c32(p), 1).start()
        if p == 0:
            R.zown_w[me] = g[:T]
        else:
            R.dqkv_snd[a] = g[:T]
            dqkv_copy(c32(p), 0).start()
        z_until(30.5 + 0.5 * p)

    with jax.named_scope("grad_qkv"):
        for p in range(4):
            dqkv_step(p)

    with jax.named_scope("grad_out"):
        R.zown_o[...] = mm(rows(R.ctx), rows(da_all), TN).astype(BF)
        z_produce(Z_OUT)
        z_produce(Z_OUT + 1)
        z_until(33.0)

    def input_step(p):
        if p > 1:
            rs_combine_pair(3, p - 1)
        a, b, x = pair(R.dqkv, c32(p))
        rs_put_pair(3, p, mm(x, rows(R.wqkv), NT))
        z_until((33.5, 34.0, 35.5, 37.0)[p])

    with jax.named_scope("input_back"):
        for p in range(4):
            input_step(p)
        rs_combine_pair(3, 3)
        z_until(39.0)

    with jax.named_scope("small_grads"):
        all_of(R.sv_rcv.at[seven], R.sv_s.at[0], R.sv_s.at[1]).wait_recv()
        acc = R.sv_rcv[0]
        for s in range(1, 8):
            acc = acc + R.sv_rcv[s]
        own = lanes(me, T)
        parts = [
            acc[0:4],
            colsum(rows(R.dqkv)[:, 0:W]),
            colsum(rows(R.dqkv)[:, 2 * W:]),
            colsum(da_all[:, :, own].reshape(8 * T, T)),
            colsum(df_all[:, :, own].reshape(8 * T, T)),
        ]
        dbi = colsum(rows(R.dz))
        parts += [dbi[:, i * T:(i + 1) * T] for i in range(FW // T)]
        parts.append(jnp.zeros((16 - 8 - FW // T, T), F32))
        R.zown_s[...] = jnp.concatenate(parts, 0).astype(BF)
        z_produce(Z_SMALL)
        z_until(41.0)

    with jax.named_scope("z_rest"):
        all_of(R.zown_w.at[seven], R.dqkv_s.at[0], R.dqkv_s.at[1]).wait_recv()
        for c in range(Z_QKV, Z_ALL):
            z_produce(c)
        z_until(44.5)
        rs_relay(3, 0)
        z_until(47.0)
        rs_relay(3, 1)
        z_until(50.0)
    with jax.named_scope("input_grad"):
        R.igrad_v[...] = R.dh1[...] + rs_whole(3)
        put_igrad.start()
    puts = [put_out, put_igrad]

    def put(i, src, dst):
        puts.append(pltpu.make_async_copy(src, dst, R.put_s.at[i]))
        puts[-1].start()

    def z_through(c):
        while any(second and at <= c for _, at, second in steps):
            z_until(steps[0][0])
        z_finish(c)

    with jax.named_scope("z_last"):
        for t in range(8):
            z_until(51.0 + 2 * t)
            z_deliver(t)
            if t == 1:
                for c in range(Z_IN):
                    z_through(c)
                put(2, R.zsum_b, R.gb)
        for c in range(Z_OUT, Z_QKV):
            z_through(c)
        put(4, R.zsum_o, R.go)
        put(5, R.zsum_s, R.gs)
        for t in range(7):
            z_through(Z_QKV + t)
            put(6 + t, R.zsum_w.at[t], R.gw.at[t])
        all_of(R.grad_i.at[seven], R.din_s.at[0], R.din_s.at[1]).wait()
        put(3, R.grad_i, R.gi)
        for c in (Z_ALL - 2, Z_ALL - 1):
            z_through(c)
        put(13, R.zsum_w.at[7], R.gw.at[7])

    with jax.named_scope("finish"):
        z_sent()
        for buf, r in ((tok_all, 0), (y1_all, 1), (df_all, 2), (da_all, 3)):
            ag_finish(buf, r)
        for ref, sem in (
            (R.vec_all, R.vec_s), (R.sv_rcv, R.sv_s), (R.zown_w, R.dqkv_s),
        ):
            all_of(ref.at[seven], sem.at[0], sem.at[1]).wait_send()
        for cp in puts:
            cp.wait()


def sharded_plan(
    tokens, segment_ids, cotangent,
    w_query, w_key, w_value, w_out, w_in, w_back,
    bias_query, bias_value, bias_out, bias_in, bias_back,
    first_gain, first_shift, second_gain, second_shift,
):
    tokens, cotangent = tokens[0], cotangent[0]
    T, D = tokens.shape
    W, FW = D // 8, w_in.shape[1] // 8
    ins = dict(
        tok=tokens, cot=cotangent, wq=w_query, wk=w_key, wv=w_value, wo=w_out, wi=w_in, wb=w_back, ids=segment_ids,
        bo=bias_out, bb=bias_back, g1=first_gain, s1=first_shift, g2=second_gain, s2=second_shift,
        bq=bias_query, bv=bias_value, bi=bias_in,
    )
    in_hbm = 8
    outs = dict(
        out=((T, D), BF), igrad=((T, D), F32), gb=((4, T, D), BF), gi=((8, T, FW), BF), go=((T, D), BF),
        gw=((8, T, 3 * W), BF), gs=((16, T), BF),
    )
    sums = dict(b=outs["gb"], i=outs["gi"], o=outs["go"], w=outs["gw"], s=outs["gs"])
    blocks = {k: ((8, T, D), BF) for k in ("tok_all", "y1_all", "df_all", "da_all")}
    scr = dict(
        **blocks,
        wqkv=((8, T, 3 * W), BF), win=((8, T, FW), BF), wb_v=(w_back.shape, BF), wo_v=(w_out.shape, BF),
        cot_v=((T, D), BF), vec=((8, T), F32), vec_all=((8, 8, T), F32), vfull=((8, D), F32), segk=((8, T, T), F32),
        q=((8, T, W), BF), k=((8, T, W), BF), v=((8, T, W), BF), vt=((W, 8 * T), BF), kt=((W, 8 * T), BF),
        pt=((W // HD, 4, 8 * T, 2 * T), BF), ctx=((8, T, W), BF),
        hid=((8, T, FW), BF), slope=((8, T, FW), F32), dz=((8, T, FW), BF),
        n1=((T, D), F32), r1=((T, 128), F32), y1=((T, D), F32), dh2=((T, D), F32), dh1=((T, D), F32),
        sv=((8, D), F32), sv_rcv=((8, 8, T), F32),
        keep=((4, T, D), F32), snd_c=((4, T, D), BF), snd_l=((4, T, D), BF),
        rcv_c=((4, 4, T, D), BF), rcv_l=((4, 4, T, D), BF),
        dk=((8 * T, W), F32), dv=((8 * T, W), F32), dqkv=((8, T, 3 * W), BF),
        dqkv_snd=((8, T, 3 * W), BF),
        **{z + k: v for z in ("zown_", "zsum_", "zmid_") for k, v in sums.items()}, grad_i=outs["gi"],
        out_v=outs["out"], igrad_v=outs["igrad"],
        **{k + "_v": (v.shape, v.dtype) for k, v in list(ins.items())[in_hbm:]},
    )
    sems = dict(
        ag_s=(4,), ag_r=(2, 4, 2), ag_f=(2, 4, 2), rs_s=(2,), rs_cr=(2, 4), rs_lr=(2, 4, 2),
        z_s=(5, 2), z_r=(30, 2), loc=(8,), small_s=(10,), put_s=(14,), vec_s=(2,), qkv_s=(2,), win_s=(2,), share_s=(2,), qshare_s=(2,), along_s=(2, 2, 3), along_r=(2, 2, 3), sv_s=(2,), din_s=(2,), dqkv_s=(2,),
    )
    names = list(ins) + list(outs) + list(scr) + list(sems)
    res = pl.pallas_call(
        partial(layer_kernel, names),
        out_shape=[jax.ShapeDtypeStruct(*s) for s in outs.values()],
        in_specs=[pl.BlockSpec(memory_space=pltpu.HBM)] * len(ins),
        out_specs=[pl.BlockSpec(memory_space=pltpu.HBM)] * len(outs),
        scratch_shapes=[pltpu.VMEM(*s) for s in scr.values()] + [pltpu.SemaphoreType.DMA(s) for s in sems.values()],
        compiler_params=pltpu.CompilerParams(collective_id=0, has_side_effects=True, vmem_limit_bytes=60 << 20),
        name="layer",
    )(*ins.values())
    firsts = [(T, D)] * 6 + [w_in.shape, w_back.shape]
    sizes = [T, T, T, FW, T, T, T, T, T]
    shapes = [(n, t) for n, t in zip(firsts, [BF] + [F32] * 7)] + [((n,), F32) for n in sizes]
    loaded = list(outs.values())
    stored = [((3, T, D), F32), ((T, D), F32), (w_in.shape, F32), (w_back.shape, F32)] + shapes[8:]
    final = pl.pallas_call(
        finish_kernel,
        out_shape=[jax.ShapeDtypeStruct(*s) for s in shapes],
        in_specs=[pl.BlockSpec(memory_space=pltpu.HBM)] * len(loaded),
        out_specs=[pl.BlockSpec(memory_space=pltpu.HBM)] * len(shapes),
        scratch_shapes=[pltpu.VMEM(*s) for s in loaded + stored]
        + [pltpu.SemaphoreType.DMA((len(loaded) + 8,)), pltpu.SemaphoreType.DMA((len(shapes) + 6,))],
        compiler_params=pltpu.CompilerParams(vmem_limit_bytes=60 << 20),
        name="finish",
    )(*res)
    return (final[0][None], final[1][None], *final[2:])


def finish_kernel(*refs):
    ins, outs, rest = refs[:7], refs[7:24], refs[24:]
    loaded, stored, (load_s, store_s) = rest[:7], rest[7:20], rest[20:]
    out, igrad, gb, gi, go, gw, gs = loaded
    qkv, o_o, o_i, o_b, *o_small = stored
    whole = {i: pltpu.make_async_copy(ins[i], loaded[i], load_s.at[i]) for i in (5, 4, 1, 0, 6)}
    pieces = [pltpu.make_async_copy(ins[2].at[j], gb.at[j], load_s.at[7 + j]) for j in range(4)]
    pairs = [pl.ds(2 * j, 2) for j in range(4)]
    pieces += [pltpu.make_async_copy(ins[3].at[p], gi.at[p], load_s.at[11 + j]) for j, p in enumerate(pairs)]
    for cp in pieces + list(whole.values()):
        cp.start()
    stores = []

    def store(src, dst):
        stores.append(pltpu.make_async_copy(src, dst, store_s.at[len(stores)]))
        stores[-1].start()

    T, width = gb.shape[1], gi.shape[2]
    for j in range(4):
        pieces[j].wait()
        part = pl.ds(j * T, T)
        o_b[part, :] = gb[j].astype(F32)
        store(o_b.at[part], outs[7].at[part])
    for j in range(4):
        pieces[4 + j].wait()
        for s in (2 * j, 2 * j + 1):
            o_i[:, s * width:(s + 1) * width] = gi[s].astype(F32)
        part = pl.ds(2 * j * width, 2 * width)
        store(o_i.at[:, part], outs[6].at[:, part])
    whole[5].wait()
    W = gw.shape[2] // 3
    for j in range(3):
        for s in range(8):
            qkv[j, :, s * W:(s + 1) * W] = gw[s, :, j * W:(j + 1) * W].astype(F32)
        store(qkv.at[j], outs[2 + j])
    whole[4].wait()
    o_o[...] = go[...].astype(F32)
    store(o_o, outs[5])
    whole[1].wait()
    store(igrad, outs[1])
    whole[0].wait()
    store(out, outs[0])
    whole[6].wait()
    v = gs[...].astype(F32)
    bq, bv, bo, bi, bb, g1, s1, g2, s2 = o_small
    for o, i in ((bq, 4), (bv, 5), (bo, 6), (bb, 7), (g1, 2), (s1, 3), (g2, 0), (s2, 1)):
        o[...] = v[i]
    n = v.shape[1]
    for i in range(bi.shape[0] // n):
        bi[i * n:(i + 1) * n] = v[8 + i]
    for i, o in enumerate(o_small):
        store(o, outs[8 + i])
    for cp in stores:
        cp.wait()


def pick_plan(mesh):
    group = mesh.shape["blk"] * mesh.shape["head"]
    return sharded_plan if (mesh.shape["dp"], group) == (4, 8) else general_plan


def flat_dot(left_side, right_side):
    return jnp.dot(
        left_side.reshape(-1, left_side.shape[-1]), right_side, preferred_element_type=jnp.float32
    )


def inner_dot(left_side, right_side):
    return jnp.einsum(
        "ra,rb->ab",
        left_side.reshape(-1, left_side.shape[-1]),
        right_side.reshape(-1, right_side.shape[-1]),
        preferred_element_type=jnp.float32,
    )


def layer_norm(value_rows, gain_row, shift_row):
    centre = jnp.mean(value_rows, -1, keepdims=True)
    centred = value_rows - centre
    spread = jnp.mean(centred * centred, -1, keepdims=True)
    return centred * lax.rsqrt(spread + 1e-05) * gain_row + shift_row


def head_view(array_in):
    return array_in.reshape(array_in.shape[0], array_in.shape[1], -1, HD)


def allowed_pairs(query_ids, key_ids):
    same_doc = (query_ids[:, :, None] == key_ids[:, None, :]) & (key_ids[:, None, :] >= 0)
    return same_doc[:, None]


def forward_step(state_now, arrived, local_data):
    running_max, running_sum, weighted = state_now
    key_block, value_block, key_ids = arrived
    query_block, query_ids = local_data
    scores = jnp.einsum(
        "gqhd,gkhd->ghqk",
        head_view(query_block),
        head_view(key_block),
        preferred_element_type=jnp.float32,
    )
    allowed = allowed_pairs(query_ids, key_ids)
    masked = jnp.where(allowed, scores, -1e30)
    new_max = jnp.maximum(running_max, jnp.max(masked, -1))
    exponents = jnp.where(allowed, jnp.exp(masked - new_max[..., None]), 0.0)
    running_sum = jnp.sum(exponents, -1)
    weighted = jnp.einsum(
        "ghqk,gkhd->ghqd",
        exponents.astype(jnp.bfloat16),
        head_view(value_block),
        preferred_element_type=jnp.float32,
    )
    return (new_max, running_sum, weighted)


def probabilities(query_block, key_block, query_ids, key_ids, log_sums):
    scores = jnp.einsum(
        "gqhd,gkhd->ghqk",
        head_view(query_block),
        head_view(key_block),
        preferred_element_type=jnp.float32,
    )
    allowed = allowed_pairs(query_ids, key_ids)
    masked = jnp.where(allowed, scores, -1e30)
    return jnp.where(allowed, jnp.exp(masked - log_sums.transpose(0, 2, 1)[..., None]), 0.0)


def score_grads(weights_now, grad_block, value_block, deltas):
    grad_weights = jnp.einsum(
        "gqhd,gkhd->ghqk",
        head_view(grad_block),
        head_view(value_block),
        preferred_element_type=jnp.float32,
    )
    return (weights_now * (grad_weights - deltas.transpose(0, 2, 1)[..., None])).astype(
        jnp.bfloat16
    )


def heads_to_rows(array_in):
    return array_in.transpose(0, 2, 1, 3).reshape(array_in.shape[0], array_in.shape[2], -1)


def general_plan(
    tokens,
    segment_ids,
    cotangent,
    w_query,
    w_key,
    w_value,
    w_out,
    w_in,
    w_back,
    bias_query,
    bias_value,
    bias_out,
    bias_in,
    bias_back,
    first_gain,
    first_shift,
    second_gain,
    second_shift,
):
    (
        query_full,
        key_full,
        value_full,
        out_full,
        in_full,
        back_full,
        query_bias,
        value_bias,
        out_bias,
        in_bias,
        back_bias,
        gain_one,
        shift_one,
        gain_two,
        shift_two,
    ) = (
        lax.all_gather(w_query, GROUP, axis=0, tiled=True),
        lax.all_gather(w_key, GROUP, axis=0, tiled=True),
        lax.all_gather(w_value, GROUP, axis=0, tiled=True),
        lax.all_gather(w_out, GROUP, axis=0, tiled=True),
        lax.all_gather(w_in, GROUP, axis=0, tiled=True),
        lax.all_gather(w_back, GROUP, axis=0, tiled=True),
        lax.all_gather(bias_query, GROUP, axis=0, tiled=True),
        lax.all_gather(bias_value, GROUP, axis=0, tiled=True),
        lax.all_gather(bias_out, GROUP, axis=0, tiled=True),
        lax.all_gather(bias_in, GROUP, axis=0, tiled=True),
        lax.all_gather(bias_back, GROUP, axis=0, tiled=True),
        lax.all_gather(first_gain, GROUP, axis=0, tiled=True),
        lax.all_gather(first_shift, GROUP, axis=0, tiled=True),
        lax.all_gather(second_gain, GROUP, axis=0, tiled=True),
        lax.all_gather(second_shift, GROUP, axis=0, tiled=True),
    )
    query_bias = query_bias.astype(jnp.float32)
    value_bias = value_bias.astype(jnp.float32)
    out_bias = out_bias.astype(jnp.float32)
    in_bias = in_bias.astype(jnp.float32)
    back_bias = back_bias.astype(jnp.float32)
    gain_one = gain_one.astype(jnp.float32)
    shift_one = shift_one.astype(jnp.float32)
    gain_two = gain_two.astype(jnp.float32)
    shift_two = shift_two.astype(jnp.float32)
    seq_count = tokens.shape[0]
    query_tok = (
        ((flat_dot(tokens, query_full) + query_bias) * 0.125)
        .astype(jnp.bfloat16)
        .reshape(tokens.shape)
    )
    key_tok = flat_dot(tokens, key_full).astype(jnp.bfloat16).reshape(tokens.shape)
    value_tok = (
        (flat_dot(tokens, value_full) + value_bias).astype(jnp.bfloat16).reshape(tokens.shape)
    )
    query_heads, key_heads, value_heads = (
        lax.all_to_all(query_tok, "head", split_axis=2, concat_axis=1, tiled=True),
        lax.all_to_all(key_tok, "head", split_axis=2, concat_axis=1, tiled=True),
        lax.all_to_all(value_tok, "head", split_axis=2, concat_axis=1, tiled=True),
    )
    rows_here = query_heads.shape[1]
    width_heads = query_heads.shape[2]
    heads_here = width_heads // HD
    start_state = (
        jnp.full((seq_count, heads_here, rows_here), -1e30, jnp.float32),
        jnp.zeros((seq_count, heads_here, rows_here), jnp.float32),
        jnp.zeros((seq_count, heads_here, rows_here, HD), jnp.float32),
    )
    running_max, running_sum, weighted = forward_step(
        start_state,
        (
            lax.all_gather(key_heads, "blk", axis=1, tiled=True),
            lax.all_gather(value_heads, "blk", axis=1, tiled=True),
            lax.all_gather(segment_ids, "blk", axis=1, tiled=True),
        ),
        (query_heads, segment_ids),
    )
    floored = jnp.maximum(running_sum, 1.0)
    ctx_heads = heads_to_rows(weighted / floored[..., None])
    log_sums = (running_max + jnp.log(floored)).transpose(0, 2, 1)
    ctx_tok = lax.all_to_all(
        ctx_heads.astype(jnp.bfloat16), "head", split_axis=1, concat_axis=2, tiled=True
    )
    first_sum = tokens.astype(jnp.float32) + (flat_dot(ctx_tok, out_full) + out_bias).reshape(
        tokens.shape
    )
    first_norm = layer_norm(first_sum, gain_one, shift_one)
    first_low = first_norm.astype(jnp.bfloat16)
    inner_rows = flat_dot(first_low, in_full) + in_bias
    hidden_low = jax.nn.gelu(inner_rows, approximate=False).astype(jnp.bfloat16)
    second_sum = first_norm + (flat_dot(hidden_low, back_full) + back_bias).reshape(tokens.shape)
    output_now, second_pull = jax.vjp(layer_norm, second_sum, gain_two, shift_two)
    grad_second, grad_gain_two, grad_shift_two = second_pull(cotangent.astype(jnp.float32))
    grad_branch = grad_second.astype(jnp.bfloat16)
    grad_back_bias = jnp.sum(grad_branch.astype(jnp.float32), (0, 1))
    grad_back = inner_dot(hidden_low, grad_branch)
    grad_hidden = flat_dot(grad_branch, back_full.T)
    unused_value, gelu_pull = jax.vjp(partial(jax.nn.gelu, approximate=False), inner_rows)
    grad_inner = gelu_pull(grad_hidden)[0].astype(jnp.bfloat16)
    grad_in_bias = jnp.sum(grad_inner.astype(jnp.float32), 0)
    grad_in = inner_dot(first_low, grad_inner)
    grad_first_norm = grad_second + flat_dot(grad_inner, in_full.T).reshape(tokens.shape)
    unused_norm, first_pull = jax.vjp(layer_norm, first_sum, gain_one, shift_one)
    grad_first, grad_gain_one, grad_shift_one = first_pull(grad_first_norm)
    grad_attn = grad_first.astype(jnp.bfloat16)
    grad_out_bias = jnp.sum(grad_attn.astype(jnp.float32), (0, 1))
    grad_out = inner_dot(ctx_tok, grad_attn)
    grad_ctx_tok = flat_dot(grad_attn, out_full.T).astype(jnp.bfloat16).reshape(tokens.shape)
    grad_ctx = lax.all_to_all(grad_ctx_tok, "head", split_axis=2, concat_axis=1, tiled=True)
    deltas = jnp.sum(head_view(grad_ctx).astype(jnp.float32) * head_view(ctx_heads), -1)
    key_block = lax.all_gather(key_heads, "blk", axis=1, tiled=True)
    value_block = lax.all_gather(value_heads, "blk", axis=1, tiled=True)
    key_ids = lax.all_gather(segment_ids, "blk", axis=1, tiled=True)
    weights_now = probabilities(query_heads, key_block, segment_ids, key_ids, log_sums)
    dscores = score_grads(weights_now, grad_ctx, value_block, deltas)
    grad_query_heads = jnp.einsum(
        "ghqk,gkhd->ghqd", dscores, head_view(key_block), preferred_element_type=jnp.float32
    )
    key_part = jnp.einsum(
        "ghqk,gqhd->gkhd", dscores, head_view(query_heads), preferred_element_type=jnp.float32
    )
    value_part = jnp.einsum(
        "ghqk,gqhd->gkhd",
        weights_now.astype(jnp.bfloat16),
        head_view(grad_ctx),
        preferred_element_type=jnp.float32,
    )
    both_parts = jnp.concatenate(
        [
            key_part.reshape(key_part.shape[0], key_part.shape[1], -1),
            value_part.reshape(value_part.shape[0], value_part.shape[1], -1),
        ],
        2,
    )
    grad_query_heads, pair_grads = (grad_query_heads, both_parts)
    pair_home = lax.psum_scatter(
        pair_grads.astype(jnp.bfloat16), "blk", scatter_dimension=1, tiled=True
    ).astype(jnp.float32)
    grad_key_heads = pair_home[:, :, :width_heads].astype(jnp.bfloat16)
    grad_value_heads = pair_home[:, :, width_heads:].astype(jnp.bfloat16)
    grad_query_rows = heads_to_rows(grad_query_heads).astype(jnp.bfloat16)
    grad_query_tok, grad_key_tok, grad_value_tok = (
        lax.all_to_all(grad_query_rows, "head", split_axis=1, concat_axis=2, tiled=True),
        lax.all_to_all(grad_key_heads, "head", split_axis=1, concat_axis=2, tiled=True),
        lax.all_to_all(grad_value_heads, "head", split_axis=1, concat_axis=2, tiled=True),
    )
    grad_query_tok = grad_query_tok * 0.125
    grad_inputs = grad_first + (
        flat_dot(grad_query_tok, query_full.T)
        + flat_dot(grad_key_tok, key_full.T)
        + flat_dot(grad_value_tok, value_full.T)
    ).reshape(tokens.shape)
    (
        shard_wq,
        shard_wk,
        shard_wv,
        shard_wo,
        shard_wi,
        shard_wb,
        shard_bq,
        shard_bv,
        shard_bo,
        shard_bi,
        shard_bb,
        shard_g1,
        shard_s1,
        shard_g2,
        shard_s2,
    ) = (
        lax.psum_scatter(
            inner_dot(tokens, grad_query_tok), GROUP, scatter_dimension=0, tiled=True
        ),
        lax.psum_scatter(
            inner_dot(tokens, grad_key_tok), GROUP, scatter_dimension=0, tiled=True
        ),
        lax.psum_scatter(
            inner_dot(tokens, grad_value_tok), GROUP, scatter_dimension=0, tiled=True
        ),
        lax.psum_scatter(grad_out, GROUP, scatter_dimension=0, tiled=True),
        lax.psum_scatter(grad_in, GROUP, scatter_dimension=0, tiled=True),
        lax.psum_scatter(grad_back, GROUP, scatter_dimension=0, tiled=True),
        lax.psum_scatter(
            jnp.sum(grad_query_tok.astype(jnp.float32), (0, 1)),
            GROUP,
            scatter_dimension=0,
            tiled=True,
        ),
        lax.psum_scatter(
            jnp.sum(grad_value_tok.astype(jnp.float32), (0, 1)),
            GROUP,
            scatter_dimension=0,
            tiled=True,
        ),
        lax.psum_scatter(grad_out_bias, GROUP, scatter_dimension=0, tiled=True),
        lax.psum_scatter(grad_in_bias, GROUP, scatter_dimension=0, tiled=True),
        lax.psum_scatter(grad_back_bias, GROUP, scatter_dimension=0, tiled=True),
        lax.psum_scatter(grad_gain_one, GROUP, scatter_dimension=0, tiled=True),
        lax.psum_scatter(grad_shift_one, GROUP, scatter_dimension=0, tiled=True),
        lax.psum_scatter(grad_gain_two, GROUP, scatter_dimension=0, tiled=True),
        lax.psum_scatter(grad_shift_two, GROUP, scatter_dimension=0, tiled=True),
    )
    (
        total_wq,
        total_wk,
        total_wv,
        total_wo,
        total_wi,
        total_wb,
        total_bq,
        total_bv,
        total_bo,
        total_bi,
        total_bb,
        total_g1,
        total_s1,
        total_g2,
        total_s2,
    ) = (
        lax.psum(shard_wq.astype(jnp.bfloat16), "dp").astype(jnp.float32),
        lax.psum(shard_wk.astype(jnp.bfloat16), "dp").astype(jnp.float32),
        lax.psum(shard_wv.astype(jnp.bfloat16), "dp").astype(jnp.float32),
        lax.psum(shard_wo.astype(jnp.bfloat16), "dp").astype(jnp.float32),
        lax.psum(shard_wi.astype(jnp.bfloat16), "dp").astype(jnp.float32),
        lax.psum(shard_wb.astype(jnp.bfloat16), "dp").astype(jnp.float32),
        lax.psum(shard_bq.astype(jnp.bfloat16), "dp").astype(jnp.float32),
        lax.psum(shard_bv.astype(jnp.bfloat16), "dp").astype(jnp.float32),
        lax.psum(shard_bo.astype(jnp.bfloat16), "dp").astype(jnp.float32),
        lax.psum(shard_bi.astype(jnp.bfloat16), "dp").astype(jnp.float32),
        lax.psum(shard_bb.astype(jnp.bfloat16), "dp").astype(jnp.float32),
        lax.psum(shard_g1.astype(jnp.bfloat16), "dp").astype(jnp.float32),
        lax.psum(shard_s1.astype(jnp.bfloat16), "dp").astype(jnp.float32),
        lax.psum(shard_g2.astype(jnp.bfloat16), "dp").astype(jnp.float32),
        lax.psum(shard_s2.astype(jnp.bfloat16), "dp").astype(jnp.float32),
    )
    return (
        output_now.astype(jnp.bfloat16),
        grad_inputs,
        total_wq,
        total_wk,
        total_wv,
        total_wo,
        total_wi,
        total_wb,
        total_bq,
        total_bv,
        total_bo,
        total_bi,
        total_bb,
        total_g1,
        total_s1,
        total_g2,
        total_s2,
    )


def solution(mesh):
    in_specs = (
        P("dp", GROUP, None),
        P("dp", "blk"),
        P("dp", GROUP, None),
        P(GROUP, None),
        P(GROUP, None),
        P(GROUP, None),
        P(GROUP, None),
        P(GROUP, None),
        P(GROUP, None),
        P(GROUP),
        P(GROUP),
        P(GROUP),
        P(GROUP),
        P(GROUP),
        P(GROUP),
        P(GROUP),
        P(GROUP),
        P(GROUP),
    )
    out_specs = (
        P("dp", GROUP, None),
        P("dp", GROUP, None),
        P(GROUP, None),
        P(GROUP, None),
        P(GROUP, None),
        P(GROUP, None),
        P(GROUP, None),
        P(GROUP, None),
        P(GROUP),
        P(GROUP),
        P(GROUP),
        P(GROUP),
        P(GROUP),
        P(GROUP),
        P(GROUP),
        P(GROUP),
        P(GROUP),
    )
    plan = pick_plan(mesh)
    return jax.shard_map(
        plan, mesh=mesh, in_specs=in_specs, out_specs=out_specs, check_vma=False
    )
```

```python
from functools import partial
from types import SimpleNamespace

import jax
import jax.numpy as jnp
from jax import lax
from jax.experimental import pallas as pl
from jax.experimental.pallas import tpu as pltpu
from jax.sharding import PartitionSpec as P

HD = 64
BF = jnp.bfloat16
F32 = jnp.float32
GROUP = ("blk", "head")
MESH = pl.DeviceIdType.MESH
NN = ((1,), (0,))
NT = ((1,), (1,))
TN = ((0,), (0,))


def mm(a, b, dims):
    return lax.dot_general(a, b, (dims, ((), ())), preferred_element_type=F32)


def norm_parts(v):
    c = v - jnp.mean(v, -1, keepdims=True)
    r = lax.rsqrt(jnp.mean(c * c, -1, keepdims=True) + 1e-05)
    return c * r, r


def norm_back(e, n, r):
    return r * (e - jnp.mean(e, -1, keepdims=True) - n * jnp.mean(e * n, -1, keepdims=True))


def colsum(x):
    return jnp.sum(x.astype(F32), 0, keepdims=True)


def when(cond):
    if isinstance(cond, bool):
        return (lambda body: body()) if cond else (lambda body: None)
    return pl.when(cond)


def rows(ref):
    x = ref[...]
    return x.reshape(-1, x.shape[-1])


def layer_kernel(names, *refs):
    R = SimpleNamespace(**dict(zip(names, refs, strict=True)))
    dp, blk, head = [lax.axis_index(a) for a in ("dp", "blk", "head")]
    core, chip_x = lax.rem(blk, 2), lax.div(blk, 2)
    T, D = R.tok.shape
    W = R.q.shape[-1]
    FW = R.wi.shape[1] // 8

    def dev(p, flip):
        hh = lax.rem(head + lax.rem(p, 2), 2)
        bb = lax.rem(chip_x + lax.div(p, 2), 2) * 2 + lax.rem(core + flip, 2)
        return (dp, bb, hh), bb * 2 + hh

    def c32(i):
        return jnp.asarray(i, jnp.int32)

    me = blk * 2 + head
    partner, partner_at = dev(c32(0), 1)
    z_end = lax.rem(dp, 3) == 0
    z_other = jnp.where(dp == 0, 1, jnp.where(dp == 3, 2, jnp.where(dp == 1, 0, 3)))
    z_mid = jnp.where(dp == 1, 2, 1)

    def rcopy(src, dst, ssem, rsem, to):
        return pltpu.make_async_remote_copy(src, dst, ssem, rsem, device_id=to, device_id_type=MESH)

    def all_of(ref, ssem, rsem):
        return rcopy(ref, ref, ssem, rsem, partner)

    seven = pl.ds(0, 7)

    def lanes(i, w):
        return pl.ds(pl.multiple_of(i * w, w), w)

    tok_all, y1_all, df_all, da_all = R.tok_all, R.y1_all, R.df_all, R.da_all
    half = (pl.ds(0, T // 2), pl.ds(T // 2, T // 2))

    def share(z):
        return pl.ds(pl.multiple_of(T // 2 + z * (T // 8), T // 8), T // 8)

    small_in = (R.ids, R.bo, R.bb, R.g1, R.s1, R.g2, R.s2, R.bq, R.bv, R.bi)
    small_v = (R.ids_v, R.bo_v, R.bb_v, R.g1_v, R.s1_v, R.g2_v, R.s2_v, R.bq_v, R.bv_v, R.bi_v)
    local = [
        pltpu.make_async_copy(R.tok, tok_all.at[me], R.loc.at[0]),
        pltpu.make_async_copy(R.wb, R.wb_v, R.loc.at[1]),
        pltpu.make_async_copy(R.wo, R.wo_v, R.loc.at[2]),
        pltpu.make_async_copy(R.wi.at[half[0], lanes(me, FW)], R.win.at[me, half[0]], R.loc.at[3]),
        pltpu.make_async_copy(R.cot, R.cot_v, R.loc.at[4]),
    ]
    local_share = pltpu.make_async_copy(R.wi.at[share(dp), lanes(me, FW)], R.win.at[me, share(dp)], R.loc.at[6])
    local_share.start()
    for j, w in enumerate((R.wq, R.wk, R.wv)):
        for part, at in ((half[0], 5), (share(dp), 7)):
            local.append(
                pltpu.make_async_copy(w.at[part, lanes(me, W)], R.wqkv.at[me, part, pl.ds(j * W, W)], R.loc.at[at])
            )
    small = [
        pltpu.make_async_copy(x, y, R.small_s.at[i])
        for i, (x, y) in enumerate(zip(small_in, small_v, strict=True))
    ]
    for cp in local + small:
        cp.start()

    bar = pltpu.get_barrier_semaphore()
    for e in range(1, 8):
        to, _ = dev(c32(e // 2), e % 2)
        pl.semaphore_signal(bar, 1, device_id=to, device_id_type=MESH)
    for j in range(1, 4):
        pl.semaphore_signal(bar, 1, device_id=(lax.rem(dp + j, 4), blk, head), device_id_type=MESH)
    pl.semaphore_wait(bar, 10)

    put_out = pltpu.make_async_copy(R.out_v, R.out, R.put_s.at[0])
    put_igrad = pltpu.make_async_copy(R.igrad_v, R.igrad, R.put_s.at[1])

    by_y, by_x, by_both = 1, 2, 3

    def piece(st, q):
        return pl.ds((2 * st + q) * (T // 4), T // 4)

    def ag_direct(buf, r, st, p, q):
        to, _ = dev(c32(p), 0)
        part = buf.at[me, piece(st, q)]
        return rcopy(part, part, R.ag_s.at[r], R.ag_r.at[st, p, q], to)

    def ag_relay(buf, r, st, q):
        via, over = (by_x, by_y) if q == 0 else (by_y, by_x)
        _, at = dev(c32(via), 0)
        to, _ = dev(c32(over), 0)
        part = buf.at[at, piece(st, q)]
        return rcopy(part, part, R.ag_s.at[r], R.ag_r.at[st, by_both, q], to)

    def ag_home(buf, r, st):
        part = buf.at[me, half[st]]
        return rcopy(part, part, R.ag_s.at[r], R.ag_f.at[st, 0, 0], partner)

    def ag_forward(buf, r, st, p, q):
        _, at = dev(c32(p), 0)
        part = buf.at[at, piece(st, q)]
        return rcopy(part, part, R.ag_s.at[r], R.ag_f.at[st, p, q], partner)

    def ag_start(buf, r, st):
        for p, q in ((by_x, 0), (by_y, 1), (by_x, 1), (by_y, 0)):
            ag_direct(buf, r, st, p, q).start()
        ag_home(buf, r, st).start()

    def ag_got(buf, r, st, p, q):
        (ag_relay(buf, r, st, q) if p == by_both else ag_direct(buf, r, st, p, q)).wait_recv()
        ag_forward(buf, r, st, p, q).start()

    def ag_near(buf, r, st):
        for p, q in ((by_x, 0), (by_y, 1)):
            ag_got(buf, r, st, p, q)
            ag_relay(buf, r, st, q).start()
        for p, q in ((by_y, 0), (by_x, 1)):
            ag_got(buf, r, st, p, q)

    def ag_far(buf, r, st):
        for q in (0, 1):
            ag_got(buf, r, st, by_both, q)

    def ag_have(buf, r, st, p):
        if p == 0:
            ag_home(buf, r, st).wait_recv()
        else:
            for q in (0, 1):
                ag_forward(buf, r, st, p, q).wait_recv()

    def ag_wait(buf, r, p, between=lambda st: None):
        for st in (0, 1):
            if p == by_y:
                ag_near(buf, r, st)
                between(st)
            if p == by_x:
                ag_far(buf, r, st)
        for st in (0, 1):
            ag_have(buf, r, st, p)

    def ag_finish(buf, r):
        all_of(buf.at[seven], R.ag_s.at[r], R.ag_r.at[0, 0, 0]).wait_send()

    def pair(buf, p):
        a, b = dev(p, 0)[1], dev(p, 1)[1]
        return a, b, jnp.concatenate([buf[a], buf[b]], 0)

    def half_pair(buf, p, st):
        a, b = dev(p, 0)[1], dev(p, 1)[1]
        return a, b, jnp.concatenate([buf[a, half[st]], buf[b, half[st]]], 0)

    def rs_chip(r, st, p):
        return rcopy(
            R.snd_c.at[p, half[st]], R.rcv_c.at[r, p, half[st]], R.rs_s.at[0], R.rs_cr.at[st, p], partner
        )

    def rs_link(r, st, p, q):
        over = p if p != by_both else (by_x, by_y)[q]
        to, _ = dev(c32(over), 0)
        return rcopy(
            R.snd_l.at[p, piece(st, q)], R.rcv_l.at[r, p, piece(st, q)], R.rs_s.at[1], R.rs_lr.at[st, p, q], to
        )

    def rs_put(r, st, p, same, other):
        R.snd_c[p, half[st]] = other.astype(BF)
        rs_chip(r, st, p).start()
        R.keep[p, half[st]] = same

    def rs_put_pair(r, p, part):
        for st in (0, 1):
            at = st * (T // 2)
            rs_put(r, st, p, part[at:at + T // 2], part[T + at:T + at + T // 2])

    def rs_combine(r, st, p):
        rs_chip(r, st, p).wait_recv()
        both = R.keep[p, half[st]] + R.rcv_c[r, p, half[st]].astype(F32)
        R.keep[p, half[st]] = both
        R.snd_l[p, half[st]] = both.astype(BF)
        for target, parts in ((by_y, (1,)), (by_x, (0,)), (by_both, (0, 1))):
            @when(p == target)
            def _():
                for q in parts:
                    rs_link(r, st, target, q).start()

    def rs_combine_pair(r, p):
        rs_combine(r, 0, p)
        rs_combine(r, 1, p)

    def rs_relay(r, st):
        for p, q in ((by_y, 0), (by_x, 1)):
            rs_link(r, st, by_both, q).wait_recv()
            rows_q = piece(st, q)
            R.snd_l[p, rows_q] = (R.keep[p, rows_q] + R.rcv_l[r, by_both, rows_q].astype(F32)).astype(BF)
            rs_link(r, st, p, q).start()

    def rs_final(r, st):
        rs_chip(r, st, c32(0)).wait_recv()
        acc = R.keep[0, half[st]] + R.rcv_c[r, 0, half[st]].astype(F32)
        for p in (by_y, by_x):
            for q in (0, 1):
                rs_link(r, st, p, q).wait_recv()
            acc = acc + R.rcv_l[r, p, half[st]].astype(F32)
        if st == 1:
            all_of(R.snd_c, R.rs_s.at[0], R.rs_cr.at[0, 0]).wait_send()
            all_of(R.snd_l.at[pl.ds(1, 3)], R.rs_s.at[1], R.rs_cr.at[0, 0]).wait_send()
        return acc

    def rs_whole(r):
        return jnp.concatenate([rs_final(r, 0), rs_final(r, 1)], 0)

    first = ((0, T // 8), (T // 8, T // 8), (T // 4, T // 4), (T // 2, T // 4), (3 * T // 4, T // 4))
    chunks = [("b", lambda x, i=i, n=n: x.at[0, pl.ds(i, n)], n) for i, n in first]
    chunks += [("b", lambda x, i=i, h=h: x.at[i, h], T // 2) for i in range(1, 4) for h in half]
    chunks += [("i", lambda x, t=t: x.at[t], T // 2) for t in range(8)]
    chunks += [("o", lambda x, h=h: x.at[h], T // 2) for h in half] + [("s", lambda x: x, 1)]
    chunks += [("w", lambda x, t=t: x.at[t], 3 * T // 8) for t in range(7)]
    chunks += [("w", lambda x, h=h: x.at[7, h], 3 * T // 16) for h in half]
    Z_IN, Z_OUT, Z_SMALL, Z_QKV, Z_ALL = 11, 19, 21, 22, len(chunks)

    def zrefs(c):
        k, cut, _ = chunks[c]
        return cut(getattr(R, "zown_" + k)), cut(getattr(R, "zsum_" + k)), cut(getattr(R, "zmid_" + k))

    kinds = "biosw"

    def z_sem(c, way):
        return R.z_s.at[kinds.index(chunks[c][0]), way]

    def z_up(c):
        own, tot, _ = zrefs(c)
        return rcopy(own, tot, z_sem(c, 0), R.z_r.at[c, 0], (z_other, blk, head))

    def z_across(c):
        own, _, mid = zrefs(c)
        return rcopy(own, mid, z_sem(c, 0), R.z_r.at[c, 1], (z_mid, blk, head))

    def z_down(c):
        _, tot, _ = zrefs(c)
        return rcopy(tot, tot, z_sem(c, 1), R.z_r.at[c, 0], (z_other, blk, head))

    row_us, hop_us = 0.0432, 2.0
    steps, sent = [], 0.0
    for c, (_, _, n) in enumerate(chunks):
        sent += n * row_us
        steps += [(sent + hop_us, c, 0), (sent + n * row_us + 2.2 * hop_us, c, 1)]
    steps.sort()
    made = set()

    def z_until(us):
        while steps and steps[0][0] <= us and steps[0][1] in made:
            _, c, second = steps.pop(0)
            (z_two if second else z_one)(c)

    def z_produce(c):
        made.add(c)

        @pl.when(z_end)
        def _():
            z_up(c).start()

    def z_one(c):
        @pl.when(jnp.logical_not(z_end))
        def _():
            own, tot, _ = zrefs(c)
            z_up(c).wait_recv()
            own[...] = (own[...].astype(F32) + tot[...].astype(F32)).astype(BF)
            z_across(c).start()

    def z_two(c):
        @pl.when(jnp.logical_not(z_end))
        def _():
            own, tot, mid = zrefs(c)
            z_across(c).wait_recv()
            tot[...] = (own[...].astype(F32) + mid[...].astype(F32)).astype(BF)
            z_down(c).start()

    def z_finish(c):
        @pl.when(z_end)
        def _():
            if not Z_IN <= c < Z_OUT:
                z_down(c).wait_recv()

    def z_sent():
        for i, k in enumerate(kinds):
            own, tot = getattr(R, "zown_" + k), getattr(R, "zsum_" + k)
            all_of(own, R.z_s.at[i, 0], R.z_r.at[0, 0]).wait_send()

            @pl.when(jnp.logical_not(z_end))
            def _():
                all_of(tot, R.z_s.at[i, 1], R.z_r.at[0, 0]).wait_send()

    def vec_copy(e):
        to, _ = dev(c32(e // 2), e % 2)
        return rcopy(R.vec, R.vec_all.at[me], R.vec_s.at[0], R.vec_s.at[1], to)

    def qkv_copy(e, j, part, sems):
        to, at = dev(c32(e // 2), e % 2)
        w = (R.wq, R.wk, R.wv)[j]
        return rcopy(w.at[part, lanes(at, W)], R.wqkv.at[me, part, pl.ds(j * W, W)], sems.at[0], sems.at[1], to)

    def win_copy(e, part, sems):
        to, at = dev(c32(e // 2), e % 2)
        return rcopy(R.wi.at[part, lanes(at, FW)], R.win.at[me, part], sems.at[0], sems.at[1], to)

    def along(i, k, way):
        sign = 1 if way == 0 else -1
        q, to = dp - sign * k, lax.rem(dp + sign + 4, 4)
        part = (R.wqkv, R.win)[i].at[:, share(q)]
        return rcopy(part, part, R.along_s.at[i, way, k], R.along_r.at[i, way, k], (to, blk, head))

    def along_do(i, k, act):
        for way, sends, gets in (
            (0, (dp <= 2) & (dp >= k), dp >= k + 1),
            (1, (dp >= 1) & (dp + k <= 3), dp + k <= 2),
        ):
            @pl.when(gets if act == 1 else sends)
            def _():
                step = along(i, k, way)
                (step.start, step.wait_recv, step.wait_send)[act]()

    def along_send(i, k):
        along_do(i, k, 0)

    def along_got(i, k):
        along_do(i, k, 1)

    def along_sent(i):
        for k in range(3):
            along_do(i, k, 2)

    far_first = (6, 7, 2, 3, 4, 5, 1)
    with jax.named_scope("start_copies"):
        for part, sems in ((share(dp), R.qshare_s), (half[0], R.qkv_s)):
            for e in far_first:
                for j in range(3):
                    qkv_copy(e, j, part, sems).start()
        local[0].wait()
        for st in (0, 1):
            ag_start(tok_all, 0, st)
        for cp in small:
            cp.wait()
        vecs = [x[...].astype(F32).reshape(1, T) for x in small_v[1:7]]
        vecs.append(R.ids_v[0:1, lanes(head, T)].astype(F32))
        R.vec[...] = jnp.concatenate(vecs + [jnp.zeros((1, T), F32)], 0)
        R.vec_all[me] = R.vec[...]
        for e in far_first:
            vec_copy(e).start()

    with jax.named_scope("wait_qkv_weights"):
        own = R.wqkv.at[me, pl.ds(0, T // 8)]
        pltpu.make_async_copy(own, own, R.loc.at[7]).wait()
        all_of(R.wqkv.at[seven, pl.ds(0, T // 8)], R.qshare_s.at[0], R.qshare_s.at[1]).wait()
        along_send(0, 0)
        along_got(0, 0)
        along_send(0, 1)
        ag_near(tok_all, 0, 0)
        along_got(0, 1)
        along_send(0, 2)
        ag_near(tok_all, 0, 1)
        ag_far(tok_all, 0, 0)
        for e in far_first:
            win_copy(e, share(dp), R.share_s).start()
        own = R.wqkv.at[me, half[0]]
        pltpu.make_async_copy(own, own, R.loc.at[5]).wait()
        all_of(R.wqkv.at[seven, half[0]], R.qkv_s.at[0], R.qkv_s.at[1]).wait()
        along_got(0, 2)
        along_sent(0)

    def qkv_step(p):
        if p == by_x:
            ag_far(tok_all, 0, 1)
            for e in far_first:
                win_copy(e, half[0], R.win_s).start()
        for st in (0, 1):
            ag_have(tok_all, 0, st, p)
        a, b, x = pair(tok_all, c32(p))
        y = mm(x, rows(R.wqkv), NN)
        qq = ((y[:, :W] + R.bq_v[...].astype(F32).reshape(1, W)) * 0.125).astype(BF)
        kk = y[:, W:2 * W].astype(BF)
        vv = (y[:, 2 * W:] + R.bv_v[...].astype(F32).reshape(1, W)).astype(BF)
        for at, sl in ((a, slice(0, T)), (b, slice(T, 2 * T))):
            R.q[at], R.k[at], R.v[at] = qq[sl], kk[sl], vv[sl]

    with jax.named_scope("project_qkv"):
        for p in range(4):
            qkv_step(p)

    with jax.named_scope("vectors"):
        all_of(R.vec_all.at[seven], R.vec_s.at[0], R.vec_s.at[1]).wait_recv()
        for s in range(8):
            v = R.vec_all[s]
            R.vfull[:, s * T:(s + 1) * T] = v
            ids = jnp.broadcast_to(v[6:7], (T, T)).T
            R.segk[s] = jnp.where(ids < 0, -2.0, ids)

    for i in (1, 2, 3, 4):
        local[i].wait()

    def head_mask(h, like):
        lane = lax.broadcasted_iota(jnp.int32, like.shape, 1)
        return jnp.where(lax.div(lane, HD) == h, like, jnp.zeros_like(like))

    heads = W // HD

    far, near_a, near_b, here = [
        [(0, by_both), (1, by_both)], [(0, by_y), (0, by_x)], [(1, by_y), (1, by_x)], [(0, 0), (1, 0)],
    ]

    def rows_of(buf, items):
        found = [half_pair(buf, c32(p), st) for st, p in items]
        return [(a, b) for a, b, _ in found], jnp.concatenate([x for _, _, x in found], 0)

    def put_rows(buf, items, places, value, lane=slice(None)):
        for i, ((st, _), (a, b)) in enumerate(zip(items, places, strict=True)):
            buf[a, half[st], lane] = value[i * T:i * T + T // 2]
            buf[b, half[st], lane] = value[i * T + T // 2:(i + 1) * T]

    def put_parts(r, items, part):
        for i, (st, p) in enumerate(items):
            rs_put(r, st, p, part[i * T:i * T + T // 2], part[i * T + T // 2:(i + 1) * T])

    def ids_of(items, places):
        return jnp.concatenate(
            [
                R.vec_all[at, 6:7, st * (T // 2):(st + 1) * (T // 2)]
                for (st, _), both in zip(items, places, strict=True)
                for at in both
            ],
            1,
        )

    def attend_step(slot, items, between):
        places, qp = rows_of(R.q, items)
        segq = ids_of(items, places)
        segk = rows(R.segk)
        allowed = jnp.concatenate([segk, segk], 1) == segq
        kk = rows(R.k)
        outs = []
        scores = [mm(kk, head_mask(h, qp), NT) for h in range(heads)]
        for h in range(heads):
            s = jnp.where(allowed, scores[h], -1e30)
            ex = jnp.exp(s - jnp.max(s, 0, keepdims=True))
            total = jnp.maximum(jnp.sum(ex, 0, keepdims=True), 1.0)
            pt = (ex * jnp.where(segq >= 0, 1.0 / total, 0.0)).astype(BF)
            R.pt[h, slot] = pt
            outs.append(mm(R.vt[h * HD:(h + 1) * HD, :], pt, NN))
            if h == 0:
                between()
        ct = jnp.concatenate(outs, 0).T.astype(BF)
        put_rows(R.ctx, items, places, ct)
        put_parts(0, items, mm(ct, R.wo_v[...], NN))

    def after_far():
        local_share.wait()
        all_of(R.win.at[seven, pl.ds(0, T // 8)], R.share_s.at[0], R.share_s.at[1]).wait()
        along_send(1, 0)

    def after_near_a():
        rs_combine_pair(0, by_both)

    def after_near_b():
        rs_combine(0, 0, by_y)
        rs_combine(0, 0, by_x)
        along_got(1, 0)
        along_send(1, 1)

    def after_here():
        rs_combine(0, 1, by_y)
        rs_combine(0, 1, by_x)
        rs_relay(0, 1)

    with jax.named_scope("attend"):
        R.vt[...] = rows(R.v).T
        attend_step(0, far, after_far)
        attend_step(1, near_a, after_near_a)
        attend_step(2, near_b, after_near_b)
        rs_relay(0, 0)
        attend_step(3, here, after_here)
        along_got(1, 1)
        along_send(1, 2)

    with jax.named_scope("first_norm"):
        for st in (0, 1):
            rs = rs_final(0, st)
            h1 = tok_all[me, half[st]].astype(F32) + rs + R.vfull[0:1]
            n1, r1 = norm_parts(h1)
            y1 = n1 * R.vfull[2:3] + R.vfull[3:4]
            R.n1[half[st]], R.y1[half[st]] = n1, y1
            R.r1[half[st]] = jnp.broadcast_to(r1, (T // 2, 128))
            y1_all[me, half[st]] = y1.astype(BF)
            ag_start(y1_all, 1, st)

    with jax.named_scope("wait_hidden_weights"):
        all_of(R.win.at[seven, half[0]], R.win_s.at[0], R.win_s.at[1]).wait()
        along_got(1, 2)
        along_sent(1)

    def hidden_step(items):
        places, x = rows_of(y1_all, items)
        z = mm(x, rows(R.win), NN) + R.bi_v[...].astype(F32).reshape(1, FW)
        cdf = 0.5 * (1.0 + lax.erf(z * 0.7071067811865476))
        low = (z * cdf).astype(BF)
        slope = cdf + z * (jnp.exp(-0.5 * z * z) * 0.3989422804014327)
        put_parts(1, items, mm(low, R.wb_v[...], NN))
        put_rows(R.hid, items, places, low)
        put_rows(R.slope, items, places, slope)

    with jax.named_scope("hidden"):
        ag_near(y1_all, 1, 0)
        for st in (0, 1):
            ag_have(y1_all, 1, st, 0)
        hidden_step(here)
        for p in (by_y, by_x):
            ag_have(y1_all, 1, 0, p)
        hidden_step(near_a)
        ag_near(y1_all, 1, 1)
        ag_far(y1_all, 1, 0)
        for p in (by_y, by_x):
            ag_have(y1_all, 1, 1, p)
            rs_combine(1, 0, p)
        hidden_step(near_b)
        ag_far(y1_all, 1, 1)
        ag_have(y1_all, 1, 0, by_both)
        hidden_step(far[:1])
        for p in (by_y, by_x):
            rs_combine(1, 1, p)
        ag_have(y1_all, 1, 1, by_both)
        rs_combine(1, 0, by_both)
        hidden_step(far[1:])
        R.kt[...] = rows(R.k).T
        rs_combine(1, 1, by_both)

    with jax.named_scope("second_norm"):
        rs_relay(1, 0)
        rs_relay(1, 1)
        for st in (0, 1):
            rs = rs_final(1, st)
            h2 = R.y1[half[st]] + rs + R.vfull[1:2]
            n2, r2 = norm_parts(h2)
            gain = R.vfull[4:5]
            R.out_v[half[st]] = (n2 * gain + R.vfull[5:6]).astype(BF)
            cot = R.cot_v[half[st]].astype(F32)
            dh2 = norm_back(cot * gain, n2, r2)
            R.dh2[half[st]] = dh2
            df_all[me, half[st]] = dh2.astype(BF)
            ag_start(df_all, 2, st)
            sums = jnp.concatenate([colsum(cot * n2), colsum(cot)], 0)
            R.sv[0:2, :] = sums if st == 0 else R.sv[0:2, :] + sums
        put_out.start()

    def grad_back(i):
        x = R.hid[:, :, i * T:(i + 1) * T].reshape(8 * T, T)
        R.zown_b[i] = mm(x, rows(df_all), TN).astype(BF)
        for c in range(5) if i == 0 else (2 * i + 3, 2 * i + 4):
            z_produce(c)

    def hidden_back_step(p):
        ag_wait(df_all, 2, p)
        if p == by_both:
            grad_back(0)
        a, b, x = pair(df_all, c32(p))
        slope = jnp.concatenate([R.slope[a], R.slope[b]], 0)
        dz = (mm(x, R.wb_v[...], NT) * slope).astype(BF)
        R.dz[a], R.dz[b] = dz[:T], dz[T:]
        if p > 1:
            rs_combine_pair(2, p - 1)
        rs_put_pair(2, p, mm(dz, rows(R.win), NT))

    with jax.named_scope("hidden_back"):
        for p in range(4):
            hidden_back_step(p)
        z_until(2.8)
        rs_combine_pair(2, 3)
        z_until(3.5)

    with jax.named_scope("grad_back"):
        for i in range(1, 4):
            grad_back(i)
        z_until(7.5)
        rs_relay(2, 0)
        z_until(8.6)
        rs_relay(2, 1)
        z_until(9.8)

    def grad_in(i):
        x = y1_all[:, :, 2 * i * T:(2 * i + 2) * T].reshape(8 * T, 2 * T)
        g = mm(x, rows(R.dz), TN).astype(BF)
        R.zown_i[2 * i], R.zown_i[2 * i + 1] = g[:T], g[T:]
        z_produce(Z_IN + 2 * i)
        z_produce(Z_IN + 2 * i + 1)

    def din_copy(t, s):
        return rcopy(R.zsum_i.at[t], R.grad_i.at[s], R.din_s.at[0], R.din_s.at[1], (dp, t // 2, t % 2))

    def z_deliver(t):
        @pl.when(z_end)
        def _():
            z_down(Z_IN + t).wait_recv()

        @pl.when(me != t)
        def _():
            din_copy(t, me).start()

        @pl.when(me == t)
        def _():
            R.grad_i[me] = R.zsum_i[t]

    with jax.named_scope("grad_in"):
        for i in range(4):
            grad_in(i)
            if i % 2:
                z_until(10.0 + i)

    with jax.named_scope("first_norm_back"):
        rs = rs_whole(2)
        dy1 = R.dh2[...] + rs
        n1 = R.n1[...]
        dh1 = norm_back(dy1 * R.vfull[2:3], n1, R.r1[:, 0:1])
        R.dh1[...] = dh1
        da_all[me] = dh1.astype(BF)
        for st in (0, 1):
            ag_start(da_all, 3, st)
        R.sv[2:3, :] = colsum(dy1 * n1)
        R.sv[3:4, :] = colsum(dy1)

    def sv_copy(e):
        to, at = dev(c32(e // 2), e % 2)
        return rcopy(R.sv.at[:, lanes(at, T)], R.sv_rcv.at[me], R.sv_s.at[0], R.sv_s.at[1], to)

    for e in far_first:
        sv_copy(e).start()
    R.sv_rcv[me] = R.sv[:, lanes(me, T)]

    z_until(13.8)

    R.dk[...] = jnp.zeros_like(R.dk)
    R.dv[...] = jnp.zeros_like(R.dv)

    def attend_back_step(slot, items, times):
        z_until(times[0])
        places, x = rows_of(da_all, items)
        _, qp = rows_of(R.q, items)
        dc = mm(x, R.wo_v[...], NT).astype(BF)
        vv = rows(R.v)
        outs = []
        for h in range(heads):
            dcm, qm = head_mask(h, dc), head_mask(h, qp)
            low = R.pt[h, slot]
            pt = low.astype(F32)
            dpt = mm(vv, dcm, NT)
            ds = (pt * (dpt - jnp.sum(pt * dpt, 0, keepdims=True))).astype(BF)
            outs.append(mm(R.kt[h * HD:(h + 1) * HD, :], ds, NN))
            R.dk[...] += mm(ds, qm, NN)
            R.dv[...] += mm(low, dcm, NN)
            z_until(times[1 + h])
        dq = jnp.concatenate(outs, 0).T.astype(BF) * 0.125
        put_rows(R.dqkv, items, places, dq, slice(0, W))

    with jax.named_scope("attend_back"):
        for st in (0, 1):
            ag_have(da_all, 3, st, 0)
        attend_back_step(3, here, (14.6, 16.0, 17.2))
        for st, slot, items, times in ((0, 1, near_a, (20.2, 21.4, 22.6)), (1, 2, near_b, (24.6, 25.8, 27.0))):
            ag_near(da_all, 3, st)
            z_until((18.0, 23.4)[st])
            if st == 1:
                ag_far(da_all, 3, 0)
            for p in (by_y, by_x):
                ag_have(da_all, 3, st, p)
            attend_back_step(slot, items, times)
        ag_far(da_all, 3, 1)
        for st in (0, 1):
            ag_have(da_all, 3, st, by_both)
        attend_back_step(0, far, (28.0, 29.2, 30.4))
        R.dqkv[:, :, W:2 * W] = R.dk[...].astype(BF).reshape(8, T, W)
        R.dqkv[:, :, 2 * W:] = R.dv[...].astype(BF).reshape(8, T, W)

    def dqkv_copy(p, flip):
        to, at = dev(p, flip)
        return rcopy(R.dqkv_snd.at[at], R.zown_w.at[me], R.dqkv_s.at[0], R.dqkv_s.at[1], to)

    def dqkv_step(p):
        a, b = dev(c32(p), 0)[1], dev(c32(p), 1)[1]
        x = jnp.concatenate([tok_all[:, :, lanes(a, T)], tok_all[:, :, lanes(b, T)]], 2).reshape(8 * T, 2 * T)
        g = mm(x, rows(R.dqkv), TN).astype(BF)
        R.dqkv_snd[b] = g[T:]
        dqkv_copy(c32(p), 1).start()
        if p == 0:
            R.zown_w[me] = g[:T]
        else:
            R.dqkv_snd[a] = g[:T]
            dqkv_copy(c32(p), 0).start()
        z_until(30.5 + 0.5 * p)

    with jax.named_scope("grad_qkv"):
        for p in range(4):
            dqkv_step(p)

    with jax.named_scope("grad_out"):
        R.zown_o[...] = mm(rows(R.ctx), rows(da_all), TN).astype(BF)
        z_produce(Z_OUT)
        z_produce(Z_OUT + 1)
        z_until(33.0)

    def input_step(p):
        if p > 1:
            rs_combine_pair(3, p - 1)
        a, b, x = pair(R.dqkv, c32(p))
        rs_put_pair(3, p, mm(x, rows(R.wqkv), NT))
        z_until((33.5, 34.0, 35.5, 37.0)[p])

    with jax.named_scope("input_back"):
        for p in range(4):
            input_step(p)
        rs_combine_pair(3, 3)
        z_until(39.0)

    with jax.named_scope("small_grads"):
        all_of(R.sv_rcv.at[seven], R.sv_s.at[0], R.sv_s.at[1]).wait_recv()
        acc = R.sv_rcv[0]
        for s in range(1, 8):
            acc = acc + R.sv_rcv[s]
        own = lanes(me, T)
        parts = [
            acc[0:4],
            colsum(rows(R.dqkv)[:, 0:W]),
            colsum(rows(R.dqkv)[:, 2 * W:]),
            colsum(da_all[:, :, own].reshape(8 * T, T)),
            colsum(df_all[:, :, own].reshape(8 * T, T)),
        ]
        dbi = colsum(rows(R.dz))
        parts += [dbi[:, i * T:(i + 1) * T] for i in range(FW // T)]
        parts.append(jnp.zeros((16 - 8 - FW // T, T), F32))
        R.zown_s[...] = jnp.concatenate(parts, 0).astype(BF)
        z_produce(Z_SMALL)
        z_until(41.0)

    with jax.named_scope("z_rest"):
        all_of(R.zown_w.at[seven], R.dqkv_s.at[0], R.dqkv_s.at[1]).wait_recv()
        for c in range(Z_QKV, Z_ALL):
            z_produce(c)
        z_until(44.5)
        rs_relay(3, 0)
        z_until(47.0)
        rs_relay(3, 1)
        z_until(50.0)
    with jax.named_scope("input_grad"):
        R.igrad_v[...] = R.dh1[...] + rs_whole(3)
        put_igrad.start()
    puts = [put_out, put_igrad]

    def put(i, src, dst):
        puts.append(pltpu.make_async_copy(src, dst, R.put_s.at[i]))
        puts[-1].start()

    def z_through(c):
        while any(second and at <= c for _, at, second in steps):
            z_until(steps[0][0])
        z_finish(c)

    with jax.named_scope("z_last"):
        for t in range(8):
            z_until(51.0 + 2 * t)
            z_deliver(t)
            if t == 1:
                for c in range(Z_IN):
                    z_through(c)
                put(2, R.zsum_b, R.gb)
        for c in range(Z_OUT, Z_QKV):
            z_through(c)
        put(4, R.zsum_o, R.go)
        put(5, R.zsum_s, R.gs)
        for t in range(7):
            z_through(Z_QKV + t)
            put(6 + t, R.zsum_w.at[t], R.gw.at[t])
        all_of(R.grad_i.at[seven], R.din_s.at[0], R.din_s.at[1]).wait()
        put(3, R.grad_i, R.gi)
        for c in (Z_ALL - 2, Z_ALL - 1):
            z_through(c)
        put(13, R.zsum_w.at[7], R.gw.at[7])

    with jax.named_scope("finish"):
        z_sent()
        for buf, r in ((tok_all, 0), (y1_all, 1), (df_all, 2), (da_all, 3)):
            ag_finish(buf, r)
        for ref, sem in (
            (R.vec_all, R.vec_s), (R.sv_rcv, R.sv_s), (R.zown_w, R.dqkv_s),
        ):
            all_of(ref.at[seven], sem.at[0], sem.at[1]).wait_send()
        for cp in puts:
            cp.wait()


def sharded_plan(
    tokens, segment_ids, cotangent,
    w_query, w_key, w_value, w_out, w_in, w_back,
    bias_query, bias_value, bias_out, bias_in, bias_back,
    first_gain, first_shift, second_gain, second_shift,
):
    tokens, cotangent = tokens[0], cotangent[0]
    T, D = tokens.shape
    W, FW = D // 8, w_in.shape[1] // 8
    ins = dict(
        tok=tokens, cot=cotangent, wq=w_query, wk=w_key, wv=w_value, wo=w_out, wi=w_in, wb=w_back, ids=segment_ids,
        bo=bias_out, bb=bias_back, g1=first_gain, s1=first_shift, g2=second_gain, s2=second_shift,
        bq=bias_query, bv=bias_value, bi=bias_in,
    )
    in_hbm = 8
    outs = dict(
        out=((T, D), BF), igrad=((T, D), F32), gb=((4, T, D), BF), gi=((8, T, FW), BF), go=((T, D), BF),
        gw=((8, T, 3 * W), BF), gs=((16, T), BF),
    )
    sums = dict(b=outs["gb"], i=outs["gi"], o=outs["go"], w=outs["gw"], s=outs["gs"])
    blocks = {k: ((8, T, D), BF) for k in ("tok_all", "y1_all", "df_all", "da_all")}
    scr = dict(
        **blocks,
        wqkv=((8, T, 3 * W), BF), win=((8, T, FW), BF), wb_v=(w_back.shape, BF), wo_v=(w_out.shape, BF),
        cot_v=((T, D), BF), vec=((8, T), F32), vec_all=((8, 8, T), F32), vfull=((8, D), F32), segk=((8, T, T), F32),
        q=((8, T, W), BF), k=((8, T, W), BF), v=((8, T, W), BF), vt=((W, 8 * T), BF), kt=((W, 8 * T), BF),
        pt=((W // HD, 4, 8 * T, 2 * T), BF), ctx=((8, T, W), BF),
        hid=((8, T, FW), BF), slope=((8, T, FW), F32), dz=((8, T, FW), BF),
        n1=((T, D), F32), r1=((T, 128), F32), y1=((T, D), F32), dh2=((T, D), F32), dh1=((T, D), F32),
        sv=((8, D), F32), sv_rcv=((8, 8, T), F32),
        keep=((4, T, D), F32), snd_c=((4, T, D), BF), snd_l=((4, T, D), BF),
        rcv_c=((4, 4, T, D), BF), rcv_l=((4, 4, T, D), BF),
        dk=((8 * T, W), F32), dv=((8 * T, W), F32), dqkv=((8, T, 3 * W), BF),
        dqkv_snd=((8, T, 3 * W), BF),
        **{z + k: v for z in ("zown_", "zsum_", "zmid_") for k, v in sums.items()}, grad_i=outs["gi"],
        out_v=outs["out"], igrad_v=outs["igrad"],
        **{k + "_v": (v.shape, v.dtype) for k, v in list(ins.items())[in_hbm:]},
    )
    sems = dict(
        ag_s=(4,), ag_r=(2, 4, 2), ag_f=(2, 4, 2), rs_s=(2,), rs_cr=(2, 4), rs_lr=(2, 4, 2),
        z_s=(5, 2), z_r=(31, 2), loc=(8,), small_s=(10,), put_s=(14,), vec_s=(2,), qkv_s=(2,), win_s=(2,), share_s=(2,), qshare_s=(2,), along_s=(2, 2, 3), along_r=(2, 2, 3), sv_s=(2,), din_s=(2,), dqkv_s=(2,),
    )
    names = list(ins) + list(outs) + list(scr) + list(sems)
    res = pl.pallas_call(
        partial(layer_kernel, names),
        out_shape=[jax.ShapeDtypeStruct(*s) for s in outs.values()],
        in_specs=[pl.BlockSpec(memory_space=pltpu.HBM)] * len(ins),
        out_specs=[pl.BlockSpec(memory_space=pltpu.HBM)] * len(outs),
        scratch_shapes=[pltpu.VMEM(*s) for s in scr.values()] + [pltpu.SemaphoreType.DMA(s) for s in sems.values()],
        compiler_params=pltpu.CompilerParams(collective_id=0, has_side_effects=True, vmem_limit_bytes=60 << 20),
        name="layer",
    )(*ins.values())
    firsts = [(T, D)] * 6 + [w_in.shape, w_back.shape]
    sizes = [T, T, T, FW, T, T, T, T, T]
    shapes = [(n, t) for n, t in zip(firsts, [BF] + [F32] * 7)] + [((n,), F32) for n in sizes]
    loaded = list(outs.values())
    stored = [((3, T, D), F32), ((T, D), F32), (w_in.shape, F32), (w_back.shape, F32)] + shapes[8:]
    final = pl.pallas_call(
        finish_kernel,
        out_shape=[jax.ShapeDtypeStruct(*s) for s in shapes],
        in_specs=[pl.BlockSpec(memory_space=pltpu.HBM)] * len(loaded),
        out_specs=[pl.BlockSpec(memory_space=pltpu.HBM)] * len(shapes),
        scratch_shapes=[pltpu.VMEM(*s) for s in loaded + stored]
        + [pltpu.SemaphoreType.DMA((len(loaded) + 8,)), pltpu.SemaphoreType.DMA((len(shapes) + 6,))],
        compiler_params=pltpu.CompilerParams(vmem_limit_bytes=60 << 20),
        name="finish",
    )(*res)
    return (final[0][None], final[1][None], *final[2:])


def finish_kernel(*refs):
    ins, outs, rest = refs[:7], refs[7:24], refs[24:]
    loaded, stored, (load_s, store_s) = rest[:7], rest[7:20], rest[20:]
    out, igrad, gb, gi, go, gw, gs = loaded
    qkv, o_o, o_i, o_b, *o_small = stored
    whole = {i: pltpu.make_async_copy(ins[i], loaded[i], load_s.at[i]) for i in (5, 4, 1, 0, 6)}
    pieces = [pltpu.make_async_copy(ins[2].at[j], gb.at[j], load_s.at[7 + j]) for j in range(4)]
    pairs = [pl.ds(2 * j, 2) for j in range(4)]
    pieces += [pltpu.make_async_copy(ins[3].at[p], gi.at[p], load_s.at[11 + j]) for j, p in enumerate(pairs)]
    for cp in pieces + list(whole.values()):
        cp.start()
    stores = []

    def store(src, dst):
        stores.append(pltpu.make_async_copy(src, dst, store_s.at[len(stores)]))
        stores[-1].start()

    T, width = gb.shape[1], gi.shape[2]
    for j in range(4):
        pieces[j].wait()
        part = pl.ds(j * T, T)
        o_b[part, :] = gb[j].astype(F32)
        store(o_b.at[part], outs[7].at[part])
    for j in range(4):
        pieces[4 + j].wait()
        for s in (2 * j, 2 * j + 1):
            o_i[:, s * width:(s + 1) * width] = gi[s].astype(F32)
        part = pl.ds(2 * j * width, 2 * width)
        store(o_i.at[:, part], outs[6].at[:, part])
    whole[5].wait()
    W = gw.shape[2] // 3
    for j in range(3):
        for s in range(8):
            qkv[j, :, s * W:(s + 1) * W] = gw[s, :, j * W:(j + 1) * W].astype(F32)
        store(qkv.at[j], outs[2 + j])
    whole[4].wait()
    o_o[...] = go[...].astype(F32)
    store(o_o, outs[5])
    whole[1].wait()
    store(igrad, outs[1])
    whole[0].wait()
    store(out, outs[0])
    whole[6].wait()
    v = gs[...].astype(F32)
    bq, bv, bo, bi, bb, g1, s1, g2, s2 = o_small
    for o, i in ((bq, 4), (bv, 5), (bo, 6), (bb, 7), (g1, 2), (s1, 3), (g2, 0), (s2, 1)):
        o[...] = v[i]
    n = v.shape[1]
    for i in range(bi.shape[0] // n):
        bi[i * n:(i + 1) * n] = v[8 + i]
    for i, o in enumerate(o_small):
        store(o, outs[8 + i])
    for cp in stores:
        cp.wait()


def pick_plan(mesh):
    group = mesh.shape["blk"] * mesh.shape["head"]
    return sharded_plan if (mesh.shape["dp"], group) == (4, 8) else general_plan


def flat_dot(left_side, right_side):
    return jnp.dot(
        left_side.reshape(-1, left_side.shape[-1]), right_side, preferred_element_type=jnp.float32
    )


def inner_dot(left_side, right_side):
    return jnp.einsum(
        "ra,rb->ab",
        left_side.reshape(-1, left_side.shape[-1]),
        right_side.reshape(-1, right_side.shape[-1]),
        preferred_element_type=jnp.float32,
    )


def layer_norm(value_rows, gain_row, shift_row):
    centre = jnp.mean(value_rows, -1, keepdims=True)
    centred = value_rows - centre
    spread = jnp.mean(centred * centred, -1, keepdims=True)
    return centred * lax.rsqrt(spread + 1e-05) * gain_row + shift_row


def head_view(array_in):
    return array_in.reshape(array_in.shape[0], array_in.shape[1], -1, HD)


def allowed_pairs(query_ids, key_ids):
    same_doc = (query_ids[:, :, None] == key_ids[:, None, :]) & (key_ids[:, None, :] >= 0)
    return same_doc[:, None]


def forward_step(state_now, arrived, local_data):
    running_max, running_sum, weighted = state_now
    key_block, value_block, key_ids = arrived
    query_block, query_ids = local_data
    scores = jnp.einsum(
        "gqhd,gkhd->ghqk",
        head_view(query_block),
        head_view(key_block),
        preferred_element_type=jnp.float32,
    )
    allowed = allowed_pairs(query_ids, key_ids)
    masked = jnp.where(allowed, scores, -1e30)
    new_max = jnp.maximum(running_max, jnp.max(masked, -1))
    exponents = jnp.where(allowed, jnp.exp(masked - new_max[..., None]), 0.0)
    running_sum = jnp.sum(exponents, -1)
    weighted = jnp.einsum(
        "ghqk,gkhd->ghqd",
        exponents.astype(jnp.bfloat16),
        head_view(value_block),
        preferred_element_type=jnp.float32,
    )
    return (new_max, running_sum, weighted)


def probabilities(query_block, key_block, query_ids, key_ids, log_sums):
    scores = jnp.einsum(
        "gqhd,gkhd->ghqk",
        head_view(query_block),
        head_view(key_block),
        preferred_element_type=jnp.float32,
    )
    allowed = allowed_pairs(query_ids, key_ids)
    masked = jnp.where(allowed, scores, -1e30)
    return jnp.where(allowed, jnp.exp(masked - log_sums.transpose(0, 2, 1)[..., None]), 0.0)


def score_grads(weights_now, grad_block, value_block, deltas):
    grad_weights = jnp.einsum(
        "gqhd,gkhd->ghqk",
        head_view(grad_block),
        head_view(value_block),
        preferred_element_type=jnp.float32,
    )
    return (weights_now * (grad_weights - deltas.transpose(0, 2, 1)[..., None])).astype(
        jnp.bfloat16
    )


def heads_to_rows(array_in):
    return array_in.transpose(0, 2, 1, 3).reshape(array_in.shape[0], array_in.shape[2], -1)


def general_plan(
    tokens,
    segment_ids,
    cotangent,
    w_query,
    w_key,
    w_value,
    w_out,
    w_in,
    w_back,
    bias_query,
    bias_value,
    bias_out,
    bias_in,
    bias_back,
    first_gain,
    first_shift,
    second_gain,
    second_shift,
):
    (
        query_full,
        key_full,
        value_full,
        out_full,
        in_full,
        back_full,
        query_bias,
        value_bias,
        out_bias,
        in_bias,
        back_bias,
        gain_one,
        shift_one,
        gain_two,
        shift_two,
    ) = (
        lax.all_gather(w_query, GROUP, axis=0, tiled=True),
        lax.all_gather(w_key, GROUP, axis=0, tiled=True),
        lax.all_gather(w_value, GROUP, axis=0, tiled=True),
        lax.all_gather(w_out, GROUP, axis=0, tiled=True),
        lax.all_gather(w_in, GROUP, axis=0, tiled=True),
        lax.all_gather(w_back, GROUP, axis=0, tiled=True),
        lax.all_gather(bias_query, GROUP, axis=0, tiled=True),
        lax.all_gather(bias_value, GROUP, axis=0, tiled=True),
        lax.all_gather(bias_out, GROUP, axis=0, tiled=True),
        lax.all_gather(bias_in, GROUP, axis=0, tiled=True),
        lax.all_gather(bias_back, GROUP, axis=0, tiled=True),
        lax.all_gather(first_gain, GROUP, axis=0, tiled=True),
        lax.all_gather(first_shift, GROUP, axis=0, tiled=True),
        lax.all_gather(second_gain, GROUP, axis=0, tiled=True),
        lax.all_gather(second_shift, GROUP, axis=0, tiled=True),
    )
    query_bias = query_bias.astype(jnp.float32)
    value_bias = value_bias.astype(jnp.float32)
    out_bias = out_bias.astype(jnp.float32)
    in_bias = in_bias.astype(jnp.float32)
    back_bias = back_bias.astype(jnp.float32)
    gain_one = gain_one.astype(jnp.float32)
    shift_one = shift_one.astype(jnp.float32)
    gain_two = gain_two.astype(jnp.float32)
    shift_two = shift_two.astype(jnp.float32)
    seq_count = tokens.shape[0]
    query_tok = (
        ((flat_dot(tokens, query_full) + query_bias) * 0.125)
        .astype(jnp.bfloat16)
        .reshape(tokens.shape)
    )
    key_tok = flat_dot(tokens, key_full).astype(jnp.bfloat16).reshape(tokens.shape)
    value_tok = (
        (flat_dot(tokens, value_full) + value_bias).astype(jnp.bfloat16).reshape(tokens.shape)
    )
    query_heads, key_heads, value_heads = (
        lax.all_to_all(query_tok, "head", split_axis=2, concat_axis=1, tiled=True),
        lax.all_to_all(key_tok, "head", split_axis=2, concat_axis=1, tiled=True),
        lax.all_to_all(value_tok, "head", split_axis=2, concat_axis=1, tiled=True),
    )
    rows_here = query_heads.shape[1]
    width_heads = query_heads.shape[2]
    heads_here = width_heads // HD
    start_state = (
        jnp.full((seq_count, heads_here, rows_here), -1e30, jnp.float32),
        jnp.zeros((seq_count, heads_here, rows_here), jnp.float32),
        jnp.zeros((seq_count, heads_here, rows_here, HD), jnp.float32),
    )
    running_max, running_sum, weighted = forward_step(
        start_state,
        (
            lax.all_gather(key_heads, "blk", axis=1, tiled=True),
            lax.all_gather(value_heads, "blk", axis=1, tiled=True),
            lax.all_gather(segment_ids, "blk", axis=1, tiled=True),
        ),
        (query_heads, segment_ids),
    )
    floored = jnp.maximum(running_sum, 1.0)
    ctx_heads = heads_to_rows(weighted / floored[..., None])
    log_sums = (running_max + jnp.log(floored)).transpose(0, 2, 1)
    ctx_tok = lax.all_to_all(
        ctx_heads.astype(jnp.bfloat16), "head", split_axis=1, concat_axis=2, tiled=True
    )
    first_sum = tokens.astype(jnp.float32) + (flat_dot(ctx_tok, out_full) + out_bias).reshape(
        tokens.shape
    )
    first_norm = layer_norm(first_sum, gain_one, shift_one)
    first_low = first_norm.astype(jnp.bfloat16)
    inner_rows = flat_dot(first_low, in_full) + in_bias
    hidden_low = jax.nn.gelu(inner_rows, approximate=False).astype(jnp.bfloat16)
    second_sum = first_norm + (flat_dot(hidden_low, back_full) + back_bias).reshape(tokens.shape)
    output_now, second_pull = jax.vjp(layer_norm, second_sum, gain_two, shift_two)
    grad_second, grad_gain_two, grad_shift_two = second_pull(cotangent.astype(jnp.float32))
    grad_branch = grad_second.astype(jnp.bfloat16)
    grad_back_bias = jnp.sum(grad_branch.astype(jnp.float32), (0, 1))
    grad_back = inner_dot(hidden_low, grad_branch)
    grad_hidden = flat_dot(grad_branch, back_full.T)
    unused_value, gelu_pull = jax.vjp(partial(jax.nn.gelu, approximate=False), inner_rows)
    grad_inner = gelu_pull(grad_hidden)[0].astype(jnp.bfloat16)
    grad_in_bias = jnp.sum(grad_inner.astype(jnp.float32), 0)
    grad_in = inner_dot(first_low, grad_inner)
    grad_first_norm = grad_second + flat_dot(grad_inner, in_full.T).reshape(tokens.shape)
    unused_norm, first_pull = jax.vjp(layer_norm, first_sum, gain_one, shift_one)
    grad_first, grad_gain_one, grad_shift_one = first_pull(grad_first_norm)
    grad_attn = grad_first.astype(jnp.bfloat16)
    grad_out_bias = jnp.sum(grad_attn.astype(jnp.float32), (0, 1))
    grad_out = inner_dot(ctx_tok, grad_attn)
    grad_ctx_tok = flat_dot(grad_attn, out_full.T).astype(jnp.bfloat16).reshape(tokens.shape)
    grad_ctx = lax.all_to_all(grad_ctx_tok, "head", split_axis=2, concat_axis=1, tiled=True)
    deltas = jnp.sum(head_view(grad_ctx).astype(jnp.float32) * head_view(ctx_heads), -1)
    key_block = lax.all_gather(key_heads, "blk", axis=1, tiled=True)
    value_block = lax.all_gather(value_heads, "blk", axis=1, tiled=True)
    key_ids = lax.all_gather(segment_ids, "blk", axis=1, tiled=True)
    weights_now = probabilities(query_heads, key_block, segment_ids, key_ids, log_sums)
    dscores = score_grads(weights_now, grad_ctx, value_block, deltas)
    grad_query_heads = jnp.einsum(
        "ghqk,gkhd->ghqd", dscores, head_view(key_block), preferred_element_type=jnp.float32
    )
    key_part = jnp.einsum(
        "ghqk,gqhd->gkhd", dscores, head_view(query_heads), preferred_element_type=jnp.float32
    )
    value_part = jnp.einsum(
        "ghqk,gqhd->gkhd",
        weights_now.astype(jnp.bfloat16),
        head_view(grad_ctx),
        preferred_element_type=jnp.float32,
    )
    both_parts = jnp.concatenate(
        [
            key_part.reshape(key_part.shape[0], key_part.shape[1], -1),
            value_part.reshape(value_part.shape[0], value_part.shape[1], -1),
        ],
        2,
    )
    grad_query_heads, pair_grads = (grad_query_heads, both_parts)
    pair_home = lax.psum_scatter(
        pair_grads.astype(jnp.bfloat16), "blk", scatter_dimension=1, tiled=True
    ).astype(jnp.float32)
    grad_key_heads = pair_home[:, :, :width_heads].astype(jnp.bfloat16)
    grad_value_heads = pair_home[:, :, width_heads:].astype(jnp.bfloat16)
    grad_query_rows = heads_to_rows(grad_query_heads).astype(jnp.bfloat16)
    grad_query_tok, grad_key_tok, grad_value_tok = (
        lax.all_to_all(grad_query_rows, "head", split_axis=1, concat_axis=2, tiled=True),
        lax.all_to_all(grad_key_heads, "head", split_axis=1, concat_axis=2, tiled=True),
        lax.all_to_all(grad_value_heads, "head", split_axis=1, concat_axis=2, tiled=True),
    )
    grad_query_tok = grad_query_tok * 0.125
    grad_inputs = grad_first + (
        flat_dot(grad_query_tok, query_full.T)
        + flat_dot(grad_key_tok, key_full.T)
        + flat_dot(grad_value_tok, value_full.T)
    ).reshape(tokens.shape)
    (
        shard_wq,
        shard_wk,
        shard_wv,
        shard_wo,
        shard_wi,
        shard_wb,
        shard_bq,
        shard_bv,
        shard_bo,
        shard_bi,
        shard_bb,
        shard_g1,
        shard_s1,
        shard_g2,
        shard_s2,
    ) = (
        lax.psum_scatter(
            inner_dot(tokens, grad_query_tok), GROUP, scatter_dimension=0, tiled=True
        ),
        lax.psum_scatter(
            inner_dot(tokens, grad_key_tok), GROUP, scatter_dimension=0, tiled=True
        ),
        lax.psum_scatter(
            inner_dot(tokens, grad_value_tok), GROUP, scatter_dimension=0, tiled=True
        ),
        lax.psum_scatter(grad_out, GROUP, scatter_dimension=0, tiled=True),
        lax.psum_scatter(grad_in, GROUP, scatter_dimension=0, tiled=True),
        lax.psum_scatter(grad_back, GROUP, scatter_dimension=0, tiled=True),
        lax.psum_scatter(
            jnp.sum(grad_query_tok.astype(jnp.float32), (0, 1)),
            GROUP,
            scatter_dimension=0,
            tiled=True,
        ),
        lax.psum_scatter(
            jnp.sum(grad_value_tok.astype(jnp.float32), (0, 1)),
            GROUP,
            scatter_dimension=0,
            tiled=True,
        ),
        lax.psum_scatter(grad_out_bias, GROUP, scatter_dimension=0, tiled=True),
        lax.psum_scatter(grad_in_bias, GROUP, scatter_dimension=0, tiled=True),
        lax.psum_scatter(grad_back_bias, GROUP, scatter_dimension=0, tiled=True),
        lax.psum_scatter(grad_gain_one, GROUP, scatter_dimension=0, tiled=True),
        lax.psum_scatter(grad_shift_one, GROUP, scatter_dimension=0, tiled=True),
        lax.psum_scatter(grad_gain_two, GROUP, scatter_dimension=0, tiled=True),
        lax.psum_scatter(grad_shift_two, GROUP, scatter_dimension=0, tiled=True),
    )
    (
        total_wq,
        total_wk,
        total_wv,
        total_wo,
        total_wi,
        total_wb,
        total_bq,
        total_bv,
        total_bo,
        total_bi,
        total_bb,
        total_g1,
        total_s1,
        total_g2,
        total_s2,
    ) = (
        lax.psum(shard_wq.astype(jnp.bfloat16), "dp").astype(jnp.float32),
        lax.psum(shard_wk.astype(jnp.bfloat16), "dp").astype(jnp.float32),
        lax.psum(shard_wv.astype(jnp.bfloat16), "dp").astype(jnp.float32),
        lax.psum(shard_wo.astype(jnp.bfloat16), "dp").astype(jnp.float32),
        lax.psum(shard_wi.astype(jnp.bfloat16), "dp").astype(jnp.float32),
        lax.psum(shard_wb.astype(jnp.bfloat16), "dp").astype(jnp.float32),
        lax.psum(shard_bq.astype(jnp.bfloat16), "dp").astype(jnp.float32),
        lax.psum(shard_bv.astype(jnp.bfloat16), "dp").astype(jnp.float32),
        lax.psum(shard_bo.astype(jnp.bfloat16), "dp").astype(jnp.float32),
        lax.psum(shard_bi.astype(jnp.bfloat16), "dp").astype(jnp.float32),
        lax.psum(shard_bb.astype(jnp.bfloat16), "dp").astype(jnp.float32),
        lax.psum(shard_g1.astype(jnp.bfloat16), "dp").astype(jnp.float32),
        lax.psum(shard_s1.astype(jnp.bfloat16), "dp").astype(jnp.float32),
        lax.psum(shard_g2.astype(jnp.bfloat16), "dp").astype(jnp.float32),
        lax.psum(shard_s2.astype(jnp.bfloat16), "dp").astype(jnp.float32),
    )
    return (
        output_now.astype(jnp.bfloat16),
        grad_inputs,
        total_wq,
        total_wk,
        total_wv,
        total_wo,
        total_wi,
        total_wb,
        total_bq,
        total_bv,
        total_bo,
        total_bi,
        total_bb,
        total_g1,
        total_s1,
        total_g2,
        total_s2,
    )


def solution(mesh):
    in_specs = (
        P("dp", GROUP, None),
        P("dp", "blk"),
        P("dp", GROUP, None),
        P(GROUP, None),
        P(GROUP, None),
        P(GROUP, None),
        P(GROUP, None),
        P(GROUP, None),
        P(GROUP, None),
        P(GROUP),
        P(GROUP),
        P(GROUP),
        P(GROUP),
        P(GROUP),
        P(GROUP),
        P(GROUP),
        P(GROUP),
        P(GROUP),
    )
    out_specs = (
        P("dp", GROUP, None),
        P("dp", GROUP, None),
        P(GROUP, None),
        P(GROUP, None),
        P(GROUP, None),
        P(GROUP, None),
        P(GROUP, None),
        P(GROUP, None),
        P(GROUP),
        P(GROUP),
        P(GROUP),
        P(GROUP),
        P(GROUP),
        P(GROUP),
        P(GROUP),
        P(GROUP),
        P(GROUP),
    )
    plan = pick_plan(mesh)
    return jax.shard_map(
        plan, mesh=mesh, in_specs=in_specs, out_specs=out_specs, check_vma=False
    )
```
